32 devices in a mesh: shard: 2 (over x), ctx: 4 (over z), tp: 4 (over y, core).
Axes of the slice: x: 2, y: 2, z: 4, core: 2. Of those that a mesh axis runs over, the one named last changes fastest.
Arguments:
- hidden_in: bfloat16 [4096, 2048], P(('shard', 'ctx'), 'tp'), may hold values from -6 to 6
- out_grad: bfloat16 [4096, 2048], P(('shard', 'ctx'), 'tp'), may hold values from -6 to 6
- seq_lengths: int32 [2, 3], P('shard'), may hold values from 1 to 1792, 2048 in all within a row
- deal_order: int32 [2, 16], P('shard'), may hold values from 0 to 15, as said below
- in_weight: bfloat16 [2048, 3, 2048], P('shard', None, 'tp'), may hold values from -0.125 to 0.125
- conv_weight: bfloat16 [3, 2048], P(None, 'tp'), may hold values from -3.5 to 3.5
- out_weight: bfloat16 [2048, 2048], P('shard', 'tp'), may hold values from -0.125 to 0.125
- norm1_gain: bfloat16 [2048], P('tp'), may hold values from 0.099609375 to 1.8984375
- norm2_gain: bfloat16 [2048], P('tp'), may hold values from 0.099609375 to 1.8984375
- gate_weight: bfloat16 [2048, 8192], P('shard', 'tp'), may hold values from -0.125 to 0.125
- up_weight: bfloat16 [2048, 8192], P('shard', 'tp'), may hold values from -0.125 to 0.125
- down_weight: bfloat16 [2048, 8192], P('shard', 'tp'), may hold values from -0.125 to 0.125
Outputs:
- block_out: bfloat16 [4096, 2048], P(('shard', 'ctx'), 'tp')
- input_grad: bfloat16 [4096, 2048], P(('shard', 'ctx'), 'tp')
- in_weight_grad: float32 [2048, 3, 2048], P('shard', None, 'tp')
- conv_weight_grad: float32 [3, 2048], P(None, 'tp')
- out_weight_grad: float32 [2048, 2048], P('shard', 'tp')
- norm1_gain_grad: float32 [2048], P('tp')
- norm2_gain_grad: float32 [2048], P('tp')
- gate_weight_grad: float32 [2048, 8192], P('shard', 'tp')
- up_weight_grad: float32 [2048, 8192], P('shard', 'tp')
- down_weight_grad: float32 [2048, 8192], P('shard', 'tp')
The draws below stay inside these ranges and needn't reach their ends.
Inputs may be any that keep to these rules, and one draw needn't show every extreme that they name: `seq_lengths`: each row sums to 2048; one entry of each row equals exactly 1792. `deal_order`: each row is a permutation; the 4 slots of each device hold exactly 1 block of every device's packed range.
All inputs are finite; a program needn't handle non-finite values.
Results may differ from the reference program's by a relative error of at most 0.012.
Values may be sent and summed in bfloat16 or wider, within the bound.
A program may use at most 320 MiB of HBM per device.

```python
import math
import jax
import jax.numpy as jnp
import numpy as np
from jax import lax

D = 2048
FF = 8192
TAPS = 3
TOK_DEV = 512
BLK = 128
NSEQ = 3
TOK_GROUP = 2048
TOKENS = 4096
NBLK = 16
CTX_BLK = 4
PEER_BLK = 1
N_SHARD = 2
N_CTX = 4


def draw_deal_order(key, part):
    key = jax.random.fold_in(key, 7)
    count = N_SHARD * N_CTX
    keys_source = jax.random.split(jax.random.fold_in(key, 1), count)
    keys_target = jax.random.split(jax.random.fold_in(key, 2), count)
    local = jnp.arange(CTX_BLK, dtype=jnp.int32)
    source_order = jax.vmap(lambda kk: jax.random.permutation(kk, local))(keys_source).reshape(N_SHARD, N_CTX, CTX_BLK)
    slot_order = jax.vmap(lambda kk: jax.random.permutation(kk, local))(keys_target).reshape(N_SHARD, N_CTX, CTX_BLK)
    source = jnp.arange(N_CTX, dtype=jnp.int32)[:, None] + 0 * local[None, :]
    target = local[None, :] // PEER_BLK + 0 * source
    within = source * PEER_BLK + local[None, :] % PEER_BLK
    slot = target[None] * CTX_BLK + slot_order[:, target, within]
    value = source[None] * CTX_BLK + source_order
    group_index = jnp.arange(N_SHARD, dtype=jnp.int32)[:, None, None] + 0 * slot
    return jnp.zeros((N_SHARD, NBLK), jnp.int32).at[group_index, slot].set(value)


def shard_levels(own_key, extent, pieces, low, top_value):
    loudness, own = 1.0, jax.random.fold_in(own_key, 6)
    for dim, parts in pieces:
        heights = jnp.exp(jax.random.uniform(jax.random.fold_in(own, dim), (parts,), jnp.float32, low / len(pieces), top_value / len(pieces)))
        loudness = loudness * jnp.repeat(heights, extent[dim] // parts).reshape([-1 if axis == dim else 1 for axis in range(len(extent))])
    return loudness


def profile(number_of, total, most, lean):
    loads = [(1 << 20) // math.isqrt(grade ** lean) + 1 for grade in range(2, number_of + 1)]
    surplus, counts = total - most - (number_of - 1), [1] * (number_of - 1)
    while surplus > 0:
        movable = [i for i in range(number_of - 1) if counts[i] < most]
        mass, budget = sum([loads[i] for i in movable]), surplus
        for i in movable:
            addition = min(most - counts[i], max(1, budget * loads[i] // mass), surplus)
            counts[i] = counts[i] + addition
            surplus = surplus - addition
    return np.array([most] + counts)


def uneven_parts(stream_key, amount, total, reach, lean):
    if amount == 2:
        one = jax.random.randint(stream_key, (), max(1, total - reach), min(reach, total - 1) + 1)
        return jnp.stack([one, total - one])
    tallies = jnp.asarray(profile(amount, total, reach, lean), jnp.int32)
    twos = (amount - 1) // 2
    donor, receiver = tallies[1:1 + 2 * twos:2], tallies[2:2 + 2 * twos:2]
    room = jnp.minimum(donor - 1, reach - receiver)
    moved = jax.random.randint(jax.random.fold_in(stream_key, 1), (twos,), 0, 1 << 20) % (room + 1)
    tallies = tallies.at[1:1 + 2 * twos:2].set(donor - moved).at[2:2 + 2 * twos:2].set(receiver + moved)
    return tallies[jax.random.permutation(jax.random.fold_in(stream_key, 2), amount)]


def scatter_about(own_key, shape, scale, limit, pieces=(), held_as=jnp.bfloat16):
    drawn = jax.random.normal(own_key, shape, jnp.float32) * scale
    if len(pieces) > 0:
        drawn = shard_levels(own_key, shape, pieces, -0.22, 0.18) * drawn
    return jnp.clip(drawn, min=-limit, max=limit).astype(held_as)


def setup_inputs(seed: int = 0) -> dict:
    keys = jax.random.split(jax.random.key(seed), 13)
    hidden_in = scatter_about(keys[0], (TOKENS, D), 1.0, 6.0, ((0, 8), (1, 4)))
    out_grad = scatter_about(keys[1], (TOKENS, D), 1.0, 6.0, ((0, 8), (1, 4)))
    seq_lengths = jax.vmap(lambda own: uneven_parts(own, NSEQ, TOK_GROUP, TOK_GROUP - TOK_DEV // 2, 0))(jax.random.split(keys[2], N_SHARD)).reshape((N_SHARD, NSEQ)).astype(jnp.int32)
    deal_order = draw_deal_order(jax.random.fold_in(keys[12], 71), 0)
    in_weight = scatter_about(keys[4], (D, 3, D), D ** -0.5, 0.125, ((0, 2), (2, 4)))
    conv_weight = scatter_about(keys[5], (TAPS, D), TAPS ** -0.5, 3.5, ((1, 4),))
    out_weight = scatter_about(keys[6], (D, D), D ** -0.5, 0.125, ((0, 2), (1, 4)))
    norm1_gain = jnp.clip(1.0 + 0.18 * jax.random.normal(keys[7], (D,), jnp.float32), 0.099609375, 1.8984375).astype(jnp.bfloat16)
    norm2_gain = jnp.clip(1.0 + 0.18 * jax.random.normal(keys[8], (D,), jnp.float32), 0.099609375, 1.8984375).astype(jnp.bfloat16)
    gate_weight = scatter_about(keys[9], (D, FF), D ** -0.5, 0.125, ((0, 2), (1, 4)))
    up_weight = scatter_about(keys[10], (D, FF), D ** -0.5, 0.125, ((0, 2), (1, 4)))
    down_weight = scatter_about(keys[11], (D, FF), (FF // 4) ** -0.5, 0.125, ((0, 2), (1, 4)))
    return dict(hidden_in=hidden_in, out_grad=out_grad, seq_lengths=seq_lengths, deal_order=deal_order, in_weight=in_weight, conv_weight=conv_weight, out_weight=out_weight, norm1_gain=norm1_gain, norm2_gain=norm2_gain, gate_weight=gate_weight, up_weight=up_weight, down_weight=down_weight)


EPS = 1e-05
PRECISE = lax.Precision.HIGHEST

@jax.custom_vjp
def low(v):
    return lax.optimization_barrier(v.astype(jnp.bfloat16)).astype(jnp.float32)

@jax.custom_vjp
def low_back(v):
    return v

def low_keep(v):
    return (low(v), None)

def low_pass(kept, grad):
    return (grad,)

def back_keep(v):
    return (v, None)

def back_low(kept, grad):
    return (low(grad),)
low.defvjp(low_keep, low_pass)
low_back.defvjp(back_keep, back_low)

def shifted(values, steps_back):
    return jnp.pad(values, ((steps_back, 0), (0, 0)))[:values.shape[0]]

def positions(lengths):
    starts = jnp.cumsum(lengths) - lengths
    where_t = jnp.arange(TOK_GROUP, dtype=jnp.int32)
    seq_begin = lax.optimization_barrier(jnp.max(jnp.where(starts[None, :] <= where_t[:, None], starts[None, :], 0), axis=1))
    return where_t - seq_begin

def rms_norm(hidden, gain):
    scale_row = lax.rsqrt(lax.optimization_barrier(jnp.mean(hidden * hidden, axis=1, keepdims=True)) + EPS)
    return hidden * scale_row * gain

def forward(hidden, in_w, conv_w, out_w, gain_one, gain_two, gate_w, up_w, down_w, position):
    first_mask = (position >= 1).astype(jnp.float32)[:, None]
    second_mask = (position >= 2).astype(jnp.float32)[:, None]
    normed = low(rms_norm(hidden, gain_one))
    projected = low_back(jnp.einsum('td,dpe->tpe', normed, in_w, precision=PRECISE))
    b_part = projected[:, 0]
    c_part = projected[:, 1]
    v_part = projected[:, 2]
    mixed = low(b_part * v_part)
    conv_out = low_back(conv_w[0] * mixed + conv_w[1] * shifted(mixed, 1) * first_mask + conv_w[2] * shifted(mixed, 2) * second_mask)
    gated = low(c_part * conv_out)
    mixer_out = low_back(jnp.dot(gated, out_w.T, precision=PRECISE))
    resid = hidden + mixer_out
    normed_two = low(rms_norm(resid, gain_two))
    gate_pre = low_back(jnp.dot(normed_two, gate_w, precision=PRECISE))
    up_pre = low_back(jnp.dot(normed_two, up_w, precision=PRECISE))
    activated = low(jax.nn.silu(gate_pre) * up_pre)
    ffn_out = low_back(jnp.dot(activated, down_w.T, precision=PRECISE))
    return resid + ffn_out

def reference(hidden_in, out_grad, seq_lengths, deal_order, in_weight, conv_weight, out_weight, norm1_gain, norm2_gain, gate_weight, up_weight, down_weight):
    weights = tuple((w.astype(jnp.float32) for w in (in_weight, conv_weight, out_weight, norm1_gain, norm2_gain, gate_weight, up_weight, down_weight)))
    groups_in = hidden_in.reshape(N_SHARD, NBLK, BLK, D)
    groups_grad = out_grad.reshape(N_SHARD, NBLK, BLK, D)

    def group_step(totals, group_item):
        x_blocks, grad_blocks, lengths, dealing = group_item
        inverse = jnp.argsort(dealing)
        x_packed = x_blocks[inverse].reshape(TOK_GROUP, D).astype(jnp.float32)
        grad_packed = grad_blocks[inverse].reshape(TOK_GROUP, D).astype(jnp.float32)
        position = positions(lengths)

        def bound_forward(hidden, *params):
            return forward(hidden, *params, position)
        result, pullback = jax.vjp(bound_forward, x_packed, *weights)
        gradients = pullback(grad_packed)
        totals = tuple((first + second for first, second in zip(totals, gradients[1:])))
        out_blocks = result.astype(jnp.bfloat16).reshape(NBLK, BLK, D)[dealing]
        back_blocks = gradients[0].astype(jnp.bfloat16).reshape(NBLK, BLK, D)[dealing]
        return (totals, (out_blocks, back_blocks))
    zeros = tuple((jnp.zeros(w.shape, jnp.float32) for w in weights))
    totals, (outs, backs) = lax.scan(group_step, zeros, (groups_in, groups_grad, seq_lengths, deal_order))
    return (outs.reshape(TOKENS, D), backs.reshape(TOKENS, D), totals[0], totals[1], totals[2], totals[3], totals[4], totals[5], totals[6], totals[7])
```

```python
import jax
import jax.numpy as jnp
from jax import lax
from jax.sharding import PartitionSpec as P

EPS = 1e-05
LOW = jnp.bfloat16
WIDE = jnp.float32
CHUNKS = 4


def shifted(value, axis, steps):
    count = lax.axis_size(axis)
    leading, last = (max(0, -steps), min(count, count - steps))
    return lax.ppermute(value, axis, [(source, source + steps) for source in range(leading, last)])


def swapped(value, axis, step):
    count = lax.axis_size(axis)
    return lax.ppermute(value, axis, [(source, source ^ step) for source in range(count)])


def matmul(left, right):
    return jnp.dot(left, right, preferred_element_type=WIDE)


def contract_rows(left, right):
    return lax.dot_general(left, right, (((0,), (0,)), ((), ())), preferred_element_type=WIDE)


def contract_cols(left, right):
    return lax.dot_general(left, right, (((1,), (1,)), ((), ())), preferred_element_type=WIDE)


def norm_back(grad_out, normed, scale_row, gain):
    scaled = grad_out * gain
    return scale_row * (scaled - normed * jnp.mean(scaled * normed, axis=1, keepdims=True))


def butterfly_sum(value, axis):
    step = 1
    while step < lax.axis_size(axis):
        value = value + swapped(value, axis, step)
        step *= 2
    return value


def sum_line(piece, rank):
    from_end = lax.ppermute(piece, "ctx", [(0, 1), (3, 2)])
    half = (piece.astype(WIDE) + from_end.astype(WIDE)).astype(LOW)
    from_middle = lax.ppermute(half, "ctx", [(1, 2), (2, 1)])
    total = (half.astype(WIDE) + from_middle.astype(WIDE)).astype(LOW)
    handed = lax.ppermute(total, "ctx", [(1, 0), (2, 3)])
    inner = jnp.logical_or(rank == 1, rank == 2)
    return jnp.where(inner, total, handed).astype(WIDE)


class Features:
    def __init__(self):
        rank = lax.axis_index("tp")
        self.rank = rank
        self.inner = rank % 2
        self.outer = rank // 2

    def gather(self, own):
        other = swapped(own, "tp", 2)
        first = self.outer == 0
        pair = jnp.stack([jnp.where(first, own, other), jnp.where(first, other, own)])
        more = swapped(pair, "tp", 1)
        even = self.inner == 0
        left, right = jnp.where(even, pair, more), jnp.where(even, more, pair)
        return jnp.concatenate([left[0], right[0], left[1], right[1]], axis=1)

    def total(self, first_half, second_half):
        even = self.inner == 0
        kept = jnp.where(even, first_half, second_half)
        sent = jnp.where(even, second_half, first_half).astype(LOW)
        pair = (kept.astype(WIDE) + swapped(sent, "tp", 1).astype(WIDE)).astype(LOW)
        both = (pair.astype(WIDE) + swapped(pair, "tp", 2).astype(WIDE)).astype(LOW)
        other = swapped(both, "tp", 1)
        return jnp.where(even, both, other), jnp.where(even, other, both)

    def scatter(self, full):
        rows, width = full.shape
        blocks = full.reshape(rows, 2, 2, width // 4)
        even = self.inner == 0
        kept = jnp.where(even, blocks[:, :, 0], blocks[:, :, 1])
        sent = jnp.where(even, blocks[:, :, 1], blocks[:, :, 0]).astype(LOW)
        pair = kept.astype(WIDE) + swapped(sent, "tp", 1).astype(WIDE)
        first = self.outer == 0
        mine = jnp.where(first, pair[:, 0], pair[:, 1])
        away = jnp.where(first, pair[:, 1], pair[:, 0]).astype(LOW)
        return mine + swapped(away, "tp", 2).astype(WIDE)

    def own(self, full, axis):
        width = full.shape[axis] // lax.axis_size("tp")
        return lax.dynamic_slice_in_dim(full, self.rank * width, width, axis)


class Shards:
    def __init__(self, tp):
        self.count = lax.axis_size("shard")
        self.rank = lax.axis_index("shard")
        self.ctx_rank = lax.axis_index("ctx")
        self.tp = tp
        self.paired = self.count == 2

    def weight(self, rows, direct):
        if not self.paired:
            return (lax.all_gather(rows, "shard", axis=0, tiled=True),)
        parts = []
        if direct < rows.shape[0]:
            share = (rows.shape[0] - direct) // lax.axis_size("ctx")
            part = lax.dynamic_slice_in_dim(rows, direct + self.ctx_rank * share, share, 0)
            parts.append(lax.all_gather(swapped(part, "shard", 1), "ctx", axis=0, tiled=True))
        if direct > 0:
            parts.insert(0, swapped(rows[:direct], "shard", 1))
        other = parts[0] if len(parts) == 1 else jnp.concatenate(parts, axis=0)
        return (rows, other)

    def split(self, full):
        if not self.paired:
            return (full,)
        width = full.shape[1] // 2
        return (
            lax.dynamic_slice_in_dim(full, self.rank * width, width, 1),
            lax.dynamic_slice_in_dim(full, (1 - self.rank) * width, width, 1),
        )

    def join(self, parts):
        if not self.paired:
            return parts[0]
        first = self.rank == 0
        return jnp.concatenate(
            [jnp.where(first, parts[0], parts[1]), jnp.where(first, parts[1], parts[0])], axis=1
        )

    def halves(self, parts):
        if self.paired:
            return parts
        return jnp.split(parts[0], 2, axis=1)

    def joined(self, halves):
        if self.paired:
            return self.join(halves)
        return jnp.concatenate(halves, axis=1)

    def columns(self, full):
        if not self.paired:
            return lax.all_to_all(full, "shard", split_axis=1, concat_axis=0, tiled=True)
        own, other = self.split(full)
        width = own.shape[1] // 2
        part = lax.dynamic_slice_in_dim(other, self.tp.inner * width, width, 1)
        got = swapped(part, "shard", 1)
        rest = swapped(got, "tp", 1)
        even = self.tp.inner == 0
        peer = jnp.concatenate([jnp.where(even, got, rest), jnp.where(even, rest, got)], axis=1)
        return jnp.concatenate([own, peer], axis=0)

    def tokens(self, own):
        if not self.paired:
            return lax.all_gather(own, "shard", axis=0, tiled=True)
        return jnp.concatenate([own, swapped(own, "shard", 1)], axis=0)

    def own_total(self, product):
        if not self.paired:
            return lax.psum_scatter(product, "shard", scatter_dimension=0, tiled=True)
        rows = product.shape[0] // 2
        return product[:rows] + swapped(product[rows:].astype(LOW), "shard", 1).astype(WIDE)

    def own_tokens(self, product):
        if not self.paired:
            return lax.all_to_all(product.astype(LOW), "shard", split_axis=0, concat_axis=1, tiled=True)
        rows = product.shape[0] // 2
        return self.join([product[:rows].astype(LOW), swapped(product[rows:].astype(LOW), "shard", 1)])


def on_device(
    hidden_in,
    out_grad,
    seq_lengths,
    deal_order,
    in_weight,
    conv_weight,
    out_weight,
    norm1_gain,
    norm2_gain,
    gate_weight,
    up_weight,
    down_weight,
):
    ctx_size = lax.axis_size("ctx")
    ctx_rank = lax.axis_index("ctx")
    tp = Features()
    shards = Shards(tp)
    row_count, col_count = hidden_in.shape
    hidden_count = gate_weight.shape[1]
    weight_rows = in_weight.shape[0]
    per_dev = deal_order.shape[1] // ctx_size
    per_peer = per_dev // ctx_size
    block_rows = row_count // per_dev
    dealing = deal_order[0].reshape(ctx_size, per_dev)
    own_blocks = lax.dynamic_index_in_dim(dealing, ctx_rank, 0, keepdims=False)
    send_order = jnp.argsort(own_blocks // per_dev, stable=True)
    wanted = jnp.where(dealing // per_dev == ctx_rank, 0, 1)
    chosen = jnp.argsort(wanted, axis=1, stable=True)[:, :per_peer]
    targets = (jnp.take_along_axis(dealing, chosen, 1) % per_dev).reshape(-1)
    placing = jnp.argsort(targets)
    returning = jnp.argsort(send_order)

    def reorder(values, index):
        blocks = values.reshape(per_dev, block_rows, values.shape[1])
        return blocks[index].reshape(row_count, values.shape[1])

    def to_packed(values):
        got = lax.all_to_all(
            reorder(values, send_order), "ctx", split_axis=0, concat_axis=0, tiled=True
        )
        return reorder(got, placing)

    def to_dealt(values):
        got = lax.all_to_all(
            reorder(values, targets), "ctx", split_axis=0, concat_axis=0, tiled=True
        )
        return reorder(got, returning)

    in_flat = in_weight.reshape(weight_rows, -1)
    in_w = shards.weight(in_flat, weight_rows // 4)
    x_packed = to_packed(hidden_in)
    gains = tp.gather(jnp.stack([norm1_gain, norm2_gain])).astype(WIDE)
    gain_one, gain_two = gains[0], gains[1]
    x_full = tp.gather(x_packed)
    out_w = shards.weight(out_weight, weight_rows)
    cot_full = tp.gather(to_packed(out_grad))

    width = hidden_count // CHUNKS

    def chunk(weight, index):
        return weight[:, index * width : (index + 1) * width]

    directs = [0, 0, weight_rows, weight_rows]
    gate_w, up_w = [], []
    for index in range(CHUNKS):
        gate_w.append(shards.weight(chunk(gate_weight, index), directs[index]))
        up_w.append(shards.weight(chunk(up_weight, index), directs[index]))

    lengths = seq_lengths[0]
    starts = jnp.cumsum(lengths) - lengths
    where_t = ctx_rank * row_count - 2 + jnp.arange(row_count + 4, dtype=jnp.int32)
    seq_begin = jnp.max(jnp.where(starts[None, :] <= where_t[:, None], starts[None, :], 0), axis=1)
    position = where_t - seq_begin
    first_own = (position[2 : row_count + 2] >= 1).astype(WIDE)[:, None]
    second_own = (position[2 : row_count + 2] >= 2).astype(WIDE)[:, None]
    first_next = (position[3 : row_count + 3] >= 1).astype(WIDE)[:, None]
    second_next = (position[4 : row_count + 4] >= 2).astype(WIDE)[:, None]

    x_float = x_full.astype(WIDE)
    scale_one = lax.rsqrt(jnp.mean(x_float * x_float, axis=1, keepdims=True) + EPS)
    normed_one = x_float * scale_one
    h_one = (normed_one * gain_one).astype(LOW)
    projected = sum(matmul(part, w) for part, w in zip(shards.split(h_one), in_w))
    b_part = projected[:, :col_count]
    c_part = projected[:, col_count : 2 * col_count]
    v_part = projected[:, 2 * col_count :]
    mixed = (b_part * v_part).astype(LOW)
    rim = shifted(mixed[-2:], "ctx", 1)
    extended = jnp.concatenate([rim, mixed], axis=0).astype(WIDE)
    conv_taps = conv_weight.astype(WIDE)
    prev_one = extended[1 : row_count + 1] * first_own
    prev_two = extended[0:row_count] * second_own
    mixed_float = extended[2:]
    conv_out = conv_taps[0] * mixed_float + conv_taps[1] * prev_one + conv_taps[2] * prev_two
    gated = (c_part * conv_out).astype(LOW)
    mixer_parts = [contract_cols(gated, w) for w in out_w]
    mixer_out = shards.joined(tp.total(*shards.halves(mixer_parts)))
    resid = x_float + mixer_out.astype(WIDE)
    scale_two = lax.rsqrt(jnp.mean(resid * resid, axis=1, keepdims=True) + EPS)
    normed_two = resid * scale_two
    h_two = (normed_two * gain_two).astype(LOW)
    h_two_parts = shards.split(h_two)

    cot_cols = shards.columns(cot_full)
    h_two_cols = shards.columns(h_two)
    h_one_cols = shards.columns(h_one)

    down_parts, gate_parts, up_parts = [], [], []
    ffn = None
    dh_parts = [None] * len(h_two_parts)
    for index in range(CHUNKS):
        down_w = chunk(down_weight, index)
        gate_pre = sum(matmul(part, w) for part, w in zip(h_two_parts, gate_w[index]))
        up_pre = sum(matmul(part, w) for part, w in zip(h_two_parts, up_w[index]))
        d_act = shards.own_total(matmul(cot_cols, down_w))
        sigmoid_gate = jax.nn.sigmoid(gate_pre)
        silu_gate = gate_pre * sigmoid_gate
        activated = (silu_gate * up_pre).astype(LOW)
        d_gate = (d_act * up_pre * sigmoid_gate * (1.0 + gate_pre * (1.0 - sigmoid_gate))).astype(LOW)
        d_up = (d_act * silu_gate).astype(LOW)
        act_all = shards.tokens(activated)
        d_gate_all = shards.tokens(d_gate)
        d_up_all = shards.tokens(d_up)
        down_parts.append(sum_line(contract_rows(cot_cols, act_all).astype(LOW), ctx_rank))
        gate_parts.append(sum_line(contract_rows(h_two_cols, d_gate_all).astype(LOW), ctx_rank))
        up_parts.append(sum_line(contract_rows(h_two_cols, d_up_all).astype(LOW), ctx_rank))
        term = contract_cols(act_all, down_w)
        ffn = term if ffn is None else ffn + term
        for place in range(len(dh_parts)):
            term = contract_cols(d_gate, gate_w[index][place]) + contract_cols(d_up, up_w[index][place])
            dh_parts[place] = term if dh_parts[place] is None else dh_parts[place] + term
    down_total = jnp.concatenate(down_parts, axis=1)
    gate_total = jnp.concatenate(gate_parts, axis=1)
    up_total = jnp.concatenate(up_parts, axis=1)

    ffn_own = tp.scatter(shards.own_tokens(ffn))
    block_out = (tp.own(resid, 1) + ffn_own).astype(LOW)
    block_dealt = to_dealt(block_out)

    dh_two = shards.joined(tp.total(*shards.halves(dh_parts))).astype(WIDE)
    gain_two_grad = tp.own(jnp.sum(dh_two * normed_two, axis=0), 0)
    d_resid = cot_full.astype(WIDE) + norm_back(dh_two, normed_two, scale_two, gain_two)
    d_resid_low = d_resid.astype(LOW)
    d_gated = sum(matmul(part, w) for part, w in zip(shards.split(d_resid_low), out_w))
    out_part = contract_rows(shards.columns(d_resid_low), shards.tokens(gated)).astype(LOW)
    out_total = sum_line(out_part, ctx_rank)
    d_conv = (d_gated * c_part).astype(LOW)
    d_c_part = d_gated * conv_out
    rim_back = shifted(d_conv[:2], "ctx", -1)
    d_conv_float = d_conv.astype(WIDE)
    back_ext = jnp.concatenate([d_conv, rim_back], axis=0).astype(WIDE)
    d_mixed = (
        conv_taps[0] * d_conv_float
        + conv_taps[1] * back_ext[1 : row_count + 1] * first_next
        + conv_taps[2] * back_ext[2:] * second_next
    )
    taps_grad = jnp.stack(
        [
            jnp.sum(d_conv_float * mixed_float, axis=0),
            jnp.sum(d_conv_float * prev_one, axis=0),
            jnp.sum(d_conv_float * prev_two, axis=0),
        ]
    )
    d_proj = [
        (d_mixed * v_part).astype(LOW),
        d_c_part.astype(LOW),
        (d_mixed * b_part).astype(LOW),
    ]
    in_parts = [
        sum_line(contract_rows(h_one_cols, shards.tokens(part)).astype(LOW), ctx_rank)
        for part in d_proj
    ]
    in_total = jnp.stack(in_parts, axis=1)
    d_proj_flat = jnp.concatenate(d_proj, axis=1)
    dh_one_parts = [contract_cols(d_proj_flat, w) for w in in_w]
    dh_one = shards.joined(tp.total(*shards.halves(dh_one_parts))).astype(WIDE)
    gain_one_grad = tp.own(jnp.sum(dh_one * normed_one, axis=0), 0)
    d_input = d_resid + norm_back(dh_one, normed_one, scale_one, gain_one)
    input_dealt = to_dealt(tp.own(d_input, 1).astype(LOW))

    small = jnp.concatenate([taps_grad, gain_one_grad[None], gain_two_grad[None]], axis=0)
    small_sum = butterfly_sum(butterfly_sum(small, "shard"), "ctx")
    return (
        block_dealt,
        input_dealt,
        in_total,
        small_sum[0:3],
        out_total,
        small_sum[3],
        small_sum[4],
        gate_total,
        up_total,
        down_total,
    )


def solution(mesh):
    placed = (
        P(("shard", "ctx"), "tp"),
        P(("shard", "ctx"), "tp"),
        P("shard", None),
        P("shard", None),
        P("shard", None, "tp"),
        P(None, "tp"),
        P("shard", "tp"),
        P("tp"),
        P("tp"),
        P("shard", "tp"),
        P("shard", "tp"),
        P("shard", "tp"),
    )
    return jax.shard_map(
        on_device,
        mesh=mesh,
        in_specs=placed,
        out_specs=(
            P(("shard", "ctx"), "tp"),
            P(("shard", "ctx"), "tp"),
            P("shard", None, "tp"),
            P(None, "tp"),
            P("shard", "tp"),
            P("tp"),
            P("tp"),
            P("shard", "tp"),
            P("shard", "tp"),
            P("shard", "tp"),
        ),
        check_vma=False,
    )
```

```python
import functools

import jax
import jax.numpy as jnp
from jax import lax
from jax.experimental import pallas as pl
from jax.experimental.pallas import tpu as pltpu
from jax.sharding import PartitionSpec as P

EPS = 1e-05
LOW = jnp.bfloat16
WIDE = jnp.float32
CHUNKS = 4


def shifted(value, axis, steps):
    count = lax.axis_size(axis)
    leading, last = (max(0, -steps), min(count, count - steps))
    return lax.ppermute(value, axis, [(source, source + steps) for source in range(leading, last)])


def swapped(value, axis, step):
    count = lax.axis_size(axis)
    return lax.ppermute(value, axis, [(source, source ^ step) for source in range(count)])


def matmul(left, right):
    return jnp.dot(left, right, preferred_element_type=WIDE)


def contract_rows(left, right):
    return lax.dot_general(left, right, (((0,), (0,)), ((), ())), preferred_element_type=WIDE)


def contract_cols(left, right):
    return lax.dot_general(left, right, (((1,), (1,)), ((), ())), preferred_element_type=WIDE)


def norm_back(grad_out, normed, scale_row, gain):
    scaled = grad_out * gain
    return scale_row * (scaled - normed * jnp.mean(scaled * normed, axis=1, keepdims=True))


def butterfly_sum(value, axis):
    step = 1
    while step < lax.axis_size(axis):
        value = value + swapped(value, axis, step)
        step *= 2
    return value


def sum_line(piece, rank):
    from_end = lax.ppermute(piece, "ctx", [(0, 1), (3, 2)])
    half = (piece.astype(WIDE) + from_end.astype(WIDE)).astype(LOW)
    from_middle = lax.ppermute(half, "ctx", [(1, 2), (2, 1)])
    total = (half.astype(WIDE) + from_middle.astype(WIDE)).astype(LOW)
    handed = lax.ppermute(total, "ctx", [(1, 0), (2, 3)])
    inner = jnp.logical_or(rank == 1, rank == 2)
    return jnp.where(inner, total, handed).astype(WIDE)


PIECE = 256
AHEAD = 4
SLOTS = 4
MESH = pl.DeviceIdType.MESH


def line_kernel(
    pieces, left_of, left_ref, right_ref, out_ref, peer, outer_part, middle_part, held,
    peer_send, peer_recv, in_send, outer_recv, middle_recv, out_send, out_recv, own_done,
):
    shard = lax.axis_index("shard")
    ctx = lax.axis_index("ctx")
    tokens = right_ref.shape[0]
    rows = left_ref.shape[1]
    middle = jnp.logical_or(ctx == 1, ctx == 2)
    end = jnp.logical_not(middle)
    low_side = ctx < 2
    inward = jnp.where(low_side, ctx + 1, ctx - 1)
    outward = jnp.where(ctx == 1, 0, 3)

    barrier = pltpu.get_barrier_semaphore()
    pl.semaphore_signal(barrier, inc=1, device_id={"shard": 1 - shard}, device_id_type=MESH)
    pl.semaphore_signal(barrier, inc=1, device_id={"ctx": inward}, device_id_type=MESH)

    @pl.when(middle)
    def _():
        pl.semaphore_signal(barrier, inc=1, device_id={"ctx": outward}, device_id_type=MESH)
        pl.semaphore_wait(barrier, 3)

    @pl.when(end)
    def _():
        pl.semaphore_wait(barrier, 2)

    def columns(index):
        return pl.ds(pl.multiple_of(index * PIECE, PIECE), PIECE)

    def peer_copy(index):
        return pltpu.make_async_remote_copy(
            src_ref=right_ref.at[:, columns(index)],
            dst_ref=peer.at[index],
            send_sem=peer_send.at[index],
            recv_sem=peer_recv.at[index],
            device_id={"shard": 1 - shard},
            device_id_type=MESH,
        )

    def end_copy(index):
        return pltpu.make_async_remote_copy(
            src_ref=held.at[index % SLOTS],
            dst_ref=outer_part.at[index],
            send_sem=in_send.at[index],
            recv_sem=outer_recv.at[index],
            device_id={"ctx": inward},
            device_id_type=MESH,
        )

    def middle_copy(index):
        return pltpu.make_async_remote_copy(
            src_ref=held.at[index % SLOTS],
            dst_ref=middle_part.at[index],
            send_sem=in_send.at[index],
            recv_sem=middle_recv.at[index],
            device_id={"ctx": inward},
            device_id_type=MESH,
        )

    def out_copy(index):
        return pltpu.make_async_remote_copy(
            src_ref=outer_part.at[index],
            dst_ref=out_ref.at[:, columns(index)],
            send_sem=out_send.at[index],
            recv_sem=out_recv.at[index],
            device_id={"ctx": outward},
            device_id_type=MESH,
        )

    def own_copy(index):
        return pltpu.make_async_copy(
            outer_part.at[index], out_ref.at[:, columns(index)], own_done.at[index]
        )

    tile = min(256, rows)

    def product(index, start):
        lines = pl.ds(pl.multiple_of(start * tile, tile), tile)
        left = left_of(index)
        own = jnp.dot(
            left_ref[left, lines, :tokens],
            right_ref[:, columns(index)],
            preferred_element_type=WIDE,
        )
        other = jnp.dot(
            left_ref[left, lines, tokens:], peer[index], preferred_element_type=WIDE
        )
        return lines, own + other

    def finish(index):
        middle_copy(index).wait_recv()

        @pl.loop(0, rows // tile)
        def _(start):
            lines = pl.ds(pl.multiple_of(start * tile, tile), tile)
            total = held[index % SLOTS, lines].astype(WIDE) + middle_part[index, lines].astype(WIDE)
            outer_part[index, lines] = total.astype(LOW)

        out_copy(index).start()
        own_copy(index).start()

    for index in range(min(AHEAD, pieces)):
        peer_copy(index).start()

    @pl.loop(0, pieces)
    def _(index):
        @pl.when(index + AHEAD < pieces)
        def _():
            peer_copy(index + AHEAD).start()

        @pl.when(index >= SLOTS)
        def _():
            end_copy(index - SLOTS).wait_send()

        peer_copy(index).wait_recv()

        @pl.when(end)
        def _():
            @pl.loop(0, rows // tile)
            def _(start):
                lines, value = product(index, start)
                held[index % SLOTS, lines] = value.astype(LOW)

            end_copy(index).start()

        @pl.when(middle)
        def _():
            end_copy(index).wait_recv()

            @pl.loop(0, rows // tile)
            def _(start):
                lines, value = product(index, start)
                value = value + outer_part[index, lines].astype(WIDE)
                held[index % SLOTS, lines] = value.astype(LOW)

            middle_copy(index).start()

            @pl.when(index >= 1)
            def _():
                finish(index - 1)

    @pl.when(middle)
    def _():
        finish(pieces - 1)

    @pl.loop(0, pieces)
    def _(index):
        peer_copy(index).wait_send()

        @pl.when(index >= pieces - SLOTS)
        def _():
            end_copy(index).wait_send()

        @pl.when(middle)
        def _():
            out_copy(index).wait_send()
            own_copy(index).wait()

        @pl.when(end)
        def _():
            out_copy(index).wait_recv()


def line_grads(lefts, rights, identity):
    left = jnp.stack([value.T for value in lefts])
    right = jnp.concatenate(rights, axis=1)
    tokens, width = right.shape
    rows = left.shape[1]
    pieces = width // PIECE
    first = rights[0].shape[1] // PIECE

    def left_of(index):
        return jnp.where(index < first, 0, 1)

    flops = 4 * tokens * rows * width
    dma = pltpu.SemaphoreType.DMA
    return pl.pallas_call(
        functools.partial(line_kernel, pieces, left_of),
        out_shape=jax.ShapeDtypeStruct((rows, width), LOW),
        in_specs=[pl.BlockSpec(memory_space=pltpu.VMEM)] * 2,
        out_specs=pl.BlockSpec(memory_space=pl.ANY),
        scratch_shapes=[
            pltpu.VMEM((pieces, tokens, PIECE), LOW),
            pltpu.VMEM((pieces, rows, PIECE), LOW),
            pltpu.VMEM((pieces, rows, PIECE), LOW),
            pltpu.VMEM((SLOTS, rows, PIECE), LOW),
        ]
        + [dma((pieces,)) for _ in range(8)],
        compiler_params=pltpu.CompilerParams(
            collective_id=identity, has_side_effects=True, vmem_limit_bytes=56 * 1024 * 1024
        ),
        cost_estimate=pl.CostEstimate(flops=flops * 8, bytes_accessed=rows * width * 64, transcendentals=0),
    )(left, right)


class Features:
    def __init__(self):
        rank = lax.axis_index("tp")
        self.rank = rank
        self.inner = rank % 2
        self.outer = rank // 2

    def gather(self, own):
        other = swapped(own, "tp", 2)
        first = self.outer == 0
        pair = jnp.stack([jnp.where(first, own, other), jnp.where(first, other, own)])
        more = swapped(pair, "tp", 1)
        even = self.inner == 0
        left, right = jnp.where(even, pair, more), jnp.where(even, more, pair)
        return jnp.concatenate([left[0], right[0], left[1], right[1]], axis=1)

    def total(self, first_half, second_half):
        even = self.inner == 0
        kept = jnp.where(even, first_half, second_half)
        sent = jnp.where(even, second_half, first_half).astype(LOW)
        pair = (kept.astype(WIDE) + swapped(sent, "tp", 1).astype(WIDE)).astype(LOW)
        both = (pair.astype(WIDE) + swapped(pair, "tp", 2).astype(WIDE)).astype(LOW)
        other = swapped(both, "tp", 1)
        return jnp.where(even, both, other), jnp.where(even, other, both)

    def scatter(self, full):
        rows, width = full.shape
        blocks = full.reshape(rows, 2, 2, width // 4)
        even = self.inner == 0
        kept = jnp.where(even, blocks[:, :, 0], blocks[:, :, 1])
        sent = jnp.where(even, blocks[:, :, 1], blocks[:, :, 0]).astype(LOW)
        pair = kept.astype(WIDE) + swapped(sent, "tp", 1).astype(WIDE)
        first = self.outer == 0
        mine = jnp.where(first, pair[:, 0], pair[:, 1])
        away = jnp.where(first, pair[:, 1], pair[:, 0]).astype(LOW)
        return mine + swapped(away, "tp", 2).astype(WIDE)

    def total_direct(self, full):
        low = full.astype(LOW)
        total = full
        for step in (1, 2, 3):
            total = total + swapped(low, "tp", step).astype(WIDE)
        return total

    def scatter_direct(self, full):
        width = full.shape[1] // 4
        total = lax.dynamic_slice_in_dim(full, self.rank * width, width, 1)
        for step in (1, 2, 3):
            block = lax.dynamic_slice_in_dim(full, (self.rank ^ step) * width, width, 1).astype(LOW)
            total = total + swapped(block, "tp", step).astype(WIDE)
        return total

    def own(self, full, axis):
        width = full.shape[axis] // lax.axis_size("tp")
        return lax.dynamic_slice_in_dim(full, self.rank * width, width, axis)


class Shards:
    def __init__(self, tp):
        self.count = lax.axis_size("shard")
        self.rank = lax.axis_index("shard")
        self.ctx_rank = lax.axis_index("ctx")
        self.tp = tp
        self.paired = self.count == 2

    def weight(self, rows, direct):
        if not self.paired:
            return (lax.all_gather(rows, "shard", axis=0, tiled=True),)
        parts = []
        if direct < rows.shape[0]:
            share = (rows.shape[0] - direct) // lax.axis_size("ctx")
            part = lax.dynamic_slice_in_dim(rows, direct + self.ctx_rank * share, share, 0)
            parts.append(lax.all_gather(swapped(part, "shard", 1), "ctx", axis=0, tiled=True))
        if direct > 0:
            parts.insert(0, swapped(rows[:direct], "shard", 1))
        other = parts[0] if len(parts) == 1 else jnp.concatenate(parts, axis=0)
        return (rows, other)

    def split(self, full):
        if not self.paired:
            return (full,)
        width = full.shape[1] // 2
        return (
            lax.dynamic_slice_in_dim(full, self.rank * width, width, 1),
            lax.dynamic_slice_in_dim(full, (1 - self.rank) * width, width, 1),
        )

    def join(self, parts):
        if not self.paired:
            return parts[0]
        first = self.rank == 0
        return jnp.concatenate(
            [jnp.where(first, parts[0], parts[1]), jnp.where(first, parts[1], parts[0])], axis=1
        )

    def halves(self, parts):
        if self.paired:
            return parts
        return jnp.split(parts[0], 2, axis=1)

    def joined(self, halves):
        if self.paired:
            return self.join(halves)
        return jnp.concatenate(halves, axis=1)

    def columns(self, full):
        if not self.paired:
            return lax.all_to_all(full, "shard", split_axis=1, concat_axis=0, tiled=True)
        own, other = self.split(full)
        width = own.shape[1] // 2
        part = lax.dynamic_slice_in_dim(other, self.tp.inner * width, width, 1)
        got = swapped(part, "shard", 1)
        rest = swapped(got, "tp", 1)
        even = self.tp.inner == 0
        peer = jnp.concatenate([jnp.where(even, got, rest), jnp.where(even, rest, got)], axis=1)
        return jnp.concatenate([own, peer], axis=0)

    def tokens(self, own):
        if not self.paired:
            return lax.all_gather(own, "shard", axis=0, tiled=True)
        return jnp.concatenate([own, swapped(own, "shard", 1)], axis=0)

    def own_total(self, product):
        if not self.paired:
            return lax.psum_scatter(product, "shard", scatter_dimension=0, tiled=True)
        rows = product.shape[0] // 2
        return product[:rows] + swapped(product[rows:].astype(LOW), "shard", 1).astype(WIDE)

    def own_tokens(self, product):
        if not self.paired:
            return lax.all_to_all(product.astype(LOW), "shard", split_axis=0, concat_axis=1, tiled=True)
        rows = product.shape[0] // 2
        return self.join([product[:rows].astype(LOW), swapped(product[rows:].astype(LOW), "shard", 1)])


def on_device(
    hidden_in,
    out_grad,
    seq_lengths,
    deal_order,
    in_weight,
    conv_weight,
    out_weight,
    norm1_gain,
    norm2_gain,
    gate_weight,
    up_weight,
    down_weight,
):
    ctx_size = lax.axis_size("ctx")
    ctx_rank = lax.axis_index("ctx")
    tp = Features()
    shards = Shards(tp)
    row_count, col_count = hidden_in.shape
    hidden_count = gate_weight.shape[1]
    weight_rows = in_weight.shape[0]
    per_dev = deal_order.shape[1] // ctx_size
    per_peer = per_dev // ctx_size
    block_rows = row_count // per_dev
    dealing = deal_order[0].reshape(ctx_size, per_dev)
    own_blocks = lax.dynamic_index_in_dim(dealing, ctx_rank, 0, keepdims=False)
    send_order = jnp.argsort(own_blocks // per_dev, stable=True)
    wanted = jnp.where(dealing // per_dev == ctx_rank, 0, 1)
    chosen = jnp.argsort(wanted, axis=1, stable=True)[:, :per_peer]
    targets = (jnp.take_along_axis(dealing, chosen, 1) % per_dev).reshape(-1)
    placing = jnp.argsort(targets)
    returning = jnp.argsort(send_order)

    def reorder(values, index):
        blocks = values.reshape(per_dev, block_rows, values.shape[1])
        return blocks[index].reshape(row_count, values.shape[1])

    def to_packed(values):
        got = lax.all_to_all(
            reorder(values, send_order), "ctx", split_axis=0, concat_axis=0, tiled=True
        )
        return reorder(got, placing)

    def to_dealt(values):
        got = lax.all_to_all(
            reorder(values, targets), "ctx", split_axis=0, concat_axis=0, tiled=True
        )
        return reorder(got, returning)

    def weight_grads(lefts, rights, identity):
        flat = [value for group in rights for value in group]
        if shards.paired:
            summed = line_grads([group[0] for group in lefts], flat, identity)
            ends = [0]
            for value in flat:
                ends.append(ends[-1] + value.shape[1])
            return [summed[:, a:b].astype(WIDE) for a, b in zip(ends, ends[1:])]
        flat_lefts = [value for group in lefts for value in group]
        return [
            sum_line(contract_rows(left, shards.tokens(right)).astype(LOW), ctx_rank)
            for left, right in zip(flat_lefts, flat)
        ]

    in_flat = in_weight.reshape(weight_rows, -1)
    in_w = shards.weight(in_flat, weight_rows // 4)
    x_packed = to_packed(hidden_in)
    gains = tp.gather(jnp.stack([norm1_gain, norm2_gain])).astype(WIDE)
    gain_one, gain_two = gains[0], gains[1]
    x_full = tp.gather(x_packed)
    out_w = shards.weight(out_weight, weight_rows)
    cot_full = tp.gather(to_packed(out_grad))

    width = hidden_count // CHUNKS

    def chunk(weight, index):
        return weight[:, index * width : (index + 1) * width]

    directs = [0, 0, weight_rows, weight_rows]
    gate_w, up_w = [], []
    for index in range(CHUNKS):
        gate_w.append(shards.weight(chunk(gate_weight, index), directs[index]))
        up_w.append(shards.weight(chunk(up_weight, index), directs[index]))

    lengths = seq_lengths[0]
    starts = jnp.cumsum(lengths) - lengths
    where_t = ctx_rank * row_count - 2 + jnp.arange(row_count + 4, dtype=jnp.int32)
    seq_begin = jnp.max(jnp.where(starts[None, :] <= where_t[:, None], starts[None, :], 0), axis=1)
    position = where_t - seq_begin
    first_own = (position[2 : row_count + 2] >= 1).astype(WIDE)[:, None]
    second_own = (position[2 : row_count + 2] >= 2).astype(WIDE)[:, None]
    first_next = (position[3 : row_count + 3] >= 1).astype(WIDE)[:, None]
    second_next = (position[4 : row_count + 4] >= 2).astype(WIDE)[:, None]

    x_float = x_full.astype(WIDE)
    scale_one = lax.rsqrt(jnp.mean(x_float * x_float, axis=1, keepdims=True) + EPS)
    normed_one = x_float * scale_one
    h_one = (normed_one * gain_one).astype(LOW)
    projected = sum(matmul(part, w) for part, w in zip(shards.split(h_one), in_w))
    b_part = projected[:, :col_count]
    c_part = projected[:, col_count : 2 * col_count]
    v_part = projected[:, 2 * col_count :]
    mixed = (b_part * v_part).astype(LOW)
    rim = shifted(mixed[-2:], "ctx", 1)
    extended = jnp.concatenate([rim, mixed], axis=0).astype(WIDE)
    conv_taps = conv_weight.astype(WIDE)
    prev_one = extended[1 : row_count + 1] * first_own
    prev_two = extended[0:row_count] * second_own
    mixed_float = extended[2:]
    conv_out = conv_taps[0] * mixed_float + conv_taps[1] * prev_one + conv_taps[2] * prev_two
    gated = (c_part * conv_out).astype(LOW)
    mixer_parts = [contract_cols(gated, w) for w in out_w]
    mixer_out = shards.joined(tp.total(*shards.halves(mixer_parts)))
    resid = x_float + mixer_out.astype(WIDE)
    scale_two = lax.rsqrt(jnp.mean(resid * resid, axis=1, keepdims=True) + EPS)
    normed_two = resid * scale_two
    h_two = (normed_two * gain_two).astype(LOW)
    h_two_parts = shards.split(h_two)

    cot_cols = shards.columns(cot_full)
    h_two_cols = shards.columns(h_two)
    h_one_cols = shards.columns(h_one)

    acts, d_gates, d_ups = [], [], []
    dh_parts = [None] * len(h_two_parts)
    for index in range(CHUNKS):
        down_rows = chunk(down_weight, index)
        gate_pre = sum(matmul(part, w) for part, w in zip(h_two_parts, gate_w[index]))
        up_pre = sum(matmul(part, w) for part, w in zip(h_two_parts, up_w[index]))
        d_act = shards.own_total(matmul(cot_cols, down_rows))
        sigmoid_gate = jax.nn.sigmoid(gate_pre)
        silu_gate = gate_pre * sigmoid_gate
        acts.append((silu_gate * up_pre).astype(LOW))
        d_gates.append(
            (d_act * up_pre * sigmoid_gate * (1.0 + gate_pre * (1.0 - sigmoid_gate))).astype(LOW)
        )
        d_ups.append((d_act * silu_gate).astype(LOW))
        for place in range(len(dh_parts)):
            term = contract_cols(d_gates[-1], gate_w[index][place])
            term = term + contract_cols(d_ups[-1], up_w[index][place])
            dh_parts[place] = term if dh_parts[place] is None else dh_parts[place] + term
    dh_two = tp.total_direct(shards.join(dh_parts))
    down_w = shards.weight(down_weight, weight_rows)
    ffn_rights = [jnp.concatenate(parts, axis=1) for parts in (acts, d_gates, d_ups)]
    down_total, gate_total, up_total = weight_grads(
        [[cot_cols], [h_two_cols, h_two_cols]], [ffn_rights[:1], ffn_rights[1:]], 0
    )
    activated = ffn_rights[0]
    ffn_own = tp.scatter_direct(shards.join([contract_cols(activated, w) for w in down_w]))
    block_out = (tp.own(resid, 1) + ffn_own).astype(LOW)

    gain_two_grad = tp.own(jnp.sum(dh_two * normed_two, axis=0), 0)
    d_resid = cot_full.astype(WIDE) + norm_back(dh_two, normed_two, scale_two, gain_two)
    d_resid_low = d_resid.astype(LOW)
    d_gated = sum(matmul(part, w) for part, w in zip(shards.split(d_resid_low), out_w))
    d_conv = (d_gated * c_part).astype(LOW)
    d_c_part = d_gated * conv_out
    rim_back = shifted(d_conv[:2], "ctx", -1)
    d_conv_float = d_conv.astype(WIDE)
    back_ext = jnp.concatenate([d_conv, rim_back], axis=0).astype(WIDE)
    d_mixed = (
        conv_taps[0] * d_conv_float
        + conv_taps[1] * back_ext[1 : row_count + 1] * first_next
        + conv_taps[2] * back_ext[2:] * second_next
    )
    taps_grad = jnp.stack(
        [
            jnp.sum(d_conv_float * mixed_float, axis=0),
            jnp.sum(d_conv_float * prev_one, axis=0),
            jnp.sum(d_conv_float * prev_two, axis=0),
        ]
    )
    d_proj = [
        (d_mixed * v_part).astype(LOW),
        d_c_part.astype(LOW),
        (d_mixed * b_part).astype(LOW),
    ]
    d_proj_flat = jnp.concatenate(d_proj, axis=1)
    dh_one = tp.total_direct(shards.join([contract_cols(d_proj_flat, w) for w in in_w]))
    out_total, in_flat_total = weight_grads(
        [[shards.columns(d_resid_low)], [h_one_cols]], [[gated], [d_proj_flat]], 1
    )
    in_total = in_flat_total.reshape(in_weight.shape)
    gain_one_grad = tp.own(jnp.sum(dh_one * normed_one, axis=0), 0)
    d_input = d_resid + norm_back(dh_one, normed_one, scale_one, gain_one)
    dealt = to_dealt(jnp.concatenate([block_out, tp.own(d_input, 1).astype(LOW)], axis=1))
    block_dealt, input_dealt = dealt[:, :col_count], dealt[:, col_count:]

    small = jnp.concatenate([taps_grad, gain_one_grad[None], gain_two_grad[None]], axis=0)
    small_sum = butterfly_sum(butterfly_sum(small, "shard"), "ctx")
    return (
        block_dealt,
        input_dealt,
        in_total,
        small_sum[0:3],
        out_total,
        small_sum[3],
        small_sum[4],
        gate_total,
        up_total,
        down_total,
    )


def solution(mesh):
    placed = (
        P(("shard", "ctx"), "tp"),
        P(("shard", "ctx"), "tp"),
        P("shard", None),
        P("shard", None),
        P("shard", None, "tp"),
        P(None, "tp"),
        P("shard", "tp"),
        P("tp"),
        P("tp"),
        P("shard", "tp"),
        P("shard", "tp"),
        P("shard", "tp"),
    )
    return jax.shard_map(
        on_device,
        mesh=mesh,
        in_specs=placed,
        out_specs=(
            P(("shard", "ctx"), "tp"),
            P(("shard", "ctx"), "tp"),
            P("shard", None, "tp"),
            P(None, "tp"),
            P("shard", "tp"),
            P("tp"),
            P("tp"),
            P("shard", "tp"),
            P("shard", "tp"),
            P("shard", "tp"),
        ),
        check_vma=False,
    )
```

```python
import functools

import jax
import jax.numpy as jnp
from jax import lax
from jax.experimental import pallas as pl
from jax.experimental.pallas import tpu as pltpu
from jax.sharding import PartitionSpec as P

EPS = 1e-05
LOW = jnp.bfloat16
WIDE = jnp.float32
CHUNKS = 4


def shifted(value, axis, steps):
    count = lax.axis_size(axis)
    leading, last = (max(0, -steps), min(count, count - steps))
    return lax.ppermute(value, axis, [(source, source + steps) for source in range(leading, last)])


def swapped(value, axis, step):
    count = lax.axis_size(axis)
    return lax.ppermute(value, axis, [(source, source ^ step) for source in range(count)])


def matmul(left, right):
    return jnp.dot(left, right, preferred_element_type=WIDE)


def contract_rows(left, right):
    return lax.dot_general(left, right, (((0,), (0,)), ((), ())), preferred_element_type=WIDE)


def contract_cols(left, right):
    return lax.dot_general(left, right, (((1,), (1,)), ((), ())), preferred_element_type=WIDE)


def added(terms):
    return sum(term.astype(WIDE) for term in terms)


def norm_back(grad_out, normed, scale_row, gain):
    scaled = grad_out * gain
    return scale_row * (scaled - normed * jnp.mean(scaled * normed, axis=1, keepdims=True))


def butterfly_sum(value, axis):
    step = 1
    while step < lax.axis_size(axis):
        value = value + swapped(value, axis, step)
        step *= 2
    return value


def sum_line(piece, rank):
    from_end = lax.ppermute(piece, "ctx", [(0, 1), (3, 2)])
    half = (piece.astype(WIDE) + from_end.astype(WIDE)).astype(LOW)
    from_middle = lax.ppermute(half, "ctx", [(1, 2), (2, 1)])
    total = (half.astype(WIDE) + from_middle.astype(WIDE)).astype(LOW)
    handed = lax.ppermute(total, "ctx", [(1, 0), (2, 3)])
    inner = jnp.logical_or(rank == 1, rank == 2)
    return jnp.where(inner, total, handed)


PIECE = 256
AHEAD = 4
SLOTS = 4
MESH = pl.DeviceIdType.MESH


def line_kernel(pieces, left_of, swap, *refs):
    if swap:
        (left_ref, right_ref, more_ref, out_ref, more_peer), refs = refs[:5], refs[5:]
    else:
        (left_ref, right_ref, out_ref), refs = refs[:3], refs[3:]
    peer, outer_part, middle_part, held, peer_send, peer_recv, in_send, outer_recv, middle_recv = refs[:9]
    out_send, out_recv, own_done, more_send, more_recv = refs[9:]
    shard = lax.axis_index("shard")
    ctx = lax.axis_index("ctx")
    tokens = right_ref.shape[0]
    rows = left_ref.shape[1]
    middle = jnp.logical_or(ctx == 1, ctx == 2)
    end = jnp.logical_not(middle)
    low_side = ctx < 2
    inward = jnp.where(low_side, ctx + 1, ctx - 1)
    outward = jnp.where(ctx == 1, 0, 3)

    barrier = pltpu.get_barrier_semaphore()
    pl.semaphore_signal(barrier, inc=1, device_id={"shard": 1 - shard}, device_id_type=MESH)
    pl.semaphore_signal(barrier, inc=1, device_id={"ctx": inward}, device_id_type=MESH)

    @pl.when(middle)
    def _():
        pl.semaphore_signal(barrier, inc=1, device_id={"ctx": outward}, device_id_type=MESH)
        pl.semaphore_wait(barrier, 3)

    @pl.when(end)
    def _():
        pl.semaphore_wait(barrier, 2)

    def columns(index):
        return pl.ds(pl.multiple_of(index * PIECE, PIECE), PIECE)

    def peer_copy(index):
        return pltpu.make_async_remote_copy(
            src_ref=right_ref.at[:, columns(index)],
            dst_ref=peer.at[index],
            send_sem=peer_send.at[index],
            recv_sem=peer_recv.at[index],
            device_id={"shard": 1 - shard},
            device_id_type=MESH,
        )

    def end_copy(index):
        return pltpu.make_async_remote_copy(
            src_ref=held.at[index % SLOTS],
            dst_ref=outer_part.at[index],
            send_sem=in_send.at[index],
            recv_sem=outer_recv.at[index],
            device_id={"ctx": inward},
            device_id_type=MESH,
        )

    def middle_copy(index):
        return pltpu.make_async_remote_copy(
            src_ref=held.at[index % SLOTS],
            dst_ref=middle_part.at[index],
            send_sem=in_send.at[index],
            recv_sem=middle_recv.at[index],
            device_id={"ctx": inward},
            device_id_type=MESH,
        )

    def out_copy(index):
        return pltpu.make_async_remote_copy(
            src_ref=outer_part.at[index],
            dst_ref=out_ref.at[:, columns(index)],
            send_sem=out_send.at[index],
            recv_sem=out_recv.at[index],
            device_id={"ctx": outward},
            device_id_type=MESH,
        )

    def own_copy(index):
        return pltpu.make_async_copy(
            outer_part.at[index], out_ref.at[:, columns(index)], own_done.at[index]
        )

    strips = min(16, pieces)

    def more_copy(index):
        size = more_ref.shape[0] // strips
        lines = pl.ds(pl.multiple_of(index * size, size), size)
        return pltpu.make_async_remote_copy(
            src_ref=more_ref.at[lines],
            dst_ref=more_peer.at[lines],
            send_sem=more_send.at[index],
            recv_sem=more_recv.at[index],
            device_id={"shard": 1 - shard},
            device_id_type=MESH,
        )

    tile = min(256, rows)

    def product(index, start):
        lines = pl.ds(pl.multiple_of(start * tile, tile), tile)
        left = left_of(index)
        own = jnp.dot(
            left_ref[left, lines, :tokens],
            right_ref[:, columns(index)],
            preferred_element_type=WIDE,
        )
        other = jnp.dot(
            left_ref[left, lines, tokens:], peer[index], preferred_element_type=WIDE
        )
        return lines, own + other

    def finish(index):
        middle_copy(index).wait_recv()

        @pl.loop(0, rows // tile)
        def _(start):
            lines = pl.ds(pl.multiple_of(start * tile, tile), tile)
            total = held[index % SLOTS, lines].astype(WIDE) + middle_part[index, lines].astype(WIDE)
            outer_part[index, lines] = total.astype(LOW)

        out_copy(index).start()
        own_copy(index).start()

    for index in range(min(AHEAD, pieces)):
        peer_copy(index).start()

    @pl.loop(0, pieces)
    def _(index):
        @pl.when(index + AHEAD < pieces)
        def _():
            peer_copy(index + AHEAD).start()

        if swap:

            @pl.when(index < strips)
            def _():
                more_copy(index).start()

        @pl.when(index >= SLOTS)
        def _():
            end_copy(index - SLOTS).wait_send()

        peer_copy(index).wait_recv()

        @pl.when(end)
        def _():
            @pl.loop(0, rows // tile)
            def _(start):
                lines, value = product(index, start)
                held[index % SLOTS, lines] = value.astype(LOW)

            end_copy(index).start()

        @pl.when(middle)
        def _():
            end_copy(index).wait_recv()

            @pl.loop(0, rows // tile)
            def _(start):
                lines, value = product(index, start)
                value = value + outer_part[index, lines].astype(WIDE)
                held[index % SLOTS, lines] = value.astype(LOW)

            middle_copy(index).start()

            @pl.when(index >= 1)
            def _():
                finish(index - 1)

    @pl.when(middle)
    def _():
        finish(pieces - 1)

    if swap:

        @pl.loop(0, strips)
        def _(index):
            more_copy(index).wait()

    @pl.loop(0, pieces)
    def _(index):
        peer_copy(index).wait_send()

        @pl.when(index >= pieces - SLOTS)
        def _():
            end_copy(index).wait_send()

        @pl.when(middle)
        def _():
            out_copy(index).wait_send()
            own_copy(index).wait()

        @pl.when(end)
        def _():
            out_copy(index).wait_recv()


def line_grads(lefts, rights, identity, more=None):
    left = jnp.stack([value.T for value in lefts])
    right = jnp.concatenate(rights, axis=1)
    tokens, width = right.shape
    rows = left.shape[1]
    pieces = width // PIECE
    first = rights[0].shape[1] // PIECE

    def left_of(index):
        return jnp.where(index < first, 0, 1)

    flops = 4 * tokens * rows * width
    dma = pltpu.SemaphoreType.DMA
    swap = more is not None
    extra = [more] if swap else []
    out_shape = [jax.ShapeDtypeStruct((rows, width), LOW)]
    out_shape += [jax.ShapeDtypeStruct(value.shape, LOW) for value in extra]
    return pl.pallas_call(
        functools.partial(line_kernel, pieces, left_of, swap),
        out_shape=out_shape,
        in_specs=[pl.BlockSpec(memory_space=pltpu.VMEM)] * 2
        + [pl.BlockSpec(memory_space=pl.ANY) for _ in extra],
        out_specs=[pl.BlockSpec(memory_space=pl.ANY) for _ in out_shape],
        scratch_shapes=[
            pltpu.VMEM((pieces, tokens, PIECE), LOW),
            pltpu.VMEM((pieces, rows, PIECE), LOW),
            pltpu.VMEM((pieces, rows, PIECE), LOW),
            pltpu.VMEM((SLOTS, rows, PIECE), LOW),
        ]
        + [dma((pieces,)) for _ in range(10)],
        compiler_params=pltpu.CompilerParams(
            collective_id=identity, has_side_effects=True, vmem_limit_bytes=56 * 1024 * 1024
        ),
        cost_estimate=pl.CostEstimate(flops=flops * 8, bytes_accessed=rows * width * 64, transcendentals=0),
    )(left, right, *extra)


def front_kernel(
    x_blocks, cot_blocks, place, gains, first_mask, second_mask, taps,
    in_w, out_w, gate_w, up_w, down_w,
    in_peer, out_peer, gate_peer, up_peer,
    x_full, h_one, proj, mixed, conv_out, gated, mixer, h_two, cot_full, cot_peer, h_two_peer, h_one_peer, acts, dh_two,
    x_got, cot_got, out_v, rim, extended, away, pair, pair_got, both_got,
    da_own, da_send, da_got, gu_v, down_v, dh_sum, ffn_v,
    send, recv, local,
):
    shard = lax.axis_index("shard")
    ctx = lax.axis_index("ctx")
    tp = lax.axis_index("tp")
    core, outer = tp % 2, tp // 2
    core_mate = tp + 1 - 2 * core
    outer_mate = lax.rem(tp + 2, 4)
    ctx_mate = ctx + 1 - 2 * (ctx % 2)
    tokens, width = x_full.shape
    part = width // 4
    half = width // 2
    blocks, block_rows = x_blocks.shape[0], x_blocks.shape[1]
    rows = out_w.shape[0]
    own_rows = pl.ds(pl.multiple_of((ctx % 2) * (rows // 2), rows // 2), rows // 2)
    other_rows = pl.ds(pl.multiple_of((1 - ctx % 2) * (rows // 2), rows // 2), rows // 2)
    hidden = gate_w.shape[1]
    chunk = hidden // CHUNKS

    barrier = pltpu.get_barrier_semaphore()
    mates = [{"shard": 1 - shard}, {"tp": core_mate}, {"tp": outer_mate}]
    mates += [{"ctx": lax.rem(ctx + step, blocks)} for step in range(1, blocks)]
    for mate in mates:
        pl.semaphore_signal(barrier, inc=1, device_id=mate, device_id_type=MESH)
    pl.semaphore_wait(barrier, len(mates))

    names = {}

    def remote(name, src, dst, mate):
        place_of = names.setdefault(name, len(names))
        return pltpu.make_async_remote_copy(
            src_ref=src, dst_ref=dst, send_sem=send.at[place_of], recv_sem=recv.at[place_of],
            device_id=mate, device_id_type=MESH,
        )

    def columns(start, size):
        return pl.ds(pl.multiple_of(start * size, size), size)

    own_part = columns(tp, part)
    own_half, peer_half = columns(shard, half), columns(1 - shard, half)

    def deal(name, source, target, step):
        to, origin = lax.rem(ctx + step, blocks), lax.rem(ctx + blocks - step, blocks)
        out = remote(name + str(step), source.at[to], target.at[ctx], {"ctx": to})
        into = remote(name + str(step), source.at[to], target.at[origin], {"ctx": to})
        return out, into

    def gather(name, full):
        mate = columns(outer_mate, part)
        return (
            remote(name + "outer", full.at[:, own_part], full.at[:, own_part], {"tp": outer_mate}),
            remote(name + "core", full.at[:, own_part], full.at[:, own_part], {"tp": core_mate}),
            remote(name + "more", full.at[:, mate], full.at[:, mate], {"tp": core_mate}),
        )

    pieces = {}
    for index, name in enumerate("bvc"):
        column = (0, 2, 1)[index]
        pieces[name] = (in_w.at[column], in_peer.at[column])
    pieces["o"] = (out_w, out_peer)
    for index in range(CHUNKS):
        strip = pl.ds(index * chunk, chunk)
        pieces["g%d" % index] = (gate_w.at[:, strip], gate_peer.at[:, strip])
        pieces["u%d" % index] = (up_w.at[:, strip], up_peer.at[:, strip])

    def over_shard(name):
        source, target = pieces[name]
        return remote(name + "x", source.at[own_rows], target.at[own_rows], {"shard": 1 - shard})

    def over_ctx(name):
        target = pieces[name][1]
        return remote(name + "z", target.at[own_rows], target.at[own_rows], {"ctx": ctx_mate})

    def pump(name):
        over_shard(name).wait_recv()
        over_ctx(name).start()

    def load(index, source, target):
        return pltpu.make_async_copy(source, target, local.at[index])

    x_deals = [deal("x", x_blocks, x_got, step) for step in range(1, blocks)]
    cot_deals = [deal("cot", cot_blocks, cot_got, step) for step in range(1, blocks)]
    for out, _ in x_deals:
        out.start()
    for name in ("b", "v"):
        over_shard(name).start()
    own_loads = [load(index, in_w.at[index], gu_v.at[1, 0, index]) for index in range(3)]
    own_loads.append(load(3, out_w, out_v.at[0]))
    own_loads.append(load(4, down_w, down_v))
    for copy in own_loads:
        copy.start()

    def packed(source, got, deals, full):
        got[ctx] = source[ctx]
        for _, into in deals:
            into.wait_recv()
        for index in range(blocks):
            total = place[index, 0] * got[0].astype(WIDE)
            for other in range(1, blocks):
                total = total + place[index, other] * got[other].astype(WIDE)
            full[index * block_rows : (index + 1) * block_rows, own_part] = total.astype(LOW)

    pump("b")
    over_shard("c").start()
    packed(x_blocks, x_got, x_deals, x_full)
    x_outer, x_core, x_more = gather("xg", x_full)
    x_outer.start()
    x_core.start()
    for out, _ in cot_deals:
        out.start()
    pump("v")
    over_shard("o").start()
    x_outer.wait_recv()
    x_more.start()
    packed(cot_blocks, cot_got, cot_deals, cot_full)
    cot_outer, cot_core, cot_more = gather("cg", cot_full)
    cot_outer.start()
    cot_core.start()
    x_core.wait_recv()
    x_more.wait_recv()

    step = min(64, tokens)

    @pl.loop(0, tokens // step)
    def _(index):
        lines = pl.ds(pl.multiple_of(index * step, step), step)
        value = x_full[lines].astype(WIDE)
        scale = lax.rsqrt(jnp.mean(value * value, axis=1, keepdims=True) + EPS)
        h_one[lines] = (value * scale * gains[0:1]).astype(LOW)

    pump("c")
    over_shard("g0").start()

    def columns_out(name, full, got):
        strip = pl.ds(pl.multiple_of((1 - shard) * half + core * part, part), part)
        target = columns(core, part)
        first = remote(name + "x", full.at[:, strip], got.at[:, target], {"shard": 1 - shard})
        second = remote(name + "core", got.at[:, target], got.at[:, target], {"tp": core_mate})
        return first, second

    cot_first, cot_second = columns_out("cc", cot_full, cot_peer)

    tile = min(256, tokens)

    def over_tiles(body):
        @pl.loop(0, tokens // tile)
        def _(index):
            body(pl.ds(pl.multiple_of(index * tile, tile), tile))

    def project(column, name):
        target = load(column, in_peer.at[column], gu_v.at[1, 1, column])
        own_loads[column].wait()
        over_ctx(name).wait_recv()
        target.start()
        target.wait()

        def body(lines):
            proj[column, lines] = jnp.dot(
                h_one[lines, own_half], gu_v[1, 0, column], preferred_element_type=WIDE
            ) + jnp.dot(h_one[lines, peer_half], gu_v[1, 1, column], preferred_element_type=WIDE)

        over_tiles(body)

    project(0, "b")
    project(2, "v")
    edge = 16
    rim_copy = remote(
        "rim", mixed.at[pl.ds(tokens - edge, edge)], rim, {"ctx": lax.rem(ctx + 1, blocks)}
    )

    def mix(lines):
        value = (proj[0, lines] * proj[2, lines]).astype(LOW)
        mixed[lines] = value
        extended[pl.ds(lines.start + 8, tile)] = value.astype(WIDE)

    over_tiles(mix)

    @pl.when(ctx < blocks - 1)
    def _():
        rim_copy.start()

    pump("o")
    over_shard("u0").start()
    cot_outer.wait_recv()
    cot_more.start()
    project(1, "c")

    @pl.when(ctx > 0)
    def _():
        rim_copy.wait_recv()
        extended[0:8] = rim[8:16].astype(WIDE)

    @pl.when(ctx == 0)
    def _():
        extended[0:8] = jnp.zeros((8, part), WIDE)

    for start in range(0, tokens, tile):
        lines = pl.ds(start, tile)
        value = taps[0:1] * extended[pl.ds(start + 8, tile)]
        value = value + taps[1:2] * (extended[pl.ds(start + 7, tile)] * first_mask[lines])
        value = value + taps[2:3] * (extended[pl.ds(start + 6, tile)] * second_mask[lines])
        conv_out[lines] = value
        gated[lines] = (proj[1, lines] * value).astype(LOW)

    pump("g0")
    cot_core.wait_recv()
    cot_more.wait_recv()
    cot_first.start()
    out_load = load(3, out_peer, out_v.at[1])
    own_loads[3].wait()
    over_ctx("o").wait_recv()
    out_load.start()
    out_load.wait()

    def to_half(lines, which):
        return lax.dot_general(
            gated[lines], out_v[which], (((1,), (1,)), ((), ())), preferred_element_type=WIDE
        )

    stages = [pl.ds(start, tile) for start in range(0, tokens, tile)]
    hops = []
    for index, lines in enumerate(stages):
        first = remote("ma%d" % index, away.at[lines], pair_got.at[lines], {"tp": core_mate})
        second = remote("mb%d" % index, pair.at[lines], both_got.at[lines], {"tp": outer_mate})
        third = remote("mc%d" % index, mixer.at[core, lines], mixer.at[core, lines], {"tp": core_mate})
        hops.append((first, second, third))
        away[lines] = to_half(lines, 1 - core).astype(LOW)
        first.start()
    for index, lines in enumerate(stages):
        value = to_half(lines, core)
        hops[index][0].wait_recv()
        pair[lines] = (value + pair_got[lines].astype(WIDE)).astype(LOW)
        hops[index][1].start()

    pump("u0")
    over_shard("g1").start()
    cot_first.wait_recv()
    over_shard("u1").start()
    cot_second.start()
    cot_second.wait_recv()
    own_loads[4].wait()

    def da_copy(index):
        strip = pl.ds(index * chunk, chunk)
        return remote("da%d" % index, da_send.at[:, strip], da_got.at[:, strip], {"shard": 1 - shard})

    for index in range(CHUNKS):
        strip = pl.ds(index * chunk, chunk)

        def send_part(lines):
            da_send[lines, strip] = jnp.dot(
                cot_peer[lines], down_v[:, strip], preferred_element_type=WIDE
            ).astype(LOW)

        over_tiles(send_part)
    pump("g1")
    da_copy(0).start()

    def own_part_of(lines):
        for index in range(CHUNKS):
            strip = pl.ds(index * chunk, chunk)
            da_own[lines, strip] = jnp.dot(
                cot_full[lines, own_half], down_v[:, strip], preferred_element_type=WIDE
            ).astype(LOW)

    over_tiles(own_part_of)

    for index, lines in enumerate(stages):
        hops[index][1].wait_recv()
        mixer[core, lines] = (pair[lines].astype(WIDE) + both_got[lines].astype(WIDE)).astype(LOW)
        hops[index][2].start()
    for index, lines in enumerate(stages):
        hops[index][2].wait_recv()

    @pl.loop(0, tokens // step)
    def _(index):
        lines = pl.ds(pl.multiple_of(index * step, step), step)
        own = x_full[lines, own_half].astype(WIDE) + mixer[0, lines].astype(WIDE)
        other = x_full[lines, peer_half].astype(WIDE) + mixer[1, lines].astype(WIDE)
        total = jnp.sum(own * own, axis=1, keepdims=True) + jnp.sum(other * other, axis=1, keepdims=True)
        scale = lax.rsqrt(total / width + EPS)
        h_two[lines, own_half] = (own * scale * gains[1:2, own_half]).astype(LOW)
        h_two[lines, peer_half] = (other * scale * gains[1:2, peer_half]).astype(LOW)

    h_two_first, h_two_second = columns_out("hc", h_two, h_two_peer)
    h_one_first, h_one_second = columns_out("ic", h_one, h_one_peer)
    pump("u1")
    da_copy(1).start()
    later = {0: [over_shard("g2")], 1: [over_shard("u2")], 2: [over_shard("u3")], 3: [h_one_first]}

    def own_weights(index):
        strip = pl.ds(index * chunk, chunk)
        slot = index % 2
        return [
            load(5 + 4 * slot, gate_w.at[:, strip], gu_v.at[slot, 0, 0]),
            load(6 + 4 * slot, up_w.at[:, strip], gu_v.at[slot, 0, 1]),
        ]

    def peer_weights(index):
        strip = pl.ds(index * chunk, chunk)
        slot = index % 2
        return [
            load(7 + 4 * slot, gate_peer.at[:, strip], gu_v.at[slot, 1, 0]),
            load(8 + 4 * slot, up_peer.at[:, strip], gu_v.at[slot, 1, 1]),
        ]

    def results(index):
        slot = index % 2
        return [
            load(13 + 3 * slot + kind, ffn_v.at[slot, kind], acts.at[:, pl.ds(kind * hidden + index * chunk, chunk)])
            for kind in range(3)
        ]

    for copy in own_weights(0):
        copy.start()
    for index in range(CHUNKS):
        slot = index % 2
        over_ctx("g%d" % index).wait_recv()
        over_ctx("u%d" % index).wait_recv()
        for copy in peer_weights(index):
            copy.start()
        if index + 1 < CHUNKS:
            for copy in own_weights(index + 1):
                copy.start()
        da_copy(index).wait_recv()
        for copy in later[index]:
            copy.start()
        for copy in own_weights(index) + peer_weights(index):
            copy.wait()
        if index > 1:
            for copy in results(index - 2):
                copy.wait()
        strip = pl.ds(index * chunk, chunk)

        def feed(lines):
            def pre(kind):
                return jnp.dot(
                    h_two[lines, own_half], gu_v[slot, 0, kind], preferred_element_type=WIDE
                ) + jnp.dot(h_two[lines, peer_half], gu_v[slot, 1, kind], preferred_element_type=WIDE)

            gate_pre, up_pre = pre(0), pre(1)
            d_act = da_own[lines, strip].astype(WIDE) + da_got[lines, strip].astype(WIDE)
            sigmoid = jax.nn.sigmoid(gate_pre)
            silu = gate_pre * sigmoid
            ffn_v[slot, 0, lines] = (silu * up_pre).astype(LOW)
            ffn_v[slot, 1, lines] = (
                d_act * up_pre * sigmoid * (1.0 + gate_pre * (1.0 - sigmoid))
            ).astype(LOW)
            ffn_v[slot, 2, lines] = (d_act * silu).astype(LOW)

        over_tiles(feed)
        for copy in results(index):
            copy.start()
        if index == 1:
            pump("g2")
            da_copy(2).start()
            pump("u2")
            over_shard("g3").start()
        if index == 2:
            pump("g3")
            da_copy(3).start()
            pump("u3")
            h_two_first.start()

        def back(lines):
            for place_of in range(2):
                term = lax.dot_general(
                    ffn_v[slot, 1, lines], gu_v[slot, place_of, 0],
                    (((1,), (1,)), ((), ())), preferred_element_type=WIDE,
                ) + lax.dot_general(
                    ffn_v[slot, 2, lines], gu_v[slot, place_of, 1],
                    (((1,), (1,)), ((), ())), preferred_element_type=WIDE,
                )
                if index > 0:
                    term = term + dh_sum[place_of, lines]
                if index + 1 < CHUNKS:
                    dh_sum[place_of, lines] = term
                else:
                    dh_two[place_of, lines] = term.astype(LOW)

        over_tiles(back)

    h_two_first.wait_recv()
    h_two_second.start()
    h_one_first.wait_recv()
    h_one_second.start()
    for index in (CHUNKS - 2, CHUNKS - 1):
        for copy in results(index):
            copy.wait()
    h_two_second.wait_recv()
    h_one_second.wait_recv()

    for out, _ in x_deals + cot_deals:
        out.wait_send()
    for copy in (x_outer, x_core, x_more, cot_outer, cot_core, cot_more, cot_first, cot_second,
                 h_two_first, h_two_second, h_one_first, h_one_second):
        copy.wait_send()
    for name in pieces:
        over_shard(name).wait_send()
        over_ctx(name).wait_send()
    for index in range(CHUNKS):
        da_copy(index).wait_send()
    for trio in hops:
        for copy in trio:
            copy.wait_send()

    @pl.when(ctx < blocks - 1)
    def _():
        rim_copy.wait_send()


FRONT_COPIES = 64


def front(x_blocks, cot_blocks, place, gains, first_mask, second_mask, taps, in_w, out_w, gate_w, up_w, down_w):
    tokens = x_blocks.shape[0] * x_blocks.shape[1]
    part = x_blocks.shape[2]
    width = gains.shape[1]
    half = width // 2
    rows, hidden = gate_w.shape
    chunk = hidden // CHUNKS
    vmem = pl.BlockSpec(memory_space=pltpu.VMEM)
    hbm = pl.BlockSpec(memory_space=pl.ANY)
    shape = jax.ShapeDtypeStruct
    outs = [
        (shape(in_w.shape, LOW), hbm),
        (shape(out_w.shape, LOW), hbm),
        (shape(gate_w.shape, LOW), hbm),
        (shape(up_w.shape, LOW), hbm),
        (shape((tokens, width), LOW), vmem),
        (shape((tokens, width), LOW), vmem),
        (shape((3, tokens, part), WIDE), vmem),
        (shape((tokens, part), LOW), vmem),
        (shape((tokens, part), WIDE), vmem),
        (shape((tokens, part), LOW), vmem),
        (shape((2, tokens, half), LOW), vmem),
        (shape((tokens, width), LOW), vmem),
        (shape((tokens, width), LOW), vmem),
        (shape((tokens, half), LOW), vmem),
        (shape((tokens, half), LOW), vmem),
        (shape((tokens, half), LOW), vmem),
        (shape((tokens, 3 * hidden), LOW), hbm),
        (shape((2, tokens, half), LOW), vmem),
    ]
    low, wide = (lambda *dims: pltpu.VMEM(dims, LOW)), (lambda *dims: pltpu.VMEM(dims, WIDE))
    scratch = [
        low(*x_blocks.shape),
        low(*x_blocks.shape),
        low(2, rows, part),
        low(16, part),
        wide(tokens + 8, part),
        low(tokens, half),
        low(tokens, half),
        low(tokens, half),
        low(tokens, half),
        low(tokens, hidden),
        low(tokens, hidden),
        low(tokens, hidden),
        low(2, 2, 3, rows, chunk),
        low(rows, hidden),
        wide(2, tokens, half),
        low(2, 3, tokens, chunk),
        pltpu.SemaphoreType.DMA((FRONT_COPIES,)),
        pltpu.SemaphoreType.DMA((FRONT_COPIES,)),
        pltpu.SemaphoreType.DMA((24,)),
    ]
    return pl.pallas_call(
        front_kernel,
        out_shape=[value for value, _ in outs],
        in_specs=[vmem, vmem, pl.BlockSpec(memory_space=pltpu.SMEM), vmem, vmem, vmem, vmem]
        + [hbm] * 5,
        out_specs=[spec for _, spec in outs],
        scratch_shapes=scratch,
        compiler_params=pltpu.CompilerParams(
            collective_id=2, has_side_effects=True, vmem_limit_bytes=63 * 1024 * 1024
        ),
        cost_estimate=pl.CostEstimate(
            flops=2 * tokens * width * hidden * 64, bytes_accessed=1 << 29, transcendentals=0
        ),
    )(x_blocks, cot_blocks, place, gains, first_mask, second_mask, taps, in_w, out_w, gate_w, up_w, down_w)


class Features:
    def __init__(self):
        rank = lax.axis_index("tp")
        self.rank = rank
        self.inner = rank % 2
        self.outer = rank // 2

    def gather(self, own):
        other = swapped(own, "tp", 2)
        first = self.outer == 0
        pair = jnp.stack([jnp.where(first, own, other), jnp.where(first, other, own)])
        more = swapped(pair, "tp", 1)
        even = self.inner == 0
        left, right = jnp.where(even, pair, more), jnp.where(even, more, pair)
        return jnp.concatenate([left[0], right[0], left[1], right[1]], axis=1)

    def total(self, first_half, second_half):
        even = self.inner == 0
        kept = jnp.where(even, first_half, second_half)
        sent = jnp.where(even, second_half, first_half).astype(LOW)
        pair = (kept.astype(WIDE) + swapped(sent, "tp", 1).astype(WIDE)).astype(LOW)
        both = (pair.astype(WIDE) + swapped(pair, "tp", 2).astype(WIDE)).astype(LOW)
        other = swapped(both, "tp", 1)
        return jnp.where(even, both, other), jnp.where(even, other, both)

    def scatter(self, full):
        rows, width = full.shape
        blocks = full.reshape(rows, 2, 2, width // 4)
        even = self.inner == 0
        kept = jnp.where(even, blocks[:, :, 0], blocks[:, :, 1])
        sent = jnp.where(even, blocks[:, :, 1], blocks[:, :, 0]).astype(LOW)
        pair = kept.astype(WIDE) + swapped(sent, "tp", 1).astype(WIDE)
        first = self.outer == 0
        mine = jnp.where(first, pair[:, 0], pair[:, 1])
        away = jnp.where(first, pair[:, 1], pair[:, 0]).astype(LOW)
        return mine + swapped(away, "tp", 2).astype(WIDE)

    def all_terms(self, full):
        low = full.astype(LOW)
        return [low] + [swapped(low, "tp", step) for step in (1, 2, 3)]

    def own_terms(self, full):
        width = full.shape[1] // 4
        blocks = [
            lax.dynamic_slice_in_dim(full, (self.rank ^ step) * width, width, 1).astype(LOW)
            for step in range(4)
        ]
        return blocks[:1] + [swapped(blocks[step], "tp", step) for step in (1, 2, 3)]

    def own(self, full, axis):
        width = full.shape[axis] // lax.axis_size("tp")
        return lax.dynamic_slice_in_dim(full, self.rank * width, width, axis)


class Shards:
    def __init__(self, tp):
        self.count = lax.axis_size("shard")
        self.rank = lax.axis_index("shard")
        self.ctx_rank = lax.axis_index("ctx")
        self.tp = tp
        self.paired = self.count == 2

    def weight(self, rows):
        if not self.paired:
            return (lax.all_gather(rows, "shard", axis=0, tiled=True),)
        return (rows, swapped(rows, "shard", 1))

    def split(self, full):
        if not self.paired:
            return (full,)
        width = full.shape[1] // 2
        return (
            lax.dynamic_slice_in_dim(full, self.rank * width, width, 1),
            lax.dynamic_slice_in_dim(full, (1 - self.rank) * width, width, 1),
        )

    def join(self, parts):
        if not self.paired:
            return parts[0]
        first = self.rank == 0
        return jnp.concatenate(
            [jnp.where(first, parts[0], parts[1]), jnp.where(first, parts[1], parts[0])], axis=1
        )

    def columns(self, full):
        if not self.paired:
            return lax.all_to_all(full, "shard", split_axis=1, concat_axis=0, tiled=True)
        own, other = self.split(full)
        width = own.shape[1] // 2
        part = lax.dynamic_slice_in_dim(other, self.tp.inner * width, width, 1)
        got = swapped(part, "shard", 1)
        rest = swapped(got, "tp", 1)
        even = self.tp.inner == 0
        peer = jnp.concatenate([jnp.where(even, got, rest), jnp.where(even, rest, got)], axis=1)
        return jnp.concatenate([own, peer], axis=0)

    def tokens(self, own):
        if not self.paired:
            return lax.all_gather(own, "shard", axis=0, tiled=True)
        return jnp.concatenate([own, swapped(own, "shard", 1)], axis=0)

    def own_total(self, product):
        if not self.paired:
            return lax.psum_scatter(product, "shard", scatter_dimension=0, tiled=True)
        rows = product.shape[0] // 2
        return product[:rows] + swapped(product[rows:].astype(LOW), "shard", 1).astype(WIDE)

    def own_tokens(self, product):
        if not self.paired:
            return lax.all_to_all(product.astype(LOW), "shard", split_axis=0, concat_axis=1, tiled=True)
        rows = product.shape[0] // 2
        return self.join([product[:rows].astype(LOW), swapped(product[rows:].astype(LOW), "shard", 1)])


def on_device(
    hidden_in,
    out_grad,
    seq_lengths,
    deal_order,
    in_weight,
    conv_weight,
    out_weight,
    norm1_gain,
    norm2_gain,
    gate_weight,
    up_weight,
    down_weight,
):
    ctx_size = lax.axis_size("ctx")
    ctx_rank = lax.axis_index("ctx")
    tp = Features()
    shards = Shards(tp)
    row_count, col_count = hidden_in.shape
    hidden_count = gate_weight.shape[1]
    weight_rows = in_weight.shape[0]
    per_dev = deal_order.shape[1] // ctx_size
    per_peer = per_dev // ctx_size
    block_rows = row_count // per_dev
    dealing = deal_order[0].reshape(ctx_size, per_dev)
    own_blocks = lax.dynamic_index_in_dim(dealing, ctx_rank, 0, keepdims=False)
    send_order = jnp.argsort(own_blocks // per_dev, stable=True)
    wanted = jnp.where(dealing // per_dev == ctx_rank, 0, 1)
    chosen = jnp.argsort(wanted, axis=1, stable=True)[:, :per_peer]
    targets = (jnp.take_along_axis(dealing, chosen, 1) % per_dev).reshape(-1)
    placing = jnp.argsort(targets)
    returning = jnp.argsort(send_order)

    def reorder(values, index):
        blocks = values.reshape(per_dev, block_rows, values.shape[1])
        return blocks[index].reshape(row_count, values.shape[1])

    def to_packed(values):
        got = lax.all_to_all(
            reorder(values, send_order), "ctx", split_axis=0, concat_axis=0, tiled=True
        )
        return reorder(got, placing)

    def to_dealt(values):
        got = lax.all_to_all(
            reorder(values, targets), "ctx", split_axis=0, concat_axis=0, tiled=True
        )
        return reorder(got, returning)

    def weight_grads(lefts, rights, identity, more=None):
        flat = [value for group in rights for value in group]
        if shards.paired:
            got = line_grads([group[0] for group in lefts], flat, identity, more)
            ends = [0]
            for value in flat:
                ends.append(ends[-1] + value.shape[1])
            return [got[0][:, a:b] for a, b in zip(ends, ends[1:])], (more,) + tuple(got[1:])
        flat_lefts = [value for group in lefts for value in group]
        sums = [
            sum_line(contract_rows(left, shards.tokens(right)).astype(LOW), ctx_rank)
            for left, right in zip(flat_lefts, flat)
        ]
        return sums, shards.weight(more) if more is not None else ()

    lengths = seq_lengths[0]
    starts = jnp.cumsum(lengths) - lengths
    where_t = ctx_rank * row_count - 2 + jnp.arange(row_count + 4, dtype=jnp.int32)
    seq_begin = jnp.max(jnp.where(starts[None, :] <= where_t[:, None], starts[None, :], 0), axis=1)
    position = where_t - seq_begin
    first_own = (position[2 : row_count + 2] >= 1).astype(WIDE)[:, None]
    second_own = (position[2 : row_count + 2] >= 2).astype(WIDE)[:, None]
    first_next = (position[3 : row_count + 3] >= 1).astype(WIDE)[:, None]
    second_next = (position[4 : row_count + 4] >= 2).astype(WIDE)[:, None]
    conv_taps = conv_weight.astype(WIDE)
    gains = tp.gather(jnp.stack([norm1_gain, norm2_gain])).astype(WIDE)
    gain_one, gain_two = gains[0], gains[1]
    in_parts = jnp.moveaxis(in_weight, 1, 0)

    if shards.paired:
        def blocks_of(values):
            return reorder(values, send_order).reshape(per_dev, block_rows, col_count)

        place = (targets[None, :] == jnp.arange(per_dev)[:, None]).astype(WIDE)
        (
            in_peer, out_peer, _, _, x_full, h_one, proj, mixed, conv_out, gated, mixer, h_two, cot_full,
            cot_peer, h_two_peer, h_one_peer, acts, dh_two_halves,
        ) = front(
            blocks_of(hidden_in), blocks_of(out_grad), place, gains, first_own, second_own, conv_taps,
            in_parts, out_weight, gate_weight, up_weight, down_weight,
        )
        b_part, c_part, v_part = proj[0], proj[1], proj[2]
        in_w = [jnp.concatenate([w[0], w[1], w[2]], axis=1) for w in (in_parts, in_peer)]
        out_w = (out_weight, out_peer)
        mixer_out = shards.join([mixer[0], mixer[1]])
        cot_cols = jnp.concatenate([shards.split(cot_full)[0], cot_peer], axis=0)
        h_two_cols = jnp.concatenate([shards.split(h_two)[0], h_two_peer], axis=0)
        h_one_cols = jnp.concatenate([shards.split(h_one)[0], h_one_peer], axis=0)
        ffn_rights = [acts[:, kind * hidden_count : (kind + 1) * hidden_count] for kind in range(3)]
        dh_parts = [dh_two_halves[0], dh_two_halves[1]]
        x_float = x_full.astype(WIDE)
        scale_one = lax.rsqrt(jnp.mean(x_float * x_float, axis=1, keepdims=True) + EPS)
        normed_one = x_float * scale_one
        resid = x_float + mixer_out.astype(WIDE)
        scale_two = lax.rsqrt(jnp.mean(resid * resid, axis=1, keepdims=True) + EPS)
        normed_two = resid * scale_two
    else:
        in_w = shards.weight(in_weight.reshape(weight_rows, -1))
        x_full = tp.gather(to_packed(hidden_in))
        out_w = shards.weight(out_weight)
        cot_full = tp.gather(to_packed(out_grad))
        gate_w, up_w = shards.weight(gate_weight), shards.weight(up_weight)
        x_float = x_full.astype(WIDE)
        scale_one = lax.rsqrt(jnp.mean(x_float * x_float, axis=1, keepdims=True) + EPS)
        normed_one = x_float * scale_one
        h_one = (normed_one * gain_one).astype(LOW)
        projected = matmul(h_one, in_w[0])
        b_part = projected[:, :col_count]
        c_part = projected[:, col_count : 2 * col_count]
        v_part = projected[:, 2 * col_count :]
        mixed = (b_part * v_part).astype(LOW)
        rim = shifted(mixed[-2:], "ctx", 1)
        extended = jnp.concatenate([rim, mixed], axis=0).astype(WIDE)
        prev_one = extended[1 : row_count + 1] * first_own
        prev_two = extended[0:row_count] * second_own
        conv_out = (
            conv_taps[0] * extended[2:] + conv_taps[1] * prev_one + conv_taps[2] * prev_two
        )
        gated = (c_part * conv_out).astype(LOW)
        mixer_halves = jnp.split(contract_cols(gated, out_w[0]), 2, axis=1)
        mixer_out = jnp.concatenate(tp.total(*mixer_halves), axis=1)
        resid = x_float + mixer_out.astype(WIDE)
        scale_two = lax.rsqrt(jnp.mean(resid * resid, axis=1, keepdims=True) + EPS)
        normed_two = resid * scale_two
        h_two = (normed_two * gain_two).astype(LOW)
        cot_cols, h_two_cols, h_one_cols = [shards.columns(v) for v in (cot_full, h_two, h_one)]
        gate_pre, up_pre = matmul(h_two, gate_w[0]), matmul(h_two, up_w[0])
        d_act = shards.own_total(matmul(cot_cols, down_weight))
        sigmoid_gate = jax.nn.sigmoid(gate_pre)
        silu_gate = gate_pre * sigmoid_gate
        d_gate = d_act * up_pre * sigmoid_gate * (1.0 + gate_pre * (1.0 - sigmoid_gate))
        ffn_rights = [v.astype(LOW) for v in (silu_gate * up_pre, d_gate, d_act * silu_gate)]
        dh_parts = [contract_cols(ffn_rights[1], gate_w[0]) + contract_cols(ffn_rights[2], up_w[0])]

    dh_terms = tp.all_terms(shards.join(dh_parts))
    ffn_grads, down_w = weight_grads(
        [[cot_cols], [h_two_cols, h_two_cols]], [ffn_rights[:1], ffn_rights[1:]], 0, down_weight
    )
    dh_terms, down_w, ffn_grads = lax.optimization_barrier((dh_terms, down_w, ffn_grads))
    dh_two = added(dh_terms)
    ffn_terms = tp.own_terms(shards.join([contract_cols(ffn_rights[0], w) for w in down_w]))

    rim = shifted(mixed[-2:], "ctx", 1)
    extended = jnp.concatenate([rim, mixed], axis=0).astype(WIDE)
    prev_one = extended[1 : row_count + 1] * first_own
    prev_two = extended[0:row_count] * second_own
    mixed_float = extended[2:]

    gain_two_grad = tp.own(jnp.sum(dh_two * normed_two, axis=0), 0)
    d_resid = cot_full.astype(WIDE) + norm_back(dh_two, normed_two, scale_two, gain_two)
    d_resid_low = d_resid.astype(LOW)
    d_gated = sum(matmul(part, w) for part, w in zip(shards.split(d_resid_low), out_w))
    d_conv = (d_gated * c_part).astype(LOW)
    d_c_part = d_gated * conv_out
    rim_back = shifted(d_conv[:2], "ctx", -1)
    d_conv_float = d_conv.astype(WIDE)
    back_ext = jnp.concatenate([d_conv, rim_back], axis=0).astype(WIDE)
    d_mixed = (
        conv_taps[0] * d_conv_float
        + conv_taps[1] * back_ext[1 : row_count + 1] * first_next
        + conv_taps[2] * back_ext[2:] * second_next
    )
    taps_grad = jnp.stack(
        [
            jnp.sum(d_conv_float * mixed_float, axis=0),
            jnp.sum(d_conv_float * prev_one, axis=0),
            jnp.sum(d_conv_float * prev_two, axis=0),
        ]
    )
    d_proj = [
        (d_mixed * v_part).astype(LOW),
        d_c_part.astype(LOW),
        (d_mixed * b_part).astype(LOW),
    ]
    d_proj_flat = jnp.concatenate(d_proj, axis=1)
    dh_one_terms = tp.all_terms(shards.join([contract_cols(d_proj_flat, w) for w in in_w]))
    mixer_grads, _ = weight_grads(
        [[shards.columns(d_resid_low)], [h_one_cols]], [[gated], [d_proj_flat]], 1
    )
    dh_one_terms, ffn_terms, mixer_grads = lax.optimization_barrier(
        (dh_one_terms, ffn_terms, mixer_grads)
    )
    dh_one = added(dh_one_terms)
    block_out = (tp.own(resid, 1) + added(ffn_terms)).astype(LOW)
    down_total, gate_total, up_total = [value.astype(WIDE) for value in ffn_grads]
    out_total, in_flat_total = [value.astype(WIDE) for value in mixer_grads]
    in_total = in_flat_total.reshape(in_weight.shape)
    gain_one_grad = tp.own(jnp.sum(dh_one * normed_one, axis=0), 0)
    d_input = d_resid + norm_back(dh_one, normed_one, scale_one, gain_one)
    dealt = to_dealt(jnp.concatenate([block_out, tp.own(d_input, 1).astype(LOW)], axis=1))
    block_dealt, input_dealt = dealt[:, :col_count], dealt[:, col_count:]

    small = jnp.concatenate([taps_grad, gain_one_grad[None], gain_two_grad[None]], axis=0)
    small_sum = butterfly_sum(butterfly_sum(small, "shard"), "ctx")
    return (
        block_dealt,
        input_dealt,
        in_total,
        small_sum[0:3],
        out_total,
        small_sum[3],
        small_sum[4],
        gate_total,
        up_total,
        down_total,
    )


def solution(mesh):
    placed = (
        P(("shard", "ctx"), "tp"),
        P(("shard", "ctx"), "tp"),
        P("shard", None),
        P("shard", None),
        P("shard", None, "tp"),
        P(None, "tp"),
        P("shard", "tp"),
        P("tp"),
        P("tp"),
        P("shard", "tp"),
        P("shard", "tp"),
        P("shard", "tp"),
    )
    return jax.shard_map(
        on_device,
        mesh=mesh,
        in_specs=placed,
        out_specs=(
            P(("shard", "ctx"), "tp"),
            P(("shard", "ctx"), "tp"),
            P("shard", None, "tp"),
            P(None, "tp"),
            P("shard", "tp"),
            P("tp"),
            P("tp"),
            P("shard", "tp"),
            P("shard", "tp"),
            P("shard", "tp"),
        ),
        check_vma=False,
    )
```

```python
import functools

import jax
import jax.numpy as jnp
from jax import lax
from jax.experimental import pallas as pl
from jax.experimental.pallas import tpu as pltpu
from jax.sharding import PartitionSpec as P

EPS = 1e-05
LOW = jnp.bfloat16
WIDE = jnp.float32
CHUNKS = 4


def shifted(value, axis, steps):
    count = lax.axis_size(axis)
    leading, last = (max(0, -steps), min(count, count - steps))
    return lax.ppermute(value, axis, [(source, source + steps) for source in range(leading, last)])


def swapped(value, axis, step):
    count = lax.axis_size(axis)
    return lax.ppermute(value, axis, [(source, source ^ step) for source in range(count)])


def matmul(left, right):
    return jnp.dot(left, right, preferred_element_type=WIDE)


def contract_rows(left, right):
    return lax.dot_general(left, right, (((0,), (0,)), ((), ())), preferred_element_type=WIDE)


def contract_cols(left, right):
    return lax.dot_general(left, right, (((1,), (1,)), ((), ())), preferred_element_type=WIDE)


def added(terms):
    return sum(term.astype(WIDE) for term in terms)


def norm_back(grad_out, normed, scale_row, gain):
    scaled = grad_out * gain
    return scale_row * (scaled - normed * jnp.mean(scaled * normed, axis=1, keepdims=True))


def butterfly_sum(value, axis):
    step = 1
    while step < lax.axis_size(axis):
        value = value + swapped(value, axis, step)
        step *= 2
    return value


def sum_line(piece, rank):
    from_end = lax.ppermute(piece, "ctx", [(0, 1), (3, 2)])
    half = (piece.astype(WIDE) + from_end.astype(WIDE)).astype(LOW)
    from_middle = lax.ppermute(half, "ctx", [(1, 2), (2, 1)])
    total = (half.astype(WIDE) + from_middle.astype(WIDE)).astype(LOW)
    handed = lax.ppermute(total, "ctx", [(1, 0), (2, 3)])
    inner = jnp.logical_or(rank == 1, rank == 2)
    return jnp.where(inner, total, handed)


PIECE = 256
AHEAD = 4
SLOTS = 4
MESH = pl.DeviceIdType.MESH


def line_kernel(
    pieces, left_of, left_ref, right_ref, out_ref, peer, outer_part, middle_part, held,
    peer_send, peer_recv, in_send, outer_recv, middle_recv, out_send, out_recv, own_done,
):
    shard = lax.axis_index("shard")
    ctx = lax.axis_index("ctx")
    tokens = right_ref.shape[0]
    rows = left_ref.shape[1]
    middle = jnp.logical_or(ctx == 1, ctx == 2)
    end = jnp.logical_not(middle)
    low_side = ctx < 2
    inward = jnp.where(low_side, ctx + 1, ctx - 1)
    outward = jnp.where(ctx == 1, 0, 3)

    barrier = pltpu.get_barrier_semaphore()
    pl.semaphore_signal(barrier, inc=1, device_id={"shard": 1 - shard}, device_id_type=MESH)
    pl.semaphore_signal(barrier, inc=1, device_id={"ctx": inward}, device_id_type=MESH)

    @pl.when(middle)
    def _():
        pl.semaphore_signal(barrier, inc=1, device_id={"ctx": outward}, device_id_type=MESH)
        pl.semaphore_wait(barrier, 3)

    @pl.when(end)
    def _():
        pl.semaphore_wait(barrier, 2)

    def columns(index):
        return pl.ds(pl.multiple_of(index * PIECE, PIECE), PIECE)

    def peer_copy(index):
        return pltpu.make_async_remote_copy(
            src_ref=right_ref.at[:, columns(index)],
            dst_ref=peer.at[index],
            send_sem=peer_send.at[index],
            recv_sem=peer_recv.at[index],
            device_id={"shard": 1 - shard},
            device_id_type=MESH,
        )

    def end_copy(index):
        return pltpu.make_async_remote_copy(
            src_ref=held.at[index % SLOTS],
            dst_ref=outer_part.at[index],
            send_sem=in_send.at[index],
            recv_sem=outer_recv.at[index],
            device_id={"ctx": inward},
            device_id_type=MESH,
        )

    def middle_copy(index):
        return pltpu.make_async_remote_copy(
            src_ref=held.at[index % SLOTS],
            dst_ref=middle_part.at[index],
            send_sem=in_send.at[index],
            recv_sem=middle_recv.at[index],
            device_id={"ctx": inward},
            device_id_type=MESH,
        )

    def out_copy(index):
        return pltpu.make_async_remote_copy(
            src_ref=outer_part.at[index],
            dst_ref=out_ref.at[:, columns(index)],
            send_sem=out_send.at[index],
            recv_sem=out_recv.at[index],
            device_id={"ctx": outward},
            device_id_type=MESH,
        )

    def own_copy(index):
        return pltpu.make_async_copy(
            outer_part.at[index], out_ref.at[:, columns(index)], own_done.at[index]
        )

    tile = min(256, rows)

    def product(index, start):
        lines = pl.ds(pl.multiple_of(start * tile, tile), tile)
        left = left_of(index)
        own = jnp.dot(
            left_ref[left, lines, :tokens],
            right_ref[:, columns(index)],
            preferred_element_type=WIDE,
        )
        other = jnp.dot(
            left_ref[left, lines, tokens:], peer[index], preferred_element_type=WIDE
        )
        return lines, own + other

    def finish(index):
        middle_copy(index).wait_recv()

        @pl.loop(0, rows // tile)
        def _(start):
            lines = pl.ds(pl.multiple_of(start * tile, tile), tile)
            total = held[index % SLOTS, lines].astype(WIDE) + middle_part[index, lines].astype(WIDE)
            outer_part[index, lines] = total.astype(LOW)

        out_copy(index).start()
        own_copy(index).start()

    for index in range(min(AHEAD, pieces)):
        peer_copy(index).start()

    @pl.loop(0, pieces)
    def _(index):
        @pl.when(index + AHEAD < pieces)
        def _():
            peer_copy(index + AHEAD).start()

        @pl.when(index >= SLOTS)
        def _():
            end_copy(index - SLOTS).wait_send()

        peer_copy(index).wait_recv()

        @pl.when(end)
        def _():
            @pl.loop(0, rows // tile)
            def _(start):
                lines, value = product(index, start)
                held[index % SLOTS, lines] = value.astype(LOW)

            end_copy(index).start()

        @pl.when(middle)
        def _():
            end_copy(index).wait_recv()

            @pl.loop(0, rows // tile)
            def _(start):
                lines, value = product(index, start)
                value = value + outer_part[index, lines].astype(WIDE)
                held[index % SLOTS, lines] = value.astype(LOW)

            middle_copy(index).start()

            @pl.when(index >= 1)
            def _():
                finish(index - 1)

    @pl.when(middle)
    def _():
        finish(pieces - 1)

    @pl.loop(0, pieces)
    def _(index):
        peer_copy(index).wait_send()

        @pl.when(index >= pieces - SLOTS)
        def _():
            end_copy(index).wait_send()

        @pl.when(middle)
        def _():
            out_copy(index).wait_send()
            own_copy(index).wait()

        @pl.when(end)
        def _():
            out_copy(index).wait_recv()


def line_grads(lefts, rights, identity):
    left = jnp.stack([value.T for value in lefts])
    right = jnp.concatenate(rights, axis=1)
    tokens, width = right.shape
    rows = left.shape[1]
    pieces = width // PIECE
    first = rights[0].shape[1] // PIECE

    def left_of(index):
        return jnp.where(index < first, 0, 1)

    flops = 4 * tokens * rows * width
    dma = pltpu.SemaphoreType.DMA
    return pl.pallas_call(
        functools.partial(line_kernel, pieces, left_of),
        out_shape=jax.ShapeDtypeStruct((rows, width), LOW),
        in_specs=[pl.BlockSpec(memory_space=pltpu.VMEM)] * 2,
        out_specs=pl.BlockSpec(memory_space=pl.ANY),
        scratch_shapes=[
            pltpu.VMEM((pieces, tokens, PIECE), LOW),
            pltpu.VMEM((pieces, rows, PIECE), LOW),
            pltpu.VMEM((pieces, rows, PIECE), LOW),
            pltpu.VMEM((SLOTS, rows, PIECE), LOW),
        ]
        + [dma((pieces,)) for _ in range(8)],
        compiler_params=pltpu.CompilerParams(
            collective_id=identity, has_side_effects=True, vmem_limit_bytes=56 * 1024 * 1024
        ),
        cost_estimate=pl.CostEstimate(flops=flops * 8, bytes_accessed=rows * width * 64, transcendentals=0),
    )(left, right)


def front_kernel(
    x_blocks, cot_blocks, place, gains, first_mask, second_mask, taps,
    in_w, out_w, gate_w, up_w, down_w,
    in_peer, out_peer, gate_peer, up_peer, outer_land, middle_land, rights_peer,
    x_out, h_one_out, proj_out, mixed_out, conv_out, gated_out, mixer_out, cot_out, act_out, dh_out, grads,
    x_got, cot_got, x_full, h_one, cot_full, cot_peer, h_two, h_two_peer, proj, mixed, gated, mixer, conv_v,
    out_v, rim, extended, away, pair, pair_got, both_got, dh_got,
    da_got, in_v, gu_v, down_v, dh_sum, ffn_v, right_v, outer_v, middle_v, held, totals,
    send, recv, local, in_send, outer_recv, middle_recv, out_send, out_recv, own_done,
):
    shard = lax.axis_index("shard")
    ctx = lax.axis_index("ctx")
    tp = lax.axis_index("tp")
    core, outer = tp % 2, tp // 2
    core_mate = tp + 1 - 2 * core
    outer_mate = lax.rem(tp + 2, 4)
    ctx_mate = ctx + 1 - 2 * (ctx % 2)
    tokens, width = x_full.shape
    part = width // 4
    half = width // 2
    blocks, block_rows = x_blocks.shape[0], x_blocks.shape[1]
    rows = out_w.shape[0]
    own_rows = pl.ds(pl.multiple_of((ctx % 2) * (rows // 2), rows // 2), rows // 2)
    other_rows = pl.ds(pl.multiple_of((1 - ctx % 2) * (rows // 2), rows // 2), rows // 2)
    hidden = gate_w.shape[1]
    chunk = hidden // CHUNKS

    barrier = pltpu.get_barrier_semaphore()
    mates = [{"shard": 1 - shard}, {"tp": core_mate}, {"tp": outer_mate}]
    mates += [{"ctx": lax.rem(ctx + step, blocks)} for step in range(1, blocks)]
    for mate in mates:
        pl.semaphore_signal(barrier, inc=1, device_id=mate, device_id_type=MESH)
    pl.semaphore_wait(barrier, len(mates))

    names = {}

    def remote(name, src, dst, mate):
        place_of = names.setdefault(name, len(names))
        return pltpu.make_async_remote_copy(
            src_ref=src, dst_ref=dst, send_sem=send.at[place_of], recv_sem=recv.at[place_of],
            device_id=mate, device_id_type=MESH,
        )

    def columns(start, size):
        return pl.ds(pl.multiple_of(start * size, size), size)

    own_part = columns(tp, part)
    own_half, peer_half = columns(shard, half), columns(1 - shard, half)

    def deal(name, source, target, step):
        to, origin = lax.rem(ctx + step, blocks), lax.rem(ctx + blocks - step, blocks)
        out = remote(name + str(step), source.at[to], target.at[ctx], {"ctx": to})
        into = remote(name + str(step), source.at[to], target.at[origin], {"ctx": to})
        return out, into

    def gather(name, full):
        mate = columns(outer_mate, part)
        return (
            remote(name + "outer", full.at[:, own_part], full.at[:, own_part], {"tp": outer_mate}),
            remote(name + "core", full.at[:, own_part], full.at[:, own_part], {"tp": core_mate}),
            remote(name + "more", full.at[:, mate], full.at[:, mate], {"tp": core_mate}),
        )

    pieces = {}
    for index, name in enumerate("bvc"):
        column = (0, 2, 1)[index]
        pieces[name] = (in_w.at[column], in_peer.at[column])
    pieces["o"] = (out_w, out_peer)
    for index in range(CHUNKS):
        strip = pl.ds(index * chunk, chunk)
        pieces["g%d" % index] = (gate_w.at[:, strip], gate_peer.at[:, strip])
        pieces["u%d" % index] = (up_w.at[:, strip], up_peer.at[:, strip])

    direct = ["%s%d" % (kind, index) for kind in "gu" for index in range(2, CHUNKS)]

    def over_shard(name):
        source, target = pieces[name]
        if name in direct:
            return remote(name + "x", source, target, {"shard": 1 - shard})
        return remote(name + "x", source.at[own_rows], target.at[own_rows], {"shard": 1 - shard})

    def over_ctx(name):
        target = pieces[name][1]
        return remote(name + "z", target.at[own_rows], target.at[own_rows], {"ctx": ctx_mate})

    def pump(name):
        over_shard(name).wait_recv()
        over_ctx(name).start()

    def load(index, source, target):
        return pltpu.make_async_copy(source, target, local.at[index])

    x_deals = [deal("x", x_blocks, x_got, step) for step in range(1, blocks)]
    cot_deals = [deal("cot", cot_blocks, cot_got, step) for step in range(1, blocks)]
    for out, _ in x_deals:
        out.start()
    for name in ("b", "v", "c", "o", "g0", "u0"):
        over_shard(name).start()
    own_loads = [load(index, in_w.at[index], in_v.at[0, index]) for index in range(3)]
    own_loads.append(load(3, out_w, out_v.at[0]))
    own_loads.append(load(4, down_w, down_v))
    for copy in own_loads:
        copy.start()

    def packed(source, got, deals, full):
        got[ctx] = source[ctx]
        for _, into in deals:
            into.wait_recv()
        for index in range(blocks):
            total = place[index, 0] * got[0].astype(WIDE)
            for other in range(1, blocks):
                total = total + place[index, other] * got[other].astype(WIDE)
            full[index * block_rows : (index + 1) * block_rows, own_part] = total.astype(LOW)

    pump("b")
    packed(x_blocks, x_got, x_deals, x_full)
    x_outer, x_core, x_more = gather("xg", x_full)
    x_outer.start()
    x_core.start()
    for out, _ in cot_deals:
        out.start()
    pump("v")
    x_outer.wait_recv()
    x_more.start()
    packed(cot_blocks, cot_got, cot_deals, cot_full)
    cot_outer, cot_core, cot_more = gather("cg", cot_full)
    cot_outer.start()
    cot_core.start()
    x_core.wait_recv()
    x_more.wait_recv()

    x_store = load(5, x_full, x_out)
    x_store.start()
    step = min(64, tokens)

    @pl.loop(0, tokens // step)
    def _(index):
        lines = pl.ds(pl.multiple_of(index * step, step), step)
        value = x_full[lines].astype(WIDE)
        scale = lax.rsqrt(jnp.mean(value * value, axis=1, keepdims=True) + EPS)
        h_one[lines] = (value * scale * gains[0:1]).astype(LOW)

    h_one_store = load(6, h_one, h_one_out)
    h_one_store.start()
    pump("c")

    def columns_out(name, full, got):
        strip = pl.ds(pl.multiple_of((1 - shard) * half + core * part, part), part)
        target = columns(core, part)
        first = remote(name + "x", full.at[:, strip], got.at[:, target], {"shard": 1 - shard})
        second = remote(name + "core", got.at[:, target], got.at[:, target], {"tp": core_mate})
        return first, second

    cot_first, cot_second = columns_out("cc", cot_full, cot_peer)

    tile = min(256, tokens)

    def over_tiles(body):
        @pl.loop(0, tokens // tile)
        def _(index):
            body(pl.ds(pl.multiple_of(index * tile, tile), tile))

    def project(column, name):
        target = load(column, in_peer.at[column], in_v.at[1, column])
        own_loads[column].wait()
        over_ctx(name).wait_recv()
        target.start()
        target.wait()

        def body(lines):
            proj[column, lines] = jnp.dot(
                h_one[lines, own_half], in_v[0, column], preferred_element_type=WIDE
            ) + jnp.dot(h_one[lines, peer_half], in_v[1, column], preferred_element_type=WIDE)

        over_tiles(body)

    project(0, "b")
    project(2, "v")
    edge = 16
    rim_copy = remote(
        "rim", mixed.at[pl.ds(tokens - edge, edge)], rim, {"ctx": lax.rem(ctx + 1, blocks)}
    )

    def mix(lines):
        value = (proj[0, lines] * proj[2, lines]).astype(LOW)
        mixed[lines] = value
        extended[pl.ds(lines.start + 8, tile)] = value.astype(WIDE)

    over_tiles(mix)

    @pl.when(ctx < blocks - 1)
    def _():
        rim_copy.start()

    pump("o")
    cot_outer.wait_recv()
    cot_more.start()
    project(1, "c")

    @pl.when(ctx > 0)
    def _():
        rim_copy.wait_recv()
        extended[0:8] = rim[8:16].astype(WIDE)

    @pl.when(ctx == 0)
    def _():
        extended[0:8] = jnp.zeros((8, part), WIDE)

    for start in range(0, tokens, tile):
        lines = pl.ds(start, tile)
        value = taps[0:1] * extended[pl.ds(start + 8, tile)]
        value = value + taps[1:2] * (extended[pl.ds(start + 7, tile)] * first_mask[lines])
        value = value + taps[2:3] * (extended[pl.ds(start + 6, tile)] * second_mask[lines])
        conv_v[lines] = value
        gated[lines] = (proj[1, lines] * value).astype(LOW)

    stores = [
        load(7, proj, proj_out), load(8, mixed, mixed_out), load(9, conv_v, conv_out), load(10, gated, gated_out)
    ]
    for copy in stores:
        copy.start()

    pump("g0")
    cot_core.wait_recv()
    cot_more.wait_recv()
    cot_first.start()
    over_shard("g1").start()
    cot_store = load(11, cot_full, cot_out)
    cot_store.start()
    out_load = load(3, out_peer, out_v.at[1])
    own_loads[3].wait()
    over_ctx("o").wait_recv()
    out_load.start()
    out_load.wait()

    def to_half(lines, which):
        return lax.dot_general(
            gated[lines], out_v[which], (((1,), (1,)), ((), ())), preferred_element_type=WIDE
        )

    stages = [pl.ds(start, tile) for start in range(0, tokens, tile)]
    hops = []
    for index, lines in enumerate(stages):
        first = remote("ma%d" % index, away.at[lines], pair_got.at[lines], {"tp": core_mate})
        second = remote("mb%d" % index, pair.at[lines], both_got.at[lines], {"tp": outer_mate})
        third = remote("mc%d" % index, mixer.at[core, lines], mixer.at[core, lines], {"tp": core_mate})
        hops.append((first, second, third))
        away[lines] = to_half(lines, 1 - core).astype(LOW)
        first.start()
    for index, lines in enumerate(stages):
        value = to_half(lines, core)
        hops[index][0].wait_recv()
        pair[lines] = (value + pair_got[lines].astype(WIDE)).astype(LOW)
        hops[index][1].start()

    da_send, da_own = h_one, x_full
    pump("u0")
    cot_first.wait_recv()
    cot_second.start()
    cot_second.wait_recv()
    own_loads[4].wait()
    h_one_store.wait()

    def da_copy(index):
        strip = pl.ds(index * chunk, chunk)
        return remote("da%d" % index, da_send.at[:, strip], da_got.at[:, strip], {"shard": 1 - shard})

    for index in range(CHUNKS):
        strip = pl.ds(index * chunk, chunk)

        def send_part(lines):
            da_send[lines, strip] = jnp.dot(
                cot_peer[lines], down_v[:, strip], preferred_element_type=WIDE
            ).astype(LOW)

        over_tiles(send_part)
        if index == 0:
            da_copy(0).start()
            over_shard("u1").start()

    for index, lines in enumerate(stages):
        hops[index][1].wait_recv()
        mixer[core, lines] = (pair[lines].astype(WIDE) + both_got[lines].astype(WIDE)).astype(LOW)
        hops[index][2].start()
    pump("g1")
    for index, lines in enumerate(stages):
        hops[index][2].wait_recv()
    mixer_store = load(12, mixer, mixer_out)
    mixer_store.start()

    @pl.loop(0, tokens // step)
    def _(index):
        lines = pl.ds(pl.multiple_of(index * step, step), step)
        own = x_full[lines, own_half].astype(WIDE) + mixer[0, lines].astype(WIDE)
        other = x_full[lines, peer_half].astype(WIDE) + mixer[1, lines].astype(WIDE)
        total = jnp.sum(own * own, axis=1, keepdims=True) + jnp.sum(other * other, axis=1, keepdims=True)
        scale = lax.rsqrt(total / width + EPS)
        h_two[lines, own_half] = (own * scale * gains[1:2, own_half]).astype(LOW)
        h_two[lines, peer_half] = (other * scale * gains[1:2, peer_half]).astype(LOW)

    h_two_first, h_two_second = columns_out("hc", h_two, h_two_peer)
    x_store.wait()
    for copy in (x_outer, x_core, x_more):
        copy.wait_send()

    def own_part_of(lines):
        for index in range(CHUNKS):
            strip = pl.ds(index * chunk, chunk)
            da_own[lines, strip] = jnp.dot(
                cot_full[lines, own_half], down_v[:, strip], preferred_element_type=WIDE
            ).astype(LOW)

    over_tiles(own_part_of)

    def turned(place_of, source, start, first):
        for row in range(0, half, 256):
            for line in range(0, tokens, 256):
                block = source[pl.ds(line, 256), pl.ds(pl.multiple_of(start + row, 256), 256)]
                down_v[pl.ds(row, 256), pl.ds(place_of * half + first + line, 256)] = block.T

    turned(0, cot_full, shard * half, 0)
    turned(0, cot_peer, 0, tokens)
    turned(1, h_two, shard * half, 0)

    def own_weights(index):
        strip = pl.ds(index * chunk, chunk)
        room = gu_v if index % 2 == 0 else in_v
        base = 13 + 4 * (index % 2)
        return [
            load(base, gate_w.at[:, strip], room.at[0, 0]),
            load(base + 1, up_w.at[:, strip], room.at[0, 1]),
        ]

    def peer_weights(index):
        strip = pl.ds(index * chunk, chunk)
        room = gu_v if index % 2 == 0 else in_v
        base = 15 + 4 * (index % 2)
        return [
            load(base, gate_peer.at[:, strip], room.at[1, 0]),
            load(base + 1, up_peer.at[:, strip], room.at[1, 1]),
        ]

    def act_store(index):
        return load(21 + index % 2, ffn_v.at[index % 2, 0], act_out.at[:, pl.ds(index * chunk, chunk)])

    def right_copy(index, kind):
        strip = pl.ds(kind * hidden + index * chunk, chunk)
        return remote(
            "r%d%d" % (index, kind), ffn_v.at[index % 2, kind], rights_peer.at[:, strip], {"shard": 1 - shard}
        )

    def right_load(index, kind):
        strip = pl.ds(kind * hidden + index * chunk, chunk)
        return load(23 + kind, rights_peer.at[:, strip], right_v.at[kind])

    def ready(index):
        for kind in "gu":
            if "%s%d" % (kind, index) not in direct:
                over_ctx("%s%d" % (kind, index)).wait_recv()
        for copy in peer_weights(index):
            copy.start()

    def feed(index, lines):
        room = gu_v if index % 2 == 0 else in_v
        slot = index % 2
        strip = pl.ds(index * chunk, chunk)

        def pre(kind):
            return jnp.dot(
                h_two[lines, own_half], room[0, kind], preferred_element_type=WIDE
            ) + jnp.dot(h_two[lines, peer_half], room[1, kind], preferred_element_type=WIDE)

        gate_pre, up_pre = pre(0), pre(1)
        d_act = da_own[lines, strip].astype(WIDE) + da_got[lines, strip].astype(WIDE)
        sigmoid = jax.nn.sigmoid(gate_pre)
        silu = gate_pre * sigmoid
        ffn_v[slot, 0, lines] = (silu * up_pre).astype(LOW)
        ffn_v[slot, 1, lines] = (
            d_act * up_pre * sigmoid * (1.0 + gate_pre * (1.0 - sigmoid))
        ).astype(LOW)
        ffn_v[slot, 2, lines] = (d_act * silu).astype(LOW)

    def back(index, lines):
        room = gu_v if index % 2 == 0 else in_v
        slot = index % 2
        for place_of in range(2):
            term = lax.dot_general(
                ffn_v[slot, 1, lines], room[place_of, 0],
                (((1,), (1,)), ((), ())), preferred_element_type=WIDE,
            ) + lax.dot_general(
                ffn_v[slot, 2, lines], room[place_of, 1],
                (((1,), (1,)), ((), ())), preferred_element_type=WIDE,
            )
            if index > 0:
                term = term + dh_sum[place_of, lines]
            dh_sum[place_of, lines] = term

    def feed_start(index):
        da_copy(index).wait_recv()
        for copy in own_weights(index) + peer_weights(index):
            copy.wait()
        if index > 1:
            act_store(index - 2).wait()
            for kind in range(3):
                right_copy(index - 2, kind).wait_send()

    middle = jnp.logical_or(ctx == 1, ctx == 2)
    end = jnp.logical_not(middle)
    inward = jnp.where(ctx < 2, ctx + 1, ctx - 1)
    outward = jnp.where(ctx == 1, 0, 3)
    per_kind = chunk // PIECE
    per_chunk = 3 * per_kind
    line_rows = min(256, rows)

    def grad_columns(piece):
        index, turn = piece // per_chunk, piece % per_chunk
        kind, sub = turn // per_kind, turn % per_kind
        return pl.ds(pl.multiple_of(kind * hidden + index * chunk + sub * PIECE, PIECE), PIECE)

    def inward_copy(piece, land, sems):
        return pltpu.make_async_remote_copy(
            src_ref=held.at[piece % SLOTS], dst_ref=land.at[piece], send_sem=in_send.at[piece],
            recv_sem=sems.at[piece], device_id={"ctx": inward}, device_id_type=MESH,
        )

    def outward_copy(piece):
        return pltpu.make_async_remote_copy(
            src_ref=totals.at[piece % SLOTS], dst_ref=grads.at[:, grad_columns(piece)], send_sem=out_send.at[piece],
            recv_sem=out_recv.at[piece], device_id={"ctx": outward}, device_id_type=MESH,
        )

    def total_store(piece):
        return pltpu.make_async_copy(totals.at[piece % SLOTS], grads.at[:, grad_columns(piece)], own_done.at[piece])

    def stage_in(piece, land, room):
        copy = pltpu.make_async_copy(land.at[piece], room, local.at[26])
        copy.start()
        copy.wait()

    def finish(piece):
        inward_copy(piece, middle_land, middle_recv).wait_recv()
        stage_in(piece, middle_land, middle_v)

        @pl.when(piece >= SLOTS)
        def _():
            outward_copy(piece - SLOTS).wait_send()
            total_store(piece - SLOTS).wait()

        @pl.loop(0, rows // line_rows)
        def _(start):
            lines = pl.ds(pl.multiple_of(start * line_rows, line_rows), line_rows)
            total = held[piece % SLOTS, lines].astype(WIDE) + middle_v[lines].astype(WIDE)
            totals[piece % SLOTS, lines] = total.astype(LOW)

        outward_copy(piece).start()
        total_store(piece).start()

    def grad_piece(piece):
        index, turn = piece // per_chunk, piece % per_chunk
        kind, sub = turn // per_kind, turn % per_kind
        strip = pl.ds(pl.multiple_of(sub * PIECE, PIECE), PIECE)
        left = jnp.where(kind == 0, 0, half)

        @pl.when(piece >= SLOTS)
        def _():
            inward_copy(piece - SLOTS, outer_land, outer_recv).wait_send()

        def product(start):
            lines = pl.ds(pl.multiple_of(start * line_rows, line_rows), line_rows)
            own = jnp.dot(
                down_v[lines, pl.ds(pl.multiple_of(left, tokens), tokens)],
                ffn_v[index % 2, kind, :, strip],
                preferred_element_type=WIDE,
            )
            other = jnp.dot(
                down_v[lines, pl.ds(pl.multiple_of(left + tokens, tokens), tokens)],
                right_v[kind, :, strip],
                preferred_element_type=WIDE,
            )
            return lines, own + other

        @pl.when(end)
        def _():
            @pl.loop(0, rows // line_rows)
            def _(start):
                lines, value = product(start)
                held[piece % SLOTS, lines] = value.astype(LOW)

            inward_copy(piece, outer_land, outer_recv).start()

        @pl.when(middle)
        def _():
            inward_copy(piece, outer_land, outer_recv).wait_recv()
            stage_in(piece, outer_land, outer_v)

            @pl.loop(0, rows // line_rows)
            def _(start):
                lines, value = product(start)
                held[piece % SLOTS, lines] = (value + outer_v[lines].astype(WIDE)).astype(LOW)

            inward_copy(piece, middle_land, middle_recv).start()

            @pl.when(piece >= 1)
            def _():
                finish(piece - 1)

    def got_right(index, kind):
        right_copy(index, kind).wait_recv()
        copy = right_load(index, kind)
        copy.start()
        copy.wait()

    dh_away = remote("dh1", away, pair_got, {"tp": core_mate})
    dh_pair = remote("dh2", pair, dh_got, {"tp": outer_mate})
    dh_last = remote("dh3", mixer.at[core], mixer.at[core], {"tp": core_mate})
    tiles = [pl.ds(start, tile) for start in range(0, tokens, tile)]

    def whole_feed(index):
        feed_start(index)
        for lines in tiles:
            feed(index, lines)
        act_store(index).start()

    def whole_back(index):
        for lines in tiles:
            back(index, lines)
        if index + 1 < CHUNKS:
            for copy in own_weights(index + 1):
                copy.start()

    for copy in own_weights(0):
        copy.start()
    ready(0)
    whole_feed(0)
    right_copy(0, 0).start()
    da_copy(1).start()
    h_two_first.start()
    right_copy(0, 1).start()
    right_copy(0, 2).start()
    whole_back(0)
    pump("u1")

    def event_start():
        got_right(0, 0)

    def event_first():
        ready(1)
        whole_feed(1)
        for kind in range(3):
            right_copy(1, kind).start()
        for name in ("g2", "u2"):
            over_shard(name).start()
        da_copy(2).start()
        over_shard("g3").start()
        h_two_first.wait_recv()
        h_two_second.start()
        h_two_second.wait_recv()
        turned(1, h_two_peer, 0, tokens)
        got_right(0, 1)

    def event_second():
        over_shard("g2").wait_recv()
        over_shard("u2").wait_recv()
        ready(2)
        whole_feed(2)
        right_copy(2, 0).start()
        right_copy(2, 1).start()
        over_shard("u3").start()
        da_copy(3).start()
        right_copy(2, 2).start()
        got_right(1, 2)

    def event_third():
        over_shard("g3").wait_recv()
        over_shard("u3").wait_recv()
        ready(3)
        whole_feed(3)
        for kind in range(3):
            right_copy(3, kind).start()
        got_right(2, 2)

    def dh_one_hop():
        whole_back(3)
        mixer_store.wait()
        for trio in hops:
            for copy in trio:
                copy.wait_send()

        def body(lines):
            away[lines] = dh_sum[1 - core, lines].astype(LOW)

        over_tiles(body)
        dh_away.start()

    def dh_two_hops():
        dh_away.wait_recv()

        def body(lines):
            pair[lines] = (dh_sum[core, lines] + pair_got[lines].astype(WIDE)).astype(LOW)

        over_tiles(body)
        dh_pair.start()
        got_right(3, 0)

    def dh_three_hops():
        dh_pair.wait_recv()

        def body(lines):
            mixer[core, lines] = (pair[lines].astype(WIDE) + dh_got[lines].astype(WIDE)).astype(LOW)

        over_tiles(body)
        dh_last.start()
        got_right(3, 1)

    events = {
        0: event_start,
        2: event_first,
        3: lambda: whole_back(1),
        4: lambda: got_right(0, 2),
        6: lambda: got_right(1, 0),
        8: lambda: got_right(1, 1),
        10: event_second,
        11: lambda: whole_back(2),
        12: lambda: got_right(2, 0),
        14: lambda: got_right(2, 1),
        16: event_third,
        17: dh_one_hop,
        18: dh_two_hops,
        20: dh_three_hops,
        22: lambda: got_right(3, 2),
    }
    pieces_in_all = CHUNKS * per_chunk

    @pl.loop(0, pieces_in_all)
    def _(piece):
        for turn, event in events.items():
            pl.when(piece == turn)(event)
        grad_piece(piece)

    @pl.when(middle)
    def _():
        finish(pieces_in_all - 1)

    dh_last.wait_recv()
    dh_store = load(27, mixer, dh_out)
    dh_store.start()

    for out, _ in x_deals + cot_deals:
        out.wait_send()
    for copy in (cot_outer, cot_core, cot_more, cot_first, cot_second, h_two_first, h_two_second,
                 dh_away, dh_pair, dh_last):
        copy.wait_send()
    for name in pieces:
        over_shard(name).wait_send()
        if name not in direct:
            over_ctx(name).wait_send()
    for index in range(CHUNKS):
        da_copy(index).wait_send()
    for index in (CHUNKS - 2, CHUNKS - 1):
        act_store(index).wait()
        for kind in range(3):
            right_copy(index, kind).wait_send()
    for copy in stores + [cot_store, dh_store]:
        copy.wait()

    @pl.when(ctx < blocks - 1)
    def _():
        rim_copy.wait_send()

    @pl.loop(0, pieces_in_all)
    def _(piece):
        @pl.when(piece >= pieces_in_all - SLOTS)
        def _():
            inward_copy(piece, outer_land, outer_recv).wait_send()

            @pl.when(middle)
            def _():
                outward_copy(piece).wait_send()
                total_store(piece).wait()

        @pl.when(end)
        def _():
            outward_copy(piece).wait_recv()


FRONT_COPIES = 72


def front(x_blocks, cot_blocks, place, gains, first_mask, second_mask, taps, in_w, out_w, gate_w, up_w, down_w):
    tokens = x_blocks.shape[0] * x_blocks.shape[1]
    part = x_blocks.shape[2]
    width = gains.shape[1]
    half = width // 2
    rows, hidden = gate_w.shape
    chunk = hidden // CHUNKS
    pieces = 3 * hidden // PIECE
    vmem = pl.BlockSpec(memory_space=pltpu.VMEM)
    hbm = pl.BlockSpec(memory_space=pl.ANY)
    shape = jax.ShapeDtypeStruct
    outs = [
        shape(in_w.shape, LOW),
        shape(out_w.shape, LOW),
        shape(gate_w.shape, LOW),
        shape(up_w.shape, LOW),
        shape((pieces, rows, PIECE), LOW),
        shape((pieces, rows, PIECE), LOW),
        shape((tokens, 3 * hidden), LOW),
        shape((tokens, width), LOW),
        shape((tokens, width), LOW),
        shape((3, tokens, part), WIDE),
        shape((tokens, part), LOW),
        shape((tokens, part), WIDE),
        shape((tokens, part), LOW),
        shape((2, tokens, half), LOW),
        shape((tokens, width), LOW),
        shape((tokens, hidden), LOW),
        shape((2, tokens, half), LOW),
        shape((rows, 3 * hidden), LOW),
    ]
    low, wide = (lambda *dims: pltpu.VMEM(dims, LOW)), (lambda *dims: pltpu.VMEM(dims, WIDE))
    dma = pltpu.SemaphoreType.DMA
    scratch = [
        low(*x_blocks.shape),
        low(*x_blocks.shape),
        low(tokens, width),
        low(tokens, width),
        low(tokens, width),
        low(tokens, half),
        low(tokens, width),
        low(tokens, half),
        wide(3, tokens, part),
        low(tokens, part),
        low(tokens, part),
        low(2, tokens, half),
        wide(tokens, part),
        low(2, rows, part),
        low(16, part),
        wide(tokens + 8, part),
        low(tokens, half),
        low(tokens, half),
        low(tokens, half),
        low(tokens, half),
        low(tokens, half),
        low(tokens, hidden),
        low(2, 3, rows, part),
        low(2, 2, rows, chunk),
        low(rows, hidden),
        wide(2, tokens, half),
        low(2, 3, tokens, chunk),
        low(3, tokens, chunk),
        low(rows, PIECE),
        low(rows, PIECE),
        low(SLOTS, rows, PIECE),
        low(SLOTS, rows, PIECE),
        dma((FRONT_COPIES,)),
        dma((FRONT_COPIES,)),
        dma((28,)),
    ] + [dma((pieces,)) for _ in range(6)]
    return pl.pallas_call(
        front_kernel,
        out_shape=outs,
        in_specs=[vmem, vmem, pl.BlockSpec(memory_space=pltpu.SMEM), vmem, vmem, vmem, vmem]
        + [hbm] * 5,
        out_specs=[hbm for _ in outs],
        scratch_shapes=scratch,
        compiler_params=pltpu.CompilerParams(
            collective_id=2, has_side_effects=True, vmem_limit_bytes=63 * 1024 * 1024
        ),
        cost_estimate=pl.CostEstimate(
            flops=2 * tokens * width * hidden * 64, bytes_accessed=1 << 29, transcendentals=0
        ),
    )(x_blocks, cot_blocks, place, gains, first_mask, second_mask, taps, in_w, out_w, gate_w, up_w, down_w)


class Features:
    def __init__(self):
        rank = lax.axis_index("tp")
        self.rank = rank
        self.inner = rank % 2
        self.outer = rank // 2

    def gather(self, own):
        other = swapped(own, "tp", 2)
        first = self.outer == 0
        pair = jnp.stack([jnp.where(first, own, other), jnp.where(first, other, own)])
        more = swapped(pair, "tp", 1)
        even = self.inner == 0
        left, right = jnp.where(even, pair, more), jnp.where(even, more, pair)
        return jnp.concatenate([left[0], right[0], left[1], right[1]], axis=1)

    def total(self, first_half, second_half):
        even = self.inner == 0
        kept = jnp.where(even, first_half, second_half)
        sent = jnp.where(even, second_half, first_half).astype(LOW)
        pair = (kept.astype(WIDE) + swapped(sent, "tp", 1).astype(WIDE)).astype(LOW)
        both = (pair.astype(WIDE) + swapped(pair, "tp", 2).astype(WIDE)).astype(LOW)
        other = swapped(both, "tp", 1)
        return jnp.where(even, both, other), jnp.where(even, other, both)

    def scatter(self, full):
        rows, width = full.shape
        blocks = full.reshape(rows, 2, 2, width // 4)
        even = self.inner == 0
        kept = jnp.where(even, blocks[:, :, 0], blocks[:, :, 1])
        sent = jnp.where(even, blocks[:, :, 1], blocks[:, :, 0]).astype(LOW)
        pair = kept.astype(WIDE) + swapped(sent, "tp", 1).astype(WIDE)
        first = self.outer == 0
        mine = jnp.where(first, pair[:, 0], pair[:, 1])
        away = jnp.where(first, pair[:, 1], pair[:, 0]).astype(LOW)
        return mine + swapped(away, "tp", 2).astype(WIDE)

    def all_terms(self, full):
        low = full.astype(LOW)
        return [low] + [swapped(low, "tp", step) for step in (1, 2, 3)]

    def own_terms(self, full):
        width = full.shape[1] // 4
        blocks = [
            lax.dynamic_slice_in_dim(full, (self.rank ^ step) * width, width, 1).astype(LOW)
            for step in range(4)
        ]
        return blocks[:1] + [swapped(blocks[step], "tp", step) for step in (1, 2, 3)]

    def own(self, full, axis):
        width = full.shape[axis] // lax.axis_size("tp")
        return lax.dynamic_slice_in_dim(full, self.rank * width, width, axis)


class Shards:
    def __init__(self, tp):
        self.count = lax.axis_size("shard")
        self.rank = lax.axis_index("shard")
        self.ctx_rank = lax.axis_index("ctx")
        self.tp = tp
        self.paired = self.count == 2

    def weight(self, rows):
        if not self.paired:
            return (lax.all_gather(rows, "shard", axis=0, tiled=True),)
        return (rows, swapped(rows, "shard", 1))

    def split(self, full):
        if not self.paired:
            return (full,)
        width = full.shape[1] // 2
        return (
            lax.dynamic_slice_in_dim(full, self.rank * width, width, 1),
            lax.dynamic_slice_in_dim(full, (1 - self.rank) * width, width, 1),
        )

    def join(self, parts):
        if not self.paired:
            return parts[0]
        first = self.rank == 0
        return jnp.concatenate(
            [jnp.where(first, parts[0], parts[1]), jnp.where(first, parts[1], parts[0])], axis=1
        )

    def columns(self, full):
        if not self.paired:
            return lax.all_to_all(full, "shard", split_axis=1, concat_axis=0, tiled=True)
        own, other = self.split(full)
        width = own.shape[1] // 2
        part = lax.dynamic_slice_in_dim(other, self.tp.inner * width, width, 1)
        got = swapped(part, "shard", 1)
        rest = swapped(got, "tp", 1)
        even = self.tp.inner == 0
        peer = jnp.concatenate([jnp.where(even, got, rest), jnp.where(even, rest, got)], axis=1)
        return jnp.concatenate([own, peer], axis=0)

    def tokens(self, own):
        if not self.paired:
            return lax.all_gather(own, "shard", axis=0, tiled=True)
        return jnp.concatenate([own, swapped(own, "shard", 1)], axis=0)

    def own_total(self, product):
        if not self.paired:
            return lax.psum_scatter(product, "shard", scatter_dimension=0, tiled=True)
        rows = product.shape[0] // 2
        return product[:rows] + swapped(product[rows:].astype(LOW), "shard", 1).astype(WIDE)

    def own_tokens(self, product):
        if not self.paired:
            return lax.all_to_all(product.astype(LOW), "shard", split_axis=0, concat_axis=1, tiled=True)
        rows = product.shape[0] // 2
        return self.join([product[:rows].astype(LOW), swapped(product[rows:].astype(LOW), "shard", 1)])


def on_device(
    hidden_in,
    out_grad,
    seq_lengths,
    deal_order,
    in_weight,
    conv_weight,
    out_weight,
    norm1_gain,
    norm2_gain,
    gate_weight,
    up_weight,
    down_weight,
):
    ctx_size = lax.axis_size("ctx")
    ctx_rank = lax.axis_index("ctx")
    tp = Features()
    shards = Shards(tp)
    row_count, col_count = hidden_in.shape
    hidden_count = gate_weight.shape[1]
    weight_rows = in_weight.shape[0]
    per_dev = deal_order.shape[1] // ctx_size
    per_peer = per_dev // ctx_size
    block_rows = row_count // per_dev
    dealing = deal_order[0].reshape(ctx_size, per_dev)
    own_blocks = lax.dynamic_index_in_dim(dealing, ctx_rank, 0, keepdims=False)
    send_order = jnp.argsort(own_blocks // per_dev, stable=True)
    wanted = jnp.where(dealing // per_dev == ctx_rank, 0, 1)
    chosen = jnp.argsort(wanted, axis=1, stable=True)[:, :per_peer]
    targets = (jnp.take_along_axis(dealing, chosen, 1) % per_dev).reshape(-1)
    placing = jnp.argsort(targets)
    returning = jnp.argsort(send_order)

    def reorder(values, index):
        blocks = values.reshape(per_dev, block_rows, values.shape[1])
        return blocks[index].reshape(row_count, values.shape[1])

    def to_packed(values):
        got = lax.all_to_all(
            reorder(values, send_order), "ctx", split_axis=0, concat_axis=0, tiled=True
        )
        return reorder(got, placing)

    def to_dealt(values):
        got = lax.all_to_all(
            reorder(values, targets), "ctx", split_axis=0, concat_axis=0, tiled=True
        )
        return reorder(got, returning)

    def weight_grads(lefts, rights, identity):
        flat = [value for group in rights for value in group]
        if shards.paired:
            summed = line_grads([group[0] for group in lefts], flat, identity)
            ends = [0]
            for value in flat:
                ends.append(ends[-1] + value.shape[1])
            return [summed[:, a:b] for a, b in zip(ends, ends[1:])]
        flat_lefts = [value for group in lefts for value in group]
        return [
            sum_line(contract_rows(left, shards.tokens(right)).astype(LOW), ctx_rank)
            for left, right in zip(flat_lefts, flat)
        ]

    lengths = seq_lengths[0]
    starts = jnp.cumsum(lengths) - lengths
    where_t = ctx_rank * row_count - 2 + jnp.arange(row_count + 4, dtype=jnp.int32)
    seq_begin = jnp.max(jnp.where(starts[None, :] <= where_t[:, None], starts[None, :], 0), axis=1)
    position = where_t - seq_begin
    first_own = (position[2 : row_count + 2] >= 1).astype(WIDE)[:, None]
    second_own = (position[2 : row_count + 2] >= 2).astype(WIDE)[:, None]
    first_next = (position[3 : row_count + 3] >= 1).astype(WIDE)[:, None]
    second_next = (position[4 : row_count + 4] >= 2).astype(WIDE)[:, None]
    conv_taps = conv_weight.astype(WIDE)
    gains = tp.gather(jnp.stack([norm1_gain, norm2_gain])).astype(WIDE)
    gain_one, gain_two = gains[0], gains[1]
    in_parts = jnp.moveaxis(in_weight, 1, 0)

    if shards.paired:
        def blocks_of(values):
            return reorder(values, send_order).reshape(per_dev, block_rows, col_count)

        place = (targets[None, :] == jnp.arange(per_dev)[:, None]).astype(WIDE)
        (
            in_peer, out_peer, _, _, _, _, rights_peer, x_full, h_one, proj, mixed, conv_out, gated, mixer,
            cot_full, act, dh_halves, ffn_sums,
        ) = front(
            blocks_of(hidden_in), blocks_of(out_grad), place, gains, first_own, second_own, conv_taps,
            in_parts, out_weight, gate_weight, up_weight, down_weight,
        )
        b_part, c_part, v_part = proj[0], proj[1], proj[2]
        in_w = [jnp.concatenate([w[0], w[1], w[2]], axis=1) for w in (in_parts, in_peer)]
        out_w = (out_weight, out_peer)
        mixer_out = shards.join([mixer[0], mixer[1]])
        h_one_cols = shards.columns(h_one)
        dh_two = shards.join([dh_halves[0], dh_halves[1]]).astype(WIDE)
        act_all = jnp.concatenate([act, rights_peer[:, :hidden_count]], axis=0)
        ffn_grads = [ffn_sums[:, kind * hidden_count : (kind + 1) * hidden_count] for kind in range(3)]
        x_float = x_full.astype(WIDE)
        scale_one = lax.rsqrt(jnp.mean(x_float * x_float, axis=1, keepdims=True) + EPS)
        normed_one = x_float * scale_one
        resid = x_float + mixer_out.astype(WIDE)
        scale_two = lax.rsqrt(jnp.mean(resid * resid, axis=1, keepdims=True) + EPS)
        normed_two = resid * scale_two
    else:
        in_w = shards.weight(in_weight.reshape(weight_rows, -1))
        x_full = tp.gather(to_packed(hidden_in))
        out_w = shards.weight(out_weight)
        cot_full = tp.gather(to_packed(out_grad))
        gate_w, up_w = shards.weight(gate_weight), shards.weight(up_weight)
        x_float = x_full.astype(WIDE)
        scale_one = lax.rsqrt(jnp.mean(x_float * x_float, axis=1, keepdims=True) + EPS)
        normed_one = x_float * scale_one
        h_one = (normed_one * gain_one).astype(LOW)
        projected = matmul(h_one, in_w[0])
        b_part = projected[:, :col_count]
        c_part = projected[:, col_count : 2 * col_count]
        v_part = projected[:, 2 * col_count :]
        mixed = (b_part * v_part).astype(LOW)
        rim = shifted(mixed[-2:], "ctx", 1)
        extended = jnp.concatenate([rim, mixed], axis=0).astype(WIDE)
        prev_one = extended[1 : row_count + 1] * first_own
        prev_two = extended[0:row_count] * second_own
        conv_out = (
            conv_taps[0] * extended[2:] + conv_taps[1] * prev_one + conv_taps[2] * prev_two
        )
        gated = (c_part * conv_out).astype(LOW)
        mixer_halves = jnp.split(contract_cols(gated, out_w[0]), 2, axis=1)
        mixer_out = jnp.concatenate(tp.total(*mixer_halves), axis=1)
        resid = x_float + mixer_out.astype(WIDE)
        scale_two = lax.rsqrt(jnp.mean(resid * resid, axis=1, keepdims=True) + EPS)
        normed_two = resid * scale_two
        h_two = (normed_two * gain_two).astype(LOW)
        cot_cols, h_two_cols, h_one_cols = [shards.columns(v) for v in (cot_full, h_two, h_one)]
        gate_pre, up_pre = matmul(h_two, gate_w[0]), matmul(h_two, up_w[0])
        d_act = shards.own_total(matmul(cot_cols, down_weight))
        sigmoid_gate = jax.nn.sigmoid(gate_pre)
        silu_gate = gate_pre * sigmoid_gate
        d_gate = d_act * up_pre * sigmoid_gate * (1.0 + gate_pre * (1.0 - sigmoid_gate))
        ffn_rights = [v.astype(LOW) for v in (silu_gate * up_pre, d_gate, d_act * silu_gate)]
        act_all = shards.tokens(ffn_rights[0])
        dh_terms = tp.all_terms(
            contract_cols(ffn_rights[1], gate_w[0]) + contract_cols(ffn_rights[2], up_w[0])
        )
        dh_two = added(dh_terms)
        ffn_grads = weight_grads(
            [[cot_cols], [h_two_cols, h_two_cols]], [ffn_rights[:1], ffn_rights[1:]], 0
        )

    ffn_terms = tp.own_terms(shards.own_tokens(contract_cols(act_all, down_weight)))

    rim = shifted(mixed[-2:], "ctx", 1)
    extended = jnp.concatenate([rim, mixed], axis=0).astype(WIDE)
    prev_one = extended[1 : row_count + 1] * first_own
    prev_two = extended[0:row_count] * second_own
    mixed_float = extended[2:]

    gain_two_grad = tp.own(jnp.sum(dh_two * normed_two, axis=0), 0)
    d_resid = cot_full.astype(WIDE) + norm_back(dh_two, normed_two, scale_two, gain_two)
    d_resid_low = d_resid.astype(LOW)
    d_gated = sum(matmul(part, w) for part, w in zip(shards.split(d_resid_low), out_w))
    d_conv = (d_gated * c_part).astype(LOW)
    d_c_part = d_gated * conv_out
    rim_back = shifted(d_conv[:2], "ctx", -1)
    d_conv_float = d_conv.astype(WIDE)
    back_ext = jnp.concatenate([d_conv, rim_back], axis=0).astype(WIDE)
    d_mixed = (
        conv_taps[0] * d_conv_float
        + conv_taps[1] * back_ext[1 : row_count + 1] * first_next
        + conv_taps[2] * back_ext[2:] * second_next
    )
    taps_grad = jnp.stack(
        [
            jnp.sum(d_conv_float * mixed_float, axis=0),
            jnp.sum(d_conv_float * prev_one, axis=0),
            jnp.sum(d_conv_float * prev_two, axis=0),
        ]
    )
    d_proj = [
        (d_mixed * v_part).astype(LOW),
        d_c_part.astype(LOW),
        (d_mixed * b_part).astype(LOW),
    ]
    d_proj_flat = jnp.concatenate(d_proj, axis=1)
    dh_one_terms = tp.all_terms(shards.join([contract_cols(d_proj_flat, w) for w in in_w]))
    mixer_grads = weight_grads(
        [[shards.columns(d_resid_low)], [h_one_cols]], [[gated], [d_proj_flat]], 1
    )
    dh_one_terms, ffn_terms, mixer_grads = lax.optimization_barrier(
        (dh_one_terms, ffn_terms, mixer_grads)
    )
    dh_one = added(dh_one_terms)
    block_out = (tp.own(resid, 1) + added(ffn_terms)).astype(LOW)
    down_total, gate_total, up_total = [value.astype(WIDE) for value in ffn_grads]
    out_total, in_flat_total = [value.astype(WIDE) for value in mixer_grads]
    in_total = in_flat_total.reshape(in_weight.shape)
    gain_one_grad = tp.own(jnp.sum(dh_one * normed_one, axis=0), 0)
    d_input = d_resid + norm_back(dh_one, normed_one, scale_one, gain_one)
    dealt = to_dealt(jnp.concatenate([block_out, tp.own(d_input, 1).astype(LOW)], axis=1))
    block_dealt, input_dealt = dealt[:, :col_count], dealt[:, col_count:]

    small = jnp.concatenate([taps_grad, gain_one_grad[None], gain_two_grad[None]], axis=0)
    small_sum = butterfly_sum(butterfly_sum(small, "shard"), "ctx")
    return (
        block_dealt,
        input_dealt,
        in_total,
        small_sum[0:3],
        out_total,
        small_sum[3],
        small_sum[4],
        gate_total,
        up_total,
        down_total,
    )


def solution(mesh):
    placed = (
        P(("shard", "ctx"), "tp"),
        P(("shard", "ctx"), "tp"),
        P("shard", None),
        P("shard", None),
        P("shard", None, "tp"),
        P(None, "tp"),
        P("shard", "tp"),
        P("tp"),
        P("tp"),
        P("shard", "tp"),
        P("shard", "tp"),
        P("shard", "tp"),
    )
    return jax.shard_map(
        on_device,
        mesh=mesh,
        in_specs=placed,
        out_specs=(
            P(("shard", "ctx"), "tp"),
            P(("shard", "ctx"), "tp"),
            P("shard", None, "tp"),
            P(None, "tp"),
            P("shard", "tp"),
            P("tp"),
            P("tp"),
            P("shard", "tp"),
            P("shard", "tp"),
            P("shard", "tp"),
        ),
        check_vma=False,
    )
```

```python
import jax
import jax.numpy as jnp
from jax import lax
from jax.experimental import pallas as pl
from jax.experimental.pallas import tpu as pltpu
from jax.sharding import PartitionSpec as P

EPS = 1e-05
LOW = jnp.bfloat16
WIDE = jnp.float32
CHUNKS = 4


def shifted(value, axis, steps):
    count = lax.axis_size(axis)
    leading, last = (max(0, -steps), min(count, count - steps))
    return lax.ppermute(value, axis, [(source, source + steps) for source in range(leading, last)])


def swapped(value, axis, step):
    count = lax.axis_size(axis)
    return lax.ppermute(value, axis, [(source, source ^ step) for source in range(count)])


def matmul(left, right):
    return jnp.dot(left, right, preferred_element_type=WIDE)


def contract_rows(left, right):
    return lax.dot_general(left, right, (((0,), (0,)), ((), ())), preferred_element_type=WIDE)


def contract_cols(left, right):
    return lax.dot_general(left, right, (((1,), (1,)), ((), ())), preferred_element_type=WIDE)


def added(terms):
    return sum(term.astype(WIDE) for term in terms)


def norm_back(grad_out, normed, scale_row, gain):
    scaled = grad_out * gain
    return scale_row * (scaled - normed * jnp.mean(scaled * normed, axis=1, keepdims=True))


def butterfly_sum(value, axis):
    step = 1
    while step < lax.axis_size(axis):
        value = value + swapped(value, axis, step)
        step *= 2
    return value


def sum_line(piece, rank):
    from_end = lax.ppermute(piece, "ctx", [(0, 1), (3, 2)])
    half = (piece.astype(WIDE) + from_end.astype(WIDE)).astype(LOW)
    from_middle = lax.ppermute(half, "ctx", [(1, 2), (2, 1)])
    total = (half.astype(WIDE) + from_middle.astype(WIDE)).astype(LOW)
    handed = lax.ppermute(total, "ctx", [(1, 0), (2, 3)])
    inner = jnp.logical_or(rank == 1, rank == 2)
    return jnp.where(inner, total, handed)


PIECE = 256
AHEAD = 4
SLOTS = 4
TOTALS = 2
MESH = pl.DeviceIdType.MESH


def front_kernel(
    x_blocks, cot_blocks, place, gains, masks, taps,
    in_w, out_w, gate_w, up_w, down_w,
    in_peer, out_peer, gate_peer, up_peer, outer_land, middle_land, rights_peer,
    x_out, h_one_out, mixer_out, act_out, grads, dealt, tap_sums, gain_sums,
    x_got, cot_got, x_full, h_one, cot_full, cot_peer, h_two, h_two_peer, proj, mixed, gated, mixer, conv_v,
    out_v, rim, extended, away, pair, pair_got, both_got, dh_got,
    da_got, in_v, gu_v, down_v, dh_sum, ffn_v, right_v, outer_v, middle_v, held, totals, d_ext, edge_v, rim_back,
    send, recv, local, in_send, outer_recv, middle_recv, out_send, out_recv, own_done,
):
    shard = lax.axis_index("shard")
    ctx = lax.axis_index("ctx")
    tp = lax.axis_index("tp")
    core, outer = tp % 2, tp // 2
    core_mate = tp + 1 - 2 * core
    outer_mate = lax.rem(tp + 2, 4)
    ctx_mate = ctx + 1 - 2 * (ctx % 2)
    tokens, width = x_full.shape
    part = width // 4
    half = width // 2
    blocks, block_rows = x_blocks.shape[0], x_blocks.shape[1]
    rows = out_w.shape[0]
    own_rows = pl.ds(pl.multiple_of((ctx % 2) * (rows // 2), rows // 2), rows // 2)
    other_rows = pl.ds(pl.multiple_of((1 - ctx % 2) * (rows // 2), rows // 2), rows // 2)
    hidden = gate_w.shape[1]
    chunk = hidden // CHUNKS

    barrier = pltpu.get_barrier_semaphore()
    mates = [{"shard": 1 - shard}, {"tp": core_mate}, {"tp": outer_mate}]
    mates += [{"ctx": lax.rem(ctx + step, blocks)} for step in range(1, blocks)]
    for mate in mates:
        pl.semaphore_signal(barrier, inc=1, device_id=mate, device_id_type=MESH)
    pl.semaphore_wait(barrier, len(mates))

    names = {}

    def remote(name, src, dst, mate):
        place_of = names.setdefault(name, len(names))
        return pltpu.make_async_remote_copy(
            src_ref=src, dst_ref=dst, send_sem=send.at[place_of], recv_sem=recv.at[place_of],
            device_id=mate, device_id_type=MESH,
        )

    def columns(start, size):
        return pl.ds(pl.multiple_of(start * size, size), size)

    own_part = columns(tp, part)
    own_half, peer_half = columns(shard, half), columns(1 - shard, half)

    def deal(name, source, target, step):
        to, origin = lax.rem(ctx + step, blocks), lax.rem(ctx + blocks - step, blocks)
        out = remote(name + str(step), source.at[to], target.at[ctx], {"ctx": to})
        into = remote(name + str(step), source.at[to], target.at[origin], {"ctx": to})
        return out, into

    def gather(name, full):
        mate = columns(outer_mate, part)
        return (
            remote(name + "outer", full.at[:, own_part], full.at[:, own_part], {"tp": outer_mate}),
            remote(name + "core", full.at[:, own_part], full.at[:, own_part], {"tp": core_mate}),
            remote(name + "more", full.at[:, mate], full.at[:, mate], {"tp": core_mate}),
        )

    pieces = {}
    for index, name in enumerate("bvc"):
        column = (0, 2, 1)[index]
        pieces[name] = (in_w.at[column], in_peer.at[column])
    pieces["o"] = (out_w, out_peer)
    for index in range(CHUNKS):
        strip = pl.ds(index * chunk, chunk)
        pieces["g%d" % index] = (gate_w.at[:, strip], gate_peer.at[:, strip])
        pieces["u%d" % index] = (up_w.at[:, strip], up_peer.at[:, strip])

    direct = ["%s%d" % (kind, index) for kind in "gu" for index in range(2, CHUNKS)]

    def over_shard(name):
        source, target = pieces[name]
        if name in direct:
            return remote(name + "x", source, target, {"shard": 1 - shard})
        return remote(name + "x", source.at[own_rows], target.at[own_rows], {"shard": 1 - shard})

    def over_ctx(name):
        target = pieces[name][1]
        return remote(name + "z", target.at[own_rows], target.at[own_rows], {"ctx": ctx_mate})

    def pump(name):
        over_shard(name).wait_recv()
        over_ctx(name).start()

    def load(index, source, target):
        return pltpu.make_async_copy(source, target, local.at[index])

    x_deals = [deal("x", x_blocks, x_got, step) for step in range(1, blocks)]
    cot_deals = [deal("cot", cot_blocks, cot_got, step) for step in range(1, blocks)]
    for out, _ in x_deals:
        out.start()
    for name in ("b", "v", "c", "o", "g0", "u0"):
        over_shard(name).start()
    own_loads = [load(index, in_w.at[index], in_v.at[0, index]) for index in range(3)]
    own_loads.append(load(3, out_w, out_v.at[0]))
    own_loads.append(load(4, down_w, down_v))
    for copy in own_loads:
        copy.start()

    def packed(source, got, deals, full):
        got[ctx] = source[ctx]
        for _, into in deals:
            into.wait_recv()
        for index in range(blocks):
            total = place[index, 0] * got[0].astype(WIDE)
            for other in range(1, blocks):
                total = total + place[index, other] * got[other].astype(WIDE)
            full[index * block_rows : (index + 1) * block_rows, own_part] = total.astype(LOW)

    pump("b")
    packed(x_blocks, x_got, x_deals, x_full)
    x_outer, x_core, x_more = gather("xg", x_full)
    x_outer.start()
    x_core.start()
    for out, _ in cot_deals:
        out.start()
    pump("v")
    x_outer.wait_recv()
    x_more.start()
    packed(cot_blocks, cot_got, cot_deals, cot_full)
    cot_outer, cot_core, cot_more = gather("cg", cot_full)
    cot_outer.start()
    cot_core.start()
    x_core.wait_recv()
    x_more.wait_recv()

    x_store = load(5, x_full, x_out)
    x_store.start()
    step = min(64, tokens)

    @pl.loop(0, tokens // step)
    def _(index):
        lines = pl.ds(pl.multiple_of(index * step, step), step)
        value = x_full[lines].astype(WIDE)
        scale = lax.rsqrt(jnp.mean(value * value, axis=1, keepdims=True) + EPS)
        h_one[lines] = (value * scale * gains[0:1]).astype(LOW)

    h_one_store = load(6, h_one, h_one_out)
    h_one_store.start()
    pump("c")

    def columns_out(name, full, got):
        strip = pl.ds(pl.multiple_of((1 - shard) * half + core * part, part), part)
        target = columns(core, part)
        first = remote(name + "x", full.at[:, strip], got.at[:, target], {"shard": 1 - shard})
        second = remote(name + "core", got.at[:, target], got.at[:, target], {"tp": core_mate})
        return first, second

    cot_first, cot_second = columns_out("cc", cot_full, cot_peer)

    tile = min(256, tokens)

    def over_tiles(body):
        @pl.loop(0, tokens // tile)
        def _(index):
            body(pl.ds(pl.multiple_of(index * tile, tile), tile))

    def project(column, name):
        target = load(column, in_peer.at[column], in_v.at[1, column])
        own_loads[column].wait()
        over_ctx(name).wait_recv()
        target.start()
        target.wait()

        def body(lines):
            proj[column, lines] = jnp.dot(
                h_one[lines, own_half], in_v[0, column], preferred_element_type=WIDE
            ) + jnp.dot(h_one[lines, peer_half], in_v[1, column], preferred_element_type=WIDE)

        over_tiles(body)

    project(0, "b")
    project(2, "v")
    edge = 16
    rim_copy = remote(
        "rim", mixed.at[pl.ds(tokens - edge, edge)], rim, {"ctx": lax.rem(ctx + 1, blocks)}
    )

    def mix(lines):
        value = (proj[0, lines] * proj[2, lines]).astype(LOW)
        mixed[lines] = value
        extended[pl.ds(lines.start + 8, tile)] = value.astype(WIDE)

    over_tiles(mix)

    @pl.when(ctx < blocks - 1)
    def _():
        rim_copy.start()

    pump("o")
    cot_outer.wait_recv()
    cot_more.start()
    project(1, "c")

    @pl.when(ctx > 0)
    def _():
        rim_copy.wait_recv()
        extended[0:8] = rim[8:16].astype(WIDE)

    @pl.when(ctx == 0)
    def _():
        extended[0:8] = jnp.zeros((8, part), WIDE)

    for start in range(0, tokens, tile):
        lines = pl.ds(start, tile)
        value = taps[0:1] * extended[pl.ds(start + 8, tile)]
        value = value + taps[1:2] * (extended[pl.ds(start + 7, tile)] * masks[lines, 0:1])
        value = value + taps[2:3] * (extended[pl.ds(start + 6, tile)] * masks[lines, 1:2])
        conv_v[lines] = value
        gated[lines] = (proj[1, lines] * value).astype(LOW)

    pump("g0")
    cot_core.wait_recv()
    cot_more.wait_recv()
    cot_first.start()
    over_shard("g1").start()
    out_load = load(3, out_peer, out_v.at[1])
    own_loads[3].wait()
    over_ctx("o").wait_recv()
    out_load.start()
    out_load.wait()

    def to_half(lines, which):
        return lax.dot_general(
            gated[lines], out_v[which], (((1,), (1,)), ((), ())), preferred_element_type=WIDE
        )

    stages = [pl.ds(start, tile) for start in range(0, tokens, tile)]
    hops = []
    for index, lines in enumerate(stages):
        first = remote("ma%d" % index, away.at[lines], pair_got.at[lines], {"tp": core_mate})
        second = remote("mb%d" % index, pair.at[lines], both_got.at[lines], {"tp": outer_mate})
        third = remote("mc%d" % index, mixer.at[core, lines], mixer.at[core, lines], {"tp": core_mate})
        hops.append((first, second, third))
        away[lines] = to_half(lines, 1 - core).astype(LOW)
        first.start()
    for index, lines in enumerate(stages):
        value = to_half(lines, core)
        hops[index][0].wait_recv()
        pair[lines] = (value + pair_got[lines].astype(WIDE)).astype(LOW)
        hops[index][1].start()

    da_send, da_own = h_one, x_full
    pump("u0")
    cot_first.wait_recv()
    cot_second.start()
    cot_second.wait()
    own_loads[4].wait()
    h_one_store.wait()

    def da_copy(index):
        strip = pl.ds(index * chunk, chunk)
        return remote("da%d" % index, da_send.at[:, strip], da_got.at[:, strip], {"shard": 1 - shard})

    for index in range(CHUNKS):
        strip = pl.ds(index * chunk, chunk)

        def send_part(lines):
            da_send[lines, strip] = jnp.dot(
                cot_peer[lines], down_v[:, strip], preferred_element_type=WIDE
            ).astype(LOW)

        over_tiles(send_part)
        if index == 0:
            da_copy(0).start()
            over_shard("u1").start()

    for index, lines in enumerate(stages):
        hops[index][1].wait_recv()
        mixer[core, lines] = (pair[lines].astype(WIDE) + both_got[lines].astype(WIDE)).astype(LOW)
        hops[index][2].start()
    pump("g1")
    for index, lines in enumerate(stages):
        hops[index][2].wait_recv()
    mixer_store = load(12, mixer, mixer_out)
    mixer_store.start()

    @pl.loop(0, tokens // step)
    def _(index):
        lines = pl.ds(pl.multiple_of(index * step, step), step)
        own = x_full[lines, own_half].astype(WIDE) + mixer[0, lines].astype(WIDE)
        other = x_full[lines, peer_half].astype(WIDE) + mixer[1, lines].astype(WIDE)
        total = jnp.sum(own * own, axis=1, keepdims=True) + jnp.sum(other * other, axis=1, keepdims=True)
        scale = lax.rsqrt(total / width + EPS)
        h_two[lines, own_half] = (own * scale * gains[1:2, own_half]).astype(LOW)
        h_two[lines, peer_half] = (other * scale * gains[1:2, peer_half]).astype(LOW)

    h_two_first, h_two_second = columns_out("hc", h_two, h_two_peer)
    x_store.wait()
    for copy in (x_outer, x_core, x_more):
        copy.wait_send()

    def own_part_of(lines):
        for index in range(CHUNKS):
            strip = pl.ds(index * chunk, chunk)
            da_own[lines, strip] = jnp.dot(
                cot_full[lines, own_half], down_v[:, strip], preferred_element_type=WIDE
            ).astype(LOW)

    over_tiles(own_part_of)

    def turned(place_of, source, start, first):
        for row in range(0, half, 256):
            for line in range(0, tokens, 256):
                block = source[pl.ds(line, 256), pl.ds(pl.multiple_of(start + row, 256), 256)]
                down_v[pl.ds(row, 256), pl.ds(place_of * half + first + line, 256)] = block.T

    turned(0, cot_full, shard * half, 0)
    turned(0, cot_peer, 0, tokens)
    turned(1, h_two, shard * half, 0)

    def own_weights(index):
        strip = pl.ds(index * chunk, chunk)
        room = gu_v if index % 2 == 0 else in_v
        base = 13 + 4 * (index % 2)
        return [
            load(base, gate_w.at[:, strip], room.at[0, 0]),
            load(base + 1, up_w.at[:, strip], room.at[0, 1]),
        ]

    def peer_weights(index):
        strip = pl.ds(index * chunk, chunk)
        room = gu_v if index % 2 == 0 else in_v
        base = 15 + 4 * (index % 2)
        return [
            load(base, gate_peer.at[:, strip], room.at[1, 0]),
            load(base + 1, up_peer.at[:, strip], room.at[1, 1]),
        ]

    def act_store(index):
        return load(21 + index % 2, ffn_v.at[index % 2, 0], act_out.at[:, pl.ds(index * chunk, chunk)])

    def right_copy(index, kind):
        strip = pl.ds(kind * hidden + index * chunk, chunk)
        return remote(
            "r%d%d" % (index, kind), ffn_v.at[index % 2, kind], rights_peer.at[:, strip], {"shard": 1 - shard}
        )

    def right_load(index, kind):
        strip = pl.ds(kind * hidden + index * chunk, chunk)
        return load(23 + kind, rights_peer.at[:, strip], right_v.at[kind])

    def ready(index):
        for kind in "gu":
            if "%s%d" % (kind, index) not in direct:
                over_ctx("%s%d" % (kind, index)).wait_recv()
        for copy in peer_weights(index):
            copy.start()

    def feed(index, lines):
        room = gu_v if index % 2 == 0 else in_v
        slot = index % 2
        strip = pl.ds(index * chunk, chunk)

        def pre(kind):
            return jnp.dot(
                h_two[lines, own_half], room[0, kind], preferred_element_type=WIDE
            ) + jnp.dot(h_two[lines, peer_half], room[1, kind], preferred_element_type=WIDE)

        gate_pre, up_pre = pre(0), pre(1)
        d_act = da_own[lines, strip].astype(WIDE) + da_got[lines, strip].astype(WIDE)
        sigmoid = jax.nn.sigmoid(gate_pre)
        silu = gate_pre * sigmoid
        ffn_v[slot, 0, lines] = (silu * up_pre).astype(LOW)
        ffn_v[slot, 1, lines] = (
            d_act * up_pre * sigmoid * (1.0 + gate_pre * (1.0 - sigmoid))
        ).astype(LOW)
        ffn_v[slot, 2, lines] = (d_act * silu).astype(LOW)

    def back(index, lines):
        room = gu_v if index % 2 == 0 else in_v
        slot = index % 2
        for place_of in range(2):
            term = lax.dot_general(
                ffn_v[slot, 1, lines], room[place_of, 0],
                (((1,), (1,)), ((), ())), preferred_element_type=WIDE,
            ) + lax.dot_general(
                ffn_v[slot, 2, lines], room[place_of, 1],
                (((1,), (1,)), ((), ())), preferred_element_type=WIDE,
            )
            if index > 0:
                term = term + dh_sum[place_of, lines]
            dh_sum[place_of, lines] = term

    def feed_start(index):
        da_copy(index).wait_recv()
        for copy in own_weights(index) + peer_weights(index):
            copy.wait()
        if index > 1:
            act_store(index - 2).wait()
            for kind in range(3):
                right_copy(index - 2, kind).wait_send()

    middle = jnp.logical_or(ctx == 1, ctx == 2)
    end = jnp.logical_not(middle)
    inward = jnp.where(ctx < 2, ctx + 1, ctx - 1)
    outward = jnp.where(ctx == 1, 0, 3)
    per_kind = chunk // PIECE
    per_chunk = 3 * per_kind
    ffn_pieces = CHUNKS * per_chunk
    pieces_in_all = ffn_pieces + 4 * part // PIECE
    line_rows = min(256, rows)

    def grad_columns(piece):
        index, turn = piece // per_chunk, piece % per_chunk
        kind, sub = turn // per_kind, turn % per_kind
        start = jnp.where(
            piece < ffn_pieces, kind * hidden + index * chunk + sub * PIECE, piece * PIECE
        )
        return pl.ds(pl.multiple_of(start, PIECE), PIECE)

    def inward_copy(piece, land, sems):
        return pltpu.make_async_remote_copy(
            src_ref=held.at[piece % SLOTS], dst_ref=land.at[piece], send_sem=in_send.at[piece],
            recv_sem=sems.at[piece], device_id={"ctx": inward}, device_id_type=MESH,
        )

    def outward_copy(piece):
        return pltpu.make_async_remote_copy(
            src_ref=totals.at[piece % TOTALS], dst_ref=grads.at[:, grad_columns(piece)], send_sem=out_send.at[piece],
            recv_sem=out_recv.at[piece], device_id={"ctx": outward}, device_id_type=MESH,
        )

    def total_store(piece):
        return pltpu.make_async_copy(totals.at[piece % TOTALS], grads.at[:, grad_columns(piece)], own_done.at[piece])

    def stage_in(piece, land, room):
        copy = pltpu.make_async_copy(land.at[piece], room, local.at[26])
        copy.start()
        copy.wait()

    def finish(piece):
        inward_copy(piece, middle_land, middle_recv).wait_recv()
        stage_in(piece, middle_land, middle_v)

        @pl.when(piece >= TOTALS)
        def _():
            outward_copy(piece - TOTALS).wait_send()
            total_store(piece - TOTALS).wait()

        @pl.loop(0, rows // line_rows)
        def _(start):
            lines = pl.ds(pl.multiple_of(start * line_rows, line_rows), line_rows)
            total = held[piece % SLOTS, lines].astype(WIDE) + middle_v[lines].astype(WIDE)
            totals[piece % TOTALS, lines] = total.astype(LOW)

        outward_copy(piece).start()
        total_store(piece).start()

    def grad_piece(piece):
        after = piece >= ffn_pieces
        turn = jnp.where(after, jnp.maximum(piece - ffn_pieces - per_kind, 0), piece % per_chunk)
        kind, sub = turn // per_kind, piece % per_kind
        slot = jnp.where(after, jnp.where(piece < ffn_pieces + per_kind, 1, 0), piece // per_chunk % 2)
        strip = pl.ds(pl.multiple_of(sub * PIECE, PIECE), PIECE)
        left_first = jnp.where(after, piece < ffn_pieces + per_kind, kind == 0)
        left = jnp.where(left_first, 0, half)

        @pl.when(piece >= SLOTS)
        def _():
            inward_copy(piece - SLOTS, outer_land, outer_recv).wait_send()

        def product(start):
            lines = pl.ds(pl.multiple_of(start * line_rows, line_rows), line_rows)
            own = jnp.dot(
                down_v[lines, pl.ds(pl.multiple_of(left, tokens), tokens)],
                ffn_v[slot, kind, :, strip],
                preferred_element_type=WIDE,
            )
            other = jnp.dot(
                down_v[lines, pl.ds(pl.multiple_of(left + tokens, tokens), tokens)],
                right_v[kind, :, strip],
                preferred_element_type=WIDE,
            )
            return lines, own + other

        @pl.when(end)
        def _():
            @pl.loop(0, rows // line_rows)
            def _(start):
                lines, value = product(start)
                held[piece % SLOTS, lines] = value.astype(LOW)

            inward_copy(piece, outer_land, outer_recv).start()

        @pl.when(middle)
        def _():
            inward_copy(piece, outer_land, outer_recv).wait_recv()
            stage_in(piece, outer_land, outer_v)

            @pl.loop(0, rows // line_rows)
            def _(start):
                lines, value = product(start)
                held[piece % SLOTS, lines] = (value + outer_v[lines].astype(WIDE)).astype(LOW)

            inward_copy(piece, middle_land, middle_recv).start()

            @pl.when(piece >= 1)
            def _():
                finish(piece - 1)

    def got_right(index, kind):
        right_copy(index, kind).wait_recv()
        copy = right_load(index, kind)
        copy.start()
        copy.wait()

    dh_away = remote("dh1", away, pair_got, {"tp": core_mate})
    dh_pair = remote("dh2", pair, dh_got, {"tp": outer_mate})
    dh_last = remote("dh3", mixer.at[core], mixer.at[core], {"tp": core_mate})
    tiles = [pl.ds(start, tile) for start in range(0, tokens, tile)]

    def whole_feed(index):
        feed_start(index)
        for lines in tiles:
            feed(index, lines)
        act_store(index).start()

    def whole_back(index):
        for lines in tiles:
            back(index, lines)
        if index + 1 < CHUNKS:
            for copy in own_weights(index + 1):
                copy.start()

    for copy in own_weights(0):
        copy.start()
    ready(0)
    whole_feed(0)
    right_copy(0, 0).start()
    da_copy(1).start()
    h_two_first.start()
    right_copy(0, 1).start()
    right_copy(0, 2).start()
    whole_back(0)
    pump("u1")

    def event_start():
        got_right(0, 0)

    def event_first():
        ready(1)
        whole_feed(1)
        for kind in range(3):
            right_copy(1, kind).start()
        for name in ("g2", "u2"):
            over_shard(name).start()
        da_copy(2).start()
        over_shard("g3").start()
        h_two_first.wait_recv()
        h_two_second.start()
        h_two_second.wait()
        turned(1, h_two_peer, 0, tokens)
        got_right(0, 1)

    def event_second():
        over_shard("g2").wait_recv()
        over_shard("u2").wait_recv()
        ready(2)
        whole_feed(2)
        right_copy(2, 0).start()
        right_copy(2, 1).start()
        over_shard("u3").start()
        da_copy(3).start()
        right_copy(2, 2).start()
        got_right(1, 2)

    back_blocks, d_resid = cot_got, dh_sum.at[1, :, pl.ds(0, part)]
    hone_first, hone_second = columns_out("ic", h_one_out, cot_peer)
    dr_first, dr_second = columns_out("dc", h_two, h_two_peer)
    mixer_rights = 3 * hidden

    def mixer_right(kind):
        source = gated if kind == 0 else ffn_v.at[0, kind - 1]
        strip = pl.ds(mixer_rights + kind * part, part)
        return remote("m%d" % kind, source, rights_peer.at[:, strip], {"shard": 1 - shard})

    def got_mixer_right(kind):
        mixer_right(kind).wait_recv()
        room = right_v.at[max(kind - 1, 0)]
        copy = load(23, rights_peer.at[:, pl.ds(mixer_rights + kind * part, part)], room)
        copy.start()
        copy.wait()

    x_reload = load(5, x_out, x_full)
    mixer_reloads = [
        load(6, mixer_out.at[0], h_one.at[:, own_half]), load(7, mixer_out.at[1], h_one.at[:, peer_half])
    ]
    h_one_reload = load(8, h_one_out.at[:, own_half], dh_got)
    in_reloads = [load(13 + column, in_w.at[column], in_v.at[0, column]) for column in range(3)]
    in_reloads += [load(16 + column, in_peer.at[column], in_v.at[1, column]) for column in range(3)]
    fine = min(32, tokens)

    def reload():
        for index in range(CHUNKS):
            da_copy(index).wait_send()
        for copy in [x_reload] + mixer_reloads + in_reloads:
            copy.start()

    def resid_back():
        dh_last.wait_recv()
        h_one_reload.start()
        for copy in [x_reload] + mixer_reloads:
            copy.wait()
        h_two_first.wait_send()
        gain_sums[...] = jnp.zeros((2, width), WIDE)

        @pl.loop(0, tokens // fine)
        def _(index):
            lines = pl.ds(pl.multiple_of(index * fine, fine), fine)

            def halves(columns_of, which):
                resid = x_full[lines, columns_of].astype(WIDE) + h_one[lines, columns_of].astype(WIDE)
                return resid, mixer[which, lines].astype(WIDE)

            own, own_grad = halves(own_half, 0)
            other, other_grad = halves(peer_half, 1)
            total = jnp.sum(own * own, axis=1, keepdims=True) + jnp.sum(other * other, axis=1, keepdims=True)
            scale = lax.rsqrt(total / width + EPS)
            own, other = own * scale, other * scale
            own_scaled, other_scaled = own_grad * gains[1:2, own_half], other_grad * gains[1:2, peer_half]
            mean = (
                jnp.sum(own_scaled * own, axis=1, keepdims=True)
                + jnp.sum(other_scaled * other, axis=1, keepdims=True)
            ) / width
            h_two[lines, own_half] = (
                cot_full[lines, own_half].astype(WIDE) + scale * (own_scaled - own * mean)
            ).astype(LOW)
            h_two[lines, peer_half] = (
                cot_full[lines, peer_half].astype(WIDE) + scale * (other_scaled - other * mean)
            ).astype(LOW)
            gain_sums[1:2, own_half] += jnp.sum(own_grad * own, axis=0, keepdims=True)
            gain_sums[1:2, peer_half] += jnp.sum(other_grad * other, axis=0, keepdims=True)
            resid = x_full[lines, own_part].astype(WIDE) + h_one[lines, own_part].astype(WIDE)
            which = jnp.where(outer == shard, 0, 1)
            scaled = mixer[which, lines, columns(core, part)].astype(WIDE) * gains[1:2, own_part]
            d_resid[lines] = cot_full[lines, own_part].astype(WIDE) + scale * (
                scaled - resid * scale * mean
            )

        dr_first.start()

    rim_out = remote(
        "rim_back", edge_v, rim_back, {"ctx": lax.rem(ctx + blocks - 1, blocks)}
    )

    def conv_back():
        act_store(CHUNKS - 2).wait()
        for kind in range(3):
            right_copy(CHUNKS - 2, kind).wait_send()

        def body(lines):
            d_gated = jnp.dot(
                h_two[lines, own_half], out_v[0], preferred_element_type=WIDE
            ) + jnp.dot(h_two[lines, peer_half], out_v[1], preferred_element_type=WIDE)
            d_ext[lines] = (d_gated * proj[1, lines]).astype(LOW).astype(WIDE)
            ffn_v[0, 1, lines] = (d_gated * conv_v[lines]).astype(LOW)

        for lines in tiles:
            body(lines)
        edge_v[...] = d_ext[0:16].astype(LOW)

        @pl.when(ctx > 0)
        def _():
            rim_out.start()

        turned(0, h_two, shard * half, 0)

    def out_ready():
        dr_first.wait_recv()
        dr_second.start()
        act_store(CHUNKS - 1).wait()
        right_copy(CHUNKS - 1, 0).wait_send()

        def body(lines):
            ffn_v[1, 0, lines] = gated[lines]

        over_tiles(body)
        dr_second.wait_recv()
        turned(0, h_two_peer, 0, tokens)
        got_mixer_right(0)

    def proj_back():
        @pl.when(ctx < blocks - 1)
        def _():
            rim_out.wait_recv()
            d_ext[tokens : tokens + 8] = rim_back[0:8].astype(WIDE)

        @pl.when(ctx == blocks - 1)
        def _():
            d_ext[tokens : tokens + 8] = jnp.zeros((8, part), WIDE)

        sums = [jnp.zeros((1, part), WIDE) for _ in range(3)]
        size = 128
        for start in range(0, tokens, size):
            lines = pl.ds(start, size)
            own = d_ext[lines]
            d_mixed = taps[0:1] * own
            d_mixed = d_mixed + taps[1:2] * (d_ext[pl.ds(start + 1, size)] * masks[lines, 2:3])
            d_mixed = d_mixed + taps[2:3] * (d_ext[pl.ds(start + 2, size)] * masks[lines, 3:4])
            ffn_v[0, 0, lines] = (d_mixed * proj[2, lines]).astype(LOW)
            ffn_v[0, 2, lines] = (d_mixed * proj[0, lines]).astype(LOW)
            for tap in range(3):
                value = own * extended[pl.ds(start + 8 - tap, size)]
                if tap > 0:
                    value = value * masks[lines, tap - 1 : tap]
                sums[tap] = sums[tap] + jnp.sum(value, axis=0, keepdims=True)
        for tap in range(3):
            tap_sums[tap : tap + 1] = sums[tap]
        for kind in range(1, 4):
            mixer_right(kind).start()

    def in_ready():
        hone_first.wait_recv()
        hone_second.start()
        h_one_reload.wait()
        turned(1, dh_got, 0, 0)
        hone_second.wait_recv()
        turned(1, cot_peer, 0, tokens)
        got_mixer_right(1)

    back_away = remote("bh1", away, pair_got, {"tp": core_mate})
    back_pair = remote("bh2", pair, both_got, {"tp": outer_mate})
    back_last = remote("bh3", mixer.at[core], mixer.at[core], {"tp": core_mate})

    def to_inputs(lines, which):
        total = None
        for column in range(3):
            term = lax.dot_general(
                ffn_v[0, column, lines], in_v[which, column],
                (((1,), (1,)), ((), ())), preferred_element_type=WIDE,
            )
            total = term if total is None else total + term
        return total

    def back_one_hop():
        for copy in (dh_away, dh_pair, dh_last):
            copy.wait_send()
        for copy in in_reloads:
            copy.wait()

        def body(lines):
            away[lines] = to_inputs(lines, 1 - core).astype(LOW)

        over_tiles(body)
        back_away.start()

        def rest(lines):
            dh_sum[0, lines] = to_inputs(lines, core)

        over_tiles(rest)

    def back_two_hops():
        back_away.wait_recv()

        def body(lines):
            pair[lines] = (dh_sum[0, lines] + pair_got[lines].astype(WIDE)).astype(LOW)

        over_tiles(body)
        back_pair.start()
        got_mixer_right(2)

    def back_three_hops():
        back_pair.wait_recv()

        def body(lines):
            mixer[core, lines] = (pair[lines].astype(WIDE) + both_got[lines].astype(WIDE)).astype(LOW)

        over_tiles(body)
        back_last.start()
        got_mixer_right(3)

    def give_back(step):
        to, origin = lax.rem(ctx + step, blocks), lax.rem(ctx + blocks - step, blocks)
        name = "give" + str(step)
        return (
            remote(name, back_blocks.at[to], dealt.at[ctx], {"ctx": to}),
            remote(name, back_blocks.at[to], dealt.at[origin], {"ctx": to}),
        )

    given = [give_back(step) for step in range(1, blocks)]
    kept = load(9, back_blocks.at[ctx], dealt.at[ctx])

    def input_back():
        back_last.wait_recv()

        @pl.loop(0, tokens // fine)
        def _(index):
            lines = pl.ds(pl.multiple_of(index * fine, fine), fine)
            own, other = x_full[lines, own_half].astype(WIDE), x_full[lines, peer_half].astype(WIDE)
            own_grad, other_grad = mixer[0, lines].astype(WIDE), mixer[1, lines].astype(WIDE)
            total = jnp.sum(own * own, axis=1, keepdims=True) + jnp.sum(other * other, axis=1, keepdims=True)
            scale = lax.rsqrt(total / width + EPS)
            own, other = own * scale, other * scale
            mean = (
                jnp.sum(own_grad * gains[0:1, own_half] * own, axis=1, keepdims=True)
                + jnp.sum(other_grad * gains[0:1, peer_half] * other, axis=1, keepdims=True)
            ) / width
            gain_sums[0:1, own_half] += jnp.sum(own_grad * own, axis=0, keepdims=True)
            gain_sums[0:1, peer_half] += jnp.sum(other_grad * other, axis=0, keepdims=True)
            which = jnp.where(outer == shard, 0, 1)
            scaled = mixer[which, lines, columns(core, part)].astype(WIDE) * gains[0:1, own_part]
            normed = x_full[lines, own_part].astype(WIDE) * scale
            d_resid[lines] = d_resid[lines] + scale * (scaled - normed * mean)

        for to in range(blocks):
            total = place[0, to] * d_resid[0:block_rows]
            for index in range(1, blocks):
                total = total + place[index, to] * d_resid[index * block_rows : (index + 1) * block_rows]
            back_blocks[to] = total.astype(LOW)
        for out, _ in given:
            out.start()
        kept.start()

    def event_third():
        over_shard("g3").wait_recv()
        over_shard("u3").wait_recv()
        ready(3)
        whole_feed(3)
        for kind in range(3):
            right_copy(3, kind).start()
        hone_first.start()
        mixer_right(0).start()
        got_right(2, 2)

    def dh_one_hop():
        whole_back(3)
        mixer_store.wait()
        for trio in hops:
            for copy in trio:
                copy.wait_send()

        def body(lines):
            away[lines] = dh_sum[1 - core, lines].astype(LOW)

        over_tiles(body)
        dh_away.start()

    def dh_two_hops():
        dh_away.wait_recv()

        def body(lines):
            pair[lines] = (dh_sum[core, lines] + pair_got[lines].astype(WIDE)).astype(LOW)

        over_tiles(body)
        dh_pair.start()
        reload()
        got_right(3, 0)

    def dh_three_hops():
        dh_pair.wait_recv()

        def body(lines):
            mixer[core, lines] = (pair[lines].astype(WIDE) + dh_got[lines].astype(WIDE)).astype(LOW)

        over_tiles(body)
        dh_last.start()
        got_right(3, 1)

    events = {
        0: event_start,
        2: event_first,
        3: lambda: whole_back(1),
        4: lambda: got_right(0, 2),
        6: lambda: got_right(1, 0),
        8: lambda: got_right(1, 1),
        10: event_second,
        11: lambda: whole_back(2),
        12: lambda: got_right(2, 0),
        14: lambda: got_right(2, 1),
        16: event_third,
        17: dh_one_hop,
        18: dh_two_hops,
        20: dh_three_hops,
        21: resid_back,
        22: lambda: got_right(3, 2),
        23: conv_back,
        24: out_ready,
        25: proj_back,
        26: in_ready,
        27: back_one_hop,
        28: back_two_hops,
        30: back_three_hops,
        31: input_back,
    }

    @pl.loop(0, pieces_in_all)
    def _(piece):
        for turn, event in events.items():
            pl.when(piece == turn)(event)
        grad_piece(piece)

    @pl.when(middle)
    def _():
        finish(pieces_in_all - 1)

    for out, _ in x_deals + cot_deals:
        out.wait_send()
    for copy in (cot_outer, cot_core, cot_more, cot_first,
                 hone_first, hone_second, dr_first, dr_second, back_away, back_pair, back_last):
        copy.wait_send()
    for name in pieces:
        over_shard(name).wait_send()
        if name not in direct:
            over_ctx(name).wait_send()
    for kind in (1, 2):
        right_copy(CHUNKS - 1, kind).wait_send()
    for kind in range(4):
        mixer_right(kind).wait_send()
    kept.wait()
    for out, into in given:
        out.wait_send()
        into.wait_recv()

    @pl.when(ctx < blocks - 1)
    def _():
        rim_copy.wait_send()

    @pl.when(ctx > 0)
    def _():
        rim_out.wait_send()

    @pl.loop(0, pieces_in_all)
    def _(piece):
        @pl.when(piece >= pieces_in_all - SLOTS)
        def _():
            inward_copy(piece, outer_land, outer_recv).wait_send()

        @pl.when(jnp.logical_and(middle, piece >= pieces_in_all - TOTALS))
        def _():
            outward_copy(piece).wait_send()
            total_store(piece).wait()

        @pl.when(end)
        def _():
            outward_copy(piece).wait_recv()


FRONT_COPIES = 88


def front(x_blocks, cot_blocks, place, gains, masks, taps, in_w, out_w, gate_w, up_w, down_w):
    tokens = x_blocks.shape[0] * x_blocks.shape[1]
    part = x_blocks.shape[2]
    width = gains.shape[1]
    half = width // 2
    rows, hidden = gate_w.shape
    chunk = hidden // CHUNKS
    pieces = (3 * hidden + width) // PIECE
    vmem = pl.BlockSpec(memory_space=pltpu.VMEM)
    hbm = pl.BlockSpec(memory_space=pl.ANY)
    shape = jax.ShapeDtypeStruct
    outs = [
        shape(in_w.shape, LOW),
        shape(out_w.shape, LOW),
        shape(gate_w.shape, LOW),
        shape(up_w.shape, LOW),
        shape((pieces, rows, PIECE), LOW),
        shape((pieces, rows, PIECE), LOW),
        shape((tokens, 3 * hidden + width), LOW),
        shape((tokens, width), LOW),
        shape((tokens, width), LOW),
        shape((2, tokens, half), LOW),
        shape((tokens, hidden), LOW),
        shape((rows, 3 * hidden + width), LOW),
        shape(x_blocks.shape, LOW),
        shape((3, part), WIDE),
        shape((2, width), WIDE),
    ]
    low, wide = (lambda *dims: pltpu.VMEM(dims, LOW)), (lambda *dims: pltpu.VMEM(dims, WIDE))
    dma = pltpu.SemaphoreType.DMA
    scratch = [
        low(*x_blocks.shape),
        low(*x_blocks.shape),
        low(tokens, width),
        low(tokens, width),
        low(tokens, width),
        low(tokens, half),
        low(tokens, width),
        low(tokens, half),
        wide(3, tokens, part),
        low(tokens, part),
        low(tokens, part),
        low(2, tokens, half),
        wide(tokens, part),
        low(2, rows, part),
        low(16, part),
        wide(tokens + 8, part),
        low(tokens, half),
        low(tokens, half),
        low(tokens, half),
        low(tokens, half),
        low(tokens, half),
        low(tokens, hidden),
        low(2, 3, rows, part),
        low(2, 2, rows, chunk),
        low(rows, hidden),
        wide(2, tokens, half),
        low(2, 3, tokens, chunk),
        low(3, tokens, chunk),
        low(rows, PIECE),
        low(rows, PIECE),
        low(SLOTS, rows, PIECE),
        low(TOTALS, rows, PIECE),
        wide(tokens + 8, part),
        low(16, part),
        low(16, part),
        dma((FRONT_COPIES,)),
        dma((FRONT_COPIES,)),
        dma((28,)),
    ] + [dma((pieces,)) for _ in range(6)]
    return pl.pallas_call(
        front_kernel,
        out_shape=outs,
        in_specs=[vmem, vmem, pl.BlockSpec(memory_space=pltpu.SMEM)] + [vmem] * 3
        + [hbm] * 5,
        out_specs=[hbm] * (len(outs) - 2) + [vmem] * 2,
        scratch_shapes=scratch,
        compiler_params=pltpu.CompilerParams(
            collective_id=2, has_side_effects=True, vmem_limit_bytes=63 * 1024 * 1024
        ),
        cost_estimate=pl.CostEstimate(
            flops=2 * tokens * width * hidden * 64, bytes_accessed=1 << 29, transcendentals=0
        ),
    )(x_blocks, cot_blocks, place, gains, masks, taps, in_w, out_w, gate_w, up_w, down_w)


class Features:
    def __init__(self):
        rank = lax.axis_index("tp")
        self.rank = rank
        self.inner = rank % 2
        self.outer = rank // 2

    def gather(self, own):
        other = swapped(own, "tp", 2)
        first = self.outer == 0
        pair = jnp.stack([jnp.where(first, own, other), jnp.where(first, other, own)])
        more = swapped(pair, "tp", 1)
        even = self.inner == 0
        left, right = jnp.where(even, pair, more), jnp.where(even, more, pair)
        return jnp.concatenate([left[0], right[0], left[1], right[1]], axis=1)

    def total(self, first_half, second_half):
        even = self.inner == 0
        kept = jnp.where(even, first_half, second_half)
        sent = jnp.where(even, second_half, first_half).astype(LOW)
        pair = (kept.astype(WIDE) + swapped(sent, "tp", 1).astype(WIDE)).astype(LOW)
        both = (pair.astype(WIDE) + swapped(pair, "tp", 2).astype(WIDE)).astype(LOW)
        other = swapped(both, "tp", 1)
        return jnp.where(even, both, other), jnp.where(even, other, both)

    def scatter(self, full):
        rows, width = full.shape
        blocks = full.reshape(rows, 2, 2, width // 4)
        even = self.inner == 0
        kept = jnp.where(even, blocks[:, :, 0], blocks[:, :, 1])
        sent = jnp.where(even, blocks[:, :, 1], blocks[:, :, 0]).astype(LOW)
        pair = kept.astype(WIDE) + swapped(sent, "tp", 1).astype(WIDE)
        first = self.outer == 0
        mine = jnp.where(first, pair[:, 0], pair[:, 1])
        away = jnp.where(first, pair[:, 1], pair[:, 0]).astype(LOW)
        return mine + swapped(away, "tp", 2).astype(WIDE)

    def all_terms(self, full):
        low = full.astype(LOW)
        return [low] + [swapped(low, "tp", step) for step in (1, 2, 3)]

    def own_terms(self, full):
        width = full.shape[1] // 4
        blocks = [
            lax.dynamic_slice_in_dim(full, (self.rank ^ step) * width, width, 1).astype(LOW)
            for step in range(4)
        ]
        return blocks[:1] + [swapped(blocks[step], "tp", step) for step in (1, 2, 3)]

    def own(self, full, axis):
        width = full.shape[axis] // lax.axis_size("tp")
        return lax.dynamic_slice_in_dim(full, self.rank * width, width, axis)


class Shards:
    def __init__(self, tp):
        self.count = lax.axis_size("shard")
        self.rank = lax.axis_index("shard")
        self.ctx_rank = lax.axis_index("ctx")
        self.tp = tp
        self.paired = self.count == 2

    def weight(self, rows):
        if not self.paired:
            return (lax.all_gather(rows, "shard", axis=0, tiled=True),)
        return (rows, swapped(rows, "shard", 1))

    def split(self, full):
        if not self.paired:
            return (full,)
        width = full.shape[1] // 2
        return (
            lax.dynamic_slice_in_dim(full, self.rank * width, width, 1),
            lax.dynamic_slice_in_dim(full, (1 - self.rank) * width, width, 1),
        )

    def join(self, parts):
        if not self.paired:
            return parts[0]
        first = self.rank == 0
        return jnp.concatenate(
            [jnp.where(first, parts[0], parts[1]), jnp.where(first, parts[1], parts[0])], axis=1
        )

    def columns(self, full):
        if not self.paired:
            return lax.all_to_all(full, "shard", split_axis=1, concat_axis=0, tiled=True)
        own, other = self.split(full)
        width = own.shape[1] // 2
        part = lax.dynamic_slice_in_dim(other, self.tp.inner * width, width, 1)
        got = swapped(part, "shard", 1)
        rest = swapped(got, "tp", 1)
        even = self.tp.inner == 0
        peer = jnp.concatenate([jnp.where(even, got, rest), jnp.where(even, rest, got)], axis=1)
        return jnp.concatenate([own, peer], axis=0)

    def tokens(self, own):
        if not self.paired:
            return lax.all_gather(own, "shard", axis=0, tiled=True)
        return jnp.concatenate([own, swapped(own, "shard", 1)], axis=0)

    def own_total(self, product):
        if not self.paired:
            return lax.psum_scatter(product, "shard", scatter_dimension=0, tiled=True)
        rows = product.shape[0] // 2
        return product[:rows] + swapped(product[rows:].astype(LOW), "shard", 1).astype(WIDE)

    def own_tokens(self, product):
        if not self.paired:
            return lax.all_to_all(product.astype(LOW), "shard", split_axis=0, concat_axis=1, tiled=True)
        rows = product.shape[0] // 2
        return self.join([product[:rows].astype(LOW), swapped(product[rows:].astype(LOW), "shard", 1)])


def on_device(
    hidden_in,
    out_grad,
    seq_lengths,
    deal_order,
    in_weight,
    conv_weight,
    out_weight,
    norm1_gain,
    norm2_gain,
    gate_weight,
    up_weight,
    down_weight,
):
    ctx_size = lax.axis_size("ctx")
    ctx_rank = lax.axis_index("ctx")
    tp = Features()
    shards = Shards(tp)
    row_count, col_count = hidden_in.shape
    hidden_count = gate_weight.shape[1]
    weight_rows = in_weight.shape[0]
    per_dev = deal_order.shape[1] // ctx_size
    per_peer = per_dev // ctx_size
    block_rows = row_count // per_dev
    dealing = deal_order[0].reshape(ctx_size, per_dev)
    own_blocks = lax.dynamic_index_in_dim(dealing, ctx_rank, 0, keepdims=False)
    send_order = jnp.argsort(own_blocks // per_dev, stable=True)
    wanted = jnp.where(dealing // per_dev == ctx_rank, 0, 1)
    chosen = jnp.argsort(wanted, axis=1, stable=True)[:, :per_peer]
    targets = (jnp.take_along_axis(dealing, chosen, 1) % per_dev).reshape(-1)
    placing = jnp.argsort(targets)
    returning = jnp.argsort(send_order)

    def reorder(values, index):
        blocks = values.reshape(per_dev, block_rows, values.shape[1])
        return blocks[index].reshape(row_count, values.shape[1])

    def to_packed(values):
        got = lax.all_to_all(
            reorder(values, send_order), "ctx", split_axis=0, concat_axis=0, tiled=True
        )
        return reorder(got, placing)

    def to_dealt(values):
        got = lax.all_to_all(
            reorder(values, targets), "ctx", split_axis=0, concat_axis=0, tiled=True
        )
        return reorder(got, returning)

    def weight_grads(lefts, rights, identity):
        flat = [value for group in rights for value in group]
        if shards.paired:
            summed = line_grads([group[0] for group in lefts], flat, identity)
            ends = [0]
            for value in flat:
                ends.append(ends[-1] + value.shape[1])
            return [summed[:, a:b] for a, b in zip(ends, ends[1:])]
        flat_lefts = [value for group in lefts for value in group]
        return [
            sum_line(contract_rows(left, shards.tokens(right)).astype(LOW), ctx_rank)
            for left, right in zip(flat_lefts, flat)
        ]

    lengths = seq_lengths[0]
    starts = jnp.cumsum(lengths) - lengths
    where_t = ctx_rank * row_count - 2 + jnp.arange(row_count + 4, dtype=jnp.int32)
    seq_begin = jnp.max(jnp.where(starts[None, :] <= where_t[:, None], starts[None, :], 0), axis=1)
    position = where_t - seq_begin
    first_own = (position[2 : row_count + 2] >= 1).astype(WIDE)[:, None]
    second_own = (position[2 : row_count + 2] >= 2).astype(WIDE)[:, None]
    first_next = (position[3 : row_count + 3] >= 1).astype(WIDE)[:, None]
    second_next = (position[4 : row_count + 4] >= 2).astype(WIDE)[:, None]
    conv_taps = conv_weight.astype(WIDE)
    gains = tp.gather(jnp.stack([norm1_gain, norm2_gain])).astype(WIDE)
    gain_one, gain_two = gains[0], gains[1]
    in_parts = jnp.moveaxis(in_weight, 1, 0)

    if shards.paired:
        def blocks_of(values):
            return reorder(values, send_order).reshape(per_dev, block_rows, col_count)

        place = (targets[None, :] == jnp.arange(per_dev)[:, None]).astype(WIDE)
        _, _, _, _, _, _, rights_peer, x_full, _, mixer, act, sums, dealt, taps_grad, gain_sums = front(
            blocks_of(hidden_in), blocks_of(out_grad), place, gains,
            jnp.concatenate([first_own, second_own, first_next, second_next], axis=1), conv_taps,
            in_parts, out_weight, gate_weight, up_weight, down_weight,
        )
        act_all = jnp.concatenate([act, rights_peer[:, :hidden_count]], axis=0)
        ffn_terms = tp.own_terms(shards.own_tokens(contract_cols(act_all, down_weight)))
        resid_own = tp.own(x_full, 1).astype(WIDE) + tp.own(shards.join([mixer[0], mixer[1]]), 1).astype(WIDE)
        block_out = (resid_own + added(ffn_terms)).astype(LOW)
        block_dealt = to_dealt(block_out)
        input_dealt = reorder(dealt.reshape(row_count, col_count), returning)
        ends = [hidden_count, 2 * hidden_count, 3 * hidden_count, 3 * hidden_count + col_count]
        parts = [value.astype(WIDE) for value in jnp.split(sums, ends, axis=1)]
        down_total, gate_total, up_total, out_total, in_flat_total = parts
        in_total = in_flat_total.reshape(in_weight.shape)
        gain_one_grad, gain_two_grad = tp.own(gain_sums, 1)
    else:
        in_w = shards.weight(in_weight.reshape(weight_rows, -1))
        x_full = tp.gather(to_packed(hidden_in))
        out_w = shards.weight(out_weight)
        cot_full = tp.gather(to_packed(out_grad))
        gate_w, up_w = shards.weight(gate_weight), shards.weight(up_weight)
        x_float = x_full.astype(WIDE)
        scale_one = lax.rsqrt(jnp.mean(x_float * x_float, axis=1, keepdims=True) + EPS)
        normed_one = x_float * scale_one
        h_one = (normed_one * gain_one).astype(LOW)
        projected = matmul(h_one, in_w[0])
        b_part = projected[:, :col_count]
        c_part = projected[:, col_count : 2 * col_count]
        v_part = projected[:, 2 * col_count :]
        mixed = (b_part * v_part).astype(LOW)
        rim = shifted(mixed[-2:], "ctx", 1)
        extended = jnp.concatenate([rim, mixed], axis=0).astype(WIDE)
        prev_one = extended[1 : row_count + 1] * first_own
        prev_two = extended[0:row_count] * second_own
        conv_out = (
            conv_taps[0] * extended[2:] + conv_taps[1] * prev_one + conv_taps[2] * prev_two
        )
        gated = (c_part * conv_out).astype(LOW)
        mixer_halves = jnp.split(contract_cols(gated, out_w[0]), 2, axis=1)
        mixer_out = jnp.concatenate(tp.total(*mixer_halves), axis=1)
        resid = x_float + mixer_out.astype(WIDE)
        scale_two = lax.rsqrt(jnp.mean(resid * resid, axis=1, keepdims=True) + EPS)
        normed_two = resid * scale_two
        h_two = (normed_two * gain_two).astype(LOW)
        cot_cols, h_two_cols, h_one_cols = [shards.columns(v) for v in (cot_full, h_two, h_one)]
        gate_pre, up_pre = matmul(h_two, gate_w[0]), matmul(h_two, up_w[0])
        d_act = shards.own_total(matmul(cot_cols, down_weight))
        sigmoid_gate = jax.nn.sigmoid(gate_pre)
        silu_gate = gate_pre * sigmoid_gate
        d_gate = d_act * up_pre * sigmoid_gate * (1.0 + gate_pre * (1.0 - sigmoid_gate))
        ffn_rights = [v.astype(LOW) for v in (silu_gate * up_pre, d_gate, d_act * silu_gate)]
        act_all = shards.tokens(ffn_rights[0])
        dh_terms = tp.all_terms(
            contract_cols(ffn_rights[1], gate_w[0]) + contract_cols(ffn_rights[2], up_w[0])
        )
        dh_two = added(dh_terms)
        ffn_grads = weight_grads(
            [[cot_cols], [h_two_cols, h_two_cols]], [ffn_rights[:1], ffn_rights[1:]], 0
        )

        ffn_terms = tp.own_terms(shards.own_tokens(contract_cols(act_all, down_weight)))

        rim = shifted(mixed[-2:], "ctx", 1)
        extended = jnp.concatenate([rim, mixed], axis=0).astype(WIDE)
        prev_one = extended[1 : row_count + 1] * first_own
        prev_two = extended[0:row_count] * second_own
        mixed_float = extended[2:]

        gain_two_grad = tp.own(jnp.sum(dh_two * normed_two, axis=0), 0)
        d_resid = cot_full.astype(WIDE) + norm_back(dh_two, normed_two, scale_two, gain_two)
        d_resid_low = d_resid.astype(LOW)
        d_gated = sum(matmul(part, w) for part, w in zip(shards.split(d_resid_low), out_w))
        d_conv = (d_gated * c_part).astype(LOW)
        d_c_part = d_gated * conv_out
        rim_back = shifted(d_conv[:2], "ctx", -1)
        d_conv_float = d_conv.astype(WIDE)
        back_ext = jnp.concatenate([d_conv, rim_back], axis=0).astype(WIDE)
        d_mixed = (
            conv_taps[0] * d_conv_float
            + conv_taps[1] * back_ext[1 : row_count + 1] * first_next
            + conv_taps[2] * back_ext[2:] * second_next
        )
        taps_grad = jnp.stack(
            [
                jnp.sum(d_conv_float * mixed_float, axis=0),
                jnp.sum(d_conv_float * prev_one, axis=0),
                jnp.sum(d_conv_float * prev_two, axis=0),
            ]
        )
        d_proj = [
            (d_mixed * v_part).astype(LOW),
            d_c_part.astype(LOW),
            (d_mixed * b_part).astype(LOW),
        ]
        d_proj_flat = jnp.concatenate(d_proj, axis=1)
        dh_one_terms = tp.all_terms(shards.join([contract_cols(d_proj_flat, w) for w in in_w]))
        mixer_grads = weight_grads(
            [[shards.columns(d_resid_low)], [h_one_cols]], [[gated], [d_proj_flat]], 1
        )
        dh_one_terms, ffn_terms, mixer_grads = lax.optimization_barrier(
            (dh_one_terms, ffn_terms, mixer_grads)
        )
        dh_one = added(dh_one_terms)
        block_out = (tp.own(resid, 1) + added(ffn_terms)).astype(LOW)
        down_total, gate_total, up_total = [value.astype(WIDE) for value in ffn_grads]
        out_total, in_flat_total = [value.astype(WIDE) for value in mixer_grads]
        in_total = in_flat_total.reshape(in_weight.shape)
        gain_one_grad = tp.own(jnp.sum(dh_one * normed_one, axis=0), 0)
        d_input = d_resid + norm_back(dh_one, normed_one, scale_one, gain_one)
        dealt = to_dealt(jnp.concatenate([block_out, tp.own(d_input, 1).astype(LOW)], axis=1))
        block_dealt, input_dealt = dealt[:, :col_count], dealt[:, col_count:]

    small = jnp.concatenate([taps_grad, gain_one_grad[None], gain_two_grad[None]], axis=0)
    small_sum = butterfly_sum(butterfly_sum(small, "shard"), "ctx")
    return (
        block_dealt,
        input_dealt,
        in_total,
        small_sum[0:3],
        out_total,
        small_sum[3],
        small_sum[4],
        gate_total,
        up_total,
        down_total,
    )


def solution(mesh):
    placed = (
        P(("shard", "ctx"), "tp"),
        P(("shard", "ctx"), "tp"),
        P("shard", None),
        P("shard", None),
        P("shard", None, "tp"),
        P(None, "tp"),
        P("shard", "tp"),
        P("tp"),
        P("tp"),
        P("shard", "tp"),
        P("shard", "tp"),
        P("shard", "tp"),
    )
    return jax.shard_map(
        on_device,
        mesh=mesh,
        in_specs=placed,
        out_specs=(
            P(("shard", "ctx"), "tp"),
            P(("shard", "ctx"), "tp"),
            P("shard", None, "tp"),
            P(None, "tp"),
            P("shard", "tp"),
            P("tp"),
            P("tp"),
            P("shard", "tp"),
            P("shard", "tp"),
            P("shard", "tp"),
        ),
        check_vma=False,
    )
```

```python
import jax
import jax.numpy as jnp
from jax import lax
from jax.experimental import pallas as pl
from jax.experimental.pallas import tpu as pltpu
from jax.sharding import PartitionSpec as P

EPS = 1e-05
LOW = jnp.bfloat16
WIDE = jnp.float32
CHUNKS = 4


def shifted(value, axis, steps):
    count = lax.axis_size(axis)
    leading, last = (max(0, -steps), min(count, count - steps))
    return lax.ppermute(value, axis, [(source, source + steps) for source in range(leading, last)])


def swapped(value, axis, step):
    count = lax.axis_size(axis)
    return lax.ppermute(value, axis, [(source, source ^ step) for source in range(count)])


def matmul(left, right):
    return jnp.dot(left, right, preferred_element_type=WIDE)


def contract_rows(left, right):
    return lax.dot_general(left, right, (((0,), (0,)), ((), ())), preferred_element_type=WIDE)


def contract_cols(left, right):
    return lax.dot_general(left, right, (((1,), (1,)), ((), ())), preferred_element_type=WIDE)


def added(terms):
    return sum(term.astype(WIDE) for term in terms)


def norm_back(grad_out, normed, scale_row, gain):
    scaled = grad_out * gain
    return scale_row * (scaled - normed * jnp.mean(scaled * normed, axis=1, keepdims=True))


def butterfly_sum(value, axis):
    step = 1
    while step < lax.axis_size(axis):
        value = value + swapped(value, axis, step)
        step *= 2
    return value


def sum_line(piece, rank):
    from_end = lax.ppermute(piece, "ctx", [(0, 1), (3, 2)])
    half = (piece.astype(WIDE) + from_end.astype(WIDE)).astype(LOW)
    from_middle = lax.ppermute(half, "ctx", [(1, 2), (2, 1)])
    total = (half.astype(WIDE) + from_middle.astype(WIDE)).astype(LOW)
    handed = lax.ppermute(total, "ctx", [(1, 0), (2, 3)])
    inner = jnp.logical_or(rank == 1, rank == 2)
    return jnp.where(inner, total, handed)


PIECE = 256
AHEAD = 4
SLOTS = 4
TOTALS = 2
MESH = pl.DeviceIdType.MESH


def front_kernel(
    x_blocks, cot_blocks, place, gains, masks, taps,
    in_w, out_w, gate_w, up_w, down_w,
    in_peer, out_peer, gate_peer, up_peer, outer_land, middle_land, rights_peer,
    x_out, h_one_out, mixer_out, act_out, grads, dealt, dealt_out, tap_sums, gain_sums,
    x_got, cot_got, x_full, h_one, cot_full, cot_peer, h_two, h_two_peer, proj, mixed, gated, mixer, conv_v,
    out_v, rim, extended, away, pair, pair_got, both_got, dh_got,
    da_got, in_v, gu_v, down_v, dh_sum, ffn_v, right_v, outer_v, middle_v, held, totals, d_ext, edge_v, rim_back,
    send, recv, local, in_send, outer_recv, middle_recv, out_send, out_recv, own_done,
):
    shard = lax.axis_index("shard")
    ctx = lax.axis_index("ctx")
    tp = lax.axis_index("tp")
    core, outer = tp % 2, tp // 2
    core_mate = tp + 1 - 2 * core
    outer_mate = lax.rem(tp + 2, 4)
    ctx_mate = ctx + 1 - 2 * (ctx % 2)
    tokens, width = x_full.shape
    part = width // 4
    half = width // 2
    blocks, block_rows = x_blocks.shape[0], x_blocks.shape[1]
    rows = out_w.shape[0]
    own_rows = pl.ds(pl.multiple_of((ctx % 2) * (rows // 2), rows // 2), rows // 2)
    other_rows = pl.ds(pl.multiple_of((1 - ctx % 2) * (rows // 2), rows // 2), rows // 2)
    hidden = gate_w.shape[1]
    chunk = hidden // CHUNKS

    barrier = pltpu.get_barrier_semaphore()
    mates = [{"shard": 1 - shard}, {"tp": core_mate}, {"tp": outer_mate}]
    mates += [{"ctx": lax.rem(ctx + step, blocks)} for step in range(1, blocks)]
    for mate in mates:
        pl.semaphore_signal(barrier, inc=1, device_id=mate, device_id_type=MESH)
    pl.semaphore_wait(barrier, len(mates))

    names = {}

    def remote(name, src, dst, mate):
        place_of = names.setdefault(name, len(names))
        return pltpu.make_async_remote_copy(
            src_ref=src, dst_ref=dst, send_sem=send.at[place_of], recv_sem=recv.at[place_of],
            device_id=mate, device_id_type=MESH,
        )

    def columns(start, size):
        return pl.ds(pl.multiple_of(start * size, size), size)

    own_part = columns(tp, part)
    own_half, peer_half = columns(shard, half), columns(1 - shard, half)

    def deal(name, source, target, step):
        to, origin = lax.rem(ctx + step, blocks), lax.rem(ctx + blocks - step, blocks)
        out = remote(name + str(step), source.at[to], target.at[ctx], {"ctx": to})
        into = remote(name + str(step), source.at[to], target.at[origin], {"ctx": to})
        return out, into

    def gather(name, full):
        mate = columns(outer_mate, part)
        return (
            remote(name + "outer", full.at[:, own_part], full.at[:, own_part], {"tp": outer_mate}),
            remote(name + "core", full.at[:, own_part], full.at[:, own_part], {"tp": core_mate}),
            remote(name + "more", full.at[:, mate], full.at[:, mate], {"tp": core_mate}),
        )

    pieces = {}
    for index, name in enumerate("bvc"):
        column = (0, 2, 1)[index]
        pieces[name] = (in_w.at[column], in_peer.at[column])
    pieces["o"] = (out_w, out_peer)
    for index in range(CHUNKS):
        strip = pl.ds(index * chunk, chunk)
        pieces["g%d" % index] = (gate_w.at[:, strip], gate_peer.at[:, strip])
        pieces["u%d" % index] = (up_w.at[:, strip], up_peer.at[:, strip])

    direct = ["%s%d" % (kind, index) for kind in "gu" for index in range(2, CHUNKS)]

    def over_shard(name):
        source, target = pieces[name]
        if name in direct:
            return remote(name + "x", source, target, {"shard": 1 - shard})
        return remote(name + "x", source.at[own_rows], target.at[own_rows], {"shard": 1 - shard})

    def over_ctx(name):
        target = pieces[name][1]
        return remote(name + "z", target.at[own_rows], target.at[own_rows], {"ctx": ctx_mate})

    def pump(name):
        over_shard(name).wait_recv()
        over_ctx(name).start()

    def load(index, source, target):
        return pltpu.make_async_copy(source, target, local.at[index])

    x_deals = [deal("x", x_blocks, x_got, step) for step in range(1, blocks)]
    cot_deals = [deal("cot", cot_blocks, cot_got, step) for step in range(1, blocks)]
    for out, _ in x_deals:
        out.start()
    for name in ("b", "v", "c", "o", "g0", "u0"):
        over_shard(name).start()
    own_loads = [load(index, in_w.at[index], in_v.at[0, index]) for index in range(3)]
    own_loads.append(load(3, out_w, out_v.at[0]))
    own_loads.append(load(4, down_w, down_v))
    for copy in own_loads:
        copy.start()

    def packed(source, got, deals, full):
        got[ctx] = source[ctx]
        for _, into in deals:
            into.wait_recv()
        for index in range(blocks):
            total = place[index, 0] * got[0].astype(WIDE)
            for other in range(1, blocks):
                total = total + place[index, other] * got[other].astype(WIDE)
            full[index * block_rows : (index + 1) * block_rows, own_part] = total.astype(LOW)

    pump("b")
    packed(x_blocks, x_got, x_deals, x_full)
    x_outer, x_core, x_more = gather("xg", x_full)
    x_outer.start()
    x_core.start()
    for out, _ in cot_deals:
        out.start()
    pump("v")
    x_outer.wait_recv()
    x_more.start()
    packed(cot_blocks, cot_got, cot_deals, cot_full)
    cot_outer, cot_core, cot_more = gather("cg", cot_full)
    cot_outer.start()
    cot_core.start()
    x_core.wait_recv()
    x_more.wait_recv()

    x_store = load(5, x_full, x_out)
    x_store.start()
    step = min(64, tokens)

    @pl.loop(0, tokens // step)
    def _(index):
        lines = pl.ds(pl.multiple_of(index * step, step), step)
        value = x_full[lines].astype(WIDE)
        scale = lax.rsqrt(jnp.mean(value * value, axis=1, keepdims=True) + EPS)
        h_one[lines] = (value * scale * gains[0:1]).astype(LOW)

    h_one_store = load(6, h_one, h_one_out)
    h_one_store.start()
    pump("c")

    def columns_out(name, full, got):
        strip = pl.ds(pl.multiple_of((1 - shard) * half + core * part, part), part)
        target = columns(core, part)
        first = remote(name + "x", full.at[:, strip], got.at[:, target], {"shard": 1 - shard})
        second = remote(name + "core", got.at[:, target], got.at[:, target], {"tp": core_mate})
        return first, second

    cot_first, cot_second = columns_out("cc", cot_full, cot_peer)

    tile = min(256, tokens)

    def over_tiles(body):
        @pl.loop(0, tokens // tile)
        def _(index):
            body(pl.ds(pl.multiple_of(index * tile, tile), tile))

    def project(column, name):
        target = load(column, in_peer.at[column], in_v.at[1, column])
        own_loads[column].wait()
        over_ctx(name).wait_recv()
        target.start()
        target.wait()

        def body(lines):
            proj[column, lines] = jnp.dot(
                h_one[lines, own_half], in_v[0, column], preferred_element_type=WIDE
            ) + jnp.dot(h_one[lines, peer_half], in_v[1, column], preferred_element_type=WIDE)

        over_tiles(body)

    project(0, "b")
    project(2, "v")
    edge = 16
    rim_copy = remote(
        "rim", mixed.at[pl.ds(tokens - edge, edge)], rim, {"ctx": lax.rem(ctx + 1, blocks)}
    )

    def mix(lines):
        value = (proj[0, lines] * proj[2, lines]).astype(LOW)
        mixed[lines] = value
        extended[pl.ds(lines.start + 8, tile)] = value.astype(WIDE)

    over_tiles(mix)

    @pl.when(ctx < blocks - 1)
    def _():
        rim_copy.start()

    pump("o")
    cot_outer.wait_recv()
    cot_more.start()
    project(1, "c")

    @pl.when(ctx > 0)
    def _():
        rim_copy.wait_recv()
        extended[0:8] = rim[8:16].astype(WIDE)

    @pl.when(ctx == 0)
    def _():
        extended[0:8] = jnp.zeros((8, part), WIDE)

    for start in range(0, tokens, tile):
        lines = pl.ds(start, tile)
        value = taps[0:1] * extended[pl.ds(start + 8, tile)]
        value = value + taps[1:2] * (extended[pl.ds(start + 7, tile)] * masks[lines, 0:1])
        value = value + taps[2:3] * (extended[pl.ds(start + 6, tile)] * masks[lines, 1:2])
        conv_v[lines] = value
        gated[lines] = (proj[1, lines] * value).astype(LOW)

    pump("g0")
    cot_core.wait_recv()
    cot_more.wait_recv()
    cot_first.start()
    over_shard("g1").start()
    out_load = load(3, out_peer, out_v.at[1])
    own_loads[3].wait()
    over_ctx("o").wait_recv()
    out_load.start()
    out_load.wait()

    def to_half(lines, which):
        return lax.dot_general(
            gated[lines], out_v[which], (((1,), (1,)), ((), ())), preferred_element_type=WIDE
        )

    stages = [pl.ds(start, tile) for start in range(0, tokens, tile)]
    hops = []
    for index, lines in enumerate(stages):
        first = remote("ma%d" % index, away.at[lines], pair_got.at[lines], {"tp": core_mate})
        second = remote("mb%d" % index, pair.at[lines], both_got.at[lines], {"tp": outer_mate})
        third = remote("mc%d" % index, mixer.at[core, lines], mixer.at[core, lines], {"tp": core_mate})
        hops.append((first, second, third))
        away[lines] = to_half(lines, 1 - core).astype(LOW)
        first.start()
    for index, lines in enumerate(stages):
        value = to_half(lines, core)
        hops[index][0].wait_recv()
        pair[lines] = (value + pair_got[lines].astype(WIDE)).astype(LOW)
        hops[index][1].start()

    da_send, da_own = h_one, x_full
    pump("u0")
    cot_first.wait_recv()
    cot_second.start()
    cot_second.wait()
    own_loads[4].wait()
    h_one_store.wait()

    def da_copy(index):
        strip = pl.ds(index * chunk, chunk)
        return remote("da%d" % index, da_send.at[:, strip], da_got.at[:, strip], {"shard": 1 - shard})

    for index in range(CHUNKS):
        strip = pl.ds(index * chunk, chunk)

        def send_part(lines):
            da_send[lines, strip] = jnp.dot(
                cot_peer[lines], down_v[:, strip], preferred_element_type=WIDE
            ).astype(LOW)

        over_tiles(send_part)
        if index == 0:
            da_copy(0).start()
            over_shard("u1").start()

    for index, lines in enumerate(stages):
        hops[index][1].wait_recv()
        mixer[core, lines] = (pair[lines].astype(WIDE) + both_got[lines].astype(WIDE)).astype(LOW)
        hops[index][2].start()
    pump("g1")
    for index, lines in enumerate(stages):
        hops[index][2].wait_recv()
    mixer_store = load(12, mixer, mixer_out)
    mixer_store.start()

    @pl.loop(0, tokens // step)
    def _(index):
        lines = pl.ds(pl.multiple_of(index * step, step), step)
        own = x_full[lines, own_half].astype(WIDE) + mixer[0, lines].astype(WIDE)
        other = x_full[lines, peer_half].astype(WIDE) + mixer[1, lines].astype(WIDE)
        total = jnp.sum(own * own, axis=1, keepdims=True) + jnp.sum(other * other, axis=1, keepdims=True)
        scale = lax.rsqrt(total / width + EPS)
        h_two[lines, own_half] = (own * scale * gains[1:2, own_half]).astype(LOW)
        h_two[lines, peer_half] = (other * scale * gains[1:2, peer_half]).astype(LOW)

    h_two_first, h_two_second = columns_out("hc", h_two, h_two_peer)
    x_store.wait()
    for copy in (x_outer, x_core, x_more):
        copy.wait_send()

    def own_part_of(lines):
        for index in range(CHUNKS):
            strip = pl.ds(index * chunk, chunk)
            da_own[lines, strip] = jnp.dot(
                cot_full[lines, own_half], down_v[:, strip], preferred_element_type=WIDE
            ).astype(LOW)

    over_tiles(own_part_of)

    def turned(place_of, source, start, first):
        for row in range(0, half, 256):
            for line in range(0, tokens, 256):
                block = source[pl.ds(line, 256), pl.ds(pl.multiple_of(start + row, 256), 256)]
                down_v[pl.ds(row, 256), pl.ds(place_of * half + first + line, 256)] = block.T

    turned(0, cot_full, shard * half, 0)
    turned(0, cot_peer, 0, tokens)
    turned(1, h_two, shard * half, 0)

    def own_weights(index):
        strip = pl.ds(index * chunk, chunk)
        room = gu_v if index % 2 == 0 else in_v
        base = 13 + 4 * (index % 2)
        return [
            load(base, gate_w.at[:, strip], room.at[0, 0]),
            load(base + 1, up_w.at[:, strip], room.at[0, 1]),
        ]

    def peer_weights(index):
        strip = pl.ds(index * chunk, chunk)
        room = gu_v if index % 2 == 0 else in_v
        base = 15 + 4 * (index % 2)
        return [
            load(base, gate_peer.at[:, strip], room.at[1, 0]),
            load(base + 1, up_peer.at[:, strip], room.at[1, 1]),
        ]

    def act_store(index):
        return load(21 + index % 2, ffn_v.at[index % 2, 0], act_out.at[:, pl.ds(index * chunk, chunk)])

    def right_copy(index, kind):
        strip = pl.ds(kind * hidden + index * chunk, chunk)
        return remote(
            "r%d%d" % (index, kind), ffn_v.at[index % 2, kind], rights_peer.at[:, strip], {"shard": 1 - shard}
        )

    def right_load(index, kind):
        strip = pl.ds(kind * hidden + index * chunk, chunk)
        return load(23 + kind, rights_peer.at[:, strip], right_v.at[kind])

    def ready(index):
        for kind in "gu":
            if "%s%d" % (kind, index) not in direct:
                over_ctx("%s%d" % (kind, index)).wait_recv()
        for copy in peer_weights(index):
            copy.start()

    def feed(index, lines):
        room = gu_v if index % 2 == 0 else in_v
        slot = index % 2
        strip = pl.ds(index * chunk, chunk)

        def pre(kind):
            return jnp.dot(
                h_two[lines, own_half], room[0, kind], preferred_element_type=WIDE
            ) + jnp.dot(h_two[lines, peer_half], room[1, kind], preferred_element_type=WIDE)

        gate_pre, up_pre = pre(0), pre(1)
        d_act = da_own[lines, strip].astype(WIDE) + da_got[lines, strip].astype(WIDE)
        sigmoid = jax.nn.sigmoid(gate_pre)
        silu = gate_pre * sigmoid
        ffn_v[slot, 0, lines] = (silu * up_pre).astype(LOW)
        ffn_v[slot, 1, lines] = (
            d_act * up_pre * sigmoid * (1.0 + gate_pre * (1.0 - sigmoid))
        ).astype(LOW)
        ffn_v[slot, 2, lines] = (d_act * silu).astype(LOW)

    def back(index, lines):
        room = gu_v if index % 2 == 0 else in_v
        slot = index % 2
        for place_of in range(2):
            term = lax.dot_general(
                ffn_v[slot, 1, lines], room[place_of, 0],
                (((1,), (1,)), ((), ())), preferred_element_type=WIDE,
            ) + lax.dot_general(
                ffn_v[slot, 2, lines], room[place_of, 1],
                (((1,), (1,)), ((), ())), preferred_element_type=WIDE,
            )
            if index > 0:
                term = term + dh_sum[place_of, lines]
            dh_sum[place_of, lines] = term

    def feed_start(index):
        da_copy(index).wait_recv()
        for copy in own_weights(index) + peer_weights(index):
            copy.wait()
        if index > 1:
            act_store(index - 2).wait()
            for kind in range(3):
                right_copy(index - 2, kind).wait_send()

    middle = jnp.logical_or(ctx == 1, ctx == 2)
    end = jnp.logical_not(middle)
    inward = jnp.where(ctx < 2, ctx + 1, ctx - 1)
    outward = jnp.where(ctx == 1, 0, 3)
    per_kind = chunk // PIECE
    per_chunk = 3 * per_kind
    ffn_pieces = CHUNKS * per_chunk
    pieces_in_all = ffn_pieces + 4 * part // PIECE
    line_rows = min(256, rows)

    def grad_columns(piece):
        index, turn = piece // per_chunk, piece % per_chunk
        kind, sub = turn // per_kind, turn % per_kind
        start = jnp.where(
            piece < ffn_pieces, kind * hidden + index * chunk + sub * PIECE, piece * PIECE
        )
        return pl.ds(pl.multiple_of(start, PIECE), PIECE)

    def inward_copy(piece, land, sems):
        return pltpu.make_async_remote_copy(
            src_ref=held.at[piece % SLOTS], dst_ref=land.at[piece], send_sem=in_send.at[piece],
            recv_sem=sems.at[piece], device_id={"ctx": inward}, device_id_type=MESH,
        )

    def outward_copy(piece):
        return pltpu.make_async_remote_copy(
            src_ref=totals.at[piece % TOTALS], dst_ref=grads.at[:, grad_columns(piece)], send_sem=out_send.at[piece],
            recv_sem=out_recv.at[piece], device_id={"ctx": outward}, device_id_type=MESH,
        )

    def total_store(piece):
        return pltpu.make_async_copy(totals.at[piece % TOTALS], grads.at[:, grad_columns(piece)], own_done.at[piece])

    def stage_in(piece, land, room):
        copy = pltpu.make_async_copy(land.at[piece], room, local.at[26])
        copy.start()
        copy.wait()

    def finish(piece):
        inward_copy(piece, middle_land, middle_recv).wait_recv()
        stage_in(piece, middle_land, middle_v)

        @pl.when(piece >= TOTALS)
        def _():
            outward_copy(piece - TOTALS).wait_send()
            total_store(piece - TOTALS).wait()

        @pl.loop(0, rows // line_rows)
        def _(start):
            lines = pl.ds(pl.multiple_of(start * line_rows, line_rows), line_rows)
            total = held[piece % SLOTS, lines].astype(WIDE) + middle_v[lines].astype(WIDE)
            totals[piece % TOTALS, lines] = total.astype(LOW)

        outward_copy(piece).start()
        total_store(piece).start()

    def grad_piece(piece):
        after = piece >= ffn_pieces
        turn = jnp.where(after, jnp.maximum(piece - ffn_pieces - per_kind, 0), piece % per_chunk)
        kind, sub = turn // per_kind, piece % per_kind
        slot = jnp.where(after, jnp.where(piece < ffn_pieces + per_kind, 1, 0), piece // per_chunk % 2)
        strip = pl.ds(pl.multiple_of(sub * PIECE, PIECE), PIECE)
        left_first = jnp.where(after, piece < ffn_pieces + per_kind, kind == 0)
        left = jnp.where(left_first, 0, half)

        @pl.when(piece >= SLOTS)
        def _():
            inward_copy(piece - SLOTS, outer_land, outer_recv).wait_send()

        def product(start):
            lines = pl.ds(pl.multiple_of(start * line_rows, line_rows), line_rows)
            own = jnp.dot(
                down_v[lines, pl.ds(pl.multiple_of(left, tokens), tokens)],
                ffn_v[slot, kind, :, strip],
                preferred_element_type=WIDE,
            )
            other = jnp.dot(
                down_v[lines, pl.ds(pl.multiple_of(left + tokens, tokens), tokens)],
                right_v[kind, :, strip],
                preferred_element_type=WIDE,
            )
            return lines, own + other

        @pl.when(end)
        def _():
            @pl.loop(0, rows // line_rows)
            def _(start):
                lines, value = product(start)
                held[piece % SLOTS, lines] = value.astype(LOW)

            inward_copy(piece, outer_land, outer_recv).start()

        @pl.when(middle)
        def _():
            inward_copy(piece, outer_land, outer_recv).wait_recv()
            stage_in(piece, outer_land, outer_v)

            @pl.loop(0, rows // line_rows)
            def _(start):
                lines, value = product(start)
                held[piece % SLOTS, lines] = (value + outer_v[lines].astype(WIDE)).astype(LOW)

            inward_copy(piece, middle_land, middle_recv).start()

            @pl.when(piece >= 1)
            def _():
                finish(piece - 1)

    def got_right(index, kind):
        right_copy(index, kind).wait_recv()
        copy = right_load(index, kind)
        copy.start()
        copy.wait()

    dh_away = remote("dh1", away, pair_got, {"tp": core_mate})
    dh_pair = remote("dh2", pair, dh_got, {"tp": outer_mate})
    dh_last = remote("dh3", mixer.at[core], mixer.at[core], {"tp": core_mate})
    tiles = [pl.ds(start, tile) for start in range(0, tokens, tile)]

    def whole_feed(index):
        feed_start(index)
        for lines in tiles:
            feed(index, lines)
        act_store(index).start()

    def whole_back(index):
        for lines in tiles:
            back(index, lines)
        if index + 1 < CHUNKS:
            for copy in own_weights(index + 1):
                copy.start()

    for copy in own_weights(0):
        copy.start()
    ready(0)
    whole_feed(0)
    right_copy(0, 0).start()
    da_copy(1).start()
    h_two_first.start()
    right_copy(0, 1).start()
    right_copy(0, 2).start()
    whole_back(0)
    pump("u1")

    def event_start():
        got_right(0, 0)

    def event_first():
        ready(1)
        whole_feed(1)
        for kind in range(3):
            right_copy(1, kind).start()
        for name in ("g2", "u2"):
            over_shard(name).start()
        da_copy(2).start()
        over_shard("g3").start()
        h_two_first.wait_recv()
        h_two_second.start()
        h_two_second.wait()
        turned(1, h_two_peer, 0, tokens)
        got_right(0, 1)

    def event_second():
        over_shard("g2").wait_recv()
        over_shard("u2").wait_recv()
        ready(2)
        whole_feed(2)
        right_copy(2, 0).start()
        right_copy(2, 1).start()
        over_shard("u3").start()
        da_copy(3).start()
        right_copy(2, 2).start()
        got_right(1, 2)

    back_blocks, d_resid, resid_own = cot_got, dh_sum.at[1, :, pl.ds(0, part)], dh_sum.at[1, :, pl.ds(part, part)]
    hone_first, hone_second = columns_out("ic", h_one_out, cot_peer)
    dr_first, dr_second = columns_out("dc", h_two, h_two_peer)
    mixer_rights = 3 * hidden

    def mixer_right(kind):
        source = gated if kind == 0 else ffn_v.at[0, kind - 1]
        strip = pl.ds(mixer_rights + kind * part, part)
        return remote("m%d" % kind, source, rights_peer.at[:, strip], {"shard": 1 - shard})

    def got_mixer_right(kind):
        mixer_right(kind).wait_recv()
        room = right_v.at[max(kind - 1, 0)]
        copy = load(23, rights_peer.at[:, pl.ds(mixer_rights + kind * part, part)], room)
        copy.start()
        copy.wait()

    x_reload = load(5, x_out, x_full)
    mixer_reloads = [
        load(6, mixer_out.at[0], h_one.at[:, own_half]), load(7, mixer_out.at[1], h_one.at[:, peer_half])
    ]
    h_one_reload = load(8, h_one_out.at[:, own_half], dh_got)
    in_reloads = [load(13 + column, in_w.at[column], in_v.at[0, column]) for column in range(3)]
    in_reloads += [load(16 + column, in_peer.at[column], in_v.at[1, column]) for column in range(3)]
    fine = min(32, tokens)

    def reload():
        for index in range(CHUNKS):
            da_copy(index).wait_send()
        act_store(CHUNKS - 1).wait()
        act_store(CHUNKS - 2).wait()
        for copy in [x_reload] + mixer_reloads + in_reloads + down_loads + [act_own_load]:
            copy.start()

    def resid_back():
        dh_last.wait_recv()
        h_one_reload.start()
        for copy in [x_reload] + mixer_reloads:
            copy.wait()
        h_two_first.wait_send()
        gain_sums[...] = jnp.zeros((2, width), WIDE)

        @pl.loop(0, tokens // fine)
        def _(index):
            lines = pl.ds(pl.multiple_of(index * fine, fine), fine)

            def halves(columns_of, which):
                resid = x_full[lines, columns_of].astype(WIDE) + h_one[lines, columns_of].astype(WIDE)
                return resid, mixer[which, lines].astype(WIDE)

            own, own_grad = halves(own_half, 0)
            other, other_grad = halves(peer_half, 1)
            total = jnp.sum(own * own, axis=1, keepdims=True) + jnp.sum(other * other, axis=1, keepdims=True)
            scale = lax.rsqrt(total / width + EPS)
            own, other = own * scale, other * scale
            own_scaled, other_scaled = own_grad * gains[1:2, own_half], other_grad * gains[1:2, peer_half]
            mean = (
                jnp.sum(own_scaled * own, axis=1, keepdims=True)
                + jnp.sum(other_scaled * other, axis=1, keepdims=True)
            ) / width
            h_two[lines, own_half] = (
                cot_full[lines, own_half].astype(WIDE) + scale * (own_scaled - own * mean)
            ).astype(LOW)
            h_two[lines, peer_half] = (
                cot_full[lines, peer_half].astype(WIDE) + scale * (other_scaled - other * mean)
            ).astype(LOW)
            gain_sums[1:2, own_half] += jnp.sum(own_grad * own, axis=0, keepdims=True)
            gain_sums[1:2, peer_half] += jnp.sum(other_grad * other, axis=0, keepdims=True)
            resid = x_full[lines, own_part].astype(WIDE) + h_one[lines, own_part].astype(WIDE)
            resid_own[lines] = resid
            which = jnp.where(outer == shard, 0, 1)
            scaled = mixer[which, lines, columns(core, part)].astype(WIDE) * gains[1:2, own_part]
            d_resid[lines] = cot_full[lines, own_part].astype(WIDE) + scale * (
                scaled - resid * scale * mean
            )

        dr_first.start()

    rim_out = remote(
        "rim_back", edge_v, rim_back, {"ctx": lax.rem(ctx + blocks - 1, blocks)}
    )

    def conv_back():
        for kind in range(3):
            right_copy(CHUNKS - 2, kind).wait_send()

        def body(lines):
            d_gated = jnp.dot(
                h_two[lines, own_half], out_v[0], preferred_element_type=WIDE
            ) + jnp.dot(h_two[lines, peer_half], out_v[1], preferred_element_type=WIDE)
            d_ext[lines] = (d_gated * proj[1, lines]).astype(LOW).astype(WIDE)
            ffn_v[0, 1, lines] = (d_gated * conv_v[lines]).astype(LOW)

        for lines in tiles:
            body(lines)
        edge_v[...] = d_ext[0:16].astype(LOW)

        @pl.when(ctx > 0)
        def _():
            rim_out.start()

        turned(0, h_two, shard * half, 0)

    def out_ready():
        dr_first.wait_recv()
        dr_second.start()
        right_copy(CHUNKS - 1, 0).wait_send()

        def body(lines):
            ffn_v[1, 0, lines] = gated[lines]

        over_tiles(body)
        dr_second.wait_recv()
        turned(0, h_two_peer, 0, tokens)
        got_mixer_right(0)

    def proj_back():
        @pl.when(ctx < blocks - 1)
        def _():
            rim_out.wait_recv()
            d_ext[tokens : tokens + 8] = rim_back[0:8].astype(WIDE)

        @pl.when(ctx == blocks - 1)
        def _():
            d_ext[tokens : tokens + 8] = jnp.zeros((8, part), WIDE)

        sums = [jnp.zeros((1, part), WIDE) for _ in range(3)]
        size = 128
        for start in range(0, tokens, size):
            lines = pl.ds(start, size)
            own = d_ext[lines]
            d_mixed = taps[0:1] * own
            d_mixed = d_mixed + taps[1:2] * (d_ext[pl.ds(start + 1, size)] * masks[lines, 2:3])
            d_mixed = d_mixed + taps[2:3] * (d_ext[pl.ds(start + 2, size)] * masks[lines, 3:4])
            ffn_v[0, 0, lines] = (d_mixed * proj[2, lines]).astype(LOW)
            ffn_v[0, 2, lines] = (d_mixed * proj[0, lines]).astype(LOW)
            for tap in range(3):
                value = own * extended[pl.ds(start + 8 - tap, size)]
                if tap > 0:
                    value = value * masks[lines, tap - 1 : tap]
                sums[tap] = sums[tap] + jnp.sum(value, axis=0, keepdims=True)
        for tap in range(3):
            tap_sums[tap : tap + 1] = sums[tap]
        for kind in range(1, 4):
            mixer_right(kind).start()

    def in_ready():
        hone_first.wait_recv()
        hone_second.start()
        h_one_reload.wait()
        turned(1, dh_got, 0, 0)
        hone_second.wait_recv()
        turned(1, cot_peer, 0, tokens)
        got_mixer_right(1)

    back_away = remote("bh1", away, pair_got, {"tp": core_mate})
    back_pair = remote("bh2", pair, both_got, {"tp": outer_mate})
    back_last = remote("bh3", mixer.at[core], mixer.at[core], {"tp": core_mate})

    def to_inputs(lines, which):
        total = None
        for column in range(3):
            term = lax.dot_general(
                ffn_v[0, column, lines], in_v[which, column],
                (((1,), (1,)), ((), ())), preferred_element_type=WIDE,
            )
            total = term if total is None else total + term
        return total

    def back_one_hop():
        for copy in (dh_away, dh_pair, dh_last):
            copy.wait_send()
        for copy in in_reloads:
            copy.wait()

        def body(lines):
            away[lines] = to_inputs(lines, 1 - core).astype(LOW)

        over_tiles(body)
        back_away.start()

        def rest(lines):
            dh_sum[0, lines] = to_inputs(lines, core)

        over_tiles(rest)

    def back_two_hops():
        back_away.wait_recv()

        def body(lines):
            pair[lines] = (dh_sum[0, lines] + pair_got[lines].astype(WIDE)).astype(LOW)

        over_tiles(body)
        back_pair.start()
        got_mixer_right(2)

    def back_three_hops():
        back_pair.wait_recv()

        def body(lines):
            mixer[core, lines] = (pair[lines].astype(WIDE) + both_got[lines].astype(WIDE)).astype(LOW)

        over_tiles(body)
        back_last.start()
        got_mixer_right(3)

    def give_back(name, block, target, step):
        to, origin = lax.rem(ctx + step, blocks), lax.rem(ctx + blocks - step, blocks)
        name = name + str(step)
        return (
            remote(name, block(to), target.at[ctx], {"ctx": to}),
            remote(name, block(to), target.at[origin], {"ctx": to}),
        )

    def out_block(to):
        return gated.at[pl.ds(pl.multiple_of(to * block_rows, block_rows), block_rows)]

    given = [give_back("give", lambda to: back_blocks.at[to], dealt, step) for step in range(1, blocks)]
    given_out = [give_back("out", out_block, dealt_out, step) for step in range(1, blocks)]
    kept = load(9, back_blocks.at[ctx], dealt.at[ctx])
    kept_out = load(10, out_block(ctx), dealt_out.at[ctx])

    down_loads = [
        load(index, down_w.at[:, pl.ds(index * chunk, chunk)], gu_v.at[index // 2, index % 2])
        for index in range(CHUNKS)
    ]
    act_own_load = load(21, act_out, da_got)
    act_peer_load = load(22, rights_peer.at[:, pl.ds(0, hidden)], da_got)
    ffn_first = remote(
        "fx", cot_full.at[:, pl.ds(half, half)], h_one.at[:, pl.ds(0, half)], {"shard": 1 - shard}
    )
    ffn_core = [
        remote("fc0", cot_full.at[:, columns(1 - core, part)], out_v.at[0, pl.ds(0, tokens)], {"tp": core_mate}),
        remote("fc1", h_one.at[:, columns(1 - core, part)], out_v.at[1, pl.ds(0, tokens)], {"tp": core_mate}),
    ]
    kept_which = jnp.where(outer == shard, 0, 1)

    def ffn_pair(which):
        return pl.ds(pl.multiple_of(half + which * part, part), part)

    ffn_outer = [
        remote(
            "fy%d" % index,
            h_one.at[pl.ds(index * block_rows, block_rows), ffn_pair(1 - kept_which)],
            x_got.at[index],
            {"tp": outer_mate},
        )
        for index in range(blocks)
    ]

    def ffn_part(start):
        def body(lines):
            total = None
            for index in range(CHUNKS):
                term = lax.dot_general(
                    da_got[lines, pl.ds(index * chunk, chunk)], gu_v[index // 2, index % 2],
                    (((1,), (1,)), ((), ())), preferred_element_type=WIDE,
                )
                total = term if total is None else total + term
            cot_full[lines, pl.ds(start, half)] = total.astype(LOW)

        over_tiles(body)

    def ffn_own():
        for copy in (cot_outer, cot_core, cot_more, cot_first):
            copy.wait_send()
        for copy in down_loads:
            copy.wait()
        act_own_load.wait()
        ffn_part(0)
        act_peer_load.start()

    def ffn_peer():
        act_peer_load.wait()
        ffn_part(half)
        ffn_first.start()

    def ffn_to_core():
        ffn_first.wait_recv()
        for copy in ffn_core:
            copy.start()

    def ffn_to_outer():
        for copy in ffn_core:
            copy.wait_recv()

        def body(lines):
            own = columns(core, part)
            h_one[lines, ffn_pair(0)] = (
                cot_full[lines, own].astype(WIDE) + out_v[0, lines].astype(WIDE)
            ).astype(LOW)
            h_one[lines, ffn_pair(1)] = (
                h_one[lines, own].astype(WIDE) + out_v[1, lines].astype(WIDE)
            ).astype(LOW)

        over_tiles(body)
        for copy in ffn_outer:
            copy.start()

    def block_back():
        mixer_right(0).wait_send()
        for index, copy in enumerate(ffn_outer):
            copy.wait_recv()
            lines = pl.ds(index * block_rows, block_rows)
            resid_own[lines] = (
                resid_own[lines] + h_one[lines, ffn_pair(kept_which)].astype(WIDE) + x_got[index].astype(WIDE)
            )
        for to in range(blocks):
            total = place[0, to] * resid_own[0:block_rows]
            for index in range(1, blocks):
                total = total + place[index, to] * resid_own[index * block_rows : (index + 1) * block_rows]
            gated[to * block_rows : (to + 1) * block_rows] = total.astype(LOW)
        for out, _ in given_out:
            out.start()
        kept_out.start()

    def input_back():
        back_last.wait_recv()

        @pl.loop(0, tokens // fine)
        def _(index):
            lines = pl.ds(pl.multiple_of(index * fine, fine), fine)
            own, other = x_full[lines, own_half].astype(WIDE), x_full[lines, peer_half].astype(WIDE)
            own_grad, other_grad = mixer[0, lines].astype(WIDE), mixer[1, lines].astype(WIDE)
            total = jnp.sum(own * own, axis=1, keepdims=True) + jnp.sum(other * other, axis=1, keepdims=True)
            scale = lax.rsqrt(total / width + EPS)
            own, other = own * scale, other * scale
            mean = (
                jnp.sum(own_grad * gains[0:1, own_half] * own, axis=1, keepdims=True)
                + jnp.sum(other_grad * gains[0:1, peer_half] * other, axis=1, keepdims=True)
            ) / width
            gain_sums[0:1, own_half] += jnp.sum(own_grad * own, axis=0, keepdims=True)
            gain_sums[0:1, peer_half] += jnp.sum(other_grad * other, axis=0, keepdims=True)
            which = jnp.where(outer == shard, 0, 1)
            scaled = mixer[which, lines, columns(core, part)].astype(WIDE) * gains[0:1, own_part]
            normed = x_full[lines, own_part].astype(WIDE) * scale
            d_resid[lines] = d_resid[lines] + scale * (scaled - normed * mean)

        for to in range(blocks):
            total = place[0, to] * d_resid[0:block_rows]
            for index in range(1, blocks):
                total = total + place[index, to] * d_resid[index * block_rows : (index + 1) * block_rows]
            back_blocks[to] = total.astype(LOW)
        for out, _ in given:
            out.start()
        kept.start()

    def event_third():
        over_shard("g3").wait_recv()
        over_shard("u3").wait_recv()
        ready(3)
        whole_feed(3)
        for kind in range(3):
            right_copy(3, kind).start()
        hone_first.start()
        mixer_right(0).start()
        got_right(2, 2)

    def dh_one_hop():
        whole_back(3)
        mixer_store.wait()
        for trio in hops:
            for copy in trio:
                copy.wait_send()

        def body(lines):
            away[lines] = dh_sum[1 - core, lines].astype(LOW)

        over_tiles(body)
        dh_away.start()

    def dh_two_hops():
        dh_away.wait_recv()

        def body(lines):
            pair[lines] = (dh_sum[core, lines] + pair_got[lines].astype(WIDE)).astype(LOW)

        over_tiles(body)
        dh_pair.start()
        reload()
        got_right(3, 0)

    def dh_three_hops():
        dh_pair.wait_recv()

        def body(lines):
            mixer[core, lines] = (pair[lines].astype(WIDE) + dh_got[lines].astype(WIDE)).astype(LOW)

        over_tiles(body)
        dh_last.start()
        got_right(3, 1)

    def last_rights():
        ffn_own()
        got_right(3, 2)

    def proj_and_ffn():
        proj_back()
        ffn_peer()

    def back_and_ffn():
        ffn_to_outer()
        back_three_hops()

    def ends_back():
        input_back()
        block_back()

    events = {
        0: event_start,
        2: event_first,
        3: lambda: whole_back(1),
        4: lambda: got_right(0, 2),
        6: lambda: got_right(1, 0),
        8: lambda: got_right(1, 1),
        10: event_second,
        11: lambda: whole_back(2),
        12: lambda: got_right(2, 0),
        14: lambda: got_right(2, 1),
        16: event_third,
        17: dh_one_hop,
        18: dh_two_hops,
        20: dh_three_hops,
        21: resid_back,
        22: last_rights,
        23: conv_back,
        24: out_ready,
        25: proj_and_ffn,
        26: in_ready,
        27: back_one_hop,
        28: back_two_hops,
        29: ffn_to_core,
        30: back_and_ffn,
        31: ends_back,
    }

    @pl.loop(0, pieces_in_all)
    def _(piece):
        for turn, event in events.items():
            pl.when(piece == turn)(event)
        grad_piece(piece)

    @pl.when(middle)
    def _():
        finish(pieces_in_all - 1)

    for out, _ in x_deals + cot_deals:
        out.wait_send()
    for copy in (hone_first, hone_second, dr_first, dr_second, back_away, back_pair, back_last,
                 ffn_first, *ffn_core, *ffn_outer):
        copy.wait_send()
    for name in pieces:
        over_shard(name).wait_send()
        if name not in direct:
            over_ctx(name).wait_send()
    for kind in (1, 2):
        right_copy(CHUNKS - 1, kind).wait_send()
    for kind in range(1, 4):
        mixer_right(kind).wait_send()
    kept.wait()
    kept_out.wait()
    for out, into in given + given_out:
        out.wait_send()
        into.wait_recv()

    @pl.when(ctx < blocks - 1)
    def _():
        rim_copy.wait_send()

    @pl.when(ctx > 0)
    def _():
        rim_out.wait_send()

    @pl.loop(0, pieces_in_all)
    def _(piece):
        @pl.when(piece >= pieces_in_all - SLOTS)
        def _():
            inward_copy(piece, outer_land, outer_recv).wait_send()

        @pl.when(jnp.logical_and(middle, piece >= pieces_in_all - TOTALS))
        def _():
            outward_copy(piece).wait_send()
            total_store(piece).wait()

        @pl.when(end)
        def _():
            outward_copy(piece).wait_recv()


FRONT_COPIES = 104


def front(x_blocks, cot_blocks, place, gains, masks, taps, in_w, out_w, gate_w, up_w, down_w):
    tokens = x_blocks.shape[0] * x_blocks.shape[1]
    part = x_blocks.shape[2]
    width = gains.shape[1]
    half = width // 2
    rows, hidden = gate_w.shape
    chunk = hidden // CHUNKS
    pieces = (3 * hidden + width) // PIECE
    vmem = pl.BlockSpec(memory_space=pltpu.VMEM)
    hbm = pl.BlockSpec(memory_space=pl.ANY)
    shape = jax.ShapeDtypeStruct
    outs = [
        shape(in_w.shape, LOW),
        shape(out_w.shape, LOW),
        shape(gate_w.shape, LOW),
        shape(up_w.shape, LOW),
        shape((pieces, rows, PIECE), LOW),
        shape((pieces, rows, PIECE), LOW),
        shape((tokens, 3 * hidden + width), LOW),
        shape((tokens, width), LOW),
        shape((tokens, width), LOW),
        shape((2, tokens, half), LOW),
        shape((tokens, hidden), LOW),
        shape((rows, 3 * hidden + width), LOW),
        shape(x_blocks.shape, LOW),
        shape(x_blocks.shape, LOW),
        shape((3, part), WIDE),
        shape((2, width), WIDE),
    ]
    low, wide = (lambda *dims: pltpu.VMEM(dims, LOW)), (lambda *dims: pltpu.VMEM(dims, WIDE))
    dma = pltpu.SemaphoreType.DMA
    scratch = [
        low(*x_blocks.shape),
        low(*x_blocks.shape),
        low(tokens, width),
        low(tokens, width),
        low(tokens, width),
        low(tokens, half),
        low(tokens, width),
        low(tokens, half),
        wide(3, tokens, part),
        low(tokens, part),
        low(tokens, part),
        low(2, tokens, half),
        wide(tokens, part),
        low(2, rows, part),
        low(16, part),
        wide(tokens + 8, part),
        low(tokens, half),
        low(tokens, half),
        low(tokens, half),
        low(tokens, half),
        low(tokens, half),
        low(tokens, hidden),
        low(2, 3, rows, part),
        low(2, 2, rows, chunk),
        low(rows, hidden),
        wide(2, tokens, half),
        low(2, 3, tokens, chunk),
        low(3, tokens, chunk),
        low(rows, PIECE),
        low(rows, PIECE),
        low(SLOTS, rows, PIECE),
        low(TOTALS, rows, PIECE),
        wide(tokens + 8, part),
        low(16, part),
        low(16, part),
        dma((FRONT_COPIES,)),
        dma((FRONT_COPIES,)),
        dma((28,)),
    ] + [dma((pieces,)) for _ in range(6)]
    return pl.pallas_call(
        front_kernel,
        out_shape=outs,
        in_specs=[vmem, vmem, pl.BlockSpec(memory_space=pltpu.SMEM)] + [vmem] * 3
        + [hbm] * 5,
        out_specs=[hbm] * (len(outs) - 2) + [vmem] * 2,
        scratch_shapes=scratch,
        compiler_params=pltpu.CompilerParams(
            collective_id=2, has_side_effects=True, vmem_limit_bytes=63 * 1024 * 1024
        ),
        cost_estimate=pl.CostEstimate(
            flops=2 * tokens * width * hidden * 64, bytes_accessed=1 << 29, transcendentals=0
        ),
    )(x_blocks, cot_blocks, place, gains, masks, taps, in_w, out_w, gate_w, up_w, down_w)


class Features:
    def __init__(self):
        rank = lax.axis_index("tp")
        self.rank = rank
        self.inner = rank % 2
        self.outer = rank // 2

    def gather(self, own):
        other = swapped(own, "tp", 2)
        first = self.outer == 0
        pair = jnp.stack([jnp.where(first, own, other), jnp.where(first, other, own)])
        more = swapped(pair, "tp", 1)
        even = self.inner == 0
        left, right = jnp.where(even, pair, more), jnp.where(even, more, pair)
        return jnp.concatenate([left[0], right[0], left[1], right[1]], axis=1)

    def total(self, first_half, second_half):
        even = self.inner == 0
        kept = jnp.where(even, first_half, second_half)
        sent = jnp.where(even, second_half, first_half).astype(LOW)
        pair = (kept.astype(WIDE) + swapped(sent, "tp", 1).astype(WIDE)).astype(LOW)
        both = (pair.astype(WIDE) + swapped(pair, "tp", 2).astype(WIDE)).astype(LOW)
        other = swapped(both, "tp", 1)
        return jnp.where(even, both, other), jnp.where(even, other, both)

    def scatter(self, full):
        rows, width = full.shape
        blocks = full.reshape(rows, 2, 2, width // 4)
        even = self.inner == 0
        kept = jnp.where(even, blocks[:, :, 0], blocks[:, :, 1])
        sent = jnp.where(even, blocks[:, :, 1], blocks[:, :, 0]).astype(LOW)
        pair = kept.astype(WIDE) + swapped(sent, "tp", 1).astype(WIDE)
        first = self.outer == 0
        mine = jnp.where(first, pair[:, 0], pair[:, 1])
        away = jnp.where(first, pair[:, 1], pair[:, 0]).astype(LOW)
        return mine + swapped(away, "tp", 2).astype(WIDE)

    def all_terms(self, full):
        low = full.astype(LOW)
        return [low] + [swapped(low, "tp", step) for step in (1, 2, 3)]

    def own_terms(self, full):
        width = full.shape[1] // 4
        blocks = [
            lax.dynamic_slice_in_dim(full, (self.rank ^ step) * width, width, 1).astype(LOW)
            for step in range(4)
        ]
        return blocks[:1] + [swapped(blocks[step], "tp", step) for step in (1, 2, 3)]

    def own(self, full, axis):
        width = full.shape[axis] // lax.axis_size("tp")
        return lax.dynamic_slice_in_dim(full, self.rank * width, width, axis)


class Shards:
    def __init__(self, tp):
        self.count = lax.axis_size("shard")
        self.rank = lax.axis_index("shard")
        self.ctx_rank = lax.axis_index("ctx")
        self.tp = tp
        self.paired = self.count == 2

    def weight(self, rows):
        if not self.paired:
            return (lax.all_gather(rows, "shard", axis=0, tiled=True),)
        return (rows, swapped(rows, "shard", 1))

    def split(self, full):
        if not self.paired:
            return (full,)
        width = full.shape[1] // 2
        return (
            lax.dynamic_slice_in_dim(full, self.rank * width, width, 1),
            lax.dynamic_slice_in_dim(full, (1 - self.rank) * width, width, 1),
        )

    def join(self, parts):
        if not self.paired:
            return parts[0]
        first = self.rank == 0
        return jnp.concatenate(
            [jnp.where(first, parts[0], parts[1]), jnp.where(first, parts[1], parts[0])], axis=1
        )

    def columns(self, full):
        if not self.paired:
            return lax.all_to_all(full, "shard", split_axis=1, concat_axis=0, tiled=True)
        own, other = self.split(full)
        width = own.shape[1] // 2
        part = lax.dynamic_slice_in_dim(other, self.tp.inner * width, width, 1)
        got = swapped(part, "shard", 1)
        rest = swapped(got, "tp", 1)
        even = self.tp.inner == 0
        peer = jnp.concatenate([jnp.where(even, got, rest), jnp.where(even, rest, got)], axis=1)
        return jnp.concatenate([own, peer], axis=0)

    def tokens(self, own):
        if not self.paired:
            return lax.all_gather(own, "shard", axis=0, tiled=True)
        return jnp.concatenate([own, swapped(own, "shard", 1)], axis=0)

    def own_total(self, product):
        if not self.paired:
            return lax.psum_scatter(product, "shard", scatter_dimension=0, tiled=True)
        rows = product.shape[0] // 2
        return product[:rows] + swapped(product[rows:].astype(LOW), "shard", 1).astype(WIDE)

    def own_tokens(self, product):
        if not self.paired:
            return lax.all_to_all(product.astype(LOW), "shard", split_axis=0, concat_axis=1, tiled=True)
        rows = product.shape[0] // 2
        return self.join([product[:rows].astype(LOW), swapped(product[rows:].astype(LOW), "shard", 1)])


def on_device(
    hidden_in,
    out_grad,
    seq_lengths,
    deal_order,
    in_weight,
    conv_weight,
    out_weight,
    norm1_gain,
    norm2_gain,
    gate_weight,
    up_weight,
    down_weight,
):
    ctx_size = lax.axis_size("ctx")
    ctx_rank = lax.axis_index("ctx")
    tp = Features()
    shards = Shards(tp)
    row_count, col_count = hidden_in.shape
    hidden_count = gate_weight.shape[1]
    weight_rows = in_weight.shape[0]
    per_dev = deal_order.shape[1] // ctx_size
    per_peer = per_dev // ctx_size
    block_rows = row_count // per_dev
    dealing = deal_order[0].reshape(ctx_size, per_dev)
    own_blocks = lax.dynamic_index_in_dim(dealing, ctx_rank, 0, keepdims=False)
    send_order = jnp.argsort(own_blocks // per_dev, stable=True)
    wanted = jnp.where(dealing // per_dev == ctx_rank, 0, 1)
    chosen = jnp.argsort(wanted, axis=1, stable=True)[:, :per_peer]
    targets = (jnp.take_along_axis(dealing, chosen, 1) % per_dev).reshape(-1)
    placing = jnp.argsort(targets)
    returning = jnp.argsort(send_order)

    def reorder(values, index):
        blocks = values.reshape(per_dev, block_rows, values.shape[1])
        return blocks[index].reshape(row_count, values.shape[1])

    def to_packed(values):
        got = lax.all_to_all(
            reorder(values, send_order), "ctx", split_axis=0, concat_axis=0, tiled=True
        )
        return reorder(got, placing)

    def to_dealt(values):
        got = lax.all_to_all(
            reorder(values, targets), "ctx", split_axis=0, concat_axis=0, tiled=True
        )
        return reorder(got, returning)

    def weight_grads(lefts, rights, identity):
        flat = [value for group in rights for value in group]
        if shards.paired:
            summed = line_grads([group[0] for group in lefts], flat, identity)
            ends = [0]
            for value in flat:
                ends.append(ends[-1] + value.shape[1])
            return [summed[:, a:b] for a, b in zip(ends, ends[1:])]
        flat_lefts = [value for group in lefts for value in group]
        return [
            sum_line(contract_rows(left, shards.tokens(right)).astype(LOW), ctx_rank)
            for left, right in zip(flat_lefts, flat)
        ]

    lengths = seq_lengths[0]
    starts = jnp.cumsum(lengths) - lengths
    where_t = ctx_rank * row_count - 2 + jnp.arange(row_count + 4, dtype=jnp.int32)
    seq_begin = jnp.max(jnp.where(starts[None, :] <= where_t[:, None], starts[None, :], 0), axis=1)
    position = where_t - seq_begin
    first_own = (position[2 : row_count + 2] >= 1).astype(WIDE)[:, None]
    second_own = (position[2 : row_count + 2] >= 2).astype(WIDE)[:, None]
    first_next = (position[3 : row_count + 3] >= 1).astype(WIDE)[:, None]
    second_next = (position[4 : row_count + 4] >= 2).astype(WIDE)[:, None]
    conv_taps = conv_weight.astype(WIDE)
    gains = tp.gather(jnp.stack([norm1_gain, norm2_gain])).astype(WIDE)
    gain_one, gain_two = gains[0], gains[1]
    in_parts = jnp.moveaxis(in_weight, 1, 0)

    if shards.paired:
        def blocks_of(values):
            return reorder(values, send_order).reshape(per_dev, block_rows, col_count)

        place = (targets[None, :] == jnp.arange(per_dev)[:, None]).astype(WIDE)
        *_, sums, dealt, dealt_out, taps_grad, gain_sums = front(
            blocks_of(hidden_in), blocks_of(out_grad), place, gains,
            jnp.concatenate([first_own, second_own, first_next, second_next], axis=1), conv_taps,
            in_parts, out_weight, gate_weight, up_weight, down_weight,
        )
        block_dealt = reorder(dealt_out.reshape(row_count, col_count), returning)
        input_dealt = reorder(dealt.reshape(row_count, col_count), returning)
        ends = [hidden_count, 2 * hidden_count, 3 * hidden_count, 3 * hidden_count + col_count]
        parts = [value.astype(WIDE) for value in jnp.split(sums, ends, axis=1)]
        down_total, gate_total, up_total, out_total, in_flat_total = parts
        in_total = in_flat_total.reshape(in_weight.shape)
        gain_one_grad, gain_two_grad = tp.own(gain_sums, 1)
    else:
        in_w = shards.weight(in_weight.reshape(weight_rows, -1))
        x_full = tp.gather(to_packed(hidden_in))
        out_w = shards.weight(out_weight)
        cot_full = tp.gather(to_packed(out_grad))
        gate_w, up_w = shards.weight(gate_weight), shards.weight(up_weight)
        x_float = x_full.astype(WIDE)
        scale_one = lax.rsqrt(jnp.mean(x_float * x_float, axis=1, keepdims=True) + EPS)
        normed_one = x_float * scale_one
        h_one = (normed_one * gain_one).astype(LOW)
        projected = matmul(h_one, in_w[0])
        b_part = projected[:, :col_count]
        c_part = projected[:, col_count : 2 * col_count]
        v_part = projected[:, 2 * col_count :]
        mixed = (b_part * v_part).astype(LOW)
        rim = shifted(mixed[-2:], "ctx", 1)
        extended = jnp.concatenate([rim, mixed], axis=0).astype(WIDE)
        prev_one = extended[1 : row_count + 1] * first_own
        prev_two = extended[0:row_count] * second_own
        conv_out = (
            conv_taps[0] * extended[2:] + conv_taps[1] * prev_one + conv_taps[2] * prev_two
        )
        gated = (c_part * conv_out).astype(LOW)
        mixer_halves = jnp.split(contract_cols(gated, out_w[0]), 2, axis=1)
        mixer_out = jnp.concatenate(tp.total(*mixer_halves), axis=1)
        resid = x_float + mixer_out.astype(WIDE)
        scale_two = lax.rsqrt(jnp.mean(resid * resid, axis=1, keepdims=True) + EPS)
        normed_two = resid * scale_two
        h_two = (normed_two * gain_two).astype(LOW)
        cot_cols, h_two_cols, h_one_cols = [shards.columns(v) for v in (cot_full, h_two, h_one)]
        gate_pre, up_pre = matmul(h_two, gate_w[0]), matmul(h_two, up_w[0])
        d_act = shards.own_total(matmul(cot_cols, down_weight))
        sigmoid_gate = jax.nn.sigmoid(gate_pre)
        silu_gate = gate_pre * sigmoid_gate
        d_gate = d_act * up_pre * sigmoid_gate * (1.0 + gate_pre * (1.0 - sigmoid_gate))
        ffn_rights = [v.astype(LOW) for v in (silu_gate * up_pre, d_gate, d_act * silu_gate)]
        act_all = shards.tokens(ffn_rights[0])
        dh_terms = tp.all_terms(
            contract_cols(ffn_rights[1], gate_w[0]) + contract_cols(ffn_rights[2], up_w[0])
        )
        dh_two = added(dh_terms)
        ffn_grads = weight_grads(
            [[cot_cols], [h_two_cols, h_two_cols]], [ffn_rights[:1], ffn_rights[1:]], 0
        )

        ffn_terms = tp.own_terms(shards.own_tokens(contract_cols(act_all, down_weight)))

        rim = shifted(mixed[-2:], "ctx", 1)
        extended = jnp.concatenate([rim, mixed], axis=0).astype(WIDE)
        prev_one = extended[1 : row_count + 1] * first_own
        prev_two = extended[0:row_count] * second_own
        mixed_float = extended[2:]

        gain_two_grad = tp.own(jnp.sum(dh_two * normed_two, axis=0), 0)
        d_resid = cot_full.astype(WIDE) + norm_back(dh_two, normed_two, scale_two, gain_two)
        d_resid_low = d_resid.astype(LOW)
        d_gated = sum(matmul(part, w) for part, w in zip(shards.split(d_resid_low), out_w))
        d_conv = (d_gated * c_part).astype(LOW)
        d_c_part = d_gated * conv_out
        rim_back = shifted(d_conv[:2], "ctx", -1)
        d_conv_float = d_conv.astype(WIDE)
        back_ext = jnp.concatenate([d_conv, rim_back], axis=0).astype(WIDE)
        d_mixed = (
            conv_taps[0] * d_conv_float
            + conv_taps[1] * back_ext[1 : row_count + 1] * first_next
            + conv_taps[2] * back_ext[2:] * second_next
        )
        taps_grad = jnp.stack(
            [
                jnp.sum(d_conv_float * mixed_float, axis=0),
                jnp.sum(d_conv_float * prev_one, axis=0),
                jnp.sum(d_conv_float * prev_two, axis=0),
            ]
        )
        d_proj = [
            (d_mixed * v_part).astype(LOW),
            d_c_part.astype(LOW),
            (d_mixed * b_part).astype(LOW),
        ]
        d_proj_flat = jnp.concatenate(d_proj, axis=1)
        dh_one_terms = tp.all_terms(shards.join([contract_cols(d_proj_flat, w) for w in in_w]))
        mixer_grads = weight_grads(
            [[shards.columns(d_resid_low)], [h_one_cols]], [[gated], [d_proj_flat]], 1
        )
        dh_one_terms, ffn_terms, mixer_grads = lax.optimization_barrier(
            (dh_one_terms, ffn_terms, mixer_grads)
        )
        dh_one = added(dh_one_terms)
        block_out = (tp.own(resid, 1) + added(ffn_terms)).astype(LOW)
        down_total, gate_total, up_total = [value.astype(WIDE) for value in ffn_grads]
        out_total, in_flat_total = [value.astype(WIDE) for value in mixer_grads]
        in_total = in_flat_total.reshape(in_weight.shape)
        gain_one_grad = tp.own(jnp.sum(dh_one * normed_one, axis=0), 0)
        d_input = d_resid + norm_back(dh_one, normed_one, scale_one, gain_one)
        dealt = to_dealt(jnp.concatenate([block_out, tp.own(d_input, 1).astype(LOW)], axis=1))
        block_dealt, input_dealt = dealt[:, :col_count], dealt[:, col_count:]

    small = jnp.concatenate([taps_grad, gain_one_grad[None], gain_two_grad[None]], axis=0)
    small_sum = butterfly_sum(butterfly_sum(small, "shard"), "ctx")
    return (
        block_dealt,
        input_dealt,
        in_total,
        small_sum[0:3],
        out_total,
        small_sum[3],
        small_sum[4],
        gate_total,
        up_total,
        down_total,
    )


def solution(mesh):
    placed = (
        P(("shard", "ctx"), "tp"),
        P(("shard", "ctx"), "tp"),
        P("shard", None),
        P("shard", None),
        P("shard", None, "tp"),
        P(None, "tp"),
        P("shard", "tp"),
        P("tp"),
        P("tp"),
        P("shard", "tp"),
        P("shard", "tp"),
        P("shard", "tp"),
    )
    return jax.shard_map(
        on_device,
        mesh=mesh,
        in_specs=placed,
        out_specs=(
            P(("shard", "ctx"), "tp"),
            P(("shard", "ctx"), "tp"),
            P("shard", None, "tp"),
            P(None, "tp"),
            P("shard", "tp"),
            P("tp"),
            P("tp"),
            P("shard", "tp"),
            P("shard", "tp"),
            P("shard", "tp"),
        ),
        check_vma=False,
    )
```

```python
import jax
import jax.numpy as jnp
from jax import lax
from jax.experimental import pallas as pl
from jax.experimental.pallas import tpu as pltpu
from jax.sharding import PartitionSpec as P

EPS = 1e-05
LOW = jnp.bfloat16
WIDE = jnp.float32
CHUNKS = 4


def shifted(value, axis, steps):
    count = lax.axis_size(axis)
    leading, last = (max(0, -steps), min(count, count - steps))
    return lax.ppermute(value, axis, [(source, source + steps) for source in range(leading, last)])


def swapped(value, axis, step):
    count = lax.axis_size(axis)
    return lax.ppermute(value, axis, [(source, source ^ step) for source in range(count)])


def matmul(left, right):
    return jnp.dot(left, right, preferred_element_type=WIDE)


def contract_rows(left, right):
    return lax.dot_general(left, right, (((0,), (0,)), ((), ())), preferred_element_type=WIDE)


def contract_cols(left, right):
    return lax.dot_general(left, right, (((1,), (1,)), ((), ())), preferred_element_type=WIDE)


def added(terms):
    return sum(term.astype(WIDE) for term in terms)


def norm_back(grad_out, normed, scale_row, gain):
    scaled = grad_out * gain
    return scale_row * (scaled - normed * jnp.mean(scaled * normed, axis=1, keepdims=True))


def butterfly_sum(value, axis):
    step = 1
    while step < lax.axis_size(axis):
        value = value + swapped(value, axis, step)
        step *= 2
    return value


def sum_line(piece, rank):
    from_end = lax.ppermute(piece, "ctx", [(0, 1), (3, 2)])
    half = (piece.astype(WIDE) + from_end.astype(WIDE)).astype(LOW)
    from_middle = lax.ppermute(half, "ctx", [(1, 2), (2, 1)])
    total = (half.astype(WIDE) + from_middle.astype(WIDE)).astype(LOW)
    handed = lax.ppermute(total, "ctx", [(1, 0), (2, 3)])
    inner = jnp.logical_or(rank == 1, rank == 2)
    return jnp.where(inner, total, handed)


PIECE = 256
AHEAD = 4
SLOTS = 4
TOTALS = 2
MESH = pl.DeviceIdType.MESH


def front_kernel(
    x_in, cot_in, sending, place, own_gains, masks, taps,
    in_w, out_w, gate_w, up_w, down_w,
    in_peer, out_peer, gate_peer, up_peer, outer_land, middle_land, rights_peer,
    x_out, h_one_out, mixer_out, act_out, grads, dealt, dealt_out, small_sums,
    x_blocks, cot_blocks, gains, gain_sums, small, small_got, x_got, cot_got, x_full, h_one, cot_full, cot_peer, h_two, h_two_peer, proj, mixed, gated, mixer, conv_v,
    out_v, rim, extended, away, pair, pair_got, both_got, dh_got,
    da_got, in_v, gu_v, down_v, dh_sum, ffn_v, right_v, outer_v, middle_v, held, totals, d_ext, edge_v, rim_back,
    send, recv, local, in_send, outer_recv, middle_recv, out_send, out_recv, own_done,
):
    shard = lax.axis_index("shard")
    ctx = lax.axis_index("ctx")
    tp = lax.axis_index("tp")
    core, outer = tp % 2, tp // 2
    core_mate = tp + 1 - 2 * core
    outer_mate = lax.rem(tp + 2, 4)
    ctx_mate = ctx + 1 - 2 * (ctx % 2)
    tokens, width = x_full.shape
    part = width // 4
    half = width // 2
    blocks, block_rows = x_blocks.shape[0], x_blocks.shape[1]
    rows = out_w.shape[0]
    own_rows = pl.ds(pl.multiple_of((ctx % 2) * (rows // 2), rows // 2), rows // 2)
    other_rows = pl.ds(pl.multiple_of((1 - ctx % 2) * (rows // 2), rows // 2), rows // 2)
    hidden = gate_w.shape[1]
    chunk = hidden // CHUNKS

    barrier = pltpu.get_barrier_semaphore()
    mates = [{"shard": 1 - shard}, {"tp": core_mate}, {"tp": outer_mate}]
    mates += [{"ctx": lax.rem(ctx + step, blocks)} for step in range(1, blocks)]
    for mate in mates:
        pl.semaphore_signal(barrier, inc=1, device_id=mate, device_id_type=MESH)
    pl.semaphore_wait(barrier, len(mates))

    names = {}

    def remote(name, src, dst, mate):
        place_of = names.setdefault(name, len(names))
        return pltpu.make_async_remote_copy(
            src_ref=src, dst_ref=dst, send_sem=send.at[place_of], recv_sem=recv.at[place_of],
            device_id=mate, device_id_type=MESH,
        )

    def columns(start, size):
        return pl.ds(pl.multiple_of(start * size, size), size)

    own_part = columns(tp, part)
    own_half, peer_half = columns(shard, half), columns(1 - shard, half)

    def deal(name, source, target, step):
        to, origin = lax.rem(ctx + step, blocks), lax.rem(ctx + blocks - step, blocks)
        out = remote(name + str(step), source.at[to], target.at[ctx], {"ctx": to})
        into = remote(name + str(step), source.at[to], target.at[origin], {"ctx": to})
        return out, into

    def gather(name, full):
        mate = columns(outer_mate, part)
        return (
            remote(name + "outer", full.at[:, own_part], full.at[:, own_part], {"tp": outer_mate}),
            remote(name + "core", full.at[:, own_part], full.at[:, own_part], {"tp": core_mate}),
            remote(name + "more", full.at[:, mate], full.at[:, mate], {"tp": core_mate}),
        )

    pieces = {}
    for index, name in enumerate("bvc"):
        column = (0, 2, 1)[index]
        pieces[name] = (in_w.at[column], in_peer.at[column])
    pieces["o"] = (out_w, out_peer)
    for index in range(CHUNKS):
        strip = pl.ds(index * chunk, chunk)
        pieces["g%d" % index] = (gate_w.at[:, strip], gate_peer.at[:, strip])
        pieces["u%d" % index] = (up_w.at[:, strip], up_peer.at[:, strip])

    direct = ["%s%d" % (kind, index) for kind in "gu" for index in range(2, CHUNKS)]

    def over_shard(name):
        source, target = pieces[name]
        if name in direct:
            return remote(name + "x", source, target, {"shard": 1 - shard})
        return remote(name + "x", source.at[own_rows], target.at[own_rows], {"shard": 1 - shard})

    def over_ctx(name):
        target = pieces[name][1]
        return remote(name + "z", target.at[own_rows], target.at[own_rows], {"ctx": ctx_mate})

    def pump(name):
        over_shard(name).wait_recv()
        over_ctx(name).start()

    def load(index, source, target):
        return pltpu.make_async_copy(source, target, local.at[index])

    def own_weights(index):
        strip = pl.ds(index * chunk, chunk)
        room = gu_v if index % 2 == 0 else in_v
        base = 13 + 4 * (index % 2)
        return [
            load(base, gate_w.at[:, strip], room.at[0, 0]),
            load(base + 1, up_w.at[:, strip], room.at[0, 1]),
        ]

    def peer_weights(index):
        strip = pl.ds(index * chunk, chunk)
        room = gu_v if index % 2 == 0 else in_v
        base = 15 + 4 * (index % 2)
        return [
            load(base, gate_peer.at[:, strip], room.at[1, 0]),
            load(base + 1, up_peer.at[:, strip], room.at[1, 1]),
        ]

    def to_blocks(source, target):
        for to in range(blocks):
            total = sending[to, 0] * source[0:block_rows].astype(WIDE)
            for slot in range(1, blocks):
                lines = pl.ds(slot * block_rows, block_rows)
                total = total + sending[to, slot] * source[lines].astype(WIDE)
            target[to] = total.astype(LOW)

    for name in ("b", "v", "c", "o", "g0", "u0"):
        over_shard(name).start()
    gains[:, own_part] = own_gains[...]
    gain_outer, gain_core, gain_more = gather("gg", gains)
    gain_outer.start()
    gain_core.start()
    to_blocks(x_in, x_blocks)
    x_deals = [deal("x", x_blocks, x_got, step) for step in range(1, blocks)]
    cot_deals = [deal("cot", cot_blocks, cot_got, step) for step in range(1, blocks)]
    for out, _ in x_deals:
        out.start()
    own_loads = [load(index, in_w.at[index], in_v.at[0, index]) for index in range(3)]
    own_loads.append(load(3, out_w, out_v.at[0]))
    own_loads.append(load(4, down_w, down_v))
    for copy in own_loads + own_weights(0):
        copy.start()
    to_blocks(cot_in, cot_blocks)

    def packed(source, got, deals, full):
        got[ctx] = source[ctx]
        for _, into in deals:
            into.wait_recv()
        for index in range(blocks):
            total = place[index, 0] * got[0].astype(WIDE)
            for other in range(1, blocks):
                total = total + place[index, other] * got[other].astype(WIDE)
            full[index * block_rows : (index + 1) * block_rows, own_part] = total.astype(LOW)

    pump("b")
    packed(x_blocks, x_got, x_deals, x_full)
    x_outer, x_core, x_more = gather("xg", x_full)
    x_outer.start()
    x_core.start()
    for out, _ in cot_deals:
        out.start()
    pump("v")
    x_outer.wait_recv()
    x_more.start()
    packed(cot_blocks, cot_got, cot_deals, cot_full)
    cot_outer, cot_core, cot_more = gather("cg", cot_full)
    cot_outer.start()
    cot_core.start()
    gain_outer.wait_recv()
    gain_more.start()
    x_core.wait_recv()
    x_more.wait_recv()
    gain_core.wait_recv()
    gain_more.wait_recv()

    x_store = load(5, x_full, x_out)
    x_store.start()
    step = min(64, tokens)

    @pl.loop(0, tokens // step)
    def _(index):
        lines = pl.ds(pl.multiple_of(index * step, step), step)
        value = x_full[lines].astype(WIDE)
        scale = lax.rsqrt(jnp.mean(value * value, axis=1, keepdims=True) + EPS)
        h_one[lines] = (value * scale * gains[0:1]).astype(LOW)

    h_one_store = load(6, h_one, h_one_out)
    h_one_store.start()
    pump("c")

    def columns_out(name, full, got):
        strip = pl.ds(pl.multiple_of((1 - shard) * half + core * part, part), part)
        target = columns(core, part)
        first = remote(name + "x", full.at[:, strip], got.at[:, target], {"shard": 1 - shard})
        second = remote(name + "core", got.at[:, target], got.at[:, target], {"tp": core_mate})
        return first, second

    cot_first, cot_second = columns_out("cc", cot_full, cot_peer)

    tile = min(256, tokens)

    def over_tiles(body):
        @pl.loop(0, tokens // tile)
        def _(index):
            body(pl.ds(pl.multiple_of(index * tile, tile), tile))

    def project(column, name):
        target = load(column, in_peer.at[column], in_v.at[1, column])
        own_loads[column].wait()
        over_ctx(name).wait_recv()
        target.start()
        target.wait()

        def body(lines):
            proj[column, lines] = jnp.dot(
                h_one[lines, own_half], in_v[0, column], preferred_element_type=WIDE
            ) + jnp.dot(h_one[lines, peer_half], in_v[1, column], preferred_element_type=WIDE)

        over_tiles(body)

    project(0, "b")
    project(2, "v")
    edge = 16
    rim_copy = remote(
        "rim", mixed.at[pl.ds(tokens - edge, edge)], rim, {"ctx": lax.rem(ctx + 1, blocks)}
    )

    def mix(lines):
        value = (proj[0, lines] * proj[2, lines]).astype(LOW)
        mixed[lines] = value
        extended[pl.ds(lines.start + 8, tile)] = value.astype(WIDE)

    over_tiles(mix)

    @pl.when(ctx < blocks - 1)
    def _():
        rim_copy.start()

    pump("o")
    cot_outer.wait_recv()
    cot_more.start()
    project(1, "c")

    @pl.when(ctx > 0)
    def _():
        rim_copy.wait_recv()
        extended[0:8] = rim[8:16].astype(WIDE)

    @pl.when(ctx == 0)
    def _():
        extended[0:8] = jnp.zeros((8, part), WIDE)

    for start in range(0, tokens, tile):
        lines = pl.ds(start, tile)
        value = taps[0:1] * extended[pl.ds(start + 8, tile)]
        value = value + taps[1:2] * (extended[pl.ds(start + 7, tile)] * masks[lines, 0:1])
        value = value + taps[2:3] * (extended[pl.ds(start + 6, tile)] * masks[lines, 1:2])
        conv_v[lines] = value
        gated[lines] = (proj[1, lines] * value).astype(LOW)

    pump("g0")
    cot_core.wait_recv()
    cot_more.wait_recv()
    cot_first.start()
    over_shard("g1").start()
    out_load = load(3, out_peer, out_v.at[1])
    own_loads[3].wait()
    over_ctx("o").wait_recv()
    out_load.start()
    out_load.wait()

    def to_half(lines, which):
        return lax.dot_general(
            gated[lines], out_v[which], (((1,), (1,)), ((), ())), preferred_element_type=WIDE
        )

    stages = [pl.ds(start, tile) for start in range(0, tokens, tile)]
    hops = []
    for index, lines in enumerate(stages):
        first = remote("ma%d" % index, away.at[lines], pair_got.at[lines], {"tp": core_mate})
        second = remote("mb%d" % index, pair.at[lines], both_got.at[lines], {"tp": outer_mate})
        third = remote("mc%d" % index, mixer.at[core, lines], mixer.at[core, lines], {"tp": core_mate})
        hops.append((first, second, third))
        away[lines] = to_half(lines, 1 - core).astype(LOW)
        first.start()
    for index, lines in enumerate(stages):
        value = to_half(lines, core)
        hops[index][0].wait_recv()
        pair[lines] = (value + pair_got[lines].astype(WIDE)).astype(LOW)
        hops[index][1].start()

    da_send, da_own = h_one, x_full
    pump("u0")
    cot_first.wait_recv()
    cot_second.start()
    cot_second.wait()
    own_loads[4].wait()
    h_one_store.wait()

    def da_copy(index):
        strip = pl.ds(index * chunk, chunk)
        return remote("da%d" % index, da_send.at[:, strip], da_got.at[:, strip], {"shard": 1 - shard})

    for index in range(CHUNKS):
        strip = pl.ds(index * chunk, chunk)

        def send_part(lines):
            da_send[lines, strip] = jnp.dot(
                cot_peer[lines], down_v[:, strip], preferred_element_type=WIDE
            ).astype(LOW)

        over_tiles(send_part)
        if index == 0:
            da_copy(0).start()
            over_shard("u1").start()

    def act_store(index):
        return load(21 + index % 2, ffn_v.at[index % 2, 0], act_out.at[:, pl.ds(index * chunk, chunk)])

    def right_copy(index, kind):
        strip = pl.ds(kind * hidden + index * chunk, chunk)
        return remote(
            "r%d%d" % (index, kind), ffn_v.at[index % 2, kind], rights_peer.at[:, strip], {"shard": 1 - shard}
        )

    def right_load(index, kind):
        strip = pl.ds(kind * hidden + index * chunk, chunk)
        return load(23 + kind, rights_peer.at[:, strip], right_v.at[kind])

    def ready(index):
        for kind in "gu":
            if "%s%d" % (kind, index) not in direct:
                over_ctx("%s%d" % (kind, index)).wait_recv()
        for copy in peer_weights(index):
            copy.start()

    def feed(index, lines, kinds=(0, 1, 2)):
        room = gu_v if index % 2 == 0 else in_v
        slot = index % 2
        strip = pl.ds(index * chunk, chunk)

        def pre(kind):
            return jnp.dot(
                h_two[lines, own_half], room[0, kind], preferred_element_type=WIDE
            ) + jnp.dot(h_two[lines, peer_half], room[1, kind], preferred_element_type=WIDE)

        gate_pre, up_pre = pre(0), pre(1)
        sigmoid = jax.nn.sigmoid(gate_pre)
        silu = gate_pre * sigmoid
        if 0 in kinds:
            ffn_v[slot, 0, lines] = (silu * up_pre).astype(LOW)
        if 1 not in kinds:
            return
        d_act = da_own[lines, strip].astype(WIDE) + da_got[lines, strip].astype(WIDE)
        ffn_v[slot, 1, lines] = (
            d_act * up_pre * sigmoid * (1.0 + gate_pre * (1.0 - sigmoid))
        ).astype(LOW)
        ffn_v[slot, 2, lines] = (d_act * silu).astype(LOW)

    pump("g1")
    ready(0)
    tiles = [pl.ds(start, tile) for start in range(0, tokens, tile)]
    for index, lines in enumerate(stages):
        hops[index][1].wait_recv()
        mixer[core, lines] = (pair[lines].astype(WIDE) + both_got[lines].astype(WIDE)).astype(LOW)
        hops[index][2].start()
        hops[index][2].wait_recv()

        @pl.loop(0, tile // step)
        def _(turn, start=index * tile):
            lines = pl.ds(pl.multiple_of(start + turn * step, step), step)
            own = x_full[lines, own_half].astype(WIDE) + mixer[0, lines].astype(WIDE)
            other = x_full[lines, peer_half].astype(WIDE) + mixer[1, lines].astype(WIDE)
            total = jnp.sum(own * own, axis=1, keepdims=True) + jnp.sum(other * other, axis=1, keepdims=True)
            scale = lax.rsqrt(total / width + EPS)
            h_two[lines, own_half] = (own * scale * gains[1:2, own_half]).astype(LOW)
            h_two[lines, peer_half] = (other * scale * gains[1:2, peer_half]).astype(LOW)

        if index == 0:
            for copy in own_weights(0) + peer_weights(0):
                copy.wait()
        feed(0, lines, (0,))
    right_copy(0, 0).start()
    act_store(0).start()
    mixer_store = load(12, mixer, mixer_out)
    mixer_store.start()

    h_two_first, h_two_second = columns_out("hc", h_two, h_two_peer)
    h_two_first.start()
    x_store.wait()
    for copy in (x_outer, x_core, x_more):
        copy.wait_send()

    def own_part_of(lines):
        for index in range(CHUNKS):
            strip = pl.ds(index * chunk, chunk)
            da_own[lines, strip] = jnp.dot(
                cot_full[lines, own_half], down_v[:, strip], preferred_element_type=WIDE
            ).astype(LOW)

    over_tiles(own_part_of)

    def turned(place_of, source, start, first):
        for row in range(0, half, 256):
            for line in range(0, tokens, 256):
                block = source[pl.ds(line, 256), pl.ds(pl.multiple_of(start + row, 256), 256)]
                down_v[pl.ds(row, 256), pl.ds(place_of * half + first + line, 256)] = block.T

    turned(0, cot_full, shard * half, 0)
    turned(0, cot_peer, 0, tokens)
    turned(1, h_two, shard * half, 0)

    def back(index, lines):
        room = gu_v if index % 2 == 0 else in_v
        slot = index % 2
        for place_of in range(2):
            term = lax.dot_general(
                ffn_v[slot, 1, lines], room[place_of, 0],
                (((1,), (1,)), ((), ())), preferred_element_type=WIDE,
            ) + lax.dot_general(
                ffn_v[slot, 2, lines], room[place_of, 1],
                (((1,), (1,)), ((), ())), preferred_element_type=WIDE,
            )
            if index > 0:
                term = term + dh_sum[place_of, lines]
            dh_sum[place_of, lines] = term

    def feed_start(index):
        da_copy(index).wait_recv()
        for copy in own_weights(index) + peer_weights(index):
            copy.wait()
        if index > 1:
            act_store(index - 2).wait()
            for kind in range(3):
                right_copy(index - 2, kind).wait_send()

    middle = jnp.logical_or(ctx == 1, ctx == 2)
    end = jnp.logical_not(middle)
    inward = jnp.where(ctx < 2, ctx + 1, ctx - 1)
    outward = jnp.where(ctx == 1, 0, 3)
    per_kind = chunk // PIECE
    per_chunk = 3 * per_kind
    ffn_pieces = CHUNKS * per_chunk
    pieces_in_all = ffn_pieces + 4 * part // PIECE
    line_rows = min(256, rows)

    def grad_columns(piece):
        index, turn = piece // per_chunk, piece % per_chunk
        kind, sub = turn // per_kind, turn % per_kind
        start = jnp.where(
            piece < ffn_pieces, kind * hidden + index * chunk + sub * PIECE, piece * PIECE
        )
        return pl.ds(pl.multiple_of(start, PIECE), PIECE)

    def inward_copy(piece, land, sems):
        return pltpu.make_async_remote_copy(
            src_ref=held.at[piece % SLOTS], dst_ref=land.at[piece], send_sem=in_send.at[piece],
            recv_sem=sems.at[piece], device_id={"ctx": inward}, device_id_type=MESH,
        )

    def outward_copy(piece):
        return pltpu.make_async_remote_copy(
            src_ref=totals.at[piece % TOTALS], dst_ref=grads.at[:, grad_columns(piece)], send_sem=out_send.at[piece],
            recv_sem=out_recv.at[piece], device_id={"ctx": outward}, device_id_type=MESH,
        )

    def total_store(piece):
        return pltpu.make_async_copy(totals.at[piece % TOTALS], grads.at[:, grad_columns(piece)], own_done.at[piece])

    def stage_in(piece, land, room):
        copy = pltpu.make_async_copy(land.at[piece], room, local.at[26])
        copy.start()
        copy.wait()

    def finish(piece):
        inward_copy(piece, middle_land, middle_recv).wait_recv()
        stage_in(piece, middle_land, middle_v)

        @pl.when(piece >= TOTALS)
        def _():
            outward_copy(piece - TOTALS).wait_send()
            total_store(piece - TOTALS).wait()

        @pl.loop(0, rows // line_rows)
        def _(start):
            lines = pl.ds(pl.multiple_of(start * line_rows, line_rows), line_rows)
            total = held[piece % SLOTS, lines].astype(WIDE) + middle_v[lines].astype(WIDE)
            totals[piece % TOTALS, lines] = total.astype(LOW)

        outward_copy(piece).start()
        total_store(piece).start()

    def grad_piece(piece):
        after = piece >= ffn_pieces
        turn = jnp.where(after, jnp.maximum(piece - ffn_pieces - per_kind, 0), piece % per_chunk)
        kind, sub = turn // per_kind, piece % per_kind
        slot = jnp.where(after, jnp.where(piece < ffn_pieces + per_kind, 1, 0), piece // per_chunk % 2)
        strip = pl.ds(pl.multiple_of(sub * PIECE, PIECE), PIECE)
        left_first = jnp.where(after, piece < ffn_pieces + per_kind, kind == 0)
        left = jnp.where(left_first, 0, half)

        @pl.when(piece >= SLOTS)
        def _():
            inward_copy(piece - SLOTS, outer_land, outer_recv).wait_send()

        def product(start):
            lines = pl.ds(pl.multiple_of(start * line_rows, line_rows), line_rows)
            own = jnp.dot(
                down_v[lines, pl.ds(pl.multiple_of(left, tokens), tokens)],
                ffn_v[slot, kind, :, strip],
                preferred_element_type=WIDE,
            )
            other = jnp.dot(
                down_v[lines, pl.ds(pl.multiple_of(left + tokens, tokens), tokens)],
                right_v[kind, :, strip],
                preferred_element_type=WIDE,
            )
            return lines, own + other

        @pl.when(end)
        def _():
            @pl.loop(0, rows // line_rows)
            def _(start):
                lines, value = product(start)
                held[piece % SLOTS, lines] = value.astype(LOW)

            inward_copy(piece, outer_land, outer_recv).start()

        @pl.when(middle)
        def _():
            inward_copy(piece, outer_land, outer_recv).wait_recv()
            stage_in(piece, outer_land, outer_v)

            @pl.loop(0, rows // line_rows)
            def _(start):
                lines, value = product(start)
                held[piece % SLOTS, lines] = (value + outer_v[lines].astype(WIDE)).astype(LOW)

            inward_copy(piece, middle_land, middle_recv).start()

            @pl.when(piece >= 1)
            def _():
                finish(piece - 1)

    def got_right(index, kind):
        right_copy(index, kind).wait_recv()
        copy = right_load(index, kind)
        copy.start()
        copy.wait()

    dh_away = remote("dh1", away, pair_got, {"tp": core_mate})
    dh_pair = remote("dh2", pair, dh_got, {"tp": outer_mate})
    dh_last = remote("dh3", mixer.at[core], mixer.at[core], {"tp": core_mate})
    def whole_feed(index):
        feed_start(index)
        for lines in tiles:
            feed(index, lines)
        act_store(index).start()

    def whole_back(index):
        for lines in tiles:
            back(index, lines)
        if index + 1 < CHUNKS:
            for copy in own_weights(index + 1):
                copy.start()

    da_copy(0).wait_recv()
    for lines in tiles:
        feed(0, lines, (1, 2))
    right_copy(0, 1).start()
    right_copy(0, 2).start()
    da_copy(1).start()
    whole_back(0)
    pump("u1")

    def event_start():
        got_right(0, 0)

    def event_columns():
        h_two_first.wait_recv()
        h_two_second.start()
        h_two_second.wait()
        turned(1, h_two_peer, 0, tokens)
        got_right(0, 1)

    def event_first():
        got_right(0, 2)
        ready(1)
        whole_feed(1)
        for kind in range(3):
            right_copy(1, kind).start()
        for name in ("g2", "u2"):
            over_shard(name).start()
        da_copy(2).start()
        over_shard("g3").start()

    def event_second():
        over_shard("g2").wait_recv()
        over_shard("u2").wait_recv()
        ready(2)
        whole_feed(2)
        right_copy(2, 0).start()
        right_copy(2, 1).start()
        over_shard("u3").start()
        da_copy(3).start()
        right_copy(2, 2).start()
        got_right(1, 2)

    back_blocks, d_resid, resid_own = cot_got, dh_sum.at[1, :, pl.ds(0, part)], dh_sum.at[1, :, pl.ds(part, part)]
    hone_first, hone_second = columns_out("ic", h_one_out, cot_peer)
    dr_first, dr_second = columns_out("dc", h_two, h_two_peer)
    mixer_rights = 3 * hidden

    def mixer_right(kind):
        source = gated if kind == 0 else ffn_v.at[0, kind - 1]
        strip = pl.ds(mixer_rights + kind * part, part)
        return remote("m%d" % kind, source, rights_peer.at[:, strip], {"shard": 1 - shard})

    def got_mixer_right(kind):
        mixer_right(kind).wait_recv()
        room = right_v.at[max(kind - 1, 0)]
        copy = load(23, rights_peer.at[:, pl.ds(mixer_rights + kind * part, part)], room)
        copy.start()
        copy.wait()

    x_reload = load(5, x_out, x_full)
    mixer_reloads = [
        load(6, mixer_out.at[0], h_one.at[:, own_half]), load(7, mixer_out.at[1], h_one.at[:, peer_half])
    ]
    h_one_reload = load(8, h_one_out.at[:, own_half], dh_got)
    in_reloads = [load(13 + column, in_w.at[column], in_v.at[0, column]) for column in range(3)]
    in_reloads += [load(16 + column, in_peer.at[column], in_v.at[1, column]) for column in range(3)]
    fine = min(32, tokens)

    def reload():
        for index in range(CHUNKS):
            da_copy(index).wait_send()
        act_store(CHUNKS - 1).wait()
        act_store(CHUNKS - 2).wait()
        for copy in [x_reload] + mixer_reloads + in_reloads + down_loads + [act_own_load]:
            copy.start()

    def resid_back():
        dh_last.wait_recv()
        h_one_reload.start()
        for copy in [x_reload] + mixer_reloads:
            copy.wait()
        h_two_first.wait_send()
        gain_sums[...] = jnp.zeros((2, width), WIDE)

        @pl.loop(0, tokens // fine)
        def _(index):
            lines = pl.ds(pl.multiple_of(index * fine, fine), fine)

            def halves(columns_of, which):
                resid = x_full[lines, columns_of].astype(WIDE) + h_one[lines, columns_of].astype(WIDE)
                return resid, mixer[which, lines].astype(WIDE)

            own, own_grad = halves(own_half, 0)
            other, other_grad = halves(peer_half, 1)
            total = jnp.sum(own * own, axis=1, keepdims=True) + jnp.sum(other * other, axis=1, keepdims=True)
            scale = lax.rsqrt(total / width + EPS)
            own, other = own * scale, other * scale
            own_scaled, other_scaled = own_grad * gains[1:2, own_half], other_grad * gains[1:2, peer_half]
            mean = (
                jnp.sum(own_scaled * own, axis=1, keepdims=True)
                + jnp.sum(other_scaled * other, axis=1, keepdims=True)
            ) / width
            h_two[lines, own_half] = (
                cot_full[lines, own_half].astype(WIDE) + scale * (own_scaled - own * mean)
            ).astype(LOW)
            h_two[lines, peer_half] = (
                cot_full[lines, peer_half].astype(WIDE) + scale * (other_scaled - other * mean)
            ).astype(LOW)
            gain_sums[1:2, own_half] += jnp.sum(own_grad * own, axis=0, keepdims=True)
            gain_sums[1:2, peer_half] += jnp.sum(other_grad * other, axis=0, keepdims=True)
            resid = x_full[lines, own_part].astype(WIDE) + h_one[lines, own_part].astype(WIDE)
            resid_own[lines] = resid
            which = jnp.where(outer == shard, 0, 1)
            scaled = mixer[which, lines, columns(core, part)].astype(WIDE) * gains[1:2, own_part]
            d_resid[lines] = cot_full[lines, own_part].astype(WIDE) + scale * (
                scaled - resid * scale * mean
            )

        dr_first.start()

    rim_out = remote(
        "rim_back", edge_v, rim_back, {"ctx": lax.rem(ctx + blocks - 1, blocks)}
    )

    def conv_back():
        for kind in range(3):
            right_copy(CHUNKS - 2, kind).wait_send()

        def body(lines):
            d_gated = jnp.dot(
                h_two[lines, own_half], out_v[0], preferred_element_type=WIDE
            ) + jnp.dot(h_two[lines, peer_half], out_v[1], preferred_element_type=WIDE)
            d_ext[lines] = (d_gated * proj[1, lines]).astype(LOW).astype(WIDE)
            ffn_v[0, 1, lines] = (d_gated * conv_v[lines]).astype(LOW)

        for lines in tiles:
            body(lines)
        edge_v[...] = d_ext[0:16].astype(LOW)

        @pl.when(ctx > 0)
        def _():
            rim_out.start()

        turned(0, h_two, shard * half, 0)

    def out_ready():
        dr_first.wait_recv()
        dr_second.start()
        right_copy(CHUNKS - 1, 0).wait_send()

        def body(lines):
            ffn_v[1, 0, lines] = gated[lines]

        over_tiles(body)
        dr_second.wait_recv()
        turned(0, h_two_peer, 0, tokens)
        got_mixer_right(0)

    def proj_back():
        @pl.when(ctx < blocks - 1)
        def _():
            rim_out.wait_recv()
            d_ext[tokens : tokens + 8] = rim_back[0:8].astype(WIDE)

        @pl.when(ctx == blocks - 1)
        def _():
            d_ext[tokens : tokens + 8] = jnp.zeros((8, part), WIDE)

        sums = [jnp.zeros((1, part), WIDE) for _ in range(3)]
        size = 128
        for start in range(0, tokens, size):
            lines = pl.ds(start, size)
            own = d_ext[lines]
            d_mixed = taps[0:1] * own
            d_mixed = d_mixed + taps[1:2] * (d_ext[pl.ds(start + 1, size)] * masks[lines, 2:3])
            d_mixed = d_mixed + taps[2:3] * (d_ext[pl.ds(start + 2, size)] * masks[lines, 3:4])
            ffn_v[0, 0, lines] = (d_mixed * proj[2, lines]).astype(LOW)
            ffn_v[0, 2, lines] = (d_mixed * proj[0, lines]).astype(LOW)
            for tap in range(3):
                value = own * extended[pl.ds(start + 8 - tap, size)]
                if tap > 0:
                    value = value * masks[lines, tap - 1 : tap]
                sums[tap] = sums[tap] + jnp.sum(value, axis=0, keepdims=True)
        small[...] = jnp.zeros(small.shape, WIDE)
        for tap in range(3):
            small[tap : tap + 1] = sums[tap]
        for kind in range(1, 4):
            mixer_right(kind).start()

    def in_ready():
        hone_first.wait_recv()
        hone_second.start()
        h_one_reload.wait()
        turned(1, dh_got, 0, 0)
        hone_second.wait_recv()
        turned(1, cot_peer, 0, tokens)
        got_mixer_right(1)

    back_away = remote("bh1", away, pair_got, {"tp": core_mate})
    back_pair = remote("bh2", pair, both_got, {"tp": outer_mate})
    back_last = remote("bh3", mixer.at[core], mixer.at[core], {"tp": core_mate})

    def to_inputs(lines, which):
        total = None
        for column in range(3):
            term = lax.dot_general(
                ffn_v[0, column, lines], in_v[which, column],
                (((1,), (1,)), ((), ())), preferred_element_type=WIDE,
            )
            total = term if total is None else total + term
        return total

    def back_one_hop():
        for copy in (dh_away, dh_pair, dh_last):
            copy.wait_send()
        for copy in in_reloads:
            copy.wait()

        def body(lines):
            away[lines] = to_inputs(lines, 1 - core).astype(LOW)

        over_tiles(body)
        back_away.start()

        def rest(lines):
            dh_sum[0, lines] = to_inputs(lines, core)

        over_tiles(rest)

    def back_two_hops():
        back_away.wait_recv()

        def body(lines):
            pair[lines] = (dh_sum[0, lines] + pair_got[lines].astype(WIDE)).astype(LOW)

        over_tiles(body)
        back_pair.start()
        got_mixer_right(2)

    def back_three_hops():
        back_pair.wait_recv()

        def body(lines):
            mixer[core, lines] = (pair[lines].astype(WIDE) + both_got[lines].astype(WIDE)).astype(LOW)

        over_tiles(body)
        back_last.start()
        got_mixer_right(3)

    def give_back(name, block, target, step):
        to, origin = lax.rem(ctx + step, blocks), lax.rem(ctx + blocks - step, blocks)
        name = name + str(step)
        return (
            remote(name, block(to), target.at[ctx], {"ctx": to}),
            remote(name, block(to), target.at[origin], {"ctx": to}),
        )

    def out_block(to):
        return gated.at[pl.ds(pl.multiple_of(to * block_rows, block_rows), block_rows)]

    given = [give_back("give", lambda to: back_blocks.at[to], dealt, step) for step in range(1, blocks)]
    given_out = [give_back("out", out_block, dealt_out, step) for step in range(1, blocks)]
    kept = load(9, back_blocks.at[ctx], dealt.at[ctx])
    kept_out = load(10, out_block(ctx), dealt_out.at[ctx])

    down_loads = [
        load(index, down_w.at[:, pl.ds(index * chunk, chunk)], gu_v.at[index // 2, index % 2])
        for index in range(CHUNKS)
    ]
    act_own_load = load(21, act_out, da_got)
    act_peer_load = load(22, rights_peer.at[:, pl.ds(0, hidden)], da_got)
    ffn_first = remote(
        "fx", cot_full.at[:, pl.ds(half, half)], h_one.at[:, pl.ds(0, half)], {"shard": 1 - shard}
    )
    ffn_core = [
        remote("fc0", cot_full.at[:, columns(1 - core, part)], out_v.at[0, pl.ds(0, tokens)], {"tp": core_mate}),
        remote("fc1", h_one.at[:, columns(1 - core, part)], out_v.at[1, pl.ds(0, tokens)], {"tp": core_mate}),
    ]
    kept_which = jnp.where(outer == shard, 0, 1)

    def ffn_pair(which):
        return pl.ds(pl.multiple_of(half + which * part, part), part)

    ffn_outer = [
        remote(
            "fy%d" % index,
            h_one.at[pl.ds(index * block_rows, block_rows), ffn_pair(1 - kept_which)],
            x_got.at[index],
            {"tp": outer_mate},
        )
        for index in range(blocks)
    ]

    def ffn_part(start):
        def body(lines):
            total = None
            for index in range(CHUNKS):
                term = lax.dot_general(
                    da_got[lines, pl.ds(index * chunk, chunk)], gu_v[index // 2, index % 2],
                    (((1,), (1,)), ((), ())), preferred_element_type=WIDE,
                )
                total = term if total is None else total + term
            cot_full[lines, pl.ds(start, half)] = total.astype(LOW)

        over_tiles(body)

    def ffn_own():
        for copy in (cot_outer, cot_core, cot_more, cot_first):
            copy.wait_send()
        for copy in down_loads:
            copy.wait()
        act_own_load.wait()
        ffn_part(0)
        act_peer_load.start()

    def ffn_peer():
        act_peer_load.wait()
        ffn_part(half)
        ffn_first.start()

    def ffn_to_core():
        ffn_first.wait_recv()
        for copy in ffn_core:
            copy.start()

    def ffn_to_outer():
        for copy in ffn_core:
            copy.wait_recv()

        def body(lines):
            own = columns(core, part)
            h_one[lines, ffn_pair(0)] = (
                cot_full[lines, own].astype(WIDE) + out_v[0, lines].astype(WIDE)
            ).astype(LOW)
            h_one[lines, ffn_pair(1)] = (
                h_one[lines, own].astype(WIDE) + out_v[1, lines].astype(WIDE)
            ).astype(LOW)

        over_tiles(body)
        for copy in ffn_outer:
            copy.start()

    def block_back():
        mixer_right(0).wait_send()
        for index, copy in enumerate(ffn_outer):
            copy.wait_recv()
            lines = pl.ds(index * block_rows, block_rows)
            resid_own[lines] = (
                resid_own[lines] + h_one[lines, ffn_pair(kept_which)].astype(WIDE) + x_got[index].astype(WIDE)
            )
        for to in range(blocks):
            total = place[0, to] * resid_own[0:block_rows]
            for index in range(1, blocks):
                total = total + place[index, to] * resid_own[index * block_rows : (index + 1) * block_rows]
            gated[to * block_rows : (to + 1) * block_rows] = total.astype(LOW)
        for out, _ in given_out:
            out.start()
        kept_out.start()

    def input_back():
        back_last.wait_recv()

        @pl.loop(0, tokens // fine)
        def _(index):
            lines = pl.ds(pl.multiple_of(index * fine, fine), fine)
            own, other = x_full[lines, own_half].astype(WIDE), x_full[lines, peer_half].astype(WIDE)
            own_grad, other_grad = mixer[0, lines].astype(WIDE), mixer[1, lines].astype(WIDE)
            total = jnp.sum(own * own, axis=1, keepdims=True) + jnp.sum(other * other, axis=1, keepdims=True)
            scale = lax.rsqrt(total / width + EPS)
            own, other = own * scale, other * scale
            mean = (
                jnp.sum(own_grad * gains[0:1, own_half] * own, axis=1, keepdims=True)
                + jnp.sum(other_grad * gains[0:1, peer_half] * other, axis=1, keepdims=True)
            ) / width
            gain_sums[0:1, own_half] += jnp.sum(own_grad * own, axis=0, keepdims=True)
            gain_sums[0:1, peer_half] += jnp.sum(other_grad * other, axis=0, keepdims=True)
            which = jnp.where(outer == shard, 0, 1)
            scaled = mixer[which, lines, columns(core, part)].astype(WIDE) * gains[0:1, own_part]
            normed = x_full[lines, own_part].astype(WIDE) * scale
            d_resid[lines] = d_resid[lines] + scale * (scaled - normed * mean)

        for to in range(blocks):
            total = place[0, to] * d_resid[0:block_rows]
            for index in range(1, blocks):
                total = total + place[index, to] * d_resid[index * block_rows : (index + 1) * block_rows]
            back_blocks[to] = total.astype(LOW)
        for out, _ in given:
            out.start()
        kept.start()

    def event_third():
        over_shard("g3").wait_recv()
        over_shard("u3").wait_recv()
        ready(3)
        whole_feed(3)
        for kind in range(3):
            right_copy(3, kind).start()
        hone_first.start()
        mixer_right(0).start()
        got_right(2, 2)

    def dh_one_hop():
        whole_back(3)
        mixer_store.wait()
        for trio in hops:
            for copy in trio:
                copy.wait_send()

        def body(lines):
            away[lines] = dh_sum[1 - core, lines].astype(LOW)

        over_tiles(body)
        dh_away.start()

    def dh_two_hops():
        dh_away.wait_recv()

        def body(lines):
            pair[lines] = (dh_sum[core, lines] + pair_got[lines].astype(WIDE)).astype(LOW)

        over_tiles(body)
        dh_pair.start()
        reload()
        got_right(3, 0)

    def dh_three_hops():
        dh_pair.wait_recv()

        def body(lines):
            mixer[core, lines] = (pair[lines].astype(WIDE) + dh_got[lines].astype(WIDE)).astype(LOW)

        over_tiles(body)
        dh_last.start()
        got_right(3, 1)

    def last_rights():
        ffn_own()
        got_right(3, 2)

    def proj_and_ffn():
        proj_back()
        ffn_peer()

    def back_and_ffn():
        ffn_to_outer()
        back_three_hops()

    small_shard = remote("ss", small, small_got.at[blocks], {"shard": 1 - shard})

    def small_ctx(step):
        to, origin = lax.rem(ctx + step, blocks), lax.rem(ctx + blocks - step, blocks)
        return (
            remote("sc%d" % step, small_got.at[ctx], small_got.at[ctx], {"ctx": to}),
            remote("sc%d" % step, small_got.at[ctx], small_got.at[origin], {"ctx": to}),
        )

    small_steps = [small_ctx(step) for step in range(1, blocks)]

    def ends_back():
        input_back()
        block_back()
        small[3:5] = gain_sums[:, own_part]
        small_shard.start()

    events = {
        0: event_start,
        2: event_columns,
        4: event_first,
        5: lambda: whole_back(1),
        6: lambda: got_right(1, 0),
        8: lambda: got_right(1, 1),
        10: event_second,
        11: lambda: whole_back(2),
        12: lambda: got_right(2, 0),
        14: lambda: got_right(2, 1),
        16: event_third,
        17: dh_one_hop,
        18: dh_two_hops,
        20: dh_three_hops,
        21: resid_back,
        22: last_rights,
        23: conv_back,
        24: out_ready,
        25: proj_and_ffn,
        26: in_ready,
        27: back_one_hop,
        28: back_two_hops,
        29: ffn_to_core,
        30: back_and_ffn,
        31: ends_back,
    }

    @pl.loop(0, pieces_in_all)
    def _(piece):
        for turn, event in events.items():
            pl.when(piece == turn)(event)
        grad_piece(piece)

    small_shard.wait_recv()
    small_got[ctx] = small[...] + small_got[blocks]
    for out, _ in small_steps:
        out.start()

    @pl.when(middle)
    def _():
        finish(pieces_in_all - 1)

    for _, into in small_steps:
        into.wait_recv()
    total = small_got[0]
    for index in range(1, blocks):
        total = total + small_got[index]
    small_sums[...] = total

    for out, _ in x_deals + cot_deals:
        out.wait_send()
    for out, _ in small_steps:
        out.wait_send()
    for copy in (small_shard, gain_outer, gain_core, gain_more, hone_first, hone_second, dr_first, dr_second, back_away, back_pair, back_last,
                 ffn_first, *ffn_core, *ffn_outer):
        copy.wait_send()
    for name in pieces:
        over_shard(name).wait_send()
        if name not in direct:
            over_ctx(name).wait_send()
    for kind in (1, 2):
        right_copy(CHUNKS - 1, kind).wait_send()
    for kind in range(1, 4):
        mixer_right(kind).wait_send()
    kept.wait()
    kept_out.wait()
    for out, into in given + given_out:
        out.wait_send()
        into.wait_recv()

    @pl.when(ctx < blocks - 1)
    def _():
        rim_copy.wait_send()

    @pl.when(ctx > 0)
    def _():
        rim_out.wait_send()

    @pl.loop(0, pieces_in_all)
    def _(piece):
        @pl.when(piece >= pieces_in_all - SLOTS)
        def _():
            inward_copy(piece, outer_land, outer_recv).wait_send()

        @pl.when(jnp.logical_and(middle, piece >= pieces_in_all - TOTALS))
        def _():
            outward_copy(piece).wait_send()
            total_store(piece).wait()

        @pl.when(end)
        def _():
            outward_copy(piece).wait_recv()


FRONT_COPIES = 112


def front(x_in, cot_in, sending, place, own_gains, masks, taps, in_w, out_w, gate_w, up_w, down_w):
    tokens, part = x_in.shape
    blocks = place.shape[0]
    block_shape = (blocks, tokens // blocks, part)
    rows, hidden = gate_w.shape
    width = 4 * part
    half = width // 2
    chunk = hidden // CHUNKS
    pieces = (3 * hidden + width) // PIECE
    vmem = pl.BlockSpec(memory_space=pltpu.VMEM)
    hbm = pl.BlockSpec(memory_space=pl.ANY)
    shape = jax.ShapeDtypeStruct
    outs = [
        shape(in_w.shape, LOW),
        shape(out_w.shape, LOW),
        shape(gate_w.shape, LOW),
        shape(up_w.shape, LOW),
        shape((pieces, rows, PIECE), LOW),
        shape((pieces, rows, PIECE), LOW),
        shape((tokens, 3 * hidden + width), LOW),
        shape((tokens, width), LOW),
        shape((tokens, width), LOW),
        shape((2, tokens, half), LOW),
        shape((tokens, hidden), LOW),
        shape((rows, 3 * hidden + width), LOW),
        shape(block_shape, LOW),
        shape(block_shape, LOW),
        shape((8, part), WIDE),
    ]
    low, wide = (lambda *dims: pltpu.VMEM(dims, LOW)), (lambda *dims: pltpu.VMEM(dims, WIDE))
    dma = pltpu.SemaphoreType.DMA
    scratch = [
        low(*block_shape),
        low(*block_shape),
        wide(8, width),
        wide(2, width),
        wide(8, part),
        wide(blocks + 1, 8, part),
        low(*block_shape),
        low(*block_shape),
        low(tokens, width),
        low(tokens, width),
        low(tokens, width),
        low(tokens, half),
        low(tokens, width),
        low(tokens, half),
        wide(3, tokens, part),
        low(tokens, part),
        low(tokens, part),
        low(2, tokens, half),
        wide(tokens, part),
        low(2, rows, part),
        low(16, part),
        wide(tokens + 8, part),
        low(tokens, half),
        low(tokens, half),
        low(tokens, half),
        low(tokens, half),
        low(tokens, half),
        low(tokens, hidden),
        low(2, 3, rows, part),
        low(2, 2, rows, chunk),
        low(rows, hidden),
        wide(2, tokens, half),
        low(2, 3, tokens, chunk),
        low(3, tokens, chunk),
        low(rows, PIECE),
        low(rows, PIECE),
        low(SLOTS, rows, PIECE),
        low(TOTALS, rows, PIECE),
        wide(tokens + 8, part),
        low(16, part),
        low(16, part),
        dma((FRONT_COPIES,)),
        dma((FRONT_COPIES,)),
        dma((28,)),
    ] + [dma((pieces,)) for _ in range(6)]
    return pl.pallas_call(
        front_kernel,
        out_shape=outs,
        in_specs=[vmem, vmem] + [pl.BlockSpec(memory_space=pltpu.SMEM)] * 2 + [vmem] * 3
        + [hbm] * 5,
        out_specs=[hbm] * (len(outs) - 1) + [vmem],
        scratch_shapes=scratch,
        compiler_params=pltpu.CompilerParams(
            collective_id=2, has_side_effects=True, vmem_limit_bytes=63 * 1024 * 1024
        ),
        cost_estimate=pl.CostEstimate(
            flops=2 * tokens * width * hidden * 64, bytes_accessed=1 << 29, transcendentals=0
        ),
    )(x_in, cot_in, sending, place, own_gains, masks, taps, in_w, out_w, gate_w, up_w, down_w)


class Features:
    def __init__(self):
        rank = lax.axis_index("tp")
        self.rank = rank
        self.inner = rank % 2
        self.outer = rank // 2

    def gather(self, own):
        other = swapped(own, "tp", 2)
        first = self.outer == 0
        pair = jnp.stack([jnp.where(first, own, other), jnp.where(first, other, own)])
        more = swapped(pair, "tp", 1)
        even = self.inner == 0
        left, right = jnp.where(even, pair, more), jnp.where(even, more, pair)
        return jnp.concatenate([left[0], right[0], left[1], right[1]], axis=1)

    def total(self, first_half, second_half):
        even = self.inner == 0
        kept = jnp.where(even, first_half, second_half)
        sent = jnp.where(even, second_half, first_half).astype(LOW)
        pair = (kept.astype(WIDE) + swapped(sent, "tp", 1).astype(WIDE)).astype(LOW)
        both = (pair.astype(WIDE) + swapped(pair, "tp", 2).astype(WIDE)).astype(LOW)
        other = swapped(both, "tp", 1)
        return jnp.where(even, both, other), jnp.where(even, other, both)

    def scatter(self, full):
        rows, width = full.shape
        blocks = full.reshape(rows, 2, 2, width // 4)
        even = self.inner == 0
        kept = jnp.where(even, blocks[:, :, 0], blocks[:, :, 1])
        sent = jnp.where(even, blocks[:, :, 1], blocks[:, :, 0]).astype(LOW)
        pair = kept.astype(WIDE) + swapped(sent, "tp", 1).astype(WIDE)
        first = self.outer == 0
        mine = jnp.where(first, pair[:, 0], pair[:, 1])
        away = jnp.where(first, pair[:, 1], pair[:, 0]).astype(LOW)
        return mine + swapped(away, "tp", 2).astype(WIDE)

    def all_terms(self, full):
        low = full.astype(LOW)
        return [low] + [swapped(low, "tp", step) for step in (1, 2, 3)]

    def own_terms(self, full):
        width = full.shape[1] // 4
        blocks = [
            lax.dynamic_slice_in_dim(full, (self.rank ^ step) * width, width, 1).astype(LOW)
            for step in range(4)
        ]
        return blocks[:1] + [swapped(blocks[step], "tp", step) for step in (1, 2, 3)]

    def own(self, full, axis):
        width = full.shape[axis] // lax.axis_size("tp")
        return lax.dynamic_slice_in_dim(full, self.rank * width, width, axis)


class Shards:
    def __init__(self, tp):
        self.count = lax.axis_size("shard")
        self.rank = lax.axis_index("shard")
        self.ctx_rank = lax.axis_index("ctx")
        self.tp = tp
        self.paired = self.count == 2

    def weight(self, rows):
        if not self.paired:
            return (lax.all_gather(rows, "shard", axis=0, tiled=True),)
        return (rows, swapped(rows, "shard", 1))

    def split(self, full):
        if not self.paired:
            return (full,)
        width = full.shape[1] // 2
        return (
            lax.dynamic_slice_in_dim(full, self.rank * width, width, 1),
            lax.dynamic_slice_in_dim(full, (1 - self.rank) * width, width, 1),
        )

    def join(self, parts):
        if not self.paired:
            return parts[0]
        first = self.rank == 0
        return jnp.concatenate(
            [jnp.where(first, parts[0], parts[1]), jnp.where(first, parts[1], parts[0])], axis=1
        )

    def columns(self, full):
        if not self.paired:
            return lax.all_to_all(full, "shard", split_axis=1, concat_axis=0, tiled=True)
        own, other = self.split(full)
        width = own.shape[1] // 2
        part = lax.dynamic_slice_in_dim(other, self.tp.inner * width, width, 1)
        got = swapped(part, "shard", 1)
        rest = swapped(got, "tp", 1)
        even = self.tp.inner == 0
        peer = jnp.concatenate([jnp.where(even, got, rest), jnp.where(even, rest, got)], axis=1)
        return jnp.concatenate([own, peer], axis=0)

    def tokens(self, own):
        if not self.paired:
            return lax.all_gather(own, "shard", axis=0, tiled=True)
        return jnp.concatenate([own, swapped(own, "shard", 1)], axis=0)

    def own_total(self, product):
        if not self.paired:
            return lax.psum_scatter(product, "shard", scatter_dimension=0, tiled=True)
        rows = product.shape[0] // 2
        return product[:rows] + swapped(product[rows:].astype(LOW), "shard", 1).astype(WIDE)

    def own_tokens(self, product):
        if not self.paired:
            return lax.all_to_all(product.astype(LOW), "shard", split_axis=0, concat_axis=1, tiled=True)
        rows = product.shape[0] // 2
        return self.join([product[:rows].astype(LOW), swapped(product[rows:].astype(LOW), "shard", 1)])


def deal_routes(dealing, own_blocks, ctx_rank, per_dev, per_peer):
    send_order = jnp.argsort(own_blocks // per_dev, stable=True)
    wanted = jnp.where(dealing // per_dev == ctx_rank, 0, 1)
    chosen = jnp.argsort(wanted, axis=1, stable=True)[:, :per_peer]
    targets = (jnp.take_along_axis(dealing, chosen, 1) % per_dev).reshape(-1)
    return send_order, targets, jnp.argsort(targets), jnp.argsort(send_order)


def on_device(
    hidden_in,
    out_grad,
    seq_lengths,
    deal_order,
    in_weight,
    conv_weight,
    out_weight,
    norm1_gain,
    norm2_gain,
    gate_weight,
    up_weight,
    down_weight,
):
    ctx_size = lax.axis_size("ctx")
    ctx_rank = lax.axis_index("ctx")
    tp = Features()
    shards = Shards(tp)
    row_count, col_count = hidden_in.shape
    hidden_count = gate_weight.shape[1]
    weight_rows = in_weight.shape[0]
    per_dev = deal_order.shape[1] // ctx_size
    per_peer = per_dev // ctx_size
    block_rows = row_count // per_dev
    dealing = deal_order[0].reshape(ctx_size, per_dev)
    own_blocks = lax.dynamic_index_in_dim(dealing, ctx_rank, 0, keepdims=False)

    def reorder(values, index):
        blocks = values.reshape(per_dev, block_rows, values.shape[1])
        return blocks[index].reshape(row_count, values.shape[1])

    def to_packed(values):
        got = lax.all_to_all(
            reorder(values, send_order), "ctx", split_axis=0, concat_axis=0, tiled=True
        )
        return reorder(got, placing)

    def to_dealt(values):
        got = lax.all_to_all(
            reorder(values, targets), "ctx", split_axis=0, concat_axis=0, tiled=True
        )
        return reorder(got, returning)

    def weight_grads(lefts, rights, identity):
        flat = [value for group in rights for value in group]
        if shards.paired:
            summed = line_grads([group[0] for group in lefts], flat, identity)
            ends = [0]
            for value in flat:
                ends.append(ends[-1] + value.shape[1])
            return [summed[:, a:b] for a, b in zip(ends, ends[1:])]
        flat_lefts = [value for group in lefts for value in group]
        return [
            sum_line(contract_rows(left, shards.tokens(right)).astype(LOW), ctx_rank)
            for left, right in zip(flat_lefts, flat)
        ]

    lengths = seq_lengths[0]
    starts = jnp.cumsum(lengths) - lengths
    where_t = ctx_rank * row_count - 2 + jnp.arange(row_count + 4, dtype=jnp.int32)
    seq_begin = jnp.max(jnp.where(starts[None, :] <= where_t[:, None], starts[None, :], 0), axis=1)
    position = where_t - seq_begin
    first_own = (position[2 : row_count + 2] >= 1).astype(WIDE)[:, None]
    second_own = (position[2 : row_count + 2] >= 2).astype(WIDE)[:, None]
    first_next = (position[3 : row_count + 3] >= 1).astype(WIDE)[:, None]
    second_next = (position[4 : row_count + 4] >= 2).astype(WIDE)[:, None]
    conv_taps = conv_weight.astype(WIDE)
    gains = jnp.stack([norm1_gain, norm2_gain])

    if shards.paired:
        goes_to = own_blocks // per_dev
        slots = jnp.arange(per_dev, dtype=jnp.int32)
        sending = (goes_to[None, :] == slots[:, None]).astype(WIDE)
        wants = ctx_rank * per_dev + slots
        place = jnp.sum((dealing[None] == wants[:, None, None]).astype(WIDE), axis=2)
        *_, sums, dealt, dealt_out, small_sum = front(
            hidden_in, out_grad, sending, place, jnp.pad(gains.astype(WIDE), ((0, 6), (0, 0))),
            jnp.concatenate([first_own, second_own, first_next, second_next], axis=1), conv_taps,
            jnp.moveaxis(in_weight, 1, 0), out_weight, gate_weight, up_weight, down_weight,
        )
        block_dealt = reorder(dealt_out.reshape(row_count, col_count), goes_to)
        input_dealt = reorder(dealt.reshape(row_count, col_count), goes_to)
        ends = [hidden_count, 2 * hidden_count, 3 * hidden_count, 3 * hidden_count + col_count]
        ends += [ends[-1] + col_count, ends[-1] + 2 * col_count]
        down_total, gate_total, up_total, out_total, *in_parts = jnp.split(sums, ends, axis=1)
        in_total = jnp.moveaxis(jnp.stack(in_parts).astype(WIDE), 0, 1)
        down_total, gate_total, up_total, out_total = [
            value.astype(WIDE) for value in (down_total, gate_total, up_total, out_total)
        ]
    else:
        in_w = shards.weight(in_weight.reshape(weight_rows, -1))
        send_order, targets, placing, returning = deal_routes(dealing, own_blocks, ctx_rank, per_dev, per_peer)
        full_gains = tp.gather(gains).astype(WIDE)
        gain_one, gain_two = full_gains[0], full_gains[1]
        x_full = tp.gather(to_packed(hidden_in))
        out_w = shards.weight(out_weight)
        cot_full = tp.gather(to_packed(out_grad))
        gate_w, up_w = shards.weight(gate_weight), shards.weight(up_weight)
        x_float = x_full.astype(WIDE)
        scale_one = lax.rsqrt(jnp.mean(x_float * x_float, axis=1, keepdims=True) + EPS)
        normed_one = x_float * scale_one
        h_one = (normed_one * gain_one).astype(LOW)
        projected = matmul(h_one, in_w[0])
        b_part = projected[:, :col_count]
        c_part = projected[:, col_count : 2 * col_count]
        v_part = projected[:, 2 * col_count :]
        mixed = (b_part * v_part).astype(LOW)
        rim = shifted(mixed[-2:], "ctx", 1)
        extended = jnp.concatenate([rim, mixed], axis=0).astype(WIDE)
        prev_one = extended[1 : row_count + 1] * first_own
        prev_two = extended[0:row_count] * second_own
        conv_out = (
            conv_taps[0] * extended[2:] + conv_taps[1] * prev_one + conv_taps[2] * prev_two
        )
        gated = (c_part * conv_out).astype(LOW)
        mixer_halves = jnp.split(contract_cols(gated, out_w[0]), 2, axis=1)
        mixer_out = jnp.concatenate(tp.total(*mixer_halves), axis=1)
        resid = x_float + mixer_out.astype(WIDE)
        scale_two = lax.rsqrt(jnp.mean(resid * resid, axis=1, keepdims=True) + EPS)
        normed_two = resid * scale_two
        h_two = (normed_two * gain_two).astype(LOW)
        cot_cols, h_two_cols, h_one_cols = [shards.columns(v) for v in (cot_full, h_two, h_one)]
        gate_pre, up_pre = matmul(h_two, gate_w[0]), matmul(h_two, up_w[0])
        d_act = shards.own_total(matmul(cot_cols, down_weight))
        sigmoid_gate = jax.nn.sigmoid(gate_pre)
        silu_gate = gate_pre * sigmoid_gate
        d_gate = d_act * up_pre * sigmoid_gate * (1.0 + gate_pre * (1.0 - sigmoid_gate))
        ffn_rights = [v.astype(LOW) for v in (silu_gate * up_pre, d_gate, d_act * silu_gate)]
        act_all = shards.tokens(ffn_rights[0])
        dh_terms = tp.all_terms(
            contract_cols(ffn_rights[1], gate_w[0]) + contract_cols(ffn_rights[2], up_w[0])
        )
        dh_two = added(dh_terms)
        ffn_grads = weight_grads(
            [[cot_cols], [h_two_cols, h_two_cols]], [ffn_rights[:1], ffn_rights[1:]], 0
        )

        ffn_terms = tp.own_terms(shards.own_tokens(contract_cols(act_all, down_weight)))

        rim = shifted(mixed[-2:], "ctx", 1)
        extended = jnp.concatenate([rim, mixed], axis=0).astype(WIDE)
        prev_one = extended[1 : row_count + 1] * first_own
        prev_two = extended[0:row_count] * second_own
        mixed_float = extended[2:]

        gain_two_grad = tp.own(jnp.sum(dh_two * normed_two, axis=0), 0)
        d_resid = cot_full.astype(WIDE) + norm_back(dh_two, normed_two, scale_two, gain_two)
        d_resid_low = d_resid.astype(LOW)
        d_gated = sum(matmul(part, w) for part, w in zip(shards.split(d_resid_low), out_w))
        d_conv = (d_gated * c_part).astype(LOW)
        d_c_part = d_gated * conv_out
        rim_back = shifted(d_conv[:2], "ctx", -1)
        d_conv_float = d_conv.astype(WIDE)
        back_ext = jnp.concatenate([d_conv, rim_back], axis=0).astype(WIDE)
        d_mixed = (
            conv_taps[0] * d_conv_float
            + conv_taps[1] * back_ext[1 : row_count + 1] * first_next
            + conv_taps[2] * back_ext[2:] * second_next
        )
        taps_grad = jnp.stack(
            [
                jnp.sum(d_conv_float * mixed_float, axis=0),
                jnp.sum(d_conv_float * prev_one, axis=0),
                jnp.sum(d_conv_float * prev_two, axis=0),
            ]
        )
        d_proj = [
            (d_mixed * v_part).astype(LOW),
            d_c_part.astype(LOW),
            (d_mixed * b_part).astype(LOW),
        ]
        d_proj_flat = jnp.concatenate(d_proj, axis=1)
        dh_one_terms = tp.all_terms(shards.join([contract_cols(d_proj_flat, w) for w in in_w]))
        mixer_grads = weight_grads(
            [[shards.columns(d_resid_low)], [h_one_cols]], [[gated], [d_proj_flat]], 1
        )
        dh_one_terms, ffn_terms, mixer_grads = lax.optimization_barrier(
            (dh_one_terms, ffn_terms, mixer_grads)
        )
        dh_one = added(dh_one_terms)
        block_out = (tp.own(resid, 1) + added(ffn_terms)).astype(LOW)
        down_total, gate_total, up_total = [value.astype(WIDE) for value in ffn_grads]
        out_total, in_flat_total = [value.astype(WIDE) for value in mixer_grads]
        in_total = in_flat_total.reshape(in_weight.shape)
        gain_one_grad = tp.own(jnp.sum(dh_one * normed_one, axis=0), 0)
        d_input = d_resid + norm_back(dh_one, normed_one, scale_one, gain_one)
        dealt = to_dealt(jnp.concatenate([block_out, tp.own(d_input, 1).astype(LOW)], axis=1))
        block_dealt, input_dealt = dealt[:, :col_count], dealt[:, col_count:]
        small = jnp.concatenate([taps_grad, gain_one_grad[None], gain_two_grad[None]], axis=0)
        small_sum = butterfly_sum(butterfly_sum(small, "shard"), "ctx")

    return (
        block_dealt,
        input_dealt,
        in_total,
        small_sum[0:3],
        out_total,
        small_sum[3],
        small_sum[4],
        gate_total,
        up_total,
        down_total,
    )


def solution(mesh):
    placed = (
        P(("shard", "ctx"), "tp"),
        P(("shard", "ctx"), "tp"),
        P("shard", None),
        P("shard", None),
        P("shard", None, "tp"),
        P(None, "tp"),
        P("shard", "tp"),
        P("tp"),
        P("tp"),
        P("shard", "tp"),
        P("shard", "tp"),
        P("shard", "tp"),
    )
    return jax.shard_map(
        on_device,
        mesh=mesh,
        in_specs=placed,
        out_specs=(
            P(("shard", "ctx"), "tp"),
            P(("shard", "ctx"), "tp"),
            P("shard", None, "tp"),
            P(None, "tp"),
            P("shard", "tp"),
            P("tp"),
            P("tp"),
            P("shard", "tp"),
            P("shard", "tp"),
            P("shard", "tp"),
        ),
        check_vma=False,
    )
```

```python
import jax
import jax.numpy as jnp
from jax import lax
from jax.experimental import pallas as pl
from jax.experimental.pallas import tpu as pltpu
from jax.sharding import PartitionSpec as P

EPS = 1e-05
LOW = jnp.bfloat16
WIDE = jnp.float32
CHUNKS = 4


def shifted(value, axis, steps):
    count = lax.axis_size(axis)
    leading, last = (max(0, -steps), min(count, count - steps))
    return lax.ppermute(value, axis, [(source, source + steps) for source in range(leading, last)])


def swapped(value, axis, step):
    count = lax.axis_size(axis)
    return lax.ppermute(value, axis, [(source, source ^ step) for source in range(count)])


def matmul(left, right):
    return jnp.dot(left, right, preferred_element_type=WIDE)


def contract_rows(left, right):
    return lax.dot_general(left, right, (((0,), (0,)), ((), ())), preferred_element_type=WIDE)


def contract_cols(left, right):
    return lax.dot_general(left, right, (((1,), (1,)), ((), ())), preferred_element_type=WIDE)


def added(terms):
    return sum(term.astype(WIDE) for term in terms)


def norm_back(grad_out, normed, scale_row, gain):
    scaled = grad_out * gain
    return scale_row * (scaled - normed * jnp.mean(scaled * normed, axis=1, keepdims=True))


def butterfly_sum(value, axis):
    step = 1
    while step < lax.axis_size(axis):
        value = value + swapped(value, axis, step)
        step *= 2
    return value


def sum_line(piece, rank):
    from_end = lax.ppermute(piece, "ctx", [(0, 1), (3, 2)])
    half = (piece.astype(WIDE) + from_end.astype(WIDE)).astype(LOW)
    from_middle = lax.ppermute(half, "ctx", [(1, 2), (2, 1)])
    total = (half.astype(WIDE) + from_middle.astype(WIDE)).astype(LOW)
    handed = lax.ppermute(total, "ctx", [(1, 0), (2, 3)])
    inner = jnp.logical_or(rank == 1, rank == 2)
    return jnp.where(inner, total, handed)


PIECE = 256
AHEAD = 4
SLOTS = 4
TOTALS = 2
MESH = pl.DeviceIdType.MESH


def front_kernel(
    x_in, cot_in, sending, place, own_gains, masks, taps,
    in_w, out_w, gate_w, up_w, down_w,
    in_peer, out_peer, gate_peer, up_peer, outer_land, middle_land, rights_peer,
    x_out, h_one_out, mixer_out, act_out, grads, dealt, dealt_out, small_sums,
    x_blocks, cot_blocks, gains, gain_sums, small, small_got, x_got, cot_got, x_full, h_one, cot_full, cot_peer, h_two, h_two_peer, proj, mixed, gated, mixer, conv_v,
    out_v, rim, extended, away, pair, pair_got, both_got, dh_got,
    da_got, in_v, gu_v, down_v, dh_sum, ffn_v, right_v, outer_v, middle_v, held, totals, d_ext, edge_v, rim_back,
    send, recv, local, in_send, outer_recv, middle_recv, out_send, out_recv, own_done,
):
    shard = lax.axis_index("shard")
    ctx = lax.axis_index("ctx")
    tp = lax.axis_index("tp")
    core, outer = tp % 2, tp // 2
    core_mate = tp + 1 - 2 * core
    outer_mate = lax.rem(tp + 2, 4)
    ctx_mate = ctx + 1 - 2 * (ctx % 2)
    tokens, width = x_full.shape
    part = width // 4
    half = width // 2
    blocks, block_rows = x_blocks.shape[0], x_blocks.shape[1]
    rows = out_w.shape[0]
    own_rows = pl.ds(pl.multiple_of((ctx % 2) * (rows // 2), rows // 2), rows // 2)
    other_rows = pl.ds(pl.multiple_of((1 - ctx % 2) * (rows // 2), rows // 2), rows // 2)
    hidden = gate_w.shape[1]
    chunk = hidden // CHUNKS

    barrier = pltpu.get_barrier_semaphore()
    mates = [{"shard": 1 - shard}, {"tp": core_mate}, {"tp": outer_mate}]
    mates += [{"ctx": lax.rem(ctx + step, blocks)} for step in range(1, blocks)]
    for mate in mates:
        pl.semaphore_signal(barrier, inc=1, device_id=mate, device_id_type=MESH)
    pl.semaphore_wait(barrier, len(mates))

    names = {}

    def remote(name, src, dst, mate):
        place_of = names.setdefault(name, len(names))
        return pltpu.make_async_remote_copy(
            src_ref=src, dst_ref=dst, send_sem=send.at[place_of], recv_sem=recv.at[place_of],
            device_id=mate, device_id_type=MESH,
        )

    def columns(start, size):
        return pl.ds(pl.multiple_of(start * size, size), size)

    own_part = columns(tp, part)
    own_half, peer_half = columns(shard, half), columns(1 - shard, half)

    def deal(name, source, target, step):
        to, origin = lax.rem(ctx + step, blocks), lax.rem(ctx + blocks - step, blocks)
        out = remote(name + str(step), source.at[to], target.at[ctx], {"ctx": to})
        into = remote(name + str(step), source.at[to], target.at[origin], {"ctx": to})
        return out, into

    def gather(name, full):
        mate = columns(outer_mate, part)
        return (
            remote(name + "outer", full.at[:, own_part], full.at[:, own_part], {"tp": outer_mate}),
            remote(name + "core", full.at[:, own_part], full.at[:, own_part], {"tp": core_mate}),
            remote(name + "more", full.at[:, mate], full.at[:, mate], {"tp": core_mate}),
        )

    pieces = {}
    for index, name in enumerate("bvc"):
        column = (0, 2, 1)[index]
        pieces[name] = (in_w.at[column], in_peer.at[column])
    pieces["o"] = (out_w, out_peer)
    for index in range(CHUNKS):
        strip = pl.ds(index * chunk, chunk)
        pieces["g%d" % index] = (gate_w.at[:, strip], gate_peer.at[:, strip])
        pieces["u%d" % index] = (up_w.at[:, strip], up_peer.at[:, strip])

    direct = ["g2", "u2", "u3"]

    def over_shard(name):
        source, target = pieces[name]
        if name in direct:
            return remote(name + "x", source, target, {"shard": 1 - shard})
        return remote(name + "x", source.at[own_rows], target.at[own_rows], {"shard": 1 - shard})

    def over_ctx(name):
        target = pieces[name][1]
        return remote(name + "z", target.at[own_rows], target.at[own_rows], {"ctx": ctx_mate})

    def pump(name):
        over_shard(name).wait_recv()
        over_ctx(name).start()

    def load(index, source, target):
        return pltpu.make_async_copy(source, target, local.at[index])

    def own_weights(index):
        strip = pl.ds(index * chunk, chunk)
        room = gu_v if index % 2 == 0 else in_v
        base = 13 + 4 * (index % 2)
        return [
            load(base, gate_w.at[:, strip], room.at[0, 0]),
            load(base + 1, up_w.at[:, strip], room.at[0, 1]),
        ]

    def peer_weights(index):
        strip = pl.ds(index * chunk, chunk)
        room = gu_v if index % 2 == 0 else in_v
        base = 15 + 4 * (index % 2)
        return [
            load(base, gate_peer.at[:, strip], room.at[1, 0]),
            load(base + 1, up_peer.at[:, strip], room.at[1, 1]),
        ]

    def to_blocks(source, target):
        for to in range(blocks):
            total = sending[to, 0] * source[0:block_rows].astype(WIDE)
            for slot in range(1, blocks):
                lines = pl.ds(slot * block_rows, block_rows)
                total = total + sending[to, slot] * source[lines].astype(WIDE)
            target[to] = total.astype(LOW)

    for name in ("b", "v", "c", "o", "g0", "u0"):
        over_shard(name).start()
    gains[:, own_part] = own_gains[...]
    gain_outer, gain_core, gain_more = gather("gg", gains)
    gain_outer.start()
    gain_core.start()
    to_blocks(x_in, x_blocks)
    x_deals = [deal("x", x_blocks, x_got, step) for step in range(1, blocks)]
    cot_deals = [deal("cot", cot_blocks, cot_got, step) for step in range(1, blocks)]
    for out, _ in x_deals:
        out.start()
    own_loads = [load(index, in_w.at[index], in_v.at[0, index]) for index in range(3)]
    own_loads.append(load(3, out_w, out_v.at[0]))
    own_loads.append(load(4, down_w, down_v))
    for copy in own_loads + own_weights(0):
        copy.start()
    to_blocks(cot_in, cot_blocks)

    def packed(source, got, deals, full):
        got[ctx] = source[ctx]
        for _, into in deals:
            into.wait_recv()
        for index in range(blocks):
            total = place[index, 0] * got[0].astype(WIDE)
            for other in range(1, blocks):
                total = total + place[index, other] * got[other].astype(WIDE)
            full[index * block_rows : (index + 1) * block_rows, own_part] = total.astype(LOW)

    pump("b")
    packed(x_blocks, x_got, x_deals, x_full)
    x_outer, x_core, x_more = gather("xg", x_full)
    x_outer.start()
    x_core.start()
    for out, _ in cot_deals:
        out.start()
    pump("v")
    x_outer.wait_recv()
    x_more.start()
    packed(cot_blocks, cot_got, cot_deals, cot_full)
    cot_outer, cot_core, cot_more = gather("cg", cot_full)
    cot_outer.start()
    cot_core.start()
    gain_outer.wait_recv()
    gain_more.start()
    x_core.wait_recv()
    x_more.wait_recv()
    gain_core.wait_recv()
    gain_more.wait_recv()

    x_store = load(5, x_full, x_out)
    x_store.start()
    step = min(64, tokens)

    @pl.loop(0, tokens // step)
    def _(index):
        lines = pl.ds(pl.multiple_of(index * step, step), step)
        value = x_full[lines].astype(WIDE)
        scale = lax.rsqrt(jnp.mean(value * value, axis=1, keepdims=True) + EPS)
        h_one[lines] = (value * scale * gains[0:1]).astype(LOW)

    h_one_store = load(6, h_one, h_one_out)
    h_one_store.start()
    pump("c")

    class Columns:
        def __init__(self, name, full, got):
            size = half // 4
            source = pl.ds(pl.multiple_of((1 - shard) * half + tp * size, size), size)
            own, mate = columns(tp, size), columns(outer_mate, size)
            self.shard = remote(name + "x", full.at[:, source], got.at[:, own], {"shard": 1 - shard})
            self.outer = remote(name + "y", got.at[:, own], got.at[:, own], {"tp": outer_mate})
            self.core = remote(name + "c", got.at[:, own], got.at[:, own], {"tp": core_mate})
            self.more = remote(name + "m", got.at[:, mate], got.at[:, mate], {"tp": core_mate})

        def start(self):
            self.shard.start()

        def spread(self):
            self.shard.wait_recv()
            self.outer.start()
            self.core.start()

        def done(self):
            self.outer.wait_recv()
            self.more.start()
            self.core.wait()
            self.more.wait()
            self.outer.wait_send()

        def wait_send(self):
            self.shard.wait_send()

    cot_strip, cot_target = columns(2 * (1 - shard) + core, part), columns(core, part)
    cot_first = remote("ccx", cot_full.at[:, cot_strip], cot_peer.at[:, cot_target], {"shard": 1 - shard})
    cot_second = remote("ccc", cot_peer.at[:, cot_target], cot_peer.at[:, cot_target], {"tp": core_mate})
    tile = min(256, tokens)

    def over_tiles(body):
        @pl.loop(0, tokens // tile)
        def _(index):
            body(pl.ds(pl.multiple_of(index * tile, tile), tile))

    def project(column, name):
        target = load(column, in_peer.at[column], in_v.at[1, column])
        own_loads[column].wait()
        over_ctx(name).wait_recv()
        target.start()
        target.wait()

        def body(lines):
            proj[column, lines] = jnp.dot(
                h_one[lines, own_half], in_v[0, column], preferred_element_type=WIDE
            ) + jnp.dot(h_one[lines, peer_half], in_v[1, column], preferred_element_type=WIDE)

        over_tiles(body)

    project(0, "b")
    project(2, "v")
    edge = 16
    rim_copy = remote(
        "rim", mixed.at[pl.ds(tokens - edge, edge)], rim, {"ctx": lax.rem(ctx + 1, blocks)}
    )

    def mix(lines):
        value = (proj[0, lines] * proj[2, lines]).astype(LOW)
        mixed[lines] = value
        extended[pl.ds(lines.start + 8, tile)] = value.astype(WIDE)

    over_tiles(mix)

    @pl.when(ctx < blocks - 1)
    def _():
        rim_copy.start()

    pump("o")
    cot_outer.wait_recv()
    cot_more.start()
    project(1, "c")

    @pl.when(ctx > 0)
    def _():
        rim_copy.wait_recv()
        extended[0:8] = rim[8:16].astype(WIDE)

    @pl.when(ctx == 0)
    def _():
        extended[0:8] = jnp.zeros((8, part), WIDE)

    for start in range(0, tokens, tile):
        lines = pl.ds(start, tile)
        value = taps[0:1] * extended[pl.ds(start + 8, tile)]
        value = value + taps[1:2] * (extended[pl.ds(start + 7, tile)] * masks[lines, 0:1])
        value = value + taps[2:3] * (extended[pl.ds(start + 6, tile)] * masks[lines, 1:2])
        conv_v[lines] = value
        gated[lines] = (proj[1, lines] * value).astype(LOW)

    pump("g0")
    cot_core.wait_recv()
    cot_more.wait_recv()
    cot_first.start()
    over_shard("g1").start()
    out_load = load(3, out_peer, out_v.at[1])
    own_loads[3].wait()
    over_ctx("o").wait_recv()
    out_load.start()
    out_load.wait()

    def to_half(lines, which):
        return lax.dot_general(
            gated[lines], out_v[which], (((1,), (1,)), ((), ())), preferred_element_type=WIDE
        )

    stages = [pl.ds(start, tile) for start in range(0, tokens, tile)]
    hops = []
    for index, lines in enumerate(stages):
        first = remote("ma%d" % index, away.at[lines], pair_got.at[lines], {"tp": core_mate})
        second = remote("mb%d" % index, pair.at[lines], both_got.at[lines], {"tp": outer_mate})
        third = remote("mc%d" % index, mixer.at[core, lines], mixer.at[core, lines], {"tp": core_mate})
        hops.append((first, second, third))
        away[lines] = to_half(lines, 1 - core).astype(LOW)
        first.start()
    for index, lines in enumerate(stages):
        value = to_half(lines, core)
        hops[index][0].wait_recv()
        pair[lines] = (value + pair_got[lines].astype(WIDE)).astype(LOW)
        hops[index][1].start()

    da_send, da_own = h_one, x_full
    pump("u0")
    cot_first.wait_recv()
    cot_second.start()
    cot_second.wait()
    own_loads[4].wait()
    h_one_store.wait()

    def da_copy(index):
        strip = pl.ds(index * chunk, chunk)
        return remote("da%d" % index, da_send.at[:, strip], da_got.at[:, strip], {"shard": 1 - shard})

    for index in range(CHUNKS):
        strip = pl.ds(index * chunk, chunk)

        def send_part(lines):
            da_send[lines, strip] = jnp.dot(
                cot_peer[lines], down_v[:, strip], preferred_element_type=WIDE
            ).astype(LOW)

        over_tiles(send_part)
        if index == 0:
            da_copy(0).start()
            over_shard("u1").start()

    def act_store(index):
        return load(21 + index % 2, ffn_v.at[index % 2, 0], act_out.at[:, pl.ds(index * chunk, chunk)])

    def right_copy(index, kind):
        strip = pl.ds(kind * hidden + index * chunk, chunk)
        return remote(
            "r%d%d" % (index, kind), ffn_v.at[index % 2, kind], rights_peer.at[:, strip], {"shard": 1 - shard}
        )

    def right_load(index, kind):
        strip = pl.ds(kind * hidden + index * chunk, chunk)
        return load(23 + kind, rights_peer.at[:, strip], right_v.at[kind])

    def ready(index):
        for kind in "gu":
            if "%s%d" % (kind, index) not in direct:
                over_ctx("%s%d" % (kind, index)).wait_recv()
        for copy in peer_weights(index):
            copy.start()

    def feed(index, lines, kinds=(0, 1, 2)):
        room = gu_v if index % 2 == 0 else in_v
        slot = index % 2
        strip = pl.ds(index * chunk, chunk)

        def pre(kind):
            return jnp.dot(
                h_two[lines, own_half], room[0, kind], preferred_element_type=WIDE
            ) + jnp.dot(h_two[lines, peer_half], room[1, kind], preferred_element_type=WIDE)

        gate_pre, up_pre = pre(0), pre(1)
        sigmoid = jax.nn.sigmoid(gate_pre)
        silu = gate_pre * sigmoid
        if 0 in kinds:
            ffn_v[slot, 0, lines] = (silu * up_pre).astype(LOW)
        if 1 not in kinds:
            return
        d_act = da_own[lines, strip].astype(WIDE) + da_got[lines, strip].astype(WIDE)
        ffn_v[slot, 1, lines] = (
            d_act * up_pre * sigmoid * (1.0 + gate_pre * (1.0 - sigmoid))
        ).astype(LOW)
        ffn_v[slot, 2, lines] = (d_act * silu).astype(LOW)

    pump("g1")
    ready(0)
    tiles = [pl.ds(start, tile) for start in range(0, tokens, tile)]
    for index, lines in enumerate(stages):
        hops[index][1].wait_recv()
        mixer[core, lines] = (pair[lines].astype(WIDE) + both_got[lines].astype(WIDE)).astype(LOW)
        hops[index][2].start()
        hops[index][2].wait_recv()

        @pl.loop(0, tile // step)
        def _(turn, start=index * tile):
            lines = pl.ds(pl.multiple_of(start + turn * step, step), step)
            own = x_full[lines, own_half].astype(WIDE) + mixer[0, lines].astype(WIDE)
            other = x_full[lines, peer_half].astype(WIDE) + mixer[1, lines].astype(WIDE)
            total = jnp.sum(own * own, axis=1, keepdims=True) + jnp.sum(other * other, axis=1, keepdims=True)
            scale = lax.rsqrt(total / width + EPS)
            h_two[lines, own_half] = (own * scale * gains[1:2, own_half]).astype(LOW)
            h_two[lines, peer_half] = (other * scale * gains[1:2, peer_half]).astype(LOW)

        if index == 0:
            for copy in own_weights(0) + peer_weights(0):
                copy.wait()
        feed(0, lines, (0,))
    right_copy(0, 0).start()
    act_store(0).start()
    mixer_store = load(12, mixer, mixer_out)
    mixer_store.start()

    h_two_columns = Columns("hc", h_two, h_two_peer)
    h_two_columns.start()
    x_store.wait()
    for copy in (x_outer, x_core, x_more):
        copy.wait_send()

    def own_part_of(lines):
        for index in range(CHUNKS):
            strip = pl.ds(index * chunk, chunk)
            da_own[lines, strip] = jnp.dot(
                cot_full[lines, own_half], down_v[:, strip], preferred_element_type=WIDE
            ).astype(LOW)

    over_tiles(own_part_of)

    def turned(place_of, source, start, first):
        for row in range(0, half, 256):
            for line in range(0, tokens, 256):
                block = source[pl.ds(line, 256), pl.ds(pl.multiple_of(start + row, 256), 256)]
                down_v[pl.ds(row, 256), pl.ds(place_of * half + first + line, 256)] = block.T

    turned(0, cot_full, shard * half, 0)
    turned(0, cot_peer, 0, tokens)
    turned(1, h_two, shard * half, 0)

    def back(index, lines):
        room = gu_v if index % 2 == 0 else in_v
        slot = index % 2
        for place_of in range(2):
            term = lax.dot_general(
                ffn_v[slot, 1, lines], room[place_of, 0],
                (((1,), (1,)), ((), ())), preferred_element_type=WIDE,
            ) + lax.dot_general(
                ffn_v[slot, 2, lines], room[place_of, 1],
                (((1,), (1,)), ((), ())), preferred_element_type=WIDE,
            )
            if index > 0:
                term = term + dh_sum[place_of, lines]
            dh_sum[place_of, lines] = term

    def feed_start(index):
        da_copy(index).wait_recv()
        for copy in own_weights(index) + peer_weights(index):
            copy.wait()
        if index > 1:
            act_store(index - 2).wait()
            for kind in range(3):
                right_copy(index - 2, kind).wait_send()

    middle = jnp.logical_or(ctx == 1, ctx == 2)
    end = jnp.logical_not(middle)
    inward = jnp.where(ctx < 2, ctx + 1, ctx - 1)
    outward = jnp.where(ctx == 1, 0, 3)
    per_kind = chunk // PIECE
    per_chunk = 3 * per_kind
    ffn_pieces = CHUNKS * per_chunk
    pieces_in_all = ffn_pieces + 4 * part // PIECE
    line_rows = min(256, rows)

    def grad_columns(piece):
        index, turn = piece // per_chunk, piece % per_chunk
        kind, sub = turn // per_kind, turn % per_kind
        start = jnp.where(
            piece < ffn_pieces, kind * hidden + index * chunk + sub * PIECE, piece * PIECE
        )
        return pl.ds(pl.multiple_of(start, PIECE), PIECE)

    def inward_copy(piece, land, sems):
        return pltpu.make_async_remote_copy(
            src_ref=held.at[piece % SLOTS], dst_ref=land.at[piece], send_sem=in_send.at[piece],
            recv_sem=sems.at[piece], device_id={"ctx": inward}, device_id_type=MESH,
        )

    def outward_copy(piece):
        return pltpu.make_async_remote_copy(
            src_ref=totals.at[piece % TOTALS], dst_ref=grads.at[:, grad_columns(piece)], send_sem=out_send.at[piece],
            recv_sem=out_recv.at[piece], device_id={"ctx": outward}, device_id_type=MESH,
        )

    def total_store(piece):
        return pltpu.make_async_copy(totals.at[piece % TOTALS], grads.at[:, grad_columns(piece)], own_done.at[piece])

    def stage_in(piece, land, room):
        copy = pltpu.make_async_copy(land.at[piece], room, local.at[26])
        copy.start()
        copy.wait()

    def finish(piece):
        inward_copy(piece, middle_land, middle_recv).wait_recv()
        stage_in(piece, middle_land, middle_v)

        @pl.when(piece >= TOTALS)
        def _():
            outward_copy(piece - TOTALS).wait_send()
            total_store(piece - TOTALS).wait()

        @pl.loop(0, rows // line_rows)
        def _(start):
            lines = pl.ds(pl.multiple_of(start * line_rows, line_rows), line_rows)
            total = held[piece % SLOTS, lines].astype(WIDE) + middle_v[lines].astype(WIDE)
            totals[piece % TOTALS, lines] = total.astype(LOW)

        outward_copy(piece).start()
        total_store(piece).start()

    def grad_piece(piece):
        after = piece >= ffn_pieces
        turn = jnp.where(after, jnp.maximum(piece - ffn_pieces - per_kind, 0), piece % per_chunk)
        kind, sub = turn // per_kind, piece % per_kind
        slot = jnp.where(after, jnp.where(piece < ffn_pieces + per_kind, 1, 0), piece // per_chunk % 2)
        strip = pl.ds(pl.multiple_of(sub * PIECE, PIECE), PIECE)
        left_first = jnp.where(after, piece < ffn_pieces + per_kind, kind == 0)
        left = jnp.where(left_first, 0, half)

        @pl.when(piece >= SLOTS)
        def _():
            inward_copy(piece - SLOTS, outer_land, outer_recv).wait_send()

        def product(start):
            lines = pl.ds(pl.multiple_of(start * line_rows, line_rows), line_rows)
            own = jnp.dot(
                down_v[lines, pl.ds(pl.multiple_of(left, tokens), tokens)],
                ffn_v[slot, kind, :, strip],
                preferred_element_type=WIDE,
            )
            other = jnp.dot(
                down_v[lines, pl.ds(pl.multiple_of(left + tokens, tokens), tokens)],
                right_v[kind, :, strip],
                preferred_element_type=WIDE,
            )
            return lines, own + other

        @pl.when(end)
        def _():
            @pl.loop(0, rows // line_rows)
            def _(start):
                lines, value = product(start)
                held[piece % SLOTS, lines] = value.astype(LOW)

            inward_copy(piece, outer_land, outer_recv).start()

        @pl.when(middle)
        def _():
            inward_copy(piece, outer_land, outer_recv).wait_recv()
            stage_in(piece, outer_land, outer_v)

            @pl.loop(0, rows // line_rows)
            def _(start):
                lines, value = product(start)
                held[piece % SLOTS, lines] = (value + outer_v[lines].astype(WIDE)).astype(LOW)

            inward_copy(piece, middle_land, middle_recv).start()

            @pl.when(piece >= 1)
            def _():
                finish(piece - 1)

    def got_right(index, kind):
        right_copy(index, kind).wait_recv()
        copy = right_load(index, kind)
        copy.start()
        copy.wait()

    dh_away = remote("dh1", away, pair_got, {"tp": core_mate})
    dh_pair = remote("dh2", pair, dh_got, {"tp": outer_mate})
    dh_last = remote("dh3", mixer.at[core], mixer.at[core], {"tp": core_mate})
    def whole_feed(index):
        feed_start(index)
        for lines in tiles:
            feed(index, lines)
        act_store(index).start()

    def whole_back(index):
        for lines in tiles:
            back(index, lines)
        if index + 1 < CHUNKS:
            for copy in own_weights(index + 1):
                copy.start()

    da_copy(0).wait_recv()
    for lines in tiles:
        feed(0, lines, (1, 2))
    right_copy(0, 1).start()
    right_copy(0, 2).start()
    da_copy(1).start()
    whole_back(0)
    pump("u1")

    def event_start():
        got_right(0, 0)

    def event_columns():
        h_two_columns.done()
        turned(1, h_two_peer, 0, tokens)
        got_right(0, 1)

    def event_first():
        got_right(0, 2)
        ready(1)
        whole_feed(1)
        for kind in range(3):
            right_copy(1, kind).start()
        for name in ("g2", "u2"):
            over_shard(name).start()
        da_copy(2).start()
        over_shard("g3").start()

    def event_second():
        over_shard("g2").wait_recv()
        over_shard("u2").wait_recv()
        ready(2)
        whole_feed(2)
        right_copy(2, 0).start()
        right_copy(2, 1).start()
        over_shard("u3").start()
        right_copy(2, 2).start()
        da_copy(3).start()
        got_right(1, 2)
        pump("g3")

    back_blocks, d_resid, resid_own = cot_got, dh_sum.at[1, :, pl.ds(0, part)], dh_sum.at[1, :, pl.ds(part, part)]
    h_one_columns = Columns("ic", h_one_out, cot_peer)
    dr_columns = Columns("dc", h_two, h_two_peer)
    mixer_rights = 3 * hidden

    def mixer_right(kind):
        source = gated if kind == 0 else ffn_v.at[0, kind - 1]
        strip = pl.ds(mixer_rights + kind * part, part)
        return remote("m%d" % kind, source, rights_peer.at[:, strip], {"shard": 1 - shard})

    def got_mixer_right(kind):
        mixer_right(kind).wait_recv()
        room = right_v.at[max(kind - 1, 0)]
        copy = load(23, rights_peer.at[:, pl.ds(mixer_rights + kind * part, part)], room)
        copy.start()
        copy.wait()

    x_reload = load(5, x_out, x_full)
    mixer_reloads = [
        load(6, mixer_out.at[0], h_one.at[:, own_half]), load(7, mixer_out.at[1], h_one.at[:, peer_half])
    ]
    h_one_reload = load(8, h_one_out.at[:, own_half], dh_got)
    in_reloads = [load(13 + column, in_w.at[column], in_v.at[0, column]) for column in range(3)]
    in_reloads += [load(16 + column, in_peer.at[column], in_v.at[1, column]) for column in range(3)]
    fine = min(32, tokens)

    def reload():
        for index in range(CHUNKS):
            da_copy(index).wait_send()
        act_store(CHUNKS - 1).wait()
        act_store(CHUNKS - 2).wait()
        for copy in [x_reload] + mixer_reloads + in_reloads + down_loads + [act_own_load]:
            copy.start()

    def resid_back():
        dh_last.wait_recv()
        h_one_reload.start()
        for copy in [x_reload] + mixer_reloads:
            copy.wait()
        h_two_columns.wait_send()
        gain_sums[...] = jnp.zeros((2, width), WIDE)

        @pl.loop(0, tokens // fine)
        def _(index):
            lines = pl.ds(pl.multiple_of(index * fine, fine), fine)

            def halves(columns_of, which):
                resid = x_full[lines, columns_of].astype(WIDE) + h_one[lines, columns_of].astype(WIDE)
                return resid, mixer[which, lines].astype(WIDE)

            own, own_grad = halves(own_half, 0)
            other, other_grad = halves(peer_half, 1)
            total = jnp.sum(own * own, axis=1, keepdims=True) + jnp.sum(other * other, axis=1, keepdims=True)
            scale = lax.rsqrt(total / width + EPS)
            own, other = own * scale, other * scale
            own_scaled, other_scaled = own_grad * gains[1:2, own_half], other_grad * gains[1:2, peer_half]
            mean = (
                jnp.sum(own_scaled * own, axis=1, keepdims=True)
                + jnp.sum(other_scaled * other, axis=1, keepdims=True)
            ) / width
            h_two[lines, own_half] = (
                cot_full[lines, own_half].astype(WIDE) + scale * (own_scaled - own * mean)
            ).astype(LOW)
            h_two[lines, peer_half] = (
                cot_full[lines, peer_half].astype(WIDE) + scale * (other_scaled - other * mean)
            ).astype(LOW)
            gain_sums[1:2, own_half] += jnp.sum(own_grad * own, axis=0, keepdims=True)
            gain_sums[1:2, peer_half] += jnp.sum(other_grad * other, axis=0, keepdims=True)
            resid = x_full[lines, own_part].astype(WIDE) + h_one[lines, own_part].astype(WIDE)
            resid_own[lines] = resid
            which = jnp.where(outer == shard, 0, 1)
            scaled = mixer[which, lines, columns(core, part)].astype(WIDE) * gains[1:2, own_part]
            d_resid[lines] = cot_full[lines, own_part].astype(WIDE) + scale * (
                scaled - resid * scale * mean
            )

        dr_columns.start()

    rim_out = remote(
        "rim_back", edge_v, rim_back, {"ctx": lax.rem(ctx + blocks - 1, blocks)}
    )

    def conv_back():
        for kind in range(3):
            right_copy(CHUNKS - 2, kind).wait_send()

        def body(lines):
            d_gated = jnp.dot(
                h_two[lines, own_half], out_v[0], preferred_element_type=WIDE
            ) + jnp.dot(h_two[lines, peer_half], out_v[1], preferred_element_type=WIDE)
            d_ext[lines] = (d_gated * proj[1, lines]).astype(LOW).astype(WIDE)
            ffn_v[0, 1, lines] = (d_gated * conv_v[lines]).astype(LOW)

        for lines in tiles:
            body(lines)
        edge_v[...] = d_ext[0:16].astype(LOW)

        @pl.when(ctx > 0)
        def _():
            rim_out.start()

        turned(0, h_two, shard * half, 0)

    def out_ready():
        right_copy(CHUNKS - 1, 0).wait_send()

        def body(lines):
            ffn_v[1, 0, lines] = gated[lines]

        over_tiles(body)
        dr_columns.done()
        turned(0, h_two_peer, 0, tokens)
        got_mixer_right(0)

    def proj_back():
        @pl.when(ctx < blocks - 1)
        def _():
            rim_out.wait_recv()
            d_ext[tokens : tokens + 8] = rim_back[0:8].astype(WIDE)

        @pl.when(ctx == blocks - 1)
        def _():
            d_ext[tokens : tokens + 8] = jnp.zeros((8, part), WIDE)

        sums = [jnp.zeros((1, part), WIDE) for _ in range(3)]
        size = 128
        for start in range(0, tokens, size):
            lines = pl.ds(start, size)
            own = d_ext[lines]
            d_mixed = taps[0:1] * own
            d_mixed = d_mixed + taps[1:2] * (d_ext[pl.ds(start + 1, size)] * masks[lines, 2:3])
            d_mixed = d_mixed + taps[2:3] * (d_ext[pl.ds(start + 2, size)] * masks[lines, 3:4])
            ffn_v[0, 0, lines] = (d_mixed * proj[2, lines]).astype(LOW)
            ffn_v[0, 2, lines] = (d_mixed * proj[0, lines]).astype(LOW)
            for tap in range(3):
                value = own * extended[pl.ds(start + 8 - tap, size)]
                if tap > 0:
                    value = value * masks[lines, tap - 1 : tap]
                sums[tap] = sums[tap] + jnp.sum(value, axis=0, keepdims=True)
        small[...] = jnp.zeros(small.shape, WIDE)
        for tap in range(3):
            small[tap : tap + 1] = sums[tap]
        ffn_peer()
        mixer_right(1).start()
        ffn_first[0].start()
        mixer_right(2).start()
        ffn_first[1].start()
        mixer_right(3).start()

    def in_ready():
        h_one_reload.wait()
        turned(1, dh_got, 0, 0)
        h_one_columns.done()
        turned(1, cot_peer, 0, tokens)
        got_mixer_right(1)

    back_away = remote("bh1", away, pair_got, {"tp": core_mate})
    back_pair = remote("bh2", pair, both_got, {"tp": outer_mate})
    back_last = remote("bh3", mixer.at[core], mixer.at[core], {"tp": core_mate})

    def to_inputs(lines, which):
        total = None
        for column in range(3):
            term = lax.dot_general(
                ffn_v[0, column, lines], in_v[which, column],
                (((1,), (1,)), ((), ())), preferred_element_type=WIDE,
            )
            total = term if total is None else total + term
        return total

    def back_one_hop():
        for copy in (dh_away, dh_pair, dh_last):
            copy.wait_send()
        for copy in in_reloads:
            copy.wait()

        def body(lines):
            away[lines] = to_inputs(lines, 1 - core).astype(LOW)

        over_tiles(body)
        back_away.start()

        def rest(lines):
            dh_sum[0, lines] = to_inputs(lines, core)

        over_tiles(rest)

    def back_two_hops():
        back_away.wait_recv()

        def body(lines):
            pair[lines] = (dh_sum[0, lines] + pair_got[lines].astype(WIDE)).astype(LOW)

        over_tiles(body)
        back_pair.start()

    def back_three_hops():
        back_pair.wait_recv()

        def body(lines):
            mixer[core, lines] = (pair[lines].astype(WIDE) + both_got[lines].astype(WIDE)).astype(LOW)

        over_tiles(body)
        back_last.start()

    def give_back(name, block, target, step):
        to, origin = lax.rem(ctx + step, blocks), lax.rem(ctx + blocks - step, blocks)
        name = name + str(step)
        return (
            remote(name, block(to), target.at[ctx], {"ctx": to}),
            remote(name, block(to), target.at[origin], {"ctx": to}),
        )

    def out_block(to):
        return gated.at[pl.ds(pl.multiple_of(to * block_rows, block_rows), block_rows)]

    given = [give_back("give", lambda to: back_blocks.at[to], dealt, step) for step in range(1, blocks)]
    given_out = [give_back("out", out_block, dealt_out, step) for step in range(1, blocks)]
    kept = load(9, back_blocks.at[ctx], dealt.at[ctx])
    kept_out = load(10, out_block(ctx), dealt_out.at[ctx])

    down_loads = [
        load(index, down_w.at[:, pl.ds(index * chunk, chunk)], gu_v.at[index // 2, index % 2])
        for index in range(CHUNKS)
    ]
    act_own_load = load(21, act_out, da_got)
    act_peer_load = load(22, rights_peer.at[:, pl.ds(0, hidden)], da_got)
    ffn_first = [
        remote(
            "fx%d" % index, cot_full.at[:, pl.ds(half + index * part, part)],
            h_one.at[:, pl.ds(index * part, part)], {"shard": 1 - shard},
        )
        for index in range(2)
    ]
    ffn_core = [
        remote("fc0", cot_full.at[:, columns(1 - core, part)], out_v.at[0, pl.ds(0, tokens)], {"tp": core_mate}),
        remote("fc1", h_one.at[:, columns(1 - core, part)], out_v.at[1, pl.ds(0, tokens)], {"tp": core_mate}),
    ]
    kept_which = jnp.where(outer == shard, 0, 1)

    def ffn_pair(which):
        return pl.ds(pl.multiple_of(half + which * part, part), part)

    ffn_outer = [
        remote(
            "fy%d" % index,
            h_one.at[pl.ds(index * block_rows, block_rows), ffn_pair(1 - kept_which)],
            x_got.at[index],
            {"tp": outer_mate},
        )
        for index in range(blocks)
    ]

    def ffn_part(start):
        def body(lines):
            total = None
            for index in range(CHUNKS):
                term = lax.dot_general(
                    da_got[lines, pl.ds(index * chunk, chunk)], gu_v[index // 2, index % 2],
                    (((1,), (1,)), ((), ())), preferred_element_type=WIDE,
                )
                total = term if total is None else total + term
            cot_full[lines, pl.ds(start, half)] = total.astype(LOW)

        over_tiles(body)

    def ffn_own():
        for copy in (cot_outer, cot_core, cot_more, cot_first):
            copy.wait_send()
        for copy in down_loads:
            copy.wait()
        act_own_load.wait()
        ffn_part(0)
        act_peer_load.start()

    def ffn_peer():
        act_peer_load.wait()
        ffn_part(half)

    def ffn_to_core():
        for copy in ffn_first:
            copy.wait_recv()
        for copy in ffn_core:
            copy.start()

    def ffn_to_outer():
        for copy in ffn_core:
            copy.wait_recv()

        def body(lines):
            own = columns(core, part)
            h_one[lines, ffn_pair(0)] = (
                cot_full[lines, own].astype(WIDE) + out_v[0, lines].astype(WIDE)
            ).astype(LOW)
            h_one[lines, ffn_pair(1)] = (
                h_one[lines, own].astype(WIDE) + out_v[1, lines].astype(WIDE)
            ).astype(LOW)

        over_tiles(body)
        for copy in ffn_outer:
            copy.start()

    def block_back():
        mixer_right(0).wait_send()
        for index, copy in enumerate(ffn_outer):
            copy.wait_recv()
            lines = pl.ds(index * block_rows, block_rows)
            resid_own[lines] = (
                resid_own[lines] + h_one[lines, ffn_pair(kept_which)].astype(WIDE) + x_got[index].astype(WIDE)
            )
        for to in range(blocks):
            total = place[0, to] * resid_own[0:block_rows]
            for index in range(1, blocks):
                total = total + place[index, to] * resid_own[index * block_rows : (index + 1) * block_rows]
            gated[to * block_rows : (to + 1) * block_rows] = total.astype(LOW)
        for out, _ in given_out:
            out.start()
        kept_out.start()

    def input_back():
        back_last.wait_recv()

        @pl.loop(0, tokens // fine)
        def _(index):
            lines = pl.ds(pl.multiple_of(index * fine, fine), fine)
            own, other = x_full[lines, own_half].astype(WIDE), x_full[lines, peer_half].astype(WIDE)
            own_grad, other_grad = mixer[0, lines].astype(WIDE), mixer[1, lines].astype(WIDE)
            total = jnp.sum(own * own, axis=1, keepdims=True) + jnp.sum(other * other, axis=1, keepdims=True)
            scale = lax.rsqrt(total / width + EPS)
            own, other = own * scale, other * scale
            mean = (
                jnp.sum(own_grad * gains[0:1, own_half] * own, axis=1, keepdims=True)
                + jnp.sum(other_grad * gains[0:1, peer_half] * other, axis=1, keepdims=True)
            ) / width
            gain_sums[0:1, own_half] += jnp.sum(own_grad * own, axis=0, keepdims=True)
            gain_sums[0:1, peer_half] += jnp.sum(other_grad * other, axis=0, keepdims=True)
            which = jnp.where(outer == shard, 0, 1)
            scaled = mixer[which, lines, columns(core, part)].astype(WIDE) * gains[0:1, own_part]
            normed = x_full[lines, own_part].astype(WIDE) * scale
            d_resid[lines] = d_resid[lines] + scale * (scaled - normed * mean)

        for to in range(blocks):
            total = place[0, to] * d_resid[0:block_rows]
            for index in range(1, blocks):
                total = total + place[index, to] * d_resid[index * block_rows : (index + 1) * block_rows]
            back_blocks[to] = total.astype(LOW)
        for out, _ in given:
            out.start()
        kept.start()

    def event_third():
        over_shard("u3").wait_recv()
        ready(3)
        whole_feed(3)
        for kind in range(3):
            right_copy(3, kind).start()
        h_one_columns.start()
        mixer_right(0).start()
        got_right(2, 2)

    def dh_one_hop():
        whole_back(3)
        mixer_store.wait()
        for trio in hops:
            for copy in trio:
                copy.wait_send()

        def body(lines):
            away[lines] = dh_sum[1 - core, lines].astype(LOW)

        over_tiles(body)
        dh_away.start()

    def dh_two_hops():
        dh_away.wait_recv()

        def body(lines):
            pair[lines] = (dh_sum[core, lines] + pair_got[lines].astype(WIDE)).astype(LOW)

        over_tiles(body)
        dh_pair.start()
        reload()
        got_right(3, 0)

    def dh_three_hops():
        dh_pair.wait_recv()

        def body(lines):
            mixer[core, lines] = (pair[lines].astype(WIDE) + dh_got[lines].astype(WIDE)).astype(LOW)

        over_tiles(body)
        dh_last.start()
        got_right(3, 1)

    def rights_and_conv():
        got_right(3, 2)
        conv_back()

    def spread_columns():
        h_one_columns.spread()
        dr_columns.spread()
        ffn_own()

    def back_and_right():
        got_mixer_right(2)
        back_two_hops()

    def outer_and_back():
        got_mixer_right(3)
        ffn_to_outer()
        back_three_hops()

    def ends_back():
        block_back()
        input_back()
        small[3:5] = gain_sums[:, own_part]
        small_shard.start()

    small_shard = remote("ss", small, small_got.at[blocks], {"shard": 1 - shard})

    def small_ctx(step):
        to, origin = lax.rem(ctx + step, blocks), lax.rem(ctx + blocks - step, blocks)
        return (
            remote("sc%d" % step, small_got.at[ctx], small_got.at[ctx], {"ctx": to}),
            remote("sc%d" % step, small_got.at[ctx], small_got.at[origin], {"ctx": to}),
        )

    small_steps = [small_ctx(step) for step in range(1, blocks)]

    events = {
        0: event_start,
        1: h_two_columns.spread,
        2: event_columns,
        4: event_first,
        5: lambda: whole_back(1),
        6: lambda: got_right(1, 0),
        8: lambda: got_right(1, 1),
        10: event_second,
        11: lambda: whole_back(2),
        12: lambda: got_right(2, 0),
        14: lambda: got_right(2, 1),
        16: event_third,
        17: dh_one_hop,
        18: dh_two_hops,
        20: dh_three_hops,
        21: resid_back,
        22: rights_and_conv,
        23: spread_columns,
        24: out_ready,
        25: proj_back,
        26: in_ready,
        27: back_one_hop,
        28: back_and_right,
        29: ffn_to_core,
        30: outer_and_back,
        31: ends_back,
    }

    @pl.loop(0, pieces_in_all)
    def _(piece):
        for turn, event in events.items():
            pl.when(piece == turn)(event)
        grad_piece(piece)

    small_shard.wait_recv()
    small_got[ctx] = small[...] + small_got[blocks]
    for out, _ in small_steps:
        out.start()

    @pl.when(middle)
    def _():
        finish(pieces_in_all - 1)

    for _, into in small_steps:
        into.wait_recv()
    total = small_got[0]
    for index in range(1, blocks):
        total = total + small_got[index]
    small_sums[...] = total

    for out, _ in x_deals + cot_deals:
        out.wait_send()
    for out, _ in small_steps:
        out.wait_send()
    for copy in (small_shard, gain_outer, gain_core, gain_more, h_one_columns, dr_columns, back_away, back_pair, back_last,
                 *ffn_first, *ffn_core, *ffn_outer):
        copy.wait_send()
    for name in pieces:
        over_shard(name).wait_send()
        if name not in direct:
            over_ctx(name).wait_send()
    for kind in (1, 2):
        right_copy(CHUNKS - 1, kind).wait_send()
    for kind in range(1, 4):
        mixer_right(kind).wait_send()
    kept.wait()
    kept_out.wait()
    for out, into in given + given_out:
        out.wait_send()
        into.wait_recv()

    @pl.when(ctx < blocks - 1)
    def _():
        rim_copy.wait_send()

    @pl.when(ctx > 0)
    def _():
        rim_out.wait_send()

    @pl.loop(0, pieces_in_all)
    def _(piece):
        @pl.when(piece >= pieces_in_all - SLOTS)
        def _():
            inward_copy(piece, outer_land, outer_recv).wait_send()

        @pl.when(jnp.logical_and(middle, piece >= pieces_in_all - TOTALS))
        def _():
            outward_copy(piece).wait_send()
            total_store(piece).wait()

        @pl.when(end)
        def _():
            outward_copy(piece).wait_recv()


FRONT_COPIES = 112


def front(x_in, cot_in, sending, place, own_gains, masks, taps, in_w, out_w, gate_w, up_w, down_w):
    tokens, part = x_in.shape
    blocks = place.shape[0]
    block_shape = (blocks, tokens // blocks, part)
    rows, hidden = gate_w.shape
    width = 4 * part
    half = width // 2
    chunk = hidden // CHUNKS
    pieces = (3 * hidden + width) // PIECE
    vmem = pl.BlockSpec(memory_space=pltpu.VMEM)
    hbm = pl.BlockSpec(memory_space=pl.ANY)
    shape = jax.ShapeDtypeStruct
    outs = [
        shape(in_w.shape, LOW),
        shape(out_w.shape, LOW),
        shape(gate_w.shape, LOW),
        shape(up_w.shape, LOW),
        shape((pieces, rows, PIECE), LOW),
        shape((pieces, rows, PIECE), LOW),
        shape((tokens, 3 * hidden + width + half), LOW),
        shape((tokens, width), LOW),
        shape((tokens, width), LOW),
        shape((2, tokens, half), LOW),
        shape((tokens, hidden), LOW),
        shape((rows, 3 * hidden + width), LOW),
        shape(block_shape, LOW),
        shape(block_shape, LOW),
        shape((8, part), WIDE),
    ]
    low, wide = (lambda *dims: pltpu.VMEM(dims, LOW)), (lambda *dims: pltpu.VMEM(dims, WIDE))
    dma = pltpu.SemaphoreType.DMA
    scratch = [
        low(*block_shape),
        low(*block_shape),
        wide(8, width),
        wide(2, width),
        wide(8, part),
        wide(blocks + 1, 8, part),
        low(*block_shape),
        low(*block_shape),
        low(tokens, width),
        low(tokens, width),
        low(tokens, width),
        low(tokens, half),
        low(tokens, width),
        low(tokens, half),
        wide(3, tokens, part),
        low(tokens, part),
        low(tokens, part),
        low(2, tokens, half),
        wide(tokens, part),
        low(2, rows, part),
        low(16, part),
        wide(tokens + 8, part),
        low(tokens, half),
        low(tokens, half),
        low(tokens, half),
        low(tokens, half),
        low(tokens, half),
        low(tokens, hidden),
        low(2, 3, rows, part),
        low(2, 2, rows, chunk),
        low(rows, hidden),
        wide(2, tokens, half),
        low(2, 3, tokens, chunk),
        low(3, tokens, chunk),
        low(rows, PIECE),
        low(rows, PIECE),
        low(SLOTS, rows, PIECE),
        low(TOTALS, rows, PIECE),
        wide(tokens + 8, part),
        low(16, part),
        low(16, part),
        dma((FRONT_COPIES,)),
        dma((FRONT_COPIES,)),
        dma((28,)),
    ] + [dma((pieces,)) for _ in range(6)]
    return pl.pallas_call(
        front_kernel,
        out_shape=outs,
        in_specs=[vmem, vmem] + [pl.BlockSpec(memory_space=pltpu.SMEM)] * 2 + [vmem] * 3
        + [hbm] * 5,
        out_specs=[hbm] * (len(outs) - 1) + [vmem],
        scratch_shapes=scratch,
        compiler_params=pltpu.CompilerParams(
            collective_id=2, has_side_effects=True, vmem_limit_bytes=63 * 1024 * 1024
        ),
        cost_estimate=pl.CostEstimate(
            flops=2 * tokens * width * hidden * 64, bytes_accessed=1 << 29, transcendentals=0
        ),
    )(x_in, cot_in, sending, place, own_gains, masks, taps, in_w, out_w, gate_w, up_w, down_w)


class Features:
    def __init__(self):
        rank = lax.axis_index("tp")
        self.rank = rank
        self.inner = rank % 2
        self.outer = rank // 2

    def gather(self, own):
        other = swapped(own, "tp", 2)
        first = self.outer == 0
        pair = jnp.stack([jnp.where(first, own, other), jnp.where(first, other, own)])
        more = swapped(pair, "tp", 1)
        even = self.inner == 0
        left, right = jnp.where(even, pair, more), jnp.where(even, more, pair)
        return jnp.concatenate([left[0], right[0], left[1], right[1]], axis=1)

    def total(self, first_half, second_half):
        even = self.inner == 0
        kept = jnp.where(even, first_half, second_half)
        sent = jnp.where(even, second_half, first_half).astype(LOW)
        pair = (kept.astype(WIDE) + swapped(sent, "tp", 1).astype(WIDE)).astype(LOW)
        both = (pair.astype(WIDE) + swapped(pair, "tp", 2).astype(WIDE)).astype(LOW)
        other = swapped(both, "tp", 1)
        return jnp.where(even, both, other), jnp.where(even, other, both)

    def scatter(self, full):
        rows, width = full.shape
        blocks = full.reshape(rows, 2, 2, width // 4)
        even = self.inner == 0
        kept = jnp.where(even, blocks[:, :, 0], blocks[:, :, 1])
        sent = jnp.where(even, blocks[:, :, 1], blocks[:, :, 0]).astype(LOW)
        pair = kept.astype(WIDE) + swapped(sent, "tp", 1).astype(WIDE)
        first = self.outer == 0
        mine = jnp.where(first, pair[:, 0], pair[:, 1])
        away = jnp.where(first, pair[:, 1], pair[:, 0]).astype(LOW)
        return mine + swapped(away, "tp", 2).astype(WIDE)

    def all_terms(self, full):
        low = full.astype(LOW)
        return [low] + [swapped(low, "tp", step) for step in (1, 2, 3)]

    def own_terms(self, full):
        width = full.shape[1] // 4
        blocks = [
            lax.dynamic_slice_in_dim(full, (self.rank ^ step) * width, width, 1).astype(LOW)
            for step in range(4)
        ]
        return blocks[:1] + [swapped(blocks[step], "tp", step) for step in (1, 2, 3)]

    def own(self, full, axis):
        width = full.shape[axis] // lax.axis_size("tp")
        return lax.dynamic_slice_in_dim(full, self.rank * width, width, axis)


class Shards:
    def __init__(self, tp):
        self.count = lax.axis_size("shard")
        self.rank = lax.axis_index("shard")
        self.ctx_rank = lax.axis_index("ctx")
        self.tp = tp
        self.paired = self.count == 2

    def weight(self, rows):
        if not self.paired:
            return (lax.all_gather(rows, "shard", axis=0, tiled=True),)
        return (rows, swapped(rows, "shard", 1))

    def split(self, full):
        if not self.paired:
            return (full,)
        width = full.shape[1] // 2
        return (
            lax.dynamic_slice_in_dim(full, self.rank * width, width, 1),
            lax.dynamic_slice_in_dim(full, (1 - self.rank) * width, width, 1),
        )

    def join(self, parts):
        if not self.paired:
            return parts[0]
        first = self.rank == 0
        return jnp.concatenate(
            [jnp.where(first, parts[0], parts[1]), jnp.where(first, parts[1], parts[0])], axis=1
        )

    def columns(self, full):
        if not self.paired:
            return lax.all_to_all(full, "shard", split_axis=1, concat_axis=0, tiled=True)
        own, other = self.split(full)
        width = own.shape[1] // 2
        part = lax.dynamic_slice_in_dim(other, self.tp.inner * width, width, 1)
        got = swapped(part, "shard", 1)
        rest = swapped(got, "tp", 1)
        even = self.tp.inner == 0
        peer = jnp.concatenate([jnp.where(even, got, rest), jnp.where(even, rest, got)], axis=1)
        return jnp.concatenate([own, peer], axis=0)

    def tokens(self, own):
        if not self.paired:
            return lax.all_gather(own, "shard", axis=0, tiled=True)
        return jnp.concatenate([own, swapped(own, "shard", 1)], axis=0)

    def own_total(self, product):
        if not self.paired:
            return lax.psum_scatter(product, "shard", scatter_dimension=0, tiled=True)
        rows = product.shape[0] // 2
        return product[:rows] + swapped(product[rows:].astype(LOW), "shard", 1).astype(WIDE)

    def own_tokens(self, product):
        if not self.paired:
            return lax.all_to_all(product.astype(LOW), "shard", split_axis=0, concat_axis=1, tiled=True)
        rows = product.shape[0] // 2
        return self.join([product[:rows].astype(LOW), swapped(product[rows:].astype(LOW), "shard", 1)])


def deal_routes(dealing, own_blocks, ctx_rank, per_dev, per_peer):
    send_order = jnp.argsort(own_blocks // per_dev, stable=True)
    wanted = jnp.where(dealing // per_dev == ctx_rank, 0, 1)
    chosen = jnp.argsort(wanted, axis=1, stable=True)[:, :per_peer]
    targets = (jnp.take_along_axis(dealing, chosen, 1) % per_dev).reshape(-1)
    return send_order, targets, jnp.argsort(targets), jnp.argsort(send_order)


def on_device(
    hidden_in,
    out_grad,
    seq_lengths,
    deal_order,
    in_weight,
    conv_weight,
    out_weight,
    norm1_gain,
    norm2_gain,
    gate_weight,
    up_weight,
    down_weight,
):
    ctx_size = lax.axis_size("ctx")
    ctx_rank = lax.axis_index("ctx")
    tp = Features()
    shards = Shards(tp)
    row_count, col_count = hidden_in.shape
    hidden_count = gate_weight.shape[1]
    weight_rows = in_weight.shape[0]
    per_dev = deal_order.shape[1] // ctx_size
    per_peer = per_dev // ctx_size
    block_rows = row_count // per_dev
    dealing = deal_order[0].reshape(ctx_size, per_dev)
    own_blocks = lax.dynamic_index_in_dim(dealing, ctx_rank, 0, keepdims=False)

    def reorder(values, index):
        blocks = values.reshape(per_dev, block_rows, values.shape[1])
        return blocks[index].reshape(row_count, values.shape[1])

    def to_packed(values):
        got = lax.all_to_all(
            reorder(values, send_order), "ctx", split_axis=0, concat_axis=0, tiled=True
        )
        return reorder(got, placing)

    def to_dealt(values):
        got = lax.all_to_all(
            reorder(values, targets), "ctx", split_axis=0, concat_axis=0, tiled=True
        )
        return reorder(got, returning)

    def weight_grads(lefts, rights, identity):
        flat = [value for group in rights for value in group]
        if shards.paired:
            summed = line_grads([group[0] for group in lefts], flat, identity)
            ends = [0]
            for value in flat:
                ends.append(ends[-1] + value.shape[1])
            return [summed[:, a:b] for a, b in zip(ends, ends[1:])]
        flat_lefts = [value for group in lefts for value in group]
        return [
            sum_line(contract_rows(left, shards.tokens(right)).astype(LOW), ctx_rank)
            for left, right in zip(flat_lefts, flat)
        ]

    lengths = seq_lengths[0]
    starts = jnp.cumsum(lengths) - lengths
    where_t = ctx_rank * row_count - 2 + jnp.arange(row_count + 4, dtype=jnp.int32)
    seq_begin = jnp.max(jnp.where(starts[None, :] <= where_t[:, None], starts[None, :], 0), axis=1)
    position = where_t - seq_begin
    first_own = (position[2 : row_count + 2] >= 1).astype(WIDE)[:, None]
    second_own = (position[2 : row_count + 2] >= 2).astype(WIDE)[:, None]
    first_next = (position[3 : row_count + 3] >= 1).astype(WIDE)[:, None]
    second_next = (position[4 : row_count + 4] >= 2).astype(WIDE)[:, None]
    conv_taps = conv_weight.astype(WIDE)
    gains = jnp.stack([norm1_gain, norm2_gain])

    if shards.paired:
        goes_to = own_blocks // per_dev
        slots = jnp.arange(per_dev, dtype=jnp.int32)
        sending = (goes_to[None, :] == slots[:, None]).astype(WIDE)
        wants = ctx_rank * per_dev + slots
        place = jnp.sum((dealing[None] == wants[:, None, None]).astype(WIDE), axis=2)
        *_, sums, dealt, dealt_out, small_sum = front(
            hidden_in, out_grad, sending, place, jnp.pad(gains.astype(WIDE), ((0, 6), (0, 0))),
            jnp.concatenate([first_own, second_own, first_next, second_next], axis=1), conv_taps,
            jnp.moveaxis(in_weight, 1, 0), out_weight, gate_weight, up_weight, down_weight,
        )
        block_dealt = reorder(dealt_out.reshape(row_count, col_count), goes_to)
        input_dealt = reorder(dealt.reshape(row_count, col_count), goes_to)
        ends = [hidden_count, 2 * hidden_count, 3 * hidden_count, 3 * hidden_count + col_count]
        ends += [ends[-1] + col_count, ends[-1] + 2 * col_count]
        down_total, gate_total, up_total, out_total, *in_parts = jnp.split(sums, ends, axis=1)
        in_total = jnp.moveaxis(jnp.stack(in_parts).astype(WIDE), 0, 1)
        down_total, gate_total, up_total, out_total = [
            value.astype(WIDE) for value in (down_total, gate_total, up_total, out_total)
        ]
    else:
        in_w = shards.weight(in_weight.reshape(weight_rows, -1))
        send_order, targets, placing, returning = deal_routes(dealing, own_blocks, ctx_rank, per_dev, per_peer)
        full_gains = tp.gather(gains).astype(WIDE)
        gain_one, gain_two = full_gains[0], full_gains[1]
        x_full = tp.gather(to_packed(hidden_in))
        out_w = shards.weight(out_weight)
        cot_full = tp.gather(to_packed(out_grad))
        gate_w, up_w = shards.weight(gate_weight), shards.weight(up_weight)
        x_float = x_full.astype(WIDE)
        scale_one = lax.rsqrt(jnp.mean(x_float * x_float, axis=1, keepdims=True) + EPS)
        normed_one = x_float * scale_one
        h_one = (normed_one * gain_one).astype(LOW)
        projected = matmul(h_one, in_w[0])
        b_part = projected[:, :col_count]
        c_part = projected[:, col_count : 2 * col_count]
        v_part = projected[:, 2 * col_count :]
        mixed = (b_part * v_part).astype(LOW)
        rim = shifted(mixed[-2:], "ctx", 1)
        extended = jnp.concatenate([rim, mixed], axis=0).astype(WIDE)
        prev_one = extended[1 : row_count + 1] * first_own
        prev_two = extended[0:row_count] * second_own
        conv_out = (
            conv_taps[0] * extended[2:] + conv_taps[1] * prev_one + conv_taps[2] * prev_two
        )
        gated = (c_part * conv_out).astype(LOW)
        mixer_halves = jnp.split(contract_cols(gated, out_w[0]), 2, axis=1)
        mixer_out = jnp.concatenate(tp.total(*mixer_halves), axis=1)
        resid = x_float + mixer_out.astype(WIDE)
        scale_two = lax.rsqrt(jnp.mean(resid * resid, axis=1, keepdims=True) + EPS)
        normed_two = resid * scale_two
        h_two = (normed_two * gain_two).astype(LOW)
        cot_cols, h_two_cols, h_one_cols = [shards.columns(v) for v in (cot_full, h_two, h_one)]
        gate_pre, up_pre = matmul(h_two, gate_w[0]), matmul(h_two, up_w[0])
        d_act = shards.own_total(matmul(cot_cols, down_weight))
        sigmoid_gate = jax.nn.sigmoid(gate_pre)
        silu_gate = gate_pre * sigmoid_gate
        d_gate = d_act * up_pre * sigmoid_gate * (1.0 + gate_pre * (1.0 - sigmoid_gate))
        ffn_rights = [v.astype(LOW) for v in (silu_gate * up_pre, d_gate, d_act * silu_gate)]
        act_all = shards.tokens(ffn_rights[0])
        dh_terms = tp.all_terms(
            contract_cols(ffn_rights[1], gate_w[0]) + contract_cols(ffn_rights[2], up_w[0])
        )
        dh_two = added(dh_terms)
        ffn_grads = weight_grads(
            [[cot_cols], [h_two_cols, h_two_cols]], [ffn_rights[:1], ffn_rights[1:]], 0
        )

        ffn_terms = tp.own_terms(shards.own_tokens(contract_cols(act_all, down_weight)))

        rim = shifted(mixed[-2:], "ctx", 1)
        extended = jnp.concatenate([rim, mixed], axis=0).astype(WIDE)
        prev_one = extended[1 : row_count + 1] * first_own
        prev_two = extended[0:row_count] * second_own
        mixed_float = extended[2:]

        gain_two_grad = tp.own(jnp.sum(dh_two * normed_two, axis=0), 0)
        d_resid = cot_full.astype(WIDE) + norm_back(dh_two, normed_two, scale_two, gain_two)
        d_resid_low = d_resid.astype(LOW)
        d_gated = sum(matmul(part, w) for part, w in zip(shards.split(d_resid_low), out_w))
        d_conv = (d_gated * c_part).astype(LOW)
        d_c_part = d_gated * conv_out
        rim_back = shifted(d_conv[:2], "ctx", -1)
        d_conv_float = d_conv.astype(WIDE)
        back_ext = jnp.concatenate([d_conv, rim_back], axis=0).astype(WIDE)
        d_mixed = (
            conv_taps[0] * d_conv_float
            + conv_taps[1] * back_ext[1 : row_count + 1] * first_next
            + conv_taps[2] * back_ext[2:] * second_next
        )
        taps_grad = jnp.stack(
            [
                jnp.sum(d_conv_float * mixed_float, axis=0),
                jnp.sum(d_conv_float * prev_one, axis=0),
                jnp.sum(d_conv_float * prev_two, axis=0),
            ]
        )
        d_proj = [
            (d_mixed * v_part).astype(LOW),
            d_c_part.astype(LOW),
            (d_mixed * b_part).astype(LOW),
        ]
        d_proj_flat = jnp.concatenate(d_proj, axis=1)
        dh_one_terms = tp.all_terms(shards.join([contract_cols(d_proj_flat, w) for w in in_w]))
        mixer_grads = weight_grads(
            [[shards.columns(d_resid_low)], [h_one_cols]], [[gated], [d_proj_flat]], 1
        )
        dh_one_terms, ffn_terms, mixer_grads = lax.optimization_barrier(
            (dh_one_terms, ffn_terms, mixer_grads)
        )
        dh_one = added(dh_one_terms)
        block_out = (tp.own(resid, 1) + added(ffn_terms)).astype(LOW)
        down_total, gate_total, up_total = [value.astype(WIDE) for value in ffn_grads]
        out_total, in_flat_total = [value.astype(WIDE) for value in mixer_grads]
        in_total = in_flat_total.reshape(in_weight.shape)
        gain_one_grad = tp.own(jnp.sum(dh_one * normed_one, axis=0), 0)
        d_input = d_resid + norm_back(dh_one, normed_one, scale_one, gain_one)
        dealt = to_dealt(jnp.concatenate([block_out, tp.own(d_input, 1).astype(LOW)], axis=1))
        block_dealt, input_dealt = dealt[:, :col_count], dealt[:, col_count:]
        small = jnp.concatenate([taps_grad, gain_one_grad[None], gain_two_grad[None]], axis=0)
        small_sum = butterfly_sum(butterfly_sum(small, "shard"), "ctx")

    return (
        block_dealt,
        input_dealt,
        in_total,
        small_sum[0:3],
        out_total,
        small_sum[3],
        small_sum[4],
        gate_total,
        up_total,
        down_total,
    )


def solution(mesh):
    placed = (
        P(("shard", "ctx"), "tp"),
        P(("shard", "ctx"), "tp"),
        P("shard", None),
        P("shard", None),
        P("shard", None, "tp"),
        P(None, "tp"),
        P("shard", "tp"),
        P("tp"),
        P("tp"),
        P("shard", "tp"),
        P("shard", "tp"),
        P("shard", "tp"),
    )
    return jax.shard_map(
        on_device,
        mesh=mesh,
        in_specs=placed,
        out_specs=(
            P(("shard", "ctx"), "tp"),
            P(("shard", "ctx"), "tp"),
            P("shard", None, "tp"),
            P(None, "tp"),
            P("shard", "tp"),
            P("tp"),
            P("tp"),
            P("shard", "tp"),
            P("shard", "tp"),
            P("shard", "tp"),
        ),
        check_vma=False,
    )
```

```python
import jax
import jax.numpy as jnp
from jax import lax
from jax.experimental import pallas as pl
from jax.experimental.pallas import tpu as pltpu
from jax.sharding import PartitionSpec as P

EPS = 1e-05
LOW = jnp.bfloat16
WIDE = jnp.float32
CHUNKS = 4


def shifted(value, axis, steps):
    count = lax.axis_size(axis)
    leading, last = (max(0, -steps), min(count, count - steps))
    return lax.ppermute(value, axis, [(source, source + steps) for source in range(leading, last)])


def swapped(value, axis, step):
    count = lax.axis_size(axis)
    return lax.ppermute(value, axis, [(source, source ^ step) for source in range(count)])


def matmul(left, right):
    return jnp.dot(left, right, preferred_element_type=WIDE)


def contract_rows(left, right):
    return lax.dot_general(left, right, (((0,), (0,)), ((), ())), preferred_element_type=WIDE)


def contract_cols(left, right):
    return lax.dot_general(left, right, (((1,), (1,)), ((), ())), preferred_element_type=WIDE)


def added(terms):
    return sum(term.astype(WIDE) for term in terms)


def norm_back(grad_out, normed, scale_row, gain):
    scaled = grad_out * gain
    return scale_row * (scaled - normed * jnp.mean(scaled * normed, axis=1, keepdims=True))


def butterfly_sum(value, axis):
    step = 1
    while step < lax.axis_size(axis):
        value = value + swapped(value, axis, step)
        step *= 2
    return value


def sum_line(piece, rank):
    from_end = lax.ppermute(piece, "ctx", [(0, 1), (3, 2)])
    half = (piece.astype(WIDE) + from_end.astype(WIDE)).astype(LOW)
    from_middle = lax.ppermute(half, "ctx", [(1, 2), (2, 1)])
    total = (half.astype(WIDE) + from_middle.astype(WIDE)).astype(LOW)
    handed = lax.ppermute(total, "ctx", [(1, 0), (2, 3)])
    inner = jnp.logical_or(rank == 1, rank == 2)
    return jnp.where(inner, total, handed)


PIECE = 256
AHEAD = 4
SLOTS = 4
TOTALS = 2
MESH = pl.DeviceIdType.MESH


def front_kernel(
    x_in, cot_in, sending, place, own_gains, masks, taps,
    in_w, out_w, gate_w, up_w, down_w,
    in_peer, out_peer, gate_peer, up_peer, outer_land, middle_land, rights_peer,
    x_out, h_one_out, mixer_out, act_out, grads, dealt, dealt_out, small_sums,
    x_blocks, cot_blocks, gains, gain_sums, small, small_got, x_got, cot_got, x_full, h_one, cot_full, cot_peer, h_two, h_two_peer, proj, mixed, gated, mixer, conv_v,
    out_v, rim, extended, away, pair, pair_got, both_got, dh_got,
    da_got, in_v, gu_v, down_v, dh_sum, ffn_v, right_v, outer_v, middle_v, held, totals, d_ext, edge_v, rim_back,
    send, recv, local, in_send, outer_recv, middle_recv, out_send, out_recv, own_done,
):
    shard = lax.axis_index("shard")
    ctx = lax.axis_index("ctx")
    tp = lax.axis_index("tp")
    core, outer = tp % 2, tp // 2
    core_mate = tp + 1 - 2 * core
    outer_mate = lax.rem(tp + 2, 4)
    ctx_mate = ctx + 1 - 2 * (ctx % 2)
    tokens, width = x_full.shape
    part = width // 4
    half = width // 2
    blocks, block_rows = x_blocks.shape[0], x_blocks.shape[1]
    rows = out_w.shape[0]
    own_rows = pl.ds(pl.multiple_of((ctx % 2) * (rows // 2), rows // 2), rows // 2)
    other_rows = pl.ds(pl.multiple_of((1 - ctx % 2) * (rows // 2), rows // 2), rows // 2)
    hidden = gate_w.shape[1]
    chunk = hidden // CHUNKS

    barrier = pltpu.get_barrier_semaphore()
    mates = [{"shard": 1 - shard}, {"tp": core_mate}, {"tp": outer_mate}]
    mates += [{"ctx": lax.rem(ctx + step, blocks)} for step in range(1, blocks)]
    for mate in mates:
        pl.semaphore_signal(barrier, inc=1, device_id=mate, device_id_type=MESH)
    pl.semaphore_wait(barrier, len(mates))

    names = {}

    def remote(name, src, dst, mate):
        place_of = names.setdefault(name, len(names))
        return pltpu.make_async_remote_copy(
            src_ref=src, dst_ref=dst, send_sem=send.at[place_of], recv_sem=recv.at[place_of],
            device_id=mate, device_id_type=MESH,
        )

    def columns(start, size):
        return pl.ds(pl.multiple_of(start * size, size), size)

    own_part = columns(tp, part)
    own_half, peer_half = columns(shard, half), columns(1 - shard, half)

    def deal(name, source, target, step):
        to, origin = lax.rem(ctx + step, blocks), lax.rem(ctx + blocks - step, blocks)
        out = remote(name + str(step), source.at[to], target.at[ctx], {"ctx": to})
        into = remote(name + str(step), source.at[to], target.at[origin], {"ctx": to})
        return out, into

    def gather(name, full):
        mate = columns(outer_mate, part)
        return (
            remote(name + "outer", full.at[:, own_part], full.at[:, own_part], {"tp": outer_mate}),
            remote(name + "core", full.at[:, own_part], full.at[:, own_part], {"tp": core_mate}),
            remote(name + "more", full.at[:, mate], full.at[:, mate], {"tp": core_mate}),
        )

    pieces = {}
    for index, name in enumerate("bvc"):
        column = (0, 2, 1)[index]
        pieces[name] = (in_w.at[column], in_peer.at[column])
    pieces["o"] = (out_w, out_peer)
    for index in range(CHUNKS):
        strip = pl.ds(index * chunk, chunk)
        pieces["g%d" % index] = (gate_w.at[:, strip], gate_peer.at[:, strip])
        pieces["u%d" % index] = (up_w.at[:, strip], up_peer.at[:, strip])

    direct = ["g2", "u2", "u3"]

    def over_shard(name):
        source, target = pieces[name]
        if name in direct:
            return remote(name + "x", source, target, {"shard": 1 - shard})
        return remote(name + "x", source.at[own_rows], target.at[own_rows], {"shard": 1 - shard})

    def over_ctx(name):
        target = pieces[name][1]
        return remote(name + "z", target.at[own_rows], target.at[own_rows], {"ctx": ctx_mate})

    def pump(name):
        over_shard(name).wait_recv()
        over_ctx(name).start()

    def load(index, source, target):
        return pltpu.make_async_copy(source, target, local.at[index])

    def own_weights(index):
        strip = pl.ds(index * chunk, chunk)
        room = gu_v if index % 2 == 0 else in_v
        base = 13 + 4 * (index % 2)
        return [
            load(base, gate_w.at[:, strip], room.at[0, 0]),
            load(base + 1, up_w.at[:, strip], room.at[0, 1]),
        ]

    def peer_weights(index):
        strip = pl.ds(index * chunk, chunk)
        room = gu_v if index % 2 == 0 else in_v
        base = 15 + 4 * (index % 2)
        return [
            load(base, gate_peer.at[:, strip], room.at[1, 0]),
            load(base + 1, up_peer.at[:, strip], room.at[1, 1]),
        ]

    def to_blocks(source, target):
        for to in range(blocks):
            total = sending[to, 0] * source[0:block_rows].astype(WIDE)
            for slot in range(1, blocks):
                lines = pl.ds(slot * block_rows, block_rows)
                total = total + sending[to, slot] * source[lines].astype(WIDE)
            target[to] = total.astype(LOW)

    for name in ("b", "v", "c", "o", "g0", "u0"):
        over_shard(name).start()
    gains[:, own_part] = own_gains[...]
    gain_outer, gain_core, gain_more = gather("gg", gains)
    gain_outer.start()
    gain_core.start()
    to_blocks(x_in, x_blocks)
    x_deals = [deal("x", x_blocks, x_got, step) for step in range(1, blocks)]
    cot_deals = [deal("cot", cot_blocks, cot_got, step) for step in range(1, blocks)]
    for out, _ in x_deals:
        out.start()
    own_loads = [load(index, in_w.at[index], in_v.at[0, index]) for index in range(3)]
    own_loads.append(load(3, out_w, out_v.at[0]))
    own_loads.append(load(4, down_w, down_v))
    for copy in own_loads + own_weights(0):
        copy.start()
    to_blocks(cot_in, cot_blocks)

    def packed(source, got, deals, full):
        got[ctx] = source[ctx]
        for _, into in deals:
            into.wait_recv()
        for index in range(blocks):
            total = place[index, 0] * got[0].astype(WIDE)
            for other in range(1, blocks):
                total = total + place[index, other] * got[other].astype(WIDE)
            full[index * block_rows : (index + 1) * block_rows, own_part] = total.astype(LOW)

    pump("b")
    packed(x_blocks, x_got, x_deals, x_full)
    x_outer, x_core, x_more = gather("xg", x_full)
    x_outer.start()
    x_core.start()
    for out, _ in cot_deals:
        out.start()
    pump("v")
    x_outer.wait_recv()
    x_more.start()
    packed(cot_blocks, cot_got, cot_deals, cot_full)
    cot_outer, cot_core, cot_more = gather("cg", cot_full)
    cot_outer.start()
    cot_core.start()
    gain_outer.wait_recv()
    gain_more.start()
    x_core.wait_recv()
    x_more.wait_recv()
    gain_core.wait_recv()
    gain_more.wait_recv()

    x_store = load(5, x_full, x_out)
    x_store.start()
    step = min(64, tokens)

    @pl.loop(0, tokens // step)
    def _(index):
        lines = pl.ds(pl.multiple_of(index * step, step), step)
        value = x_full[lines].astype(WIDE)
        scale = lax.rsqrt(jnp.mean(value * value, axis=1, keepdims=True) + EPS)
        h_one[lines] = (value * scale * gains[0:1]).astype(LOW)

    h_one_store = load(6, h_one, h_one_out)
    h_one_store.start()
    pump("c")

    class Columns:
        def __init__(self, name, full, got):
            size = half // 4
            source = pl.ds(pl.multiple_of((1 - shard) * half + tp * size, size), size)
            own, mate = columns(tp, size), columns(outer_mate, size)
            self.shard = remote(name + "x", full.at[:, source], got.at[:, own], {"shard": 1 - shard})
            self.outer = remote(name + "y", got.at[:, own], got.at[:, own], {"tp": outer_mate})
            self.core = remote(name + "c", got.at[:, own], got.at[:, own], {"tp": core_mate})
            self.more = remote(name + "m", got.at[:, mate], got.at[:, mate], {"tp": core_mate})

        def start(self):
            self.shard.start()

        def spread(self):
            self.shard.wait_recv()
            self.outer.start()
            self.core.start()

        def done(self):
            self.outer.wait_recv()
            self.more.start()
            self.core.wait()
            self.more.wait()
            self.outer.wait_send()

        def wait_send(self):
            self.shard.wait_send()

    cot_strip, cot_target = columns(2 * (1 - shard) + core, part), columns(core, part)
    cot_first = remote("ccx", cot_full.at[:, cot_strip], cot_peer.at[:, cot_target], {"shard": 1 - shard})
    cot_second = remote("ccc", cot_peer.at[:, cot_target], cot_peer.at[:, cot_target], {"tp": core_mate})
    tile = min(256, tokens)

    def over_tiles(body):
        @pl.loop(0, tokens // tile)
        def _(index):
            body(pl.ds(pl.multiple_of(index * tile, tile), tile))

    def project(column, name):
        target = load(column, in_peer.at[column], in_v.at[1, column])
        own_loads[column].wait()
        over_ctx(name).wait_recv()
        target.start()
        target.wait()

        def body(lines):
            proj[column, lines] = jnp.dot(
                h_one[lines, own_half], in_v[0, column], preferred_element_type=WIDE
            ) + jnp.dot(h_one[lines, peer_half], in_v[1, column], preferred_element_type=WIDE)

        over_tiles(body)

    project(0, "b")
    project(2, "v")
    edge = 16
    rim_copy = remote(
        "rim", mixed.at[pl.ds(tokens - edge, edge)], rim, {"ctx": lax.rem(ctx + 1, blocks)}
    )

    def mix(lines):
        value = (proj[0, lines] * proj[2, lines]).astype(LOW)
        mixed[lines] = value
        extended[pl.ds(lines.start + 8, tile)] = value.astype(WIDE)

    over_tiles(mix)

    @pl.when(ctx < blocks - 1)
    def _():
        rim_copy.start()

    pump("o")
    cot_outer.wait_recv()
    cot_more.start()
    project(1, "c")

    @pl.when(ctx > 0)
    def _():
        rim_copy.wait_recv()
        extended[0:8] = rim[8:16].astype(WIDE)

    @pl.when(ctx == 0)
    def _():
        extended[0:8] = jnp.zeros((8, part), WIDE)

    for start in range(0, tokens, tile):
        lines = pl.ds(start, tile)
        value = taps[0:1] * extended[pl.ds(start + 8, tile)]
        value = value + taps[1:2] * (extended[pl.ds(start + 7, tile)] * masks[lines, 0:1])
        value = value + taps[2:3] * (extended[pl.ds(start + 6, tile)] * masks[lines, 1:2])
        conv_v[lines] = value
        gated[lines] = (proj[1, lines] * value).astype(LOW)

    pump("g0")
    cot_core.wait_recv()
    cot_more.wait_recv()
    cot_first.start()
    over_shard("g1").start()
    out_load = load(3, out_peer, out_v.at[1])
    own_loads[3].wait()
    over_ctx("o").wait_recv()
    out_load.start()
    out_load.wait()

    def to_half(lines, which):
        return lax.dot_general(
            gated[lines], out_v[which], (((1,), (1,)), ((), ())), preferred_element_type=WIDE
        )

    stages = [pl.ds(start, tile) for start in range(0, tokens, tile)]
    hops = []
    for index, lines in enumerate(stages):
        first = remote("ma%d" % index, away.at[lines], pair_got.at[lines], {"tp": core_mate})
        second = remote("mb%d" % index, pair.at[lines], both_got.at[lines], {"tp": outer_mate})
        third = remote("mc%d" % index, mixer.at[core, lines], mixer.at[core, lines], {"tp": core_mate})
        hops.append((first, second, third))
        away[lines] = to_half(lines, 1 - core).astype(LOW)
        first.start()
    for index, lines in enumerate(stages):
        value = to_half(lines, core)
        hops[index][0].wait_recv()
        pair[lines] = (value + pair_got[lines].astype(WIDE)).astype(LOW)
        hops[index][1].start()

    da_send, da_own = h_one, x_full
    pump("u0")
    cot_first.wait_recv()
    cot_second.start()
    cot_second.wait()
    own_loads[4].wait()
    h_one_store.wait()

    def da_copy(index):
        strip = pl.ds(index * chunk, chunk)
        return remote("da%d" % index, da_send.at[:, strip], da_got.at[:, strip], {"shard": 1 - shard})

    for index in range(CHUNKS):
        strip = pl.ds(index * chunk, chunk)

        def send_part(lines):
            da_send[lines, strip] = jnp.dot(
                cot_peer[lines], down_v[:, strip], preferred_element_type=WIDE
            ).astype(LOW)

        over_tiles(send_part)
        if index == 0:
            da_copy(0).start()
            over_shard("u1").start()

    def act_store(index):
        return load(21 + index % 2, ffn_v.at[index % 2, 0], act_out.at[:, pl.ds(index * chunk, chunk)])

    def right_copy(index, kind):
        strip = pl.ds(kind * hidden + index * chunk, chunk)
        return remote(
            "r%d%d" % (index, kind), ffn_v.at[index % 2, kind], rights_peer.at[:, strip], {"shard": 1 - shard}
        )

    def right_load(index, kind):
        strip = pl.ds(kind * hidden + index * chunk, chunk)
        return load(23 + kind, rights_peer.at[:, strip], right_v.at[kind])

    def ready(index):
        for kind in "gu":
            if "%s%d" % (kind, index) not in direct:
                over_ctx("%s%d" % (kind, index)).wait_recv()
        for copy in peer_weights(index):
            copy.start()

    def feed(index, lines, kinds=(0, 1, 2)):
        room = gu_v if index % 2 == 0 else in_v
        slot = index % 2
        strip = pl.ds(index * chunk, chunk)

        def pre(kind):
            return jnp.dot(
                h_two[lines, own_half], room[0, kind], preferred_element_type=WIDE
            ) + jnp.dot(h_two[lines, peer_half], room[1, kind], preferred_element_type=WIDE)

        gate_pre, up_pre = pre(0), pre(1)
        sigmoid = jax.nn.sigmoid(gate_pre)
        silu = gate_pre * sigmoid
        if 0 in kinds:
            ffn_v[slot, 0, lines] = (silu * up_pre).astype(LOW)
        if 1 not in kinds:
            return
        d_act = da_own[lines, strip].astype(WIDE) + da_got[lines, strip].astype(WIDE)
        ffn_v[slot, 1, lines] = (
            d_act * up_pre * sigmoid * (1.0 + gate_pre * (1.0 - sigmoid))
        ).astype(LOW)
        ffn_v[slot, 2, lines] = (d_act * silu).astype(LOW)

    pump("g1")
    ready(0)
    tiles = [pl.ds(start, tile) for start in range(0, tokens, tile)]
    for index, lines in enumerate(stages):
        hops[index][1].wait_recv()
        mixer[core, lines] = (pair[lines].astype(WIDE) + both_got[lines].astype(WIDE)).astype(LOW)
        hops[index][2].start()
        hops[index][2].wait_recv()

        @pl.loop(0, tile // step)
        def _(turn, start=index * tile):
            lines = pl.ds(pl.multiple_of(start + turn * step, step), step)
            own = x_full[lines, own_half].astype(WIDE) + mixer[0, lines].astype(WIDE)
            other = x_full[lines, peer_half].astype(WIDE) + mixer[1, lines].astype(WIDE)
            total = jnp.sum(own * own, axis=1, keepdims=True) + jnp.sum(other * other, axis=1, keepdims=True)
            scale = lax.rsqrt(total / width + EPS)
            h_two[lines, own_half] = (own * scale * gains[1:2, own_half]).astype(LOW)
            h_two[lines, peer_half] = (other * scale * gains[1:2, peer_half]).astype(LOW)

        if index == 0:
            for copy in own_weights(0) + peer_weights(0):
                copy.wait()
        feed(0, lines, (0,))
    right_copy(0, 0).start()
    act_store(0).start()
    mixer_store = load(12, mixer, mixer_out)
    mixer_store.start()

    h_two_columns = Columns("hc", h_two, h_two_peer)
    h_two_columns.start()
    x_store.wait()
    for copy in (x_outer, x_core, x_more):
        copy.wait_send()

    def own_part_of(lines):
        for index in range(CHUNKS):
            strip = pl.ds(index * chunk, chunk)
            da_own[lines, strip] = jnp.dot(
                cot_full[lines, own_half], down_v[:, strip], preferred_element_type=WIDE
            ).astype(LOW)

    over_tiles(own_part_of)

    def turned(place_of, source, start, first):
        for row in range(0, half, 256):
            for line in range(0, tokens, 256):
                block = source[pl.ds(line, 256), pl.ds(pl.multiple_of(start + row, 256), 256)]
                down_v[pl.ds(row, 256), pl.ds(place_of * half + first + line, 256)] = block.T

    turned(0, cot_full, shard * half, 0)
    turned(0, cot_peer, 0, tokens)
    turned(1, h_two, shard * half, 0)

    def back(index, lines):
        room = gu_v if index % 2 == 0 else in_v
        slot = index % 2
        for place_of in range(2):
            term = lax.dot_general(
                ffn_v[slot, 1, lines], room[place_of, 0],
                (((1,), (1,)), ((), ())), preferred_element_type=WIDE,
            ) + lax.dot_general(
                ffn_v[slot, 2, lines], room[place_of, 1],
                (((1,), (1,)), ((), ())), preferred_element_type=WIDE,
            )
            if index > 0:
                term = term + dh_sum[place_of, lines]
            dh_sum[place_of, lines] = term

    def feed_start(index):
        da_copy(index).wait_recv()
        for copy in own_weights(index) + peer_weights(index):
            copy.wait()
        if index > 1:
            act_store(index - 2).wait()
            for kind in range(3):
                right_copy(index - 2, kind).wait_send()

    middle = jnp.logical_or(ctx == 1, ctx == 2)
    end = jnp.logical_not(middle)
    inward = jnp.where(ctx < 2, ctx + 1, ctx - 1)
    outward = jnp.where(ctx == 1, 0, 3)
    per_kind = chunk // PIECE
    per_chunk = 3 * per_kind
    ffn_pieces = CHUNKS * per_chunk
    pieces_in_all = ffn_pieces + 4 * part // PIECE
    line_rows = min(256, rows)

    def grad_columns(piece):
        index, turn = piece // per_chunk, piece % per_chunk
        kind, sub = turn // per_kind, turn % per_kind
        start = jnp.where(
            piece < ffn_pieces, kind * hidden + index * chunk + sub * PIECE, piece * PIECE
        )
        return pl.ds(pl.multiple_of(start, PIECE), PIECE)

    def inward_copy(piece, land, sems):
        return pltpu.make_async_remote_copy(
            src_ref=held.at[piece % SLOTS], dst_ref=land.at[piece], send_sem=in_send.at[piece],
            recv_sem=sems.at[piece], device_id={"ctx": inward}, device_id_type=MESH,
        )

    def outward_copy(piece):
        return pltpu.make_async_remote_copy(
            src_ref=totals.at[piece % TOTALS], dst_ref=grads.at[:, grad_columns(piece)], send_sem=out_send.at[piece],
            recv_sem=out_recv.at[piece], device_id={"ctx": outward}, device_id_type=MESH,
        )

    def total_store(piece):
        return pltpu.make_async_copy(totals.at[piece % TOTALS], grads.at[:, grad_columns(piece)], own_done.at[piece])

    def stage_in(piece, land, room):
        copy = pltpu.make_async_copy(land.at[piece], room, local.at[26])
        copy.start()
        copy.wait()

    def finish(piece):
        inward_copy(piece, middle_land, middle_recv).wait_recv()
        stage_in(piece, middle_land, middle_v)

        @pl.when(piece >= TOTALS)
        def _():
            outward_copy(piece - TOTALS).wait_send()
            total_store(piece - TOTALS).wait()

        @pl.loop(0, rows // line_rows)
        def _(start):
            lines = pl.ds(pl.multiple_of(start * line_rows, line_rows), line_rows)
            total = held[piece % SLOTS, lines].astype(WIDE) + middle_v[lines].astype(WIDE)
            totals[piece % TOTALS, lines] = total.astype(LOW)

        outward_copy(piece).start()
        total_store(piece).start()

    def grad_piece(piece):
        after = piece >= ffn_pieces
        turn = jnp.where(after, jnp.maximum(piece - ffn_pieces - per_kind, 0), piece % per_chunk)
        kind, sub = turn // per_kind, piece % per_kind
        slot = jnp.where(after, jnp.where(piece < ffn_pieces + per_kind, 1, 0), piece // per_chunk % 2)
        strip = pl.ds(pl.multiple_of(sub * PIECE, PIECE), PIECE)
        left_first = jnp.where(after, piece < ffn_pieces + per_kind, kind == 0)
        left = jnp.where(left_first, 0, half)

        @pl.when(piece >= SLOTS)
        def _():
            inward_copy(piece - SLOTS, outer_land, outer_recv).wait_send()

        def product(start):
            lines = pl.ds(pl.multiple_of(start * line_rows, line_rows), line_rows)
            own = jnp.dot(
                down_v[lines, pl.ds(pl.multiple_of(left, tokens), tokens)],
                ffn_v[slot, kind, :, strip],
                preferred_element_type=WIDE,
            )
            other = jnp.dot(
                down_v[lines, pl.ds(pl.multiple_of(left + tokens, tokens), tokens)],
                right_v[kind, :, strip],
                preferred_element_type=WIDE,
            )
            return lines, own + other

        @pl.when(end)
        def _():
            @pl.loop(0, rows // line_rows)
            def _(start):
                lines, value = product(start)
                held[piece % SLOTS, lines] = value.astype(LOW)

            inward_copy(piece, outer_land, outer_recv).start()

        @pl.when(middle)
        def _():
            inward_copy(piece, outer_land, outer_recv).wait_recv()
            stage_in(piece, outer_land, outer_v)

            @pl.loop(0, rows // line_rows)
            def _(start):
                lines, value = product(start)
                held[piece % SLOTS, lines] = (value + outer_v[lines].astype(WIDE)).astype(LOW)

            inward_copy(piece, middle_land, middle_recv).start()

            @pl.when(piece >= 1)
            def _():
                finish(piece - 1)

    def got_right(index, kind):
        right_copy(index, kind).wait_recv()
        copy = right_load(index, kind)
        copy.start()
        copy.wait()

    dh_away = remote("dh1", away, pair_got, {"tp": core_mate})
    dh_pair = remote("dh2", pair, dh_got, {"tp": outer_mate})
    dh_last = remote("dh3", mixer.at[core], mixer.at[core], {"tp": core_mate})
    def whole_feed(index):
        feed_start(index)
        for lines in tiles:
            feed(index, lines)
        act_store(index).start()

    def whole_back(index):
        for lines in tiles:
            back(index, lines)
        if index + 1 < CHUNKS:
            for copy in own_weights(index + 1):
                copy.start()

    da_copy(0).wait_recv()
    for lines in tiles:
        feed(0, lines, (1, 2))
    right_copy(0, 1).start()
    right_copy(0, 2).start()
    da_copy(1).start()
    whole_back(0)
    pump("u1")

    def event_start():
        got_right(0, 0)

    def event_columns():
        h_two_columns.done()
        turned(1, h_two_peer, 0, tokens)
        got_right(0, 1)

    def event_first():
        got_right(0, 2)
        ready(1)
        whole_feed(1)
        for kind in range(3):
            right_copy(1, kind).start()
        for name in ("g2", "u2"):
            over_shard(name).start()
        da_copy(2).start()
        over_shard("g3").start()

    def event_second():
        over_shard("g2").wait_recv()
        over_shard("u2").wait_recv()
        ready(2)
        whole_feed(2)
        right_copy(2, 0).start()
        right_copy(2, 1).start()
        over_shard("u3").start()
        right_copy(2, 2).start()
        da_copy(3).start()
        got_right(2, 0)

    def back_second():
        whole_back(2)
        pump("g3")

    back_blocks, d_resid, resid_own = cot_got, dh_sum.at[1, :, pl.ds(0, part)], dh_sum.at[1, :, pl.ds(part, part)]
    h_one_columns = Columns("ic", h_one_out, cot_peer)
    dr_columns = Columns("dc", h_two, h_two_peer)
    mixer_rights = 3 * hidden

    def mixer_right(kind):
        source = gated if kind == 0 else ffn_v.at[0, kind - 1]
        strip = pl.ds(mixer_rights + kind * part, part)
        return remote("m%d" % kind, source, rights_peer.at[:, strip], {"shard": 1 - shard})

    def got_mixer_right(kind):
        mixer_right(kind).wait_recv()
        room = right_v.at[max(kind - 1, 0)]
        copy = load(23, rights_peer.at[:, pl.ds(mixer_rights + kind * part, part)], room)
        copy.start()
        copy.wait()

    x_reload = load(5, x_out, x_full)
    mixer_reloads = [
        load(6, mixer_out.at[0], h_one.at[:, own_half]), load(7, mixer_out.at[1], h_one.at[:, peer_half])
    ]
    h_one_reload = load(8, h_one_out.at[:, own_half], dh_got)
    in_reloads = [load(13 + column, in_w.at[column], in_v.at[0, column]) for column in range(3)]
    in_reloads += [load(16 + column, in_peer.at[column], in_v.at[1, column]) for column in range(3)]
    fine = min(32, tokens)

    def reload():
        for index in range(CHUNKS):
            da_copy(index).wait_send()
        act_store(CHUNKS - 1).wait()
        act_store(CHUNKS - 2).wait()
        for copy in [x_reload] + mixer_reloads + in_reloads + down_loads + [act_own_load]:
            copy.start()

    def resid_back():
        dh_last.wait_recv()
        h_one_reload.start()
        for copy in [x_reload] + mixer_reloads:
            copy.wait()
        h_two_columns.wait_send()
        gain_sums[...] = jnp.zeros((2, width), WIDE)

        @pl.loop(0, tokens // fine)
        def _(index):
            lines = pl.ds(pl.multiple_of(index * fine, fine), fine)

            def halves(columns_of, which):
                resid = x_full[lines, columns_of].astype(WIDE) + h_one[lines, columns_of].astype(WIDE)
                return resid, mixer[which, lines].astype(WIDE)

            own, own_grad = halves(own_half, 0)
            other, other_grad = halves(peer_half, 1)
            total = jnp.sum(own * own, axis=1, keepdims=True) + jnp.sum(other * other, axis=1, keepdims=True)
            scale = lax.rsqrt(total / width + EPS)
            own, other = own * scale, other * scale
            own_scaled, other_scaled = own_grad * gains[1:2, own_half], other_grad * gains[1:2, peer_half]
            mean = (
                jnp.sum(own_scaled * own, axis=1, keepdims=True)
                + jnp.sum(other_scaled * other, axis=1, keepdims=True)
            ) / width
            h_two[lines, own_half] = (
                cot_full[lines, own_half].astype(WIDE) + scale * (own_scaled - own * mean)
            ).astype(LOW)
            h_two[lines, peer_half] = (
                cot_full[lines, peer_half].astype(WIDE) + scale * (other_scaled - other * mean)
            ).astype(LOW)
            gain_sums[1:2, own_half] += jnp.sum(own_grad * own, axis=0, keepdims=True)
            gain_sums[1:2, peer_half] += jnp.sum(other_grad * other, axis=0, keepdims=True)
            resid = x_full[lines, own_part].astype(WIDE) + h_one[lines, own_part].astype(WIDE)
            resid_own[lines] = resid
            which = jnp.where(outer == shard, 0, 1)
            scaled = mixer[which, lines, columns(core, part)].astype(WIDE) * gains[1:2, own_part]
            d_resid[lines] = cot_full[lines, own_part].astype(WIDE) + scale * (
                scaled - resid * scale * mean
            )

        dr_columns.start()

    rim_out = remote(
        "rim_back", edge_v, rim_back, {"ctx": lax.rem(ctx + blocks - 1, blocks)}
    )

    def conv_back():
        for kind in range(3):
            right_copy(CHUNKS - 2, kind).wait_send()

        def body(lines):
            d_gated = jnp.dot(
                h_two[lines, own_half], out_v[0], preferred_element_type=WIDE
            ) + jnp.dot(h_two[lines, peer_half], out_v[1], preferred_element_type=WIDE)
            d_ext[lines] = (d_gated * proj[1, lines]).astype(LOW).astype(WIDE)
            ffn_v[0, 1, lines] = (d_gated * conv_v[lines]).astype(LOW)

        for lines in tiles:
            body(lines)
        edge_v[...] = d_ext[0:16].astype(LOW)

        @pl.when(ctx > 0)
        def _():
            rim_out.start()

        turned(0, h_two, shard * half, 0)

    def out_ready():
        right_copy(CHUNKS - 1, 0).wait_send()

        def body(lines):
            ffn_v[1, 0, lines] = gated[lines]

        over_tiles(body)
        dr_columns.done()
        turned(0, h_two_peer, 0, tokens)
        got_mixer_right(0)

    def proj_back():
        @pl.when(ctx < blocks - 1)
        def _():
            rim_out.wait_recv()
            d_ext[tokens : tokens + 8] = rim_back[0:8].astype(WIDE)

        @pl.when(ctx == blocks - 1)
        def _():
            d_ext[tokens : tokens + 8] = jnp.zeros((8, part), WIDE)

        sums = [jnp.zeros((1, part), WIDE) for _ in range(3)]
        size = 128
        for start in range(0, tokens, size):
            lines = pl.ds(start, size)
            own = d_ext[lines]
            d_mixed = taps[0:1] * own
            d_mixed = d_mixed + taps[1:2] * (d_ext[pl.ds(start + 1, size)] * masks[lines, 2:3])
            d_mixed = d_mixed + taps[2:3] * (d_ext[pl.ds(start + 2, size)] * masks[lines, 3:4])
            ffn_v[0, 0, lines] = (d_mixed * proj[2, lines]).astype(LOW)
            ffn_v[0, 2, lines] = (d_mixed * proj[0, lines]).astype(LOW)
            for tap in range(3):
                value = own * extended[pl.ds(start + 8 - tap, size)]
                if tap > 0:
                    value = value * masks[lines, tap - 1 : tap]
                sums[tap] = sums[tap] + jnp.sum(value, axis=0, keepdims=True)
        small[...] = jnp.zeros(small.shape, WIDE)
        for tap in range(3):
            small[tap : tap + 1] = sums[tap]
        ffn_peer()
        mixer_right(1).start()
        ffn_first[0].start()
        mixer_right(2).start()
        ffn_first[1].start()
        mixer_right(3).start()

    def in_ready():
        h_one_reload.wait()
        turned(1, dh_got, 0, 0)
        h_one_columns.done()
        turned(1, cot_peer, 0, tokens)
        got_mixer_right(1)

    back_away = remote("bh1", away, pair_got, {"tp": core_mate})
    back_pair = remote("bh2", pair, both_got, {"tp": outer_mate})
    back_last = remote("bh3", mixer.at[core], mixer.at[core], {"tp": core_mate})

    def to_inputs(lines, which):
        total = None
        for column in range(3):
            term = lax.dot_general(
                ffn_v[0, column, lines], in_v[which, column],
                (((1,), (1,)), ((), ())), preferred_element_type=WIDE,
            )
            total = term if total is None else total + term
        return total

    def back_one_hop():
        for copy in (dh_away, dh_pair, dh_last):
            copy.wait_send()
        for copy in in_reloads:
            copy.wait()

        def body(lines):
            away[lines] = to_inputs(lines, 1 - core).astype(LOW)

        over_tiles(body)
        back_away.start()

        def rest(lines):
            dh_sum[0, lines] = to_inputs(lines, core)

        over_tiles(rest)

    def back_two_hops():
        back_away.wait_recv()

        def body(lines):
            pair[lines] = (dh_sum[0, lines] + pair_got[lines].astype(WIDE)).astype(LOW)

        over_tiles(body)
        back_pair.start()

    def back_three_hops():
        back_pair.wait_recv()

        def body(lines):
            mixer[core, lines] = (pair[lines].astype(WIDE) + both_got[lines].astype(WIDE)).astype(LOW)

        over_tiles(body)
        back_last.start()

    def give_back(name, block, target, step):
        to, origin = lax.rem(ctx + step, blocks), lax.rem(ctx + blocks - step, blocks)
        name = name + str(step)
        return (
            remote(name, block(to), target.at[ctx], {"ctx": to}),
            remote(name, block(to), target.at[origin], {"ctx": to}),
        )

    def out_block(to):
        return gated.at[pl.ds(pl.multiple_of(to * block_rows, block_rows), block_rows)]

    given = [give_back("give", lambda to: back_blocks.at[to], dealt, step) for step in range(1, blocks)]
    given_out = [give_back("out", out_block, dealt_out, step) for step in range(1, blocks)]
    kept = load(9, back_blocks.at[ctx], dealt.at[ctx])
    kept_out = load(10, out_block(ctx), dealt_out.at[ctx])

    down_loads = [
        load(index, down_w.at[:, pl.ds(index * chunk, chunk)], gu_v.at[index // 2, index % 2])
        for index in range(CHUNKS)
    ]
    act_own_load = load(21, act_out, da_got)
    act_peer_load = load(22, rights_peer.at[:, pl.ds(0, hidden)], da_got)
    ffn_first = [
        remote(
            "fx%d" % index, cot_full.at[:, pl.ds(half + index * part, part)],
            h_one.at[:, pl.ds(index * part, part)], {"shard": 1 - shard},
        )
        for index in range(2)
    ]
    ffn_core = [
        remote("fc0", cot_full.at[:, columns(1 - core, part)], out_v.at[0, pl.ds(0, tokens)], {"tp": core_mate}),
        remote("fc1", h_one.at[:, columns(1 - core, part)], out_v.at[1, pl.ds(0, tokens)], {"tp": core_mate}),
    ]
    kept_which = jnp.where(outer == shard, 0, 1)

    def ffn_pair(which):
        return pl.ds(pl.multiple_of(half + which * part, part), part)

    ffn_outer = [
        remote(
            "fy%d" % index,
            h_one.at[pl.ds(index * block_rows, block_rows), ffn_pair(1 - kept_which)],
            x_got.at[index],
            {"tp": outer_mate},
        )
        for index in range(blocks)
    ]

    def ffn_part(start):
        def body(lines):
            total = None
            for index in range(CHUNKS):
                term = lax.dot_general(
                    da_got[lines, pl.ds(index * chunk, chunk)], gu_v[index // 2, index % 2],
                    (((1,), (1,)), ((), ())), preferred_element_type=WIDE,
                )
                total = term if total is None else total + term
            cot_full[lines, pl.ds(start, half)] = total.astype(LOW)

        over_tiles(body)

    def ffn_own():
        for copy in (cot_outer, cot_core, cot_more, cot_first):
            copy.wait_send()
        for copy in down_loads:
            copy.wait()
        act_own_load.wait()
        ffn_part(0)
        act_peer_load.start()

    def ffn_peer():
        act_peer_load.wait()
        ffn_part(half)

    def ffn_to_core():
        for copy in ffn_first:
            copy.wait_recv()
        for copy in ffn_core:
            copy.start()

    def ffn_to_outer():
        for copy in ffn_core:
            copy.wait_recv()

        def body(lines):
            own = columns(core, part)
            h_one[lines, ffn_pair(0)] = (
                cot_full[lines, own].astype(WIDE) + out_v[0, lines].astype(WIDE)
            ).astype(LOW)
            h_one[lines, ffn_pair(1)] = (
                h_one[lines, own].astype(WIDE) + out_v[1, lines].astype(WIDE)
            ).astype(LOW)

        over_tiles(body)
        for copy in ffn_outer:
            copy.start()

    def block_back():
        mixer_right(0).wait_send()
        for index, copy in enumerate(ffn_outer):
            copy.wait_recv()
            lines = pl.ds(index * block_rows, block_rows)
            resid_own[lines] = (
                resid_own[lines] + h_one[lines, ffn_pair(kept_which)].astype(WIDE) + x_got[index].astype(WIDE)
            )
        for to in range(blocks):
            total = place[0, to] * resid_own[0:block_rows]
            for index in range(1, blocks):
                total = total + place[index, to] * resid_own[index * block_rows : (index + 1) * block_rows]
            gated[to * block_rows : (to + 1) * block_rows] = total.astype(LOW)
        for out, _ in given_out:
            out.start()
        kept_out.start()

    def input_back():
        back_last.wait_recv()

        @pl.loop(0, tokens // fine)
        def _(index):
            lines = pl.ds(pl.multiple_of(index * fine, fine), fine)
            own, other = x_full[lines, own_half].astype(WIDE), x_full[lines, peer_half].astype(WIDE)
            own_grad, other_grad = mixer[0, lines].astype(WIDE), mixer[1, lines].astype(WIDE)
            total = jnp.sum(own * own, axis=1, keepdims=True) + jnp.sum(other * other, axis=1, keepdims=True)
            scale = lax.rsqrt(total / width + EPS)
            own, other = own * scale, other * scale
            mean = (
                jnp.sum(own_grad * gains[0:1, own_half] * own, axis=1, keepdims=True)
                + jnp.sum(other_grad * gains[0:1, peer_half] * other, axis=1, keepdims=True)
            ) / width
            gain_sums[0:1, own_half] += jnp.sum(own_grad * own, axis=0, keepdims=True)
            gain_sums[0:1, peer_half] += jnp.sum(other_grad * other, axis=0, keepdims=True)
            which = jnp.where(outer == shard, 0, 1)
            scaled = mixer[which, lines, columns(core, part)].astype(WIDE) * gains[0:1, own_part]
            normed = x_full[lines, own_part].astype(WIDE) * scale
            d_resid[lines] = d_resid[lines] + scale * (scaled - normed * mean)

        for to in range(blocks):
            total = place[0, to] * d_resid[0:block_rows]
            for index in range(1, blocks):
                total = total + place[index, to] * d_resid[index * block_rows : (index + 1) * block_rows]
            back_blocks[to] = total.astype(LOW)
        for out, _ in given:
            out.start()
        kept.start()

    def event_third():
        over_shard("u3").wait_recv()
        ready(3)
        whole_feed(3)
        for kind in range(3):
            right_copy(3, kind).start()
        h_one_columns.start()
        mixer_right(0).start()
        got_right(2, 2)

    def dh_one_hop():
        whole_back(3)
        mixer_store.wait()
        for trio in hops:
            for copy in trio:
                copy.wait_send()

        def body(lines):
            away[lines] = dh_sum[1 - core, lines].astype(LOW)

        over_tiles(body)
        dh_away.start()

    def dh_two_hops():
        dh_away.wait_recv()

        def body(lines):
            pair[lines] = (dh_sum[core, lines] + pair_got[lines].astype(WIDE)).astype(LOW)

        over_tiles(body)
        dh_pair.start()
        reload()
        got_right(3, 0)

    def dh_three_hops():
        dh_pair.wait_recv()

        def body(lines):
            mixer[core, lines] = (pair[lines].astype(WIDE) + dh_got[lines].astype(WIDE)).astype(LOW)

        over_tiles(body)
        dh_last.start()
        got_right(3, 1)

    def rights_and_conv():
        got_right(3, 2)
        conv_back()

    def spread_columns():
        h_one_columns.spread()
        dr_columns.spread()
        ffn_own()

    def back_and_right():
        got_mixer_right(2)
        back_two_hops()

    def outer_and_back():
        got_mixer_right(3)
        ffn_to_outer()
        back_three_hops()

    def ends_back():
        block_back()
        input_back()
        small[3:5] = gain_sums[:, own_part]
        small_shard.start()

    small_shard = remote("ss", small, small_got.at[blocks], {"shard": 1 - shard})

    def small_ctx(step):
        to, origin = lax.rem(ctx + step, blocks), lax.rem(ctx + blocks - step, blocks)
        return (
            remote("sc%d" % step, small_got.at[ctx], small_got.at[ctx], {"ctx": to}),
            remote("sc%d" % step, small_got.at[ctx], small_got.at[origin], {"ctx": to}),
        )

    small_steps = [small_ctx(step) for step in range(1, blocks)]

    events = {
        0: event_start,
        1: h_two_columns.spread,
        2: event_columns,
        4: event_first,
        5: lambda: whole_back(1),
        6: lambda: got_right(1, 0),
        8: lambda: got_right(1, 1),
        10: lambda: got_right(1, 2),
        12: event_second,
        13: back_second,
        14: lambda: got_right(2, 1),
        16: event_third,
        17: dh_one_hop,
        18: dh_two_hops,
        20: dh_three_hops,
        21: resid_back,
        22: rights_and_conv,
        23: spread_columns,
        24: out_ready,
        25: proj_back,
        26: in_ready,
        27: back_one_hop,
        28: back_and_right,
        29: ffn_to_core,
        30: outer_and_back,
        31: ends_back,
    }

    @pl.loop(0, pieces_in_all)
    def _(piece):
        for turn, event in events.items():
            pl.when(piece == turn)(event)
        grad_piece(piece)

    small_shard.wait_recv()
    small_got[ctx] = small[...] + small_got[blocks]
    for out, _ in small_steps:
        out.start()

    @pl.when(middle)
    def _():
        finish(pieces_in_all - 1)

    for _, into in small_steps:
        into.wait_recv()
    total = small_got[0]
    for index in range(1, blocks):
        total = total + small_got[index]
    small_sums[...] = total

    for out, _ in x_deals + cot_deals:
        out.wait_send()
    for out, _ in small_steps:
        out.wait_send()
    for copy in (small_shard, gain_outer, gain_core, gain_more, h_one_columns, dr_columns, back_away, back_pair, back_last,
                 *ffn_first, *ffn_core, *ffn_outer):
        copy.wait_send()
    for name in pieces:
        over_shard(name).wait_send()
        if name not in direct:
            over_ctx(name).wait_send()
    for kind in (1, 2):
        right_copy(CHUNKS - 1, kind).wait_send()
    for kind in range(1, 4):
        mixer_right(kind).wait_send()
    kept.wait()
    kept_out.wait()
    for out, into in given + given_out:
        out.wait_send()
        into.wait_recv()

    @pl.when(ctx < blocks - 1)
    def _():
        rim_copy.wait_send()

    @pl.when(ctx > 0)
    def _():
        rim_out.wait_send()

    @pl.loop(0, pieces_in_all)
    def _(piece):
        @pl.when(piece >= pieces_in_all - SLOTS)
        def _():
            inward_copy(piece, outer_land, outer_recv).wait_send()

        @pl.when(jnp.logical_and(middle, piece >= pieces_in_all - TOTALS))
        def _():
            outward_copy(piece).wait_send()
            total_store(piece).wait()

        @pl.when(end)
        def _():
            outward_copy(piece).wait_recv()


FRONT_COPIES = 112


def front(x_in, cot_in, sending, place, own_gains, masks, taps, in_w, out_w, gate_w, up_w, down_w):
    tokens, part = x_in.shape
    blocks = place.shape[0]
    block_shape = (blocks, tokens // blocks, part)
    rows, hidden = gate_w.shape
    width = 4 * part
    half = width // 2
    chunk = hidden // CHUNKS
    pieces = (3 * hidden + width) // PIECE
    vmem = pl.BlockSpec(memory_space=pltpu.VMEM)
    hbm = pl.BlockSpec(memory_space=pl.ANY)
    shape = jax.ShapeDtypeStruct
    outs = [
        shape(in_w.shape, LOW),
        shape(out_w.shape, LOW),
        shape(gate_w.shape, LOW),
        shape(up_w.shape, LOW),
        shape((pieces, rows, PIECE), LOW),
        shape((pieces, rows, PIECE), LOW),
        shape((tokens, 3 * hidden + width + half), LOW),
        shape((tokens, width), LOW),
        shape((tokens, width), LOW),
        shape((2, tokens, half), LOW),
        shape((tokens, hidden), LOW),
        shape((rows, 3 * hidden + width), LOW),
        shape(block_shape, LOW),
        shape(block_shape, LOW),
        shape((8, part), WIDE),
    ]
    low, wide = (lambda *dims: pltpu.VMEM(dims, LOW)), (lambda *dims: pltpu.VMEM(dims, WIDE))
    dma = pltpu.SemaphoreType.DMA
    scratch = [
        low(*block_shape),
        low(*block_shape),
        wide(8, width),
        wide(2, width),
        wide(8, part),
        wide(blocks + 1, 8, part),
        low(*block_shape),
        low(*block_shape),
        low(tokens, width),
        low(tokens, width),
        low(tokens, width),
        low(tokens, half),
        low(tokens, width),
        low(tokens, half),
        wide(3, tokens, part),
        low(tokens, part),
        low(tokens, part),
        low(2, tokens, half),
        wide(tokens, part),
        low(2, rows, part),
        low(16, part),
        wide(tokens + 8, part),
        low(tokens, half),
        low(tokens, half),
        low(tokens, half),
        low(tokens, half),
        low(tokens, half),
        low(tokens, hidden),
        low(2, 3, rows, part),
        low(2, 2, rows, chunk),
        low(rows, hidden),
        wide(2, tokens, half),
        low(2, 3, tokens, chunk),
        low(3, tokens, chunk),
        low(rows, PIECE),
        low(rows, PIECE),
        low(SLOTS, rows, PIECE),
        low(TOTALS, rows, PIECE),
        wide(tokens + 8, part),
        low(16, part),
        low(16, part),
        dma((FRONT_COPIES,)),
        dma((FRONT_COPIES,)),
        dma((28,)),
    ] + [dma((pieces,)) for _ in range(6)]
    return pl.pallas_call(
        front_kernel,
        out_shape=outs,
        in_specs=[vmem, vmem] + [pl.BlockSpec(memory_space=pltpu.SMEM)] * 2 + [vmem] * 3
        + [hbm] * 5,
        out_specs=[hbm] * (len(outs) - 1) + [vmem],
        scratch_shapes=scratch,
        compiler_params=pltpu.CompilerParams(
            collective_id=2, has_side_effects=True, vmem_limit_bytes=63 * 1024 * 1024
        ),
        cost_estimate=pl.CostEstimate(
            flops=2 * tokens * width * hidden * 64, bytes_accessed=1 << 29, transcendentals=0
        ),
    )(x_in, cot_in, sending, place, own_gains, masks, taps, in_w, out_w, gate_w, up_w, down_w)


class Features:
    def __init__(self):
        rank = lax.axis_index("tp")
        self.rank = rank
        self.inner = rank % 2
        self.outer = rank // 2

    def gather(self, own):
        other = swapped(own, "tp", 2)
        first = self.outer == 0
        pair = jnp.stack([jnp.where(first, own, other), jnp.where(first, other, own)])
        more = swapped(pair, "tp", 1)
        even = self.inner == 0
        left, right = jnp.where(even, pair, more), jnp.where(even, more, pair)
        return jnp.concatenate([left[0], right[0], left[1], right[1]], axis=1)

    def total(self, first_half, second_half):
        even = self.inner == 0
        kept = jnp.where(even, first_half, second_half)
        sent = jnp.where(even, second_half, first_half).astype(LOW)
        pair = (kept.astype(WIDE) + swapped(sent, "tp", 1).astype(WIDE)).astype(LOW)
        both = (pair.astype(WIDE) + swapped(pair, "tp", 2).astype(WIDE)).astype(LOW)
        other = swapped(both, "tp", 1)
        return jnp.where(even, both, other), jnp.where(even, other, both)

    def scatter(self, full):
        rows, width = full.shape
        blocks = full.reshape(rows, 2, 2, width // 4)
        even = self.inner == 0
        kept = jnp.where(even, blocks[:, :, 0], blocks[:, :, 1])
        sent = jnp.where(even, blocks[:, :, 1], blocks[:, :, 0]).astype(LOW)
        pair = kept.astype(WIDE) + swapped(sent, "tp", 1).astype(WIDE)
        first = self.outer == 0
        mine = jnp.where(first, pair[:, 0], pair[:, 1])
        away = jnp.where(first, pair[:, 1], pair[:, 0]).astype(LOW)
        return mine + swapped(away, "tp", 2).astype(WIDE)

    def all_terms(self, full):
        low = full.astype(LOW)
        return [low] + [swapped(low, "tp", step) for step in (1, 2, 3)]

    def own_terms(self, full):
        width = full.shape[1] // 4
        blocks = [
            lax.dynamic_slice_in_dim(full, (self.rank ^ step) * width, width, 1).astype(LOW)
            for step in range(4)
        ]
        return blocks[:1] + [swapped(blocks[step], "tp", step) for step in (1, 2, 3)]

    def own(self, full, axis):
        width = full.shape[axis] // lax.axis_size("tp")
        return lax.dynamic_slice_in_dim(full, self.rank * width, width, axis)


class Shards:
    def __init__(self, tp):
        self.count = lax.axis_size("shard")
        self.rank = lax.axis_index("shard")
        self.ctx_rank = lax.axis_index("ctx")
        self.tp = tp
        self.paired = self.count == 2

    def weight(self, rows):
        if not self.paired:
            return (lax.all_gather(rows, "shard", axis=0, tiled=True),)
        return (rows, swapped(rows, "shard", 1))

    def split(self, full):
        if not self.paired:
            return (full,)
        width = full.shape[1] // 2
        return (
            lax.dynamic_slice_in_dim(full, self.rank * width, width, 1),
            lax.dynamic_slice_in_dim(full, (1 - self.rank) * width, width, 1),
        )

    def join(self, parts):
        if not self.paired:
            return parts[0]
        first = self.rank == 0
        return jnp.concatenate(
            [jnp.where(first, parts[0], parts[1]), jnp.where(first, parts[1], parts[0])], axis=1
        )

    def columns(self, full):
        if not self.paired:
            return lax.all_to_all(full, "shard", split_axis=1, concat_axis=0, tiled=True)
        own, other = self.split(full)
        width = own.shape[1] // 2
        part = lax.dynamic_slice_in_dim(other, self.tp.inner * width, width, 1)
        got = swapped(part, "shard", 1)
        rest = swapped(got, "tp", 1)
        even = self.tp.inner == 0
        peer = jnp.concatenate([jnp.where(even, got, rest), jnp.where(even, rest, got)], axis=1)
        return jnp.concatenate([own, peer], axis=0)

    def tokens(self, own):
        if not self.paired:
            return lax.all_gather(own, "shard", axis=0, tiled=True)
        return jnp.concatenate([own, swapped(own, "shard", 1)], axis=0)

    def own_total(self, product):
        if not self.paired:
            return lax.psum_scatter(product, "shard", scatter_dimension=0, tiled=True)
        rows = product.shape[0] // 2
        return product[:rows] + swapped(product[rows:].astype(LOW), "shard", 1).astype(WIDE)

    def own_tokens(self, product):
        if not self.paired:
            return lax.all_to_all(product.astype(LOW), "shard", split_axis=0, concat_axis=1, tiled=True)
        rows = product.shape[0] // 2
        return self.join([product[:rows].astype(LOW), swapped(product[rows:].astype(LOW), "shard", 1)])


def deal_routes(dealing, own_blocks, ctx_rank, per_dev, per_peer):
    send_order = jnp.argsort(own_blocks // per_dev, stable=True)
    wanted = jnp.where(dealing // per_dev == ctx_rank, 0, 1)
    chosen = jnp.argsort(wanted, axis=1, stable=True)[:, :per_peer]
    targets = (jnp.take_along_axis(dealing, chosen, 1) % per_dev).reshape(-1)
    return send_order, targets, jnp.argsort(targets), jnp.argsort(send_order)


def on_device(
    hidden_in,
    out_grad,
    seq_lengths,
    deal_order,
    in_weight,
    conv_weight,
    out_weight,
    norm1_gain,
    norm2_gain,
    gate_weight,
    up_weight,
    down_weight,
):
    ctx_size = lax.axis_size("ctx")
    ctx_rank = lax.axis_index("ctx")
    tp = Features()
    shards = Shards(tp)
    row_count, col_count = hidden_in.shape
    hidden_count = gate_weight.shape[1]
    weight_rows = in_weight.shape[0]
    per_dev = deal_order.shape[1] // ctx_size
    per_peer = per_dev // ctx_size
    block_rows = row_count // per_dev
    dealing = deal_order[0].reshape(ctx_size, per_dev)
    own_blocks = lax.dynamic_index_in_dim(dealing, ctx_rank, 0, keepdims=False)

    def reorder(values, index):
        blocks = values.reshape(per_dev, block_rows, values.shape[1])
        return blocks[index].reshape(row_count, values.shape[1])

    def to_packed(values):
        got = lax.all_to_all(
            reorder(values, send_order), "ctx", split_axis=0, concat_axis=0, tiled=True
        )
        return reorder(got, placing)

    def to_dealt(values):
        got = lax.all_to_all(
            reorder(values, targets), "ctx", split_axis=0, concat_axis=0, tiled=True
        )
        return reorder(got, returning)

    def weight_grads(lefts, rights, identity):
        flat = [value for group in rights for value in group]
        if shards.paired:
            summed = line_grads([group[0] for group in lefts], flat, identity)
            ends = [0]
            for value in flat:
                ends.append(ends[-1] + value.shape[1])
            return [summed[:, a:b] for a, b in zip(ends, ends[1:])]
        flat_lefts = [value for group in lefts for value in group]
        return [
            sum_line(contract_rows(left, shards.tokens(right)).astype(LOW), ctx_rank)
            for left, right in zip(flat_lefts, flat)
        ]

    lengths = seq_lengths[0]
    starts = jnp.cumsum(lengths) - lengths
    where_t = ctx_rank * row_count - 2 + jnp.arange(row_count + 4, dtype=jnp.int32)
    seq_begin = jnp.max(jnp.where(starts[None, :] <= where_t[:, None], starts[None, :], 0), axis=1)
    position = where_t - seq_begin
    first_own = (position[2 : row_count + 2] >= 1).astype(WIDE)[:, None]
    second_own = (position[2 : row_count + 2] >= 2).astype(WIDE)[:, None]
    first_next = (position[3 : row_count + 3] >= 1).astype(WIDE)[:, None]
    second_next = (position[4 : row_count + 4] >= 2).astype(WIDE)[:, None]
    conv_taps = conv_weight.astype(WIDE)
    gains = jnp.stack([norm1_gain, norm2_gain])

    if shards.paired:
        goes_to = own_blocks // per_dev
        slots = jnp.arange(per_dev, dtype=jnp.int32)
        sending = (goes_to[None, :] == slots[:, None]).astype(WIDE)
        wants = ctx_rank * per_dev + slots
        place = jnp.sum((dealing[None] == wants[:, None, None]).astype(WIDE), axis=2)
        *_, sums, dealt, dealt_out, small_sum = front(
            hidden_in, out_grad, sending, place, jnp.pad(gains.astype(WIDE), ((0, 6), (0, 0))),
            jnp.concatenate([first_own, second_own, first_next, second_next], axis=1), conv_taps,
            jnp.moveaxis(in_weight, 1, 0), out_weight, gate_weight, up_weight, down_weight,
        )
        block_dealt = reorder(dealt_out.reshape(row_count, col_count), goes_to)
        input_dealt = reorder(dealt.reshape(row_count, col_count), goes_to)
        ends = [hidden_count, 2 * hidden_count, 3 * hidden_count, 3 * hidden_count + col_count]
        ends += [ends[-1] + col_count, ends[-1] + 2 * col_count]
        down_total, gate_total, up_total, out_total, *in_parts = jnp.split(sums, ends, axis=1)
        in_total = jnp.moveaxis(jnp.stack(in_parts).astype(WIDE), 0, 1)
        down_total, gate_total, up_total, out_total = [
            value.astype(WIDE) for value in (down_total, gate_total, up_total, out_total)
        ]
    else:
        in_w = shards.weight(in_weight.reshape(weight_rows, -1))
        send_order, targets, placing, returning = deal_routes(dealing, own_blocks, ctx_rank, per_dev, per_peer)
        full_gains = tp.gather(gains).astype(WIDE)
        gain_one, gain_two = full_gains[0], full_gains[1]
        x_full = tp.gather(to_packed(hidden_in))
        out_w = shards.weight(out_weight)
        cot_full = tp.gather(to_packed(out_grad))
        gate_w, up_w = shards.weight(gate_weight), shards.weight(up_weight)
        x_float = x_full.astype(WIDE)
        scale_one = lax.rsqrt(jnp.mean(x_float * x_float, axis=1, keepdims=True) + EPS)
        normed_one = x_float * scale_one
        h_one = (normed_one * gain_one).astype(LOW)
        projected = matmul(h_one, in_w[0])
        b_part = projected[:, :col_count]
        c_part = projected[:, col_count : 2 * col_count]
        v_part = projected[:, 2 * col_count :]
        mixed = (b_part * v_part).astype(LOW)
        rim = shifted(mixed[-2:], "ctx", 1)
        extended = jnp.concatenate([rim, mixed], axis=0).astype(WIDE)
        prev_one = extended[1 : row_count + 1] * first_own
        prev_two = extended[0:row_count] * second_own
        conv_out = (
            conv_taps[0] * extended[2:] + conv_taps[1] * prev_one + conv_taps[2] * prev_two
        )
        gated = (c_part * conv_out).astype(LOW)
        mixer_halves = jnp.split(contract_cols(gated, out_w[0]), 2, axis=1)
        mixer_out = jnp.concatenate(tp.total(*mixer_halves), axis=1)
        resid = x_float + mixer_out.astype(WIDE)
        scale_two = lax.rsqrt(jnp.mean(resid * resid, axis=1, keepdims=True) + EPS)
        normed_two = resid * scale_two
        h_two = (normed_two * gain_two).astype(LOW)
        cot_cols, h_two_cols, h_one_cols = [shards.columns(v) for v in (cot_full, h_two, h_one)]
        gate_pre, up_pre = matmul(h_two, gate_w[0]), matmul(h_two, up_w[0])
        d_act = shards.own_total(matmul(cot_cols, down_weight))
        sigmoid_gate = jax.nn.sigmoid(gate_pre)
        silu_gate = gate_pre * sigmoid_gate
        d_gate = d_act * up_pre * sigmoid_gate * (1.0 + gate_pre * (1.0 - sigmoid_gate))
        ffn_rights = [v.astype(LOW) for v in (silu_gate * up_pre, d_gate, d_act * silu_gate)]
        act_all = shards.tokens(ffn_rights[0])
        dh_terms = tp.all_terms(
            contract_cols(ffn_rights[1], gate_w[0]) + contract_cols(ffn_rights[2], up_w[0])
        )
        dh_two = added(dh_terms)
        ffn_grads = weight_grads(
            [[cot_cols], [h_two_cols, h_two_cols]], [ffn_rights[:1], ffn_rights[1:]], 0
        )

        ffn_terms = tp.own_terms(shards.own_tokens(contract_cols(act_all, down_weight)))

        rim = shifted(mixed[-2:], "ctx", 1)
        extended = jnp.concatenate([rim, mixed], axis=0).astype(WIDE)
        prev_one = extended[1 : row_count + 1] * first_own
        prev_two = extended[0:row_count] * second_own
        mixed_float = extended[2:]

        gain_two_grad = tp.own(jnp.sum(dh_two * normed_two, axis=0), 0)
        d_resid = cot_full.astype(WIDE) + norm_back(dh_two, normed_two, scale_two, gain_two)
        d_resid_low = d_resid.astype(LOW)
        d_gated = sum(matmul(part, w) for part, w in zip(shards.split(d_resid_low), out_w))
        d_conv = (d_gated * c_part).astype(LOW)
        d_c_part = d_gated * conv_out
        rim_back = shifted(d_conv[:2], "ctx", -1)
        d_conv_float = d_conv.astype(WIDE)
        back_ext = jnp.concatenate([d_conv, rim_back], axis=0).astype(WIDE)
        d_mixed = (
            conv_taps[0] * d_conv_float
            + conv_taps[1] * back_ext[1 : row_count + 1] * first_next
            + conv_taps[2] * back_ext[2:] * second_next
        )
        taps_grad = jnp.stack(
            [
                jnp.sum(d_conv_float * mixed_float, axis=0),
                jnp.sum(d_conv_float * prev_one, axis=0),
                jnp.sum(d_conv_float * prev_two, axis=0),
            ]
        )
        d_proj = [
            (d_mixed * v_part).astype(LOW),
            d_c_part.astype(LOW),
            (d_mixed * b_part).astype(LOW),
        ]
        d_proj_flat = jnp.concatenate(d_proj, axis=1)
        dh_one_terms = tp.all_terms(shards.join([contract_cols(d_proj_flat, w) for w in in_w]))
        mixer_grads = weight_grads(
            [[shards.columns(d_resid_low)], [h_one_cols]], [[gated], [d_proj_flat]], 1
        )
        dh_one_terms, ffn_terms, mixer_grads = lax.optimization_barrier(
            (dh_one_terms, ffn_terms, mixer_grads)
        )
        dh_one = added(dh_one_terms)
        block_out = (tp.own(resid, 1) + added(ffn_terms)).astype(LOW)
        down_total, gate_total, up_total = [value.astype(WIDE) for value in ffn_grads]
        out_total, in_flat_total = [value.astype(WIDE) for value in mixer_grads]
        in_total = in_flat_total.reshape(in_weight.shape)
        gain_one_grad = tp.own(jnp.sum(dh_one * normed_one, axis=0), 0)
        d_input = d_resid + norm_back(dh_one, normed_one, scale_one, gain_one)
        dealt = to_dealt(jnp.concatenate([block_out, tp.own(d_input, 1).astype(LOW)], axis=1))
        block_dealt, input_dealt = dealt[:, :col_count], dealt[:, col_count:]
        small = jnp.concatenate([taps_grad, gain_one_grad[None], gain_two_grad[None]], axis=0)
        small_sum = butterfly_sum(butterfly_sum(small, "shard"), "ctx")

    return (
        block_dealt,
        input_dealt,
        in_total,
        small_sum[0:3],
        out_total,
        small_sum[3],
        small_sum[4],
        gate_total,
        up_total,
        down_total,
    )


def solution(mesh):
    placed = (
        P(("shard", "ctx"), "tp"),
        P(("shard", "ctx"), "tp"),
        P("shard", None),
        P("shard", None),
        P("shard", None, "tp"),
        P(None, "tp"),
        P("shard", "tp"),
        P("tp"),
        P("tp"),
        P("shard", "tp"),
        P("shard", "tp"),
        P("shard", "tp"),
    )
    return jax.shard_map(
        on_device,
        mesh=mesh,
        in_specs=placed,
        out_specs=(
            P(("shard", "ctx"), "tp"),
            P(("shard", "ctx"), "tp"),
            P("shard", None, "tp"),
            P(None, "tp"),
            P("shard", "tp"),
            P("tp"),
            P("tp"),
            P("shard", "tp"),
            P("shard", "tp"),
            P("shard", "tp"),
        ),
        check_vma=False,
    )
```
